128 devices in a mesh: member: 16 (over y_hi, x, core), grid: 8 (over z, y_lo).
Axes of the slice: x: 4, y: 4 (y_hi: 2, y_lo: 2; y = y_hi * 2 + y_lo), z: 4, core: 2. Of those that a mesh axis runs over, the one named last changes fastest.
Arguments:
- alpha_field: bfloat16 [16, 16, 512, 1024], P('member', None, 'grid'), may hold values from -6 to 6
- perturbation: bfloat16 [16, 2, 16, 512, 1024], P('member', None, None, 'grid'), may hold values from -1.5 to 1.5
- innovation: bfloat16 [2, 16, 512, 1024], P(None, None, 'grid'), may hold values from -6 to 6
- obs_weight: float32 [2, 16, 512], P(None, None, 'grid'), may hold values from 0.5 to 2
- row_class: int32 [16, 512], P(None, 'grid'), may hold values from 0 to 2
- column_class: int32 [16, 1024], P(None, 'grid'), may hold values from 0 to 2
- row_factor: bfloat16 [3, 1024, 1024], replicated, may hold values from 0 to 2, as said below
- column_factor: bfloat16 [3, 512, 512], replicated, may hold values from 0 to 2, as said below
- level_factor: bfloat16 [16, 16], replicated, may hold values from 0 to 2, as said below
Outputs:
- gradient: bfloat16 [16, 16, 512, 1024], P('member', None, 'grid')
- increment: bfloat16 [2, 16, 512, 1024], P(None, None, 'grid')
The draws below stay inside these ranges and needn't reach their ends.
Inputs may be any that keep to these rules, and one draw needn't show every extreme that they name: `row_factor`: zero below the diagonal. `column_factor`: zero below the diagonal. `level_factor`: zero below the diagonal.
All inputs are finite; a program needn't handle non-finite values.
Results may differ from the reference program's by a relative error of at most 0.023.
Values may be sent and summed in bfloat16 or wider, within the bound.
A program may use at most 128 MiB of HBM per device.

```python
import math
import jax
import jax.numpy as jnp
from jax import lax

NX = 1024
NY = 512
NZ = 16
NT = 2
NCLASS = 3
M = 16


def triangular(key, classes, order, short_len, long_len, rough_lo, rough_hi):
    key_len, key_rough = jax.random.split(key)
    scales = jnp.exp(jax.random.uniform(key_len, (classes, 1, 1), jnp.float32, jnp.log(short_len), jnp.log(long_len)))
    cells = jnp.arange(order, dtype=jnp.float32)
    offset = cells[None, :] - cells[:, None]
    rough = jax.random.uniform(key_rough, (classes, order, order), jnp.float32, rough_lo, rough_hi)
    decayed = jnp.exp(-jnp.maximum(offset, 0.0)[None] / scales) * rough / jnp.sqrt(scales)
    return jnp.where(offset[None] >= 0.0, decayed, 0.0)


def draw_row_factor(key, part):
    key = jax.random.fold_in(key, 11)
    table = triangular(key, NCLASS, NX, 4.0, 1.0 * NX, 0.5, 1.5)
    return table.astype(jnp.bfloat16)


def draw_column_factor(key, part):
    key = jax.random.fold_in(key, 12)
    table = triangular(key, NCLASS, NY, 3.0, 1.0 * NY, 0.5, 1.5)
    return table.astype(jnp.bfloat16)


def draw_level_factor(key, part):
    key = jax.random.fold_in(key, 13)
    table = triangular(key, 1, NZ, 1.0, 4.0, 0.5, 1.5)
    return table[0].astype(jnp.bfloat16)


def plant(drawn, own_key, low, high):
    longest = drawn.shape.index(max(drawn.shape))
    spots = []
    for shift in (0, 1):
        where = [jax.random.randint(jax.random.fold_in(own_key, axis), (), 0, length) for axis, length in enumerate(drawn.shape)]
        where[longest] = (where[longest] + shift) % drawn.shape[longest]
        spots.append(tuple(where))
    return drawn.at[spots[0]].set(low).at[spots[1]].set(high)


def block_levels(stream_key, dims, pieces, low, largest):
    def one(position, shards_of):
        draws = jax.random.uniform(jax.random.fold_in(jax.random.fold_in(stream_key, 6), position), (shards_of,), jnp.float32, low / len(pieces), largest / len(pieces))
        return jnp.repeat(jnp.exp(draws), dims[position] // shards_of).reshape((-1,) + (1,) * (len(dims) - position - 1))

    factor_of = one(*pieces[0])
    for cut in pieces[1:]:
        factor_of = factor_of * one(*cut)
    return factor_of


def scatter_about(rng, extent, width, reach, shards=(), held_as=jnp.bfloat16):
    entries = jax.random.normal(rng, extent, jnp.float32) * width
    if len(shards) > 0:
        entries = block_levels(rng, extent, shards, -0.22, 0.18) * entries
    return jnp.clip(entries, min=-reach, max=reach).astype(held_as)


def setup_inputs(seed: int = 0) -> dict:
    seeds = jax.random.split(jax.random.key(seed), 10)
    return {
        "alpha_field": scatter_about(seeds[0], (M, NZ, NY, NX), 1.0, 6.0, ((0, 16), (2, 8))),
        "perturbation": scatter_about(seeds[1], (M, NT, NZ, NY, NX), (M ** -0.5), 1.5, ((0, 16), (3, 8))),
        "innovation": scatter_about(seeds[2], (NT, NZ, NY, NX), 1.0, 6.0, ((2, 8),)),
        "obs_weight": jnp.clip(jnp.exp(math.log(2.0) - 1.3862944 * jax.random.uniform(seeds[3], (NT, NZ, NY), jnp.float32) ** block_levels(seeds[3], (NT, NZ, NY), ((2, 8),), -0.2, 0.2)), 0.5, 2.0),
        "row_class": plant(jax.random.randint(seeds[4], (NZ, NY), 0, NCLASS), jax.random.fold_in(seeds[4], 1), 0, NCLASS - 1).astype(jnp.int32),
        "column_class": plant(jax.random.randint(seeds[5], (NZ, NX), 0, NCLASS), jax.random.fold_in(seeds[5], 1), 0, NCLASS - 1).astype(jnp.int32),
        "row_factor": draw_row_factor(jax.random.fold_in(seeds[9], 71), 0),
        "column_factor": draw_column_factor(jax.random.fold_in(seeds[9], 71), 0),
        "level_factor": draw_level_factor(jax.random.fold_in(seeds[9], 71), 0),
    }


def row_filter(source, classes, factors):
    picks = classes[None] == jnp.arange(factors.shape[0], dtype=jnp.int32)[:, None, None]
    stacked = jnp.where(picks[:, None, :, :, None], source[None], jnp.zeros((), source.dtype))
    return jnp.einsum('cbzyj,cji->bzyi', stacked.astype(jnp.float32), factors.astype(jnp.float32), precision=lax.Precision.HIGHEST)


def row_adjoint(source, classes, factors):
    picks = classes[None] == jnp.arange(factors.shape[0], dtype=jnp.int32)[:, None, None]
    stacked = jnp.where(picks[:, None, :, :, None], source[None], jnp.zeros((), source.dtype))
    return jnp.einsum('cbzyi,cji->bzyj', stacked.astype(jnp.float32), factors.astype(jnp.float32), precision=lax.Precision.HIGHEST)


def column_filter(source, classes, factors):
    picks = classes[None] == jnp.arange(factors.shape[0], dtype=jnp.int32)[:, None, None]
    stacked = jnp.where(picks[:, None, :, None, :], source[None], jnp.zeros((), source.dtype))
    return jnp.einsum('cbzjx,cji->bzix', stacked.astype(jnp.float32), factors.astype(jnp.float32), precision=lax.Precision.HIGHEST)


def column_adjoint(source, classes, factors):
    picks = classes[None] == jnp.arange(factors.shape[0], dtype=jnp.int32)[:, None, None]
    stacked = jnp.where(picks[:, None, :, None, :], source[None], jnp.zeros((), source.dtype))
    return jnp.einsum('cbzix,cji->bzjx', stacked.astype(jnp.float32), factors.astype(jnp.float32), precision=lax.Precision.HIGHEST)


def level_filter(source, factor):
    return jnp.einsum('bzyx,zk->bkyx', source.astype(jnp.float32), factor.astype(jnp.float32), precision=lax.Precision.HIGHEST)


def level_adjoint(source, factor):
    return jnp.einsum('bkyx,zk->bzyx', source.astype(jnp.float32), factor.astype(jnp.float32), precision=lax.Precision.HIGHEST)


def reference(alpha_field, perturbation, innovation, obs_weight, row_class, column_class, row_factor, column_factor, level_factor):
    def localize(member):
        along_rows = row_filter(member[None], row_class, row_factor).astype(jnp.bfloat16)
        along_columns = column_filter(along_rows, column_class, column_factor).astype(jnp.bfloat16)
        return level_filter(along_columns, level_factor).astype(jnp.bfloat16)[0]

    localized = lax.map(localize, alpha_field)

    def accumulate(carry, items):
        pert_member, local_member = items
        return carry + pert_member.astype(jnp.float32) * local_member.astype(jnp.float32)[None], None

    summed, _ = lax.scan(accumulate, jnp.zeros(innovation.shape, jnp.float32), (perturbation, localized))
    increment = summed.astype(jnp.bfloat16)
    misfit = obs_weight[..., None] * (increment.astype(jnp.float32) - innovation.astype(jnp.float32))

    def adjoint(items):
        pert_member, member = items
        weighted = jnp.sum(pert_member.astype(jnp.float32) * misfit, axis=0)[None].astype(jnp.bfloat16)
        back_levels = level_adjoint(weighted, level_factor).astype(jnp.bfloat16)
        back_columns = column_adjoint(back_levels, column_class, column_factor).astype(jnp.bfloat16)
        back_rows = row_adjoint(back_columns, row_class, row_factor)[0]
        return (member.astype(jnp.float32) + back_rows).astype(jnp.bfloat16)

    gradient = lax.map(adjoint, (perturbation, alpha_field))
    return gradient, increment
```

```python
import functools

import jax
import jax.numpy as jnp
from jax import lax
from jax.experimental import pallas as pl
from jax.experimental.pallas import tpu as pltpu
from jax.sharding import PartitionSpec as P

MESH = pl.DeviceIdType.MESH
F32 = jnp.float32
BF16 = jnp.bfloat16

CLASSES = 3
LEVELS = 16
GROUP = 8
RING = 4
CHUNKS = 4
PART = LEVELS // CHUNKS
ROWS = 64
LANES = 128
NX = GROUP * LANES
NY = GROUP * ROWS
LINES = PART * ROWS
TILE = 256


def loop(count, body):
    def step(index, carry):
        body(index)
        return carry

    lax.fori_loop(0, count, step, 0)


def dot(a, b):
    return jnp.dot(a, b, preferred_element_type=F32)


def dot_nt(a, b):
    return lax.dot_general(a, b, (((1,), (1,)), ((), ())), preferred_element_type=F32)


def kernel(
    alpha_h, pert_h, innov_h, weight_ref, row_ref, col_ref, rowf_h, colf_h, level_ref,
    grad_h, inc_h,
    alpha_v, pert_v, innov_v, rowf, colf, colt, down, back, row_hot, col_hot, weight_v, masked,
    slabs, lines, filtered, local_s, local_r, core_s, core_r, x_r, y_s, y_r, inc, inc_v,
    load_sem, grad_sem, inc_sem,
    a2a_ss, a2a_rs, core_ss, core_rs, xr_ss, xr_rs, yr_ss, yr_rs,
    ya_ss, ya_rs, xa_ss, xa_rs, ca_ss, ca_rs,
):
    m = lax.axis_index("member")
    g = lax.axis_index("grid")
    y_hi = m // (2 * RING)
    x = lax.rem(m // 2, RING)
    core = lax.rem(m, 2)
    sibling = m + 1 - 2 * core
    across = m + 2 * RING - 4 * RING * y_hi

    def around(step):
        return lax.rem(x + step, RING)

    def x_peer(step):
        return y_hi * (2 * RING) + around(step) * 2 + core

    def lane(s):
        return pl.ds(pl.multiple_of(s * LANES, LANES), LANES)

    def slab_rows(s):
        return pl.ds(pl.multiple_of(s * ROWS, ROWS), ROWS)

    def part(c):
        return pl.ds(c * PART, PART)

    loads = [
        pltpu.make_async_copy(src, dst, load_sem.at[i])
        for i, (src, dst) in enumerate(
            ((alpha_h, alpha_v), (rowf_h, rowf), (colf_h, colf), (pert_h, pert_v), (innov_h, innov_v))
        )
    ]
    for load in loads:
        load.start()

    barrier = pltpu.get_barrier_semaphore()

    def greet(step):
        peer = lax.rem(g + step + 1, GROUP)
        pl.semaphore_signal(barrier, inc=1, device_id=(m, peer), device_id_type=MESH)

    loop(GROUP - 1, greet)
    for step in range(1, RING):
        pl.semaphore_signal(barrier, inc=1, device_id=(x_peer(step), g), device_id_type=MESH)
    pl.semaphore_signal(barrier, inc=1, device_id=(sibling, g), device_id_type=MESH)
    pl.semaphore_signal(barrier, inc=1, device_id=(across, g), device_id_type=MESH)

    diagonal = lax.broadcasted_iota(jnp.int32, (ROWS, ROWS), 0) == lax.broadcasted_iota(
        jnp.int32, (ROWS, ROWS), 1
    )

    def upright(line):
        spread = jnp.where(diagonal, jnp.broadcast_to(line, (ROWS, ROWS)), 0.0)
        return jnp.broadcast_to(jnp.sum(spread, axis=1, keepdims=True), (ROWS, LANES))

    def row_table(z):
        column = upright(row_ref[pl.ds(z, 1), :].astype(F32))
        for c in range(CLASSES):
            row_hot[c, slab_rows(z), :] = jnp.where(column == c, 1.0, 0.0).astype(BF16)

    def later_tables():
        def column_table(z):
            line = jnp.broadcast_to(col_ref[pl.ds(z, 1), :], (16, LANES))
            for c in range(CLASSES):
                col_hot[c, z] = jnp.where(line == c, 1.0, 0.0).astype(BF16)
            for t in range(2):
                weight_v[t, z] = upright(weight_ref[t, pl.ds(z, 1), :])

        loop(LEVELS, column_table)

        def level_table(b):
            spot = lax.broadcasted_iota(jnp.int32, (TILE, LEVELS), 0) // ROWS + b * PART
            pick = jnp.where(
                spot == lax.broadcasted_iota(jnp.int32, (TILE, LEVELS), 1), 1.0, 0.0
            ).astype(BF16)
            wide = (LEVELS, LEVELS * ROWS)
            spread = jnp.where(
                lax.broadcasted_iota(jnp.int32, wide, 0)
                == lax.broadcasted_iota(jnp.int32, wide, 1) // ROWS,
                1.0,
                0.0,
            ).astype(BF16)
            tall = (TILE, LEVELS * ROWS)
            same = lax.rem(lax.broadcasted_iota(jnp.int32, tall, 0), ROWS) == lax.rem(
                lax.broadcasted_iota(jnp.int32, tall, 1), ROWS
            )
            rows = pl.ds(pl.multiple_of(b * TILE, TILE), TILE)
            level = level_ref[...]
            down[rows, :] = jnp.where(
                same, dot(dot_nt(pick, level).astype(BF16), spread), 0.0
            ).astype(BF16)
            back[rows, :] = jnp.where(
                same, dot(dot(pick, level).astype(BF16), spread), 0.0
            ).astype(BF16)

        loop(CHUNKS, level_table)
        loads[2].wait()
        unit = jnp.where(
            lax.broadcasted_iota(jnp.int32, (NY, NY), 0)
            == lax.broadcasted_iota(jnp.int32, (NY, NY), 1),
            1.0,
            0.0,
        ).astype(BF16)

        def turn(c):
            colt[c] = dot_nt(unit, colf[c]).astype(BF16)

        loop(CLASSES, turn)
        loads[3].wait()
        loads[4].wait()

    def exchange(phase, c, src, dst):
        def send(step):
            peer = lax.rem(g + step + 1, GROUP)
            pltpu.make_async_remote_copy(
                src_ref=src(peer),
                dst_ref=dst(g),
                send_sem=a2a_ss.at[phase, c, peer],
                recv_sem=a2a_rs.at[phase, c, g],
                device_id=(m, peer),
                device_id_type=MESH,
            ).start()

        loop(GROUP - 1, send)

    def exchange_copy(phase, c, peer, block):
        return pltpu.make_async_remote_copy(
            src_ref=block,
            dst_ref=block,
            send_sem=a2a_ss.at[phase, c, peer],
            recv_sem=a2a_rs.at[phase, c, peer],
            device_id=(m, peer),
            device_id_type=MESH,
        )

    def arrived(phase, c, dst):
        def wait(step):
            peer = lax.rem(g + GROUP - 1 - step, GROUP)
            exchange_copy(phase, c, peer, dst(peer)).wait_recv()

        loop(GROUP - 1, wait)

    def sent(phase, c, src):
        def wait(step):
            peer = lax.rem(g + step + 1, GROUP)
            exchange_copy(phase, c, peer, src(peer)).wait_send()

        loop(GROUP - 1, wait)

    def line_block(c):
        return lambda s: lines.at[part(c), slab_rows(s), :]

    def filtered_block(c):
        return lambda s: filtered.at[part(c), slab_rows(s), :]

    def slab_block(c):
        return lambda s: slabs.at[c, s]

    def local_block(c):
        return lambda s: local_r.at[c, s]

    def mask_lines(c, source):
        for k in range(CLASSES):
            hot = row_hot[k, pl.ds(pl.multiple_of(c * LINES, LINES), LINES), :]
            masked[k] = source * jnp.concatenate([hot] * GROUP, axis=1)

    def row_filter(c):
        mask_lines(c, alpha_v[part(c)].reshape(LINES, NX))
        for n in range(NX // TILE):
            depth = (n + 1) * TILE
            total = sum(
                dot(masked[k, :, :depth], rowf[k, :depth, n * TILE : depth]) for k in range(CLASSES)
            ).astype(BF16)
            for half in range(2):
                slabs[c, 2 * n + half] = total[:, half * LANES : (half + 1) * LANES].reshape(
                    PART, ROWS, LANES
                )
        lines[part(c), slab_rows(g), :] = slabs[c, g]
        exchange(0, c, slab_block(c), line_block(c))

    def column_pass(c, table, upper):
        def pair(i):
            z = c * PART + 2 * i
            whole = jnp.concatenate([lines[z], lines[z + 1]], axis=1)
            blocks = []
            for k in range(CLASSES):
                hot = jnp.concatenate([col_hot[k, z], col_hot[k, z + 1]], axis=1)
                blocks.append(
                    (whole.reshape(NY // 16, 16, TILE) * hot[None]).reshape(NY, TILE)
                )
            half = NY // 2
            if upper:
                first = sum(dot(table[k, :half, :], blocks[k]) for k in range(CLASSES))
                second = sum(dot(table[k, half:, half:], blocks[k][half:]) for k in range(CLASSES))
            else:
                first = sum(dot(table[k, :half, :half], blocks[k][:half]) for k in range(CLASSES))
                second = sum(dot(table[k, half:, :], blocks[k]) for k in range(CLASSES))
            for j in range(2):
                side = slice(j * LANES, (j + 1) * LANES)
                filtered[z + j, :half, :] = first[:, side].astype(BF16)
                filtered[z + j, half:, :] = second[:, side].astype(BF16)

        loop(PART // 2, pair)

    def column_filter(c):
        arrived(0, c, line_block(c))
        column_pass(c, colt, False)

        def pair(i):
            def add(q, total):
                block = jnp.concatenate(
                    [
                        filtered[part(q), slab_rows(2 * i + j), :].reshape(TILE, LANES)
                        for j in range(2)
                    ],
                    axis=1,
                )
                table = down[
                    pl.ds(pl.multiple_of(c * TILE, TILE), TILE),
                    pl.ds(pl.multiple_of(q * TILE, TILE), TILE),
                ]
                return total + dot(table, block)

            total = lax.fori_loop(0, c + 1, add, jnp.zeros((TILE, 2 * LANES), F32)).astype(BF16)
            for j in range(2):
                local_s[c, 2 * i + j] = total[:, j * LANES : (j + 1) * LANES].reshape(
                    PART, ROWS, LANES
                )

        loop(GROUP // 2, pair)
        local_r[c, g] = local_s[c, g]
        exchange(1, c, lambda s: local_s.at[c, s], local_block(c))

    def core_copy(c):
        return pltpu.make_async_remote_copy(
            src_ref=core_s.at[c],
            dst_ref=core_r.at[c],
            send_sem=core_ss.at[c],
            recv_sem=core_rs.at[c],
            device_id=(sibling, g),
            device_id_type=MESH,
        )

    def x_copy(c, step):
        return pltpu.make_async_remote_copy(
            src_ref=core_r.at[c, pl.ds(2 * around(step), 2)],
            dst_ref=x_r.at[c, step - 1],
            send_sem=xr_ss.at[c, step - 1],
            recv_sem=xr_rs.at[c, step - 1],
            device_id=(x_peer(step), g),
            device_id_type=MESH,
        )

    def y_copy(c):
        return pltpu.make_async_remote_copy(
            src_ref=y_s.at[c],
            dst_ref=y_r.at[c],
            send_sem=yr_ss.at[c],
            recv_sem=yr_rs.at[c],
            device_id=(across, g),
            device_id_type=MESH,
        )

    def term(t, c, s):
        return pert_v[t, part(c), :, lane(s)].astype(F32) * local_r[c, s].astype(F32)

    def sum_core(c):
        arrived(1, c, local_block(c))

        def one(s):
            core_s[c, s] = term(1 - core, c, s).astype(BF16)

        loop(GROUP, one)
        core_copy(c).start()

    def sum_x(c):
        core_copy(c).wait_recv()

        def one(s):
            core_r[c, s] = (term(core, c, s) + core_r[c, s].astype(F32)).astype(BF16)

        loop(GROUP, one)
        for step in (2, 1, 3):
            x_copy(c, step).start()

    def x_total(c, j):
        total = core_r[c, 2 * x + j].astype(F32)
        for step in range(1, RING):
            total += x_r[c, step - 1, j].astype(F32)
        return total

    def sum_y(c):
        for step in range(1, RING):
            x_copy(c, step).wait_recv()
        y_s[c] = x_total(c, 1 - y_hi).astype(BF16)
        y_copy(c).start()

    def give(ss, rs, t, c, s, member):
        return pltpu.make_async_remote_copy(
            src_ref=inc.at[t, c, s],
            dst_ref=inc.at[t, c, s],
            send_sem=ss,
            recv_sem=rs,
            device_id=(member, g),
            device_id_type=MESH,
        )

    def give_y(c, s):
        return give(ya_ss.at[c], ya_rs.at[c], core, c, s, across)

    def give_x(c, turn, s, step):
        return give(
            xa_ss.at[c, turn, step - 1], xa_rs.at[c, turn, step - 1], core, c, s, x_peer(step)
        )

    def give_core(t, c, s):
        return give(ca_ss.at[c, s], ca_rs.at[c, s], t, c, s, sibling)

    mine = 2 * x + y_hi
    other = 2 * x + 1 - y_hi

    def finish(c):
        y_copy(c).wait_recv()
        inc[core, c, mine] = (x_total(c, y_hi) + y_r[c].astype(F32)).astype(BF16)
        give_y(c, mine).start()
        for step in (2, 1, 3):
            give_x(c, 0, mine, step).start()
        give_core(core, c, mine).start()

    def gather_x(c):
        give_y(c, other).wait_recv()
        for step in (2, 1, 3):
            give_x(c, 1, other, step).start()
        give_core(core, c, other).start()

    def from_x(c, turn, step):
        s = 2 * around(RING - step) + (y_hi if turn == 0 else 1 - y_hi)
        return s, give_x(c, turn, s, step)

    def gather_core(c):
        for turn in range(2):
            for step in (1, 3, 2):
                s, copy = from_x(c, turn, step)
                copy.wait_recv()
                give_core(core, c, s).start()

    def weigh(c):
        def one(s):
            give_core(1 - core, c, s).wait_recv()
            total = jnp.zeros((PART, ROWS, LANES), F32)
            for t in range(2):
                block = inc[t, c, s]
                inc_v[t, part(c), :, lane(s)] = block
                misfit = weight_v[t, part(c)] * (
                    block.astype(F32) - innov_v[t, part(c), :, lane(s)].astype(F32)
                )
                total += pert_v[t, part(c), :, lane(s)].astype(F32) * misfit
            core_s[c, s] = total.astype(BF16)

        core_copy(c).wait_send()
        loop(GROUP, one)
        inc_copy(c).start()

    def inc_copy(c):
        return pltpu.make_async_copy(
            inc_v.at[:, part(c)], inc_h.at[:, part(c)], inc_sem.at[c]
        )

    def level_adjoint(c):
        sent(0, c, slab_block(c))

        def pair(i):
            def add(q, total):
                block = jnp.concatenate(
                    [core_s[q, 2 * i + j].reshape(TILE, LANES) for j in range(2)], axis=1
                )
                table = back[
                    pl.ds(pl.multiple_of(c * TILE, TILE), TILE),
                    pl.ds(pl.multiple_of(q * TILE, TILE), TILE),
                ]
                return total + dot(table, block)

            total = lax.fori_loop(c, CHUNKS, add, jnp.zeros((TILE, 2 * LANES), F32)).astype(BF16)
            for j in range(2):
                slabs[c, 2 * i + j] = total[:, j * LANES : (j + 1) * LANES].reshape(
                    PART, ROWS, LANES
                )

        loop(GROUP // 2, pair)
        lines[part(c), slab_rows(g), :] = slabs[c, g]
        exchange(2, c, slab_block(c), line_block(c))

    def column_adjoint(c):
        arrived(2, c, line_block(c))
        column_pass(c, colf, True)
        local_r[c, g] = filtered[part(c), slab_rows(g), :]
        exchange(3, c, filtered_block(c), local_block(c))

    def grad_copy(c):
        return pltpu.make_async_copy(alpha_v.at[part(c)], grad_h.at[part(c)], grad_sem.at[c])

    def row_adjoint(c):
        arrived(3, c, local_block(c))
        mask_lines(
            c, jnp.concatenate([local_r[c, s].reshape(LINES, LANES) for s in range(GROUP)], axis=1)
        )
        for n in range(NX // TILE):
            start = n * TILE
            total = sum(
                dot_nt(masked[k, :, start:], rowf[k, start : start + TILE, start:])
                for k in range(CLASSES)
            )
            side = slice(start, start + TILE)
            alpha = alpha_v[part(c), :, side].reshape(LINES, TILE).astype(F32)
            alpha_v[part(c), :, side] = (alpha + total).astype(BF16).reshape(PART, ROWS, TILE)
        grad_copy(c).start()

    loop(LEVELS, row_table)
    loads[0].wait()
    loads[1].wait()
    pl.semaphore_wait(barrier, GROUP + RING)

    def at(step, offset, stage):
        chunk = step - offset

        @pl.when(jnp.logical_and(chunk >= 0, chunk < CHUNKS))
        def _():
            stage(chunk)

    def forward(step):
        at(step, 0, row_filter)

        @pl.when(step == 0)
        def _():
            later_tables()

        at(step, 3, sum_y)
        at(step, 1, column_filter)
        at(step, 3, finish)
        at(step, 2, sum_core)
        at(step, 3, gather_x)
        at(step, 2, sum_x)
        at(step, 4, gather_core)
        at(step, 4, weigh)

    loop(CHUNKS + 4, forward)

    def backward(step):
        at(step, 0, lambda c: level_adjoint(CHUNKS - 1 - c))
        at(step, 1, lambda c: column_adjoint(CHUNKS - 1 - c))
        at(step, 2, lambda c: row_adjoint(CHUNKS - 1 - c))

    loop(CHUNKS + 2, backward)

    def drain(c):
        sent(1, c, lambda s: local_s.at[c, s])
        sent(2, c, slab_block(c))
        sent(3, c, filtered_block(c))
        y_copy(c).wait_send()
        give_y(c, mine).wait_send()
        for step in range(1, RING):
            x_copy(c, step).wait_send()
            give_x(c, 0, mine, step).wait_send()
            give_x(c, 1, other, step).wait_send()

        def one(s):
            give_core(core, c, s).wait_send()

        loop(GROUP, one)
        inc_copy(c).wait()
        grad_copy(c).wait()

    loop(CHUNKS, drain)


def on_device(alpha, pert, innov, weight, row_class, col_class, rowf, colf, level):
    any_spec = pl.BlockSpec(memory_space=pl.ANY)
    vmem_spec = pl.BlockSpec(memory_space=pltpu.VMEM)
    dma = pltpu.SemaphoreType.DMA
    block = (PART, ROWS, LANES)
    slab = (CHUNKS, GROUP) + block
    scratch = [
        pltpu.VMEM((LEVELS, ROWS, NX), BF16),
        pltpu.VMEM((2, LEVELS, ROWS, NX), BF16),
        pltpu.VMEM((2, LEVELS, ROWS, NX), BF16),
        pltpu.VMEM((CLASSES, NX, NX), BF16),
        pltpu.VMEM((CLASSES, NY, NY), BF16),
        pltpu.VMEM((CLASSES, NY, NY), BF16),
        pltpu.VMEM((LEVELS * ROWS, LEVELS * ROWS), BF16),
        pltpu.VMEM((LEVELS * ROWS, LEVELS * ROWS), BF16),
        pltpu.VMEM((CLASSES, LEVELS * ROWS, LANES), BF16),
        pltpu.VMEM((CLASSES, LEVELS, 16, LANES), BF16),
        pltpu.VMEM((2, LEVELS, ROWS, LANES), F32),
        pltpu.VMEM((CLASSES, LINES, NX), BF16),
        pltpu.VMEM(slab, BF16),
        pltpu.VMEM((LEVELS, NY, LANES), BF16),
        pltpu.VMEM((LEVELS, NY, LANES), BF16),
        pltpu.VMEM(slab, BF16),
        pltpu.VMEM(slab, BF16),
        pltpu.VMEM(slab, BF16),
        pltpu.VMEM(slab, BF16),
        pltpu.VMEM((CHUNKS, RING - 1, 2) + block, BF16),
        pltpu.VMEM((CHUNKS,) + block, BF16),
        pltpu.VMEM((CHUNKS,) + block, BF16),
        pltpu.VMEM((2,) + slab, BF16),
        pltpu.VMEM((2, LEVELS, ROWS, NX), BF16),
        dma((5,)),
        dma((CHUNKS,)),
        dma((CHUNKS,)),
        dma((4, CHUNKS, GROUP)),
        dma((4, CHUNKS, GROUP)),
        dma((CHUNKS,)),
        dma((CHUNKS,)),
        dma((CHUNKS, RING - 1)),
        dma((CHUNKS, RING - 1)),
        dma((CHUNKS,)),
        dma((CHUNKS,)),
        dma((CHUNKS,)),
        dma((CHUNKS,)),
        dma((CHUNKS, 2, RING - 1)),
        dma((CHUNKS, 2, RING - 1)),
        dma((CHUNKS, GROUP)),
        dma((CHUNKS, GROUP)),
    ]
    gradient, increment = pl.pallas_call(
        kernel,
        out_shape=(
            jax.ShapeDtypeStruct((LEVELS, ROWS, NX), BF16),
            jax.ShapeDtypeStruct((2, LEVELS, ROWS, NX), BF16),
        ),
        in_specs=[any_spec] * 3 + [vmem_spec] * 3 + [any_spec] * 2 + [vmem_spec],
        out_specs=(any_spec, any_spec),
        scratch_shapes=scratch,
        compiler_params=pltpu.CompilerParams(
            collective_id=0, has_side_effects=True, vmem_limit_bytes=62 * 1024 * 1024
        ),
    )(alpha[0], pert[0], innov, weight, row_class, col_class, rowf, colf, level)
    return gradient[None], increment


def solution(mesh):
    return jax.shard_map(
        on_device,
        mesh=mesh,
        in_specs=(
            P("member", None, "grid", None),
            P("member", None, None, "grid", None),
            P(None, None, "grid", None),
            P(None, None, "grid"),
            P(None, "grid"),
            P(None, "grid"),
            P(),
            P(),
            P(),
        ),
        out_specs=(P("member", None, "grid", None), P(None, None, "grid", None)),
        check_vma=False,
    )
```

```python
import functools

import jax
import jax.numpy as jnp
from jax import lax
from jax.experimental import pallas as pl
from jax.experimental.pallas import tpu as pltpu
from jax.sharding import PartitionSpec as P

MESH = pl.DeviceIdType.MESH
F32 = jnp.float32
BF16 = jnp.bfloat16

CLASSES = 3
LEVELS = 16
GROUP = 8
RING = 4
CHUNKS = 4
PART = LEVELS // CHUNKS
ROWS = 64
LANES = 128
NX = GROUP * LANES
NY = GROUP * ROWS
LINES = PART * ROWS
TILE = 256


def loop(count, body):
    def step(index, carry):
        body(index)
        return carry

    lax.fori_loop(0, count, step, 0)


def dot(a, b):
    return jnp.dot(a, b, preferred_element_type=F32)


def dot_nt(a, b):
    return lax.dot_general(a, b, (((1,), (1,)), ((), ())), preferred_element_type=F32)


def kernel(
    alpha_h, pert_h, innov_h, weight_ref, row_ref, col_ref, rowf_h, colf_h, level_ref,
    grad_h, inc_h,
    alpha_v, pert_v, innov_v, rowf, colf, colt, down, back, row_hot, col_hot, weight_v, masked,
    slabs, lines, filtered, local_s, local_r, relay, core_s, core_r, x_in, x_one, x_two, y_s, y_r,
    inc, inc_v,
    load_sem, grad_sem, inc_sem,
    flat_ss, flat_rs, near_ss, near_rs, relay_ss, relay_rs, far_ss, far_rs,
    core_ss, core_rs, xin_ss, xin_rs, xone_ss, xone_rs, xtwo_ss, xtwo_rs, yr_ss, yr_rs,
    ya_ss, ya_rs, xa_ss, xa_rs, xf_ss, xf_rs, ca_ss, ca_rs,
):
    m = lax.axis_index("member")
    g = lax.axis_index("grid")
    y_hi = m // (2 * RING)
    x = lax.rem(m // 2, RING)
    core = lax.rem(m, 2)
    sibling = m + 1 - 2 * core
    across = m + 2 * RING - 4 * RING * y_hi

    z_at = g // 2
    y_lo = lax.rem(g, 2)
    flat = g + 1 - 2 * y_lo

    def around(position, way, steps=1):
        return lax.rem(position + (steps if way == 0 else RING - steps), RING)

    def x_peer(way):
        return y_hi * (2 * RING) + around(x, way) * 2 + core

    def z_peer(way, side, steps=1):
        return around(z_at, way, steps) * 2 + side

    def lane(s):
        return pl.ds(pl.multiple_of(s * LANES, LANES), LANES)

    def slab_rows(s):
        return pl.ds(pl.multiple_of(s * ROWS, ROWS), ROWS)

    def part(c):
        return pl.ds(c * PART, PART)

    loads = [
        pltpu.make_async_copy(src, dst, load_sem.at[i])
        for i, (src, dst) in enumerate(
            ((alpha_h, alpha_v), (rowf_h, rowf), (colf_h, colf), (pert_h, pert_v), (innov_h, innov_v))
        )
    ]
    for load in loads:
        load.start()

    barrier = pltpu.get_barrier_semaphore()

    partners = [(m, flat), (sibling, g), (across, g)]
    for way in range(2):
        partners += [(x_peer(way), g), (m, z_peer(way, 0)), (m, z_peer(way, 1))]
    for partner in partners:
        pl.semaphore_signal(barrier, inc=1, device_id=partner, device_id_type=MESH)

    diagonal = lax.broadcasted_iota(jnp.int32, (ROWS, ROWS), 0) == lax.broadcasted_iota(
        jnp.int32, (ROWS, ROWS), 1
    )

    def upright(line):
        spread = jnp.where(diagonal, jnp.broadcast_to(line, (ROWS, ROWS)), 0.0)
        return jnp.broadcast_to(jnp.sum(spread, axis=1, keepdims=True), (ROWS, LANES))

    def row_table(z):
        column = upright(row_ref[pl.ds(z, 1), :].astype(F32))
        for c in range(CLASSES):
            row_hot[c, slab_rows(z), :] = jnp.where(column == c, 1.0, 0.0).astype(BF16)

    def later_tables():
        def column_table(z):
            line = jnp.broadcast_to(col_ref[pl.ds(z, 1), :], (16, LANES))
            for c in range(CLASSES):
                col_hot[c, z] = jnp.where(line == c, 1.0, 0.0).astype(BF16)
            for t in range(2):
                weight_v[t, z] = upright(weight_ref[t, pl.ds(z, 1), :])

        loop(LEVELS, column_table)

        def level_table(b):
            spot = lax.broadcasted_iota(jnp.int32, (TILE, LEVELS), 0) // ROWS + b * PART
            pick = jnp.where(
                spot == lax.broadcasted_iota(jnp.int32, (TILE, LEVELS), 1), 1.0, 0.0
            ).astype(BF16)
            wide = (LEVELS, LEVELS * ROWS)
            spread = jnp.where(
                lax.broadcasted_iota(jnp.int32, wide, 0)
                == lax.broadcasted_iota(jnp.int32, wide, 1) // ROWS,
                1.0,
                0.0,
            ).astype(BF16)
            tall = (TILE, LEVELS * ROWS)
            same = lax.rem(lax.broadcasted_iota(jnp.int32, tall, 0), ROWS) == lax.rem(
                lax.broadcasted_iota(jnp.int32, tall, 1), ROWS
            )
            rows = pl.ds(pl.multiple_of(b * TILE, TILE), TILE)
            level = level_ref[...]
            down[rows, :] = jnp.where(
                same, dot(dot_nt(pick, level).astype(BF16), spread), 0.0
            ).astype(BF16)
            back[rows, :] = jnp.where(
                same, dot(dot(pick, level).astype(BF16), spread), 0.0
            ).astype(BF16)

        loop(CHUNKS, level_table)
        loads[2].wait()
        unit = jnp.where(
            lax.broadcasted_iota(jnp.int32, (NY, NY), 0)
            == lax.broadcasted_iota(jnp.int32, (NY, NY), 1),
            1.0,
            0.0,
        ).astype(BF16)

        def turn(c):
            colt[c] = dot_nt(unit, colf[c]).astype(BF16)

        loop(CLASSES, turn)
        loads[3].wait()
        loads[4].wait()

    HALF = PART // 2

    def remote(src, dst, ss, rs, member, group):
        return pltpu.make_async_remote_copy(
            src_ref=src, dst_ref=dst, send_sem=ss, recv_sem=rs,
            device_id=(member, group), device_id_type=MESH,
        )

    def flat_copy(phase, c, src, dst):
        return remote(src, dst, flat_ss.at[phase, c], flat_rs.at[phase, c], m, flat)

    def near_copy(phase, c, way, out, into, src, dst):
        return remote(
            src, dst, near_ss.at[phase, c, way, out], near_rs.at[phase, c, way, into],
            m, z_peer(way, out),
        )

    def relay_copy(phase, c, way, out, into, src, dst):
        return remote(
            src, dst, relay_ss.at[phase, c, way, out], relay_rs.at[phase, c, way, into],
            m, z_peer(way, out),
        )

    def far_copy(phase, c, way, into, src, dst):
        return remote(
            src, dst, far_ss.at[phase, c, way, into], far_rs.at[phase, c, way, into],
            m, z_peer(way, y_lo),
        )

    def each(body):
        for way in range(2):
            for side in range(2):
                body(way, side)

    def exchange(phase, c, src, dst):
        def to_relay(way, side):
            relay_copy(
                phase, c, way, side, y_lo,
                src(z_peer(way, side, 2), way), relay.at[phase, c, way, y_lo],
            ).start()

        def to_near(way, side):
            near_copy(phase, c, way, side, y_lo, src(z_peer(way, side)), dst(g)).start()

        each(to_relay)
        each(to_near)
        flat_copy(phase, c, src(flat), dst(g)).start()

    def pass_on(phase, c, dst):
        def one(way, side):
            block = relay.at[phase, c, way, side]
            relay_copy(phase, c, way, side, side, block, block).wait_recv()
            origin = z_peer(1 - way, side)
            far_copy(phase, c, way, side, block, dst(origin, way)).start()

        each(one)

    def arrived(phase, c, dst):
        block = dst(flat)
        flat_copy(phase, c, block, block).wait_recv()

        def from_near(way, side):
            block = dst(z_peer(1 - way, side))
            near_copy(phase, c, way, side, side, block, block).wait_recv()

        def from_far(way, side):
            block = dst(z_peer(way, side, 2), way)
            far_copy(phase, c, way, side, block, block).wait_recv()

        each(from_near)
        each(from_far)

    def sent(phase, c, src):
        block = src(flat)
        flat_copy(phase, c, block, block).wait_send()

        def one(way, side):
            block = src(z_peer(way, side))
            near_copy(phase, c, way, side, side, block, block).wait_send()
            block = src(z_peer(way, side, 2), way)
            relay_copy(phase, c, way, side, side, block, block).wait_send()
            block = relay.at[phase, c, way, side]
            far_copy(phase, c, way, side, block, block).wait_send()

        each(one)

    def levels(c, half):
        return part(c) if half is None else pl.ds(c * PART + half * HALF, HALF)

    def line_block(c):
        return lambda s, half=None: lines.at[levels(c, half), slab_rows(s), :]

    def filtered_block(c):
        return lambda s, half=None: filtered.at[levels(c, half), slab_rows(s), :]

    def block_of(ref, c):
        def pick(s, half=None):
            return ref.at[c, s] if half is None else ref.at[c, s, pl.ds(half * HALF, HALF)]

        return pick

    def slab_block(c):
        return block_of(slabs, c)

    def local_block(c):
        return block_of(local_r, c)

    def own_block(c):
        return block_of(local_s, c)

    def mask_lines(c, source):
        for k in range(CLASSES):
            hot = row_hot[k, pl.ds(pl.multiple_of(c * LINES, LINES), LINES), :]
            masked[k] = source * jnp.concatenate([hot] * GROUP, axis=1)

    def row_filter(c):
        mask_lines(c, alpha_v[part(c)].reshape(LINES, NX))
        for n in range(NX // TILE):
            depth = (n + 1) * TILE
            total = sum(
                dot(masked[k, :, :depth], rowf[k, :depth, n * TILE : depth]) for k in range(CLASSES)
            ).astype(BF16)
            for half in range(2):
                slabs[c, 2 * n + half] = total[:, half * LANES : (half + 1) * LANES].reshape(
                    PART, ROWS, LANES
                )
        lines[part(c), slab_rows(g), :] = slabs[c, g]
        exchange(0, c, slab_block(c), line_block(c))

    def column_pass(c, table, upper):
        def pair(i):
            z = c * PART + 2 * i
            whole = jnp.concatenate([lines[z], lines[z + 1]], axis=1)
            blocks = []
            for k in range(CLASSES):
                hot = jnp.concatenate([col_hot[k, z], col_hot[k, z + 1]], axis=1)
                blocks.append(
                    (whole.reshape(NY // 16, 16, TILE) * hot[None]).reshape(NY, TILE)
                )
            half = NY // 2
            if upper:
                first = sum(dot(table[k, :half, :], blocks[k]) for k in range(CLASSES))
                second = sum(dot(table[k, half:, half:], blocks[k][half:]) for k in range(CLASSES))
            else:
                first = sum(dot(table[k, :half, :half], blocks[k][:half]) for k in range(CLASSES))
                second = sum(dot(table[k, half:, :], blocks[k]) for k in range(CLASSES))
            for j in range(2):
                side = slice(j * LANES, (j + 1) * LANES)
                filtered[z + j, :half, :] = first[:, side].astype(BF16)
                filtered[z + j, half:, :] = second[:, side].astype(BF16)

        loop(PART // 2, pair)

    def column_filter(c):
        arrived(0, c, line_block(c))
        column_pass(c, colt, False)

        def pair(i):
            def add(q, total):
                block = jnp.concatenate(
                    [
                        filtered[part(q), slab_rows(2 * i + j), :].reshape(TILE, LANES)
                        for j in range(2)
                    ],
                    axis=1,
                )
                table = down[
                    pl.ds(pl.multiple_of(c * TILE, TILE), TILE),
                    pl.ds(pl.multiple_of(q * TILE, TILE), TILE),
                ]
                return total + dot(table, block)

            total = lax.fori_loop(0, c + 1, add, jnp.zeros((TILE, 2 * LANES), F32)).astype(BF16)
            for j in range(2):
                local_s[c, 2 * i + j] = total[:, j * LANES : (j + 1) * LANES].reshape(
                    PART, ROWS, LANES
                )

        loop(GROUP // 2, pair)
        local_r[c, g] = local_s[c, g]
        exchange(1, c, own_block(c), local_block(c))

    def core_copy(c):
        return pltpu.make_async_remote_copy(
            src_ref=core_s.at[c],
            dst_ref=core_r.at[c],
            send_sem=core_ss.at[c],
            recv_sem=core_rs.at[c],
            device_id=(sibling, g),
            device_id_type=MESH,
        )

    def xin_copy(c, way):
        slab = 2 * around(x, way, 2) + way
        return remote(
            core_r.at[c, slab], x_in.at[c, way], xin_ss.at[c, way], xin_rs.at[c, way],
            x_peer(way), g,
        )

    def xone_copy(c, way):
        slab = 2 * around(x, way) + 1 - way
        return remote(
            core_r.at[c, slab], x_one.at[c, way], xone_ss.at[c, way], xone_rs.at[c, way],
            x_peer(way), g,
        )

    def xtwo_copy(c, way):
        return remote(
            x_in.at[c, way], x_two.at[c, way], xtwo_ss.at[c, way], xtwo_rs.at[c, way],
            x_peer(way), g,
        )

    def y_copy(c):
        return pltpu.make_async_remote_copy(
            src_ref=y_s.at[c],
            dst_ref=y_r.at[c],
            send_sem=yr_ss.at[c],
            recv_sem=yr_rs.at[c],
            device_id=(across, g),
            device_id_type=MESH,
        )

    def term(t, c, s):
        return pert_v[t, part(c), :, lane(s)].astype(F32) * local_r[c, s].astype(F32)

    def sum_core(c):
        arrived(1, c, local_block(c))

        def one(s):
            core_s[c, s] = term(1 - core, c, s).astype(BF16)

        loop(GROUP, one)
        core_copy(c).start()

    def sum_x(c):
        core_copy(c).wait_recv()

        def one(s):
            core_r[c, s] = (term(core, c, s) + core_r[c, s].astype(F32)).astype(BF16)

        loop(GROUP, one)
        for way in range(2):
            xin_copy(c, way).start()
        for way in range(2):
            xone_copy(c, way).start()

    def add_x(c):
        for way in range(2):
            xin_copy(c, way).wait_recv()
            slab = 2 * around(x, way) + way
            x_in[c, way] = (x_in[c, way].astype(F32) + core_r[c, slab].astype(F32)).astype(BF16)
            xtwo_copy(c, way).start()

    def x_total(c, j):
        total = core_r[c, 2 * x + j].astype(F32) + x_two[c, j].astype(F32)
        return total + x_one[c, 1 - j].astype(F32)

    def sum_y(c):
        for way in range(2):
            xone_copy(c, way).wait_recv()
            xtwo_copy(c, way).wait_recv()
        y_s[c] = x_total(c, 1 - y_hi).astype(BF16)
        y_copy(c).start()

    def give(ss, rs, t, c, s, member):
        return pltpu.make_async_remote_copy(
            src_ref=inc.at[t, c, s],
            dst_ref=inc.at[t, c, s],
            send_sem=ss,
            recv_sem=rs,
            device_id=(member, g),
            device_id_type=MESH,
        )

    def give_y(c, s):
        return give(ya_ss.at[c], ya_rs.at[c], core, c, s, across)

    def give_x(c, turn, way, s):
        return give(xa_ss.at[c, turn, way], xa_rs.at[c, turn, way], core, c, s, x_peer(way))

    def give_far(c, turn, s):
        return give(xf_ss.at[c, turn], xf_rs.at[c, turn], core, c, s, x_peer(turn))

    def slab_of(owner, turn):
        return 2 * owner + (y_hi if turn == 0 else 1 - y_hi)

    def give_core(t, c, s):
        return give(ca_ss.at[c, s], ca_rs.at[c, s], t, c, s, sibling)

    mine = slab_of(x, 0)
    other = slab_of(x, 1)

    def finish(c):
        y_copy(c).wait_recv()
        inc[core, c, mine] = (x_total(c, y_hi) + y_r[c].astype(F32)).astype(BF16)
        give_y(c, mine).start()
        for way in range(2):
            give_x(c, 0, way, mine).start()
        give_core(core, c, mine).start()

    def gather_y(c):
        give_y(c, other).wait_recv()
        for way in range(2):
            give_x(c, 1, way, other).start()
        give_core(core, c, other).start()

    def gather_x(c):
        for turn in range(2):
            s = slab_of(around(x, 1 - turn), turn)
            give_x(c, turn, turn, s).wait_recv()
            give_far(c, turn, s).start()
            give_core(core, c, s).start()
        for turn in range(2):
            s = slab_of(around(x, turn), turn)
            give_x(c, turn, 1 - turn, s).wait_recv()
            give_core(core, c, s).start()

    def gather_far(c):
        for turn in range(2):
            s = slab_of(around(x, 0, 2), turn)
            give_far(c, turn, s).wait_recv()
            give_core(core, c, s).start()

    def weigh(c):
        def one(s):
            give_core(1 - core, c, s).wait_recv()
            total = jnp.zeros((PART, ROWS, LANES), F32)
            for t in range(2):
                block = inc[t, c, s]
                inc_v[t, part(c), :, lane(s)] = block
                misfit = weight_v[t, part(c)] * (
                    block.astype(F32) - innov_v[t, part(c), :, lane(s)].astype(F32)
                )
                total += pert_v[t, part(c), :, lane(s)].astype(F32) * misfit
            core_s[c, s] = total.astype(BF16)

        core_copy(c).wait_send()
        loop(GROUP, one)
        inc_copy(c).start()

    def inc_copy(c):
        return pltpu.make_async_copy(
            inc_v.at[:, part(c)], inc_h.at[:, part(c)], inc_sem.at[c]
        )

    def level_adjoint(c):
        sent(0, c, slab_block(c))

        def pair(i):
            def add(q, total):
                block = jnp.concatenate(
                    [core_s[q, 2 * i + j].reshape(TILE, LANES) for j in range(2)], axis=1
                )
                table = back[
                    pl.ds(pl.multiple_of(c * TILE, TILE), TILE),
                    pl.ds(pl.multiple_of(q * TILE, TILE), TILE),
                ]
                return total + dot(table, block)

            total = lax.fori_loop(c, CHUNKS, add, jnp.zeros((TILE, 2 * LANES), F32)).astype(BF16)
            for j in range(2):
                slabs[c, 2 * i + j] = total[:, j * LANES : (j + 1) * LANES].reshape(
                    PART, ROWS, LANES
                )

        loop(GROUP // 2, pair)
        lines[part(c), slab_rows(g), :] = slabs[c, g]
        exchange(2, c, slab_block(c), line_block(c))

    def column_adjoint(c):
        arrived(2, c, line_block(c))
        column_pass(c, colf, True)
        local_r[c, g] = filtered[part(c), slab_rows(g), :]
        exchange(3, c, filtered_block(c), local_block(c))

    def grad_copy(c):
        return pltpu.make_async_copy(alpha_v.at[part(c)], grad_h.at[part(c)], grad_sem.at[c])

    def row_adjoint(c):
        arrived(3, c, local_block(c))
        mask_lines(
            c, jnp.concatenate([local_r[c, s].reshape(LINES, LANES) for s in range(GROUP)], axis=1)
        )
        for n in range(NX // TILE):
            start = n * TILE
            total = sum(
                dot_nt(masked[k, :, start:], rowf[k, start : start + TILE, start:])
                for k in range(CLASSES)
            )
            side = slice(start, start + TILE)
            alpha = alpha_v[part(c), :, side].reshape(LINES, TILE).astype(F32)
            alpha_v[part(c), :, side] = (alpha + total).astype(BF16).reshape(PART, ROWS, TILE)
        grad_copy(c).start()

    loop(LEVELS, row_table)
    loads[0].wait()
    loads[1].wait()
    pl.semaphore_wait(barrier, len(partners))

    def at(step, offset, stage):
        chunk = step - offset

        @pl.when(jnp.logical_and(chunk >= 0, chunk < CHUNKS))
        def _():
            stage(chunk)

    def forward(step):
        at(step, 0, row_filter)

        @pl.when(step == 1)
        def _():
            later_tables()

        at(step, 1, lambda c: pass_on(0, c, line_block(c)))
        at(step, 2, lambda c: pass_on(1, c, local_block(c)))
        at(step, 3, add_x)
        at(step, 4, gather_x)
        at(step, 1, column_filter)
        at(step, 3, sum_y)
        at(step, 2, sum_core)
        at(step, 3, finish)
        at(step, 4, gather_far)
        at(step, 2, sum_x)
        at(step, 3, gather_y)
        at(step, 4, weigh)

    loop(CHUNKS + 4, forward)

    def backward(step):
        def down_from(stage):
            return lambda c: stage(CHUNKS - 1 - c)

        at(step, 0, down_from(level_adjoint))
        at(step, 1, down_from(lambda c: pass_on(2, c, line_block(c))))
        at(step, 2, down_from(lambda c: pass_on(3, c, local_block(c))))
        at(step, 1, down_from(column_adjoint))
        at(step, 2, down_from(row_adjoint))

    loop(CHUNKS + 2, backward)

    def drain(c):
        sent(1, c, own_block(c))
        sent(2, c, slab_block(c))
        sent(3, c, filtered_block(c))
        y_copy(c).wait_send()
        give_y(c, mine).wait_send()
        for way in range(2):
            xin_copy(c, way).wait_send()
            xone_copy(c, way).wait_send()
            xtwo_copy(c, way).wait_send()
            give_x(c, 0, way, mine).wait_send()
            give_x(c, 1, way, other).wait_send()
            give_far(c, way, mine).wait_send()

        def one(s):
            give_core(core, c, s).wait_send()

        loop(GROUP, one)
        inc_copy(c).wait()
        grad_copy(c).wait()

    loop(CHUNKS, drain)


def on_device(alpha, pert, innov, weight, row_class, col_class, rowf, colf, level):
    any_spec = pl.BlockSpec(memory_space=pl.ANY)
    vmem_spec = pl.BlockSpec(memory_space=pltpu.VMEM)
    dma = pltpu.SemaphoreType.DMA
    block = (PART, ROWS, LANES)
    slab = (CHUNKS, GROUP) + block
    scratch = [
        pltpu.VMEM((LEVELS, ROWS, NX), BF16),
        pltpu.VMEM((2, LEVELS, ROWS, NX), BF16),
        pltpu.VMEM((2, LEVELS, ROWS, NX), BF16),
        pltpu.VMEM((CLASSES, NX, NX), BF16),
        pltpu.VMEM((CLASSES, NY, NY), BF16),
        pltpu.VMEM((CLASSES, NY, NY), BF16),
        pltpu.VMEM((LEVELS * ROWS, LEVELS * ROWS), BF16),
        pltpu.VMEM((LEVELS * ROWS, LEVELS * ROWS), BF16),
        pltpu.VMEM((CLASSES, LEVELS * ROWS, LANES), BF16),
        pltpu.VMEM((CLASSES, LEVELS, 16, LANES), BF16),
        pltpu.VMEM((2, LEVELS, ROWS, LANES), F32),
        pltpu.VMEM((CLASSES, LINES, NX), BF16),
        pltpu.VMEM(slab, BF16),
        pltpu.VMEM((LEVELS, NY, LANES), BF16),
        pltpu.VMEM((LEVELS, NY, LANES), BF16),
        pltpu.VMEM(slab, BF16),
        pltpu.VMEM(slab, BF16),
        pltpu.VMEM((4, CHUNKS, 2, 2, PART // 2, ROWS, LANES), BF16),
        pltpu.VMEM(slab, BF16),
        pltpu.VMEM(slab, BF16),
        pltpu.VMEM((CHUNKS, 2) + block, BF16),
        pltpu.VMEM((CHUNKS, 2) + block, BF16),
        pltpu.VMEM((CHUNKS, 2) + block, BF16),
        pltpu.VMEM((CHUNKS,) + block, BF16),
        pltpu.VMEM((CHUNKS,) + block, BF16),
        pltpu.VMEM((2,) + slab, BF16),
        pltpu.VMEM((2, LEVELS, ROWS, NX), BF16),
        dma((5,)),
        dma((CHUNKS,)),
        dma((CHUNKS,)),
    ]
    for counts in (
        (4, CHUNKS),
        (4, CHUNKS, 2, 2),
        (4, CHUNKS, 2, 2),
        (4, CHUNKS, 2, 2),
        (CHUNKS,),
        (CHUNKS, 2),
        (CHUNKS, 2),
        (CHUNKS, 2),
        (CHUNKS,),
        (CHUNKS,),
        (CHUNKS, 2, 2),
        (CHUNKS, 2),
        (CHUNKS, GROUP),
    ):
        scratch += [dma(counts), dma(counts)]
    gradient, increment = pl.pallas_call(
        kernel,
        out_shape=(
            jax.ShapeDtypeStruct((LEVELS, ROWS, NX), BF16),
            jax.ShapeDtypeStruct((2, LEVELS, ROWS, NX), BF16),
        ),
        in_specs=[any_spec] * 3 + [vmem_spec] * 3 + [any_spec] * 2 + [vmem_spec],
        out_specs=(any_spec, any_spec),
        scratch_shapes=scratch,
        compiler_params=pltpu.CompilerParams(
            collective_id=0, has_side_effects=True, vmem_limit_bytes=62 * 1024 * 1024
        ),
    )(alpha[0], pert[0], innov, weight, row_class, col_class, rowf, colf, level)
    return gradient[None], increment


def solution(mesh):
    return jax.shard_map(
        on_device,
        mesh=mesh,
        in_specs=(
            P("member", None, "grid", None),
            P("member", None, None, "grid", None),
            P(None, None, "grid", None),
            P(None, None, "grid"),
            P(None, "grid"),
            P(None, "grid"),
            P(),
            P(),
            P(),
        ),
        out_specs=(P("member", None, "grid", None), P(None, None, "grid", None)),
        check_vma=False,
    )
```

```python
import functools

import jax
import jax.numpy as jnp
from jax import lax
from jax.experimental import pallas as pl
from jax.experimental.pallas import tpu as pltpu
from jax.sharding import PartitionSpec as P

MESH = pl.DeviceIdType.MESH
F32 = jnp.float32
BF16 = jnp.bfloat16

CLASSES = 3
LEVELS = 16
GROUP = 8
RING = 4
CHUNKS = 4
PART = LEVELS // CHUNKS
ROWS = 64
LANES = 128
NX = GROUP * LANES
NY = GROUP * ROWS
LINES = PART * ROWS
TILE = 256


def loop(count, body):
    def step(index, carry):
        body(index)
        return carry

    lax.fori_loop(0, count, step, 0)


def dot(a, b):
    return jnp.dot(a, b, preferred_element_type=F32)


def dot_nt(a, b):
    return lax.dot_general(a, b, (((1,), (1,)), ((), ())), preferred_element_type=F32)


def kernel(
    alpha_h, pert_h, innov_h, weight_ref, row_ref, col_ref, rowf_h, colf_h, level_ref,
    grad_h, inc_h,
    alpha_v, pert_v, innov_v, rowf, colf, colt, down, back, row_hot, col_hot, weight_v, masked,
    slabs, lines, filtered, local_s, local_r, core_s, core_r, x_in, x_one, x_two, y_s, y_r,
    inc, inc_v,
    alpha_sem, rowf_sem, load_sem, grad_sem, inc_sem, a2a_ss, a2a_rs, core_ss, core_rs, xin_ss, xin_rs, xone_ss, xone_rs, xtwo_ss, xtwo_rs, yr_ss, yr_rs,
    ya_ss, ya_rs, xa_ss, xa_rs, xf_ss, xf_rs, ca_ss, ca_rs,
):
    m = lax.axis_index("member")
    g = lax.axis_index("grid")
    y_hi = m // (2 * RING)
    x = lax.rem(m // 2, RING)
    core = lax.rem(m, 2)
    sibling = m + 1 - 2 * core
    across = m + 2 * RING - 4 * RING * y_hi

    def around(position, way, steps=1):
        return lax.rem(position + (steps if way == 0 else RING - steps), RING)

    def x_peer(way):
        return y_hi * (2 * RING) + around(x, way) * 2 + core

    def lane(s):
        return pl.ds(pl.multiple_of(s * LANES, LANES), LANES)

    def slab_rows(s):
        return pl.ds(pl.multiple_of(s * ROWS, ROWS), ROWS)

    def part(c):
        return pl.ds(c * PART, PART)

    barrier = pltpu.get_barrier_semaphore()

    def greet(partner):
        pl.semaphore_signal(barrier, inc=1, device_id=partner, device_id_type=MESH)

    loop(GROUP - 1, lambda step: greet((m, lax.rem(g + step + 1, GROUP))))
    for member in (x_peer(0), x_peer(1), sibling, across):
        greet((member, g))

    def alpha_load(c):
        return pltpu.make_async_copy(alpha_h.at[part(c)], alpha_v.at[part(c)], alpha_sem.at[c])

    def rowf_load(n):
        where = (slice(None), slice(0, (n + 1) * TILE), slice(n * TILE, (n + 1) * TILE))
        return pltpu.make_async_copy(rowf_h.at[where], rowf.at[where], rowf_sem.at[n])

    alpha_load(0).start()
    for n in range(NX // TILE):
        rowf_load(n).start()
    for c in range(1, CHUNKS):
        alpha_load(c).start()
    loads = [
        pltpu.make_async_copy(src, dst, load_sem.at[i])
        for i, (src, dst) in enumerate(((colf_h, colf), (pert_h, pert_v), (innov_h, innov_v)))
    ]

    diagonal = lax.broadcasted_iota(jnp.int32, (ROWS, ROWS), 0) == lax.broadcasted_iota(
        jnp.int32, (ROWS, ROWS), 1
    )

    def upright(line):
        spread = jnp.where(diagonal, jnp.broadcast_to(line, (ROWS, ROWS)), 0.0)
        return jnp.broadcast_to(jnp.sum(spread, axis=1, keepdims=True), (ROWS, LANES))

    def row_table(z):
        column = upright(row_ref[pl.ds(z, 1), :].astype(F32))
        for c in range(CLASSES):
            row_hot[c, slab_rows(z), :] = jnp.where(column == c, 1.0, 0.0).astype(BF16)

    def later_tables():
        def column_table(z):
            line = jnp.broadcast_to(col_ref[pl.ds(z, 1), :], (16, LANES))
            for c in range(CLASSES):
                col_hot[c, z] = jnp.where(line == c, 1.0, 0.0).astype(BF16)
            for t in range(2):
                weight_v[t, z] = upright(weight_ref[t, pl.ds(z, 1), :])

        loop(LEVELS, column_table)

        def level_table(b):
            spot = lax.broadcasted_iota(jnp.int32, (TILE, LEVELS), 0) // ROWS + b * PART
            pick = jnp.where(
                spot == lax.broadcasted_iota(jnp.int32, (TILE, LEVELS), 1), 1.0, 0.0
            ).astype(BF16)
            wide = (LEVELS, LEVELS * ROWS)
            spread = jnp.where(
                lax.broadcasted_iota(jnp.int32, wide, 0)
                == lax.broadcasted_iota(jnp.int32, wide, 1) // ROWS,
                1.0,
                0.0,
            ).astype(BF16)
            tall = (TILE, LEVELS * ROWS)
            same = lax.rem(lax.broadcasted_iota(jnp.int32, tall, 0), ROWS) == lax.rem(
                lax.broadcasted_iota(jnp.int32, tall, 1), ROWS
            )
            rows = pl.ds(pl.multiple_of(b * TILE, TILE), TILE)
            level = level_ref[...]
            down[rows, :] = jnp.where(
                same, dot(dot_nt(pick, level).astype(BF16), spread), 0.0
            ).astype(BF16)
            back[rows, :] = jnp.where(
                same, dot(dot(pick, level).astype(BF16), spread), 0.0
            ).astype(BF16)

        loop(CHUNKS, level_table)
        loads[0].wait()
        unit = jnp.where(
            lax.broadcasted_iota(jnp.int32, (NY, NY), 0)
            == lax.broadcasted_iota(jnp.int32, (NY, NY), 1),
            1.0,
            0.0,
        ).astype(BF16)

        def turn(c):
            colt[c] = dot_nt(unit, colf[c]).astype(BF16)

        loop(CLASSES, turn)

    def remote(src, dst, ss, rs, member, group):
        return pltpu.make_async_remote_copy(
            src_ref=src, dst_ref=dst, send_sem=ss, recv_sem=rs,
            device_id=(member, group), device_id_type=MESH,
        )

    def exchange(phase, c, src, dst):
        def send(step):
            peer = lax.rem(g + step + 1, GROUP)
            remote(
                src(peer), dst(g), a2a_ss.at[phase, c, peer], a2a_rs.at[phase, c, g], m, peer
            ).start()

        loop(GROUP - 1, send)

    def exchanged(phase, c, peer, block):
        return remote(
            block, block, a2a_ss.at[phase, c, peer], a2a_rs.at[phase, c, peer], m, peer
        )

    def arrived(phase, c, dst):
        def wait(step):
            peer = lax.rem(g + GROUP - 1 - step, GROUP)
            exchanged(phase, c, peer, dst(peer)).wait_recv()

        loop(GROUP - 1, wait)

    def sent(phase, c, src):
        def wait(step):
            peer = lax.rem(g + step + 1, GROUP)
            exchanged(phase, c, peer, src(peer)).wait_send()

        loop(GROUP - 1, wait)

    def line_block(c):
        return lambda s: lines.at[part(c), slab_rows(s), :]

    def filtered_block(c):
        return lambda s: filtered.at[part(c), slab_rows(s), :]

    def slab_block(c):
        return lambda s: slabs.at[c, s]

    def local_block(c):
        return lambda s: local_r.at[c, s]

    def own_block(c):
        return lambda s: local_s.at[c, s]

    def mask_lines(c, source):
        for k in range(CLASSES):
            hot = row_hot[k, pl.ds(pl.multiple_of(c * LINES, LINES), LINES), :]
            masked[k] = source * jnp.concatenate([hot] * GROUP, axis=1)

    def row_filter(c):
        alpha_load(c).wait()
        mask_lines(c, alpha_v[part(c)].reshape(LINES, NX))
        for n in range(NX // TILE):
            depth = (n + 1) * TILE

            @pl.when(c == 0)
            def _():
                rowf_load(n).wait()

            total = sum(
                dot(masked[k, :, :depth], rowf[k, :depth, n * TILE : depth]) for k in range(CLASSES)
            ).astype(BF16)
            for half in range(2):
                slabs[c, 2 * n + half] = total[:, half * LANES : (half + 1) * LANES].reshape(
                    PART, ROWS, LANES
                )
        lines[part(c), slab_rows(g), :] = slabs[c, g]
        exchange(0, c, slab_block(c), line_block(c))

        @pl.when(c == 0)
        def _():
            for load in loads:
                load.start()

    def column_pass(c, table, upper):
        def pair(i):
            z = c * PART + 2 * i
            whole = jnp.concatenate([lines[z], lines[z + 1]], axis=1)
            blocks = []
            for k in range(CLASSES):
                hot = jnp.concatenate([col_hot[k, z], col_hot[k, z + 1]], axis=1)
                blocks.append(
                    (whole.reshape(NY // 16, 16, TILE) * hot[None]).reshape(NY, TILE)
                )
            half = NY // 2
            if upper:
                first = sum(dot(table[k, :half, :], blocks[k]) for k in range(CLASSES))
                second = sum(dot(table[k, half:, half:], blocks[k][half:]) for k in range(CLASSES))
            else:
                first = sum(dot(table[k, :half, :half], blocks[k][:half]) for k in range(CLASSES))
                second = sum(dot(table[k, half:, :], blocks[k]) for k in range(CLASSES))
            for j in range(2):
                side = slice(j * LANES, (j + 1) * LANES)
                filtered[z + j, :half, :] = first[:, side].astype(BF16)
                filtered[z + j, half:, :] = second[:, side].astype(BF16)

        loop(PART // 2, pair)

    def column_filter(c):
        arrived(0, c, line_block(c))
        column_pass(c, colt, False)

        def pair(i):
            def add(q, total):
                block = jnp.concatenate(
                    [
                        filtered[part(q), slab_rows(2 * i + j), :].reshape(TILE, LANES)
                        for j in range(2)
                    ],
                    axis=1,
                )
                table = down[
                    pl.ds(pl.multiple_of(c * TILE, TILE), TILE),
                    pl.ds(pl.multiple_of(q * TILE, TILE), TILE),
                ]
                return total + dot(table, block)

            total = lax.fori_loop(0, c + 1, add, jnp.zeros((TILE, 2 * LANES), F32)).astype(BF16)
            for j in range(2):
                local_s[c, 2 * i + j] = total[:, j * LANES : (j + 1) * LANES].reshape(
                    PART, ROWS, LANES
                )

        loop(GROUP // 2, pair)
        local_r[c, g] = local_s[c, g]
        exchange(1, c, own_block(c), local_block(c))

    def core_copy(c):
        return pltpu.make_async_remote_copy(
            src_ref=core_s.at[c],
            dst_ref=core_r.at[c],
            send_sem=core_ss.at[c],
            recv_sem=core_rs.at[c],
            device_id=(sibling, g),
            device_id_type=MESH,
        )

    def xin_copy(c, way):
        slab = 2 * around(x, way, 2) + way
        return remote(
            core_r.at[c, slab], x_in.at[c, way], xin_ss.at[c, way], xin_rs.at[c, way],
            x_peer(way), g,
        )

    def xone_copy(c, way):
        slab = 2 * around(x, way) + 1 - way
        return remote(
            core_r.at[c, slab], x_one.at[c, way], xone_ss.at[c, way], xone_rs.at[c, way],
            x_peer(way), g,
        )

    def xtwo_copy(c, way):
        return remote(
            x_in.at[c, way], x_two.at[c, way], xtwo_ss.at[c, way], xtwo_rs.at[c, way],
            x_peer(way), g,
        )

    def y_copy(c):
        return pltpu.make_async_remote_copy(
            src_ref=y_s.at[c],
            dst_ref=y_r.at[c],
            send_sem=yr_ss.at[c],
            recv_sem=yr_rs.at[c],
            device_id=(across, g),
            device_id_type=MESH,
        )

    def term(t, c, s):
        return pert_v[t, part(c), :, lane(s)].astype(F32) * local_r[c, s].astype(F32)

    def sum_core(c):
        arrived(1, c, local_block(c))

        @pl.when(c == 0)
        def _():
            loads[1].wait()
            loads[2].wait()

        def one(s):
            core_s[c, s] = term(1 - core, c, s).astype(BF16)

        loop(GROUP, one)
        core_copy(c).start()

    def sum_x(c):
        core_copy(c).wait_recv()

        def one(s):
            core_r[c, s] = (term(core, c, s) + core_r[c, s].astype(F32)).astype(BF16)

        loop(GROUP, one)
        for way in range(2):
            xin_copy(c, way).start()
        for way in range(2):
            xone_copy(c, way).start()

    def add_x(c):
        for way in range(2):
            xin_copy(c, way).wait_recv()
            slab = 2 * around(x, way) + way
            x_in[c, way] = (x_in[c, way].astype(F32) + core_r[c, slab].astype(F32)).astype(BF16)
            xtwo_copy(c, way).start()

    def x_total(c, j):
        total = core_r[c, 2 * x + j].astype(F32) + x_two[c, j].astype(F32)
        return total + x_one[c, 1 - j].astype(F32)

    def sum_y(c):
        for way in range(2):
            xone_copy(c, way).wait_recv()
            xtwo_copy(c, way).wait_recv()
        y_s[c] = x_total(c, 1 - y_hi).astype(BF16)
        y_copy(c).start()

    def give(ss, rs, t, c, s, member):
        return pltpu.make_async_remote_copy(
            src_ref=inc.at[t, c, s],
            dst_ref=inc.at[t, c, s],
            send_sem=ss,
            recv_sem=rs,
            device_id=(member, g),
            device_id_type=MESH,
        )

    def give_y(c, s):
        return give(ya_ss.at[c], ya_rs.at[c], core, c, s, across)

    def give_x(c, turn, way, s):
        return give(xa_ss.at[c, turn, way], xa_rs.at[c, turn, way], core, c, s, x_peer(way))

    def give_far(c, turn, s):
        return give(xf_ss.at[c, turn], xf_rs.at[c, turn], core, c, s, x_peer(turn))

    def slab_of(owner, turn):
        return 2 * owner + (y_hi if turn == 0 else 1 - y_hi)

    def give_core(t, c, s):
        return give(ca_ss.at[c, s], ca_rs.at[c, s], t, c, s, sibling)

    mine = slab_of(x, 0)
    other = slab_of(x, 1)

    def finish(c):
        y_copy(c).wait_recv()
        inc[core, c, mine] = (x_total(c, y_hi) + y_r[c].astype(F32)).astype(BF16)
        give_y(c, mine).start()
        for way in range(2):
            give_x(c, 0, way, mine).start()
        give_core(core, c, mine).start()

    def gather_y(c):
        give_y(c, other).wait_recv()
        for way in range(2):
            give_x(c, 1, way, other).start()
        give_core(core, c, other).start()

    def gather_x(c):
        for turn in range(2):
            s = slab_of(around(x, 1 - turn), turn)
            give_x(c, turn, turn, s).wait_recv()
            give_far(c, turn, s).start()
            give_core(core, c, s).start()
        for turn in range(2):
            s = slab_of(around(x, turn), turn)
            give_x(c, turn, 1 - turn, s).wait_recv()
            give_core(core, c, s).start()

    def gather_far(c):
        for turn in range(2):
            s = slab_of(around(x, 0, 2), turn)
            give_far(c, turn, s).wait_recv()
            give_core(core, c, s).start()

    def weigh(c):
        def one(s):
            give_core(1 - core, c, s).wait_recv()
            total = jnp.zeros((PART, ROWS, LANES), F32)
            for t in range(2):
                block = inc[t, c, s]
                inc_v[t, part(c), :, lane(s)] = block
                misfit = weight_v[t, part(c)] * (
                    block.astype(F32) - innov_v[t, part(c), :, lane(s)].astype(F32)
                )
                total += pert_v[t, part(c), :, lane(s)].astype(F32) * misfit
            core_s[c, s] = total.astype(BF16)

        core_copy(c).wait_send()
        loop(GROUP, one)
        inc_copy(c).start()

    def inc_copy(c):
        return pltpu.make_async_copy(
            inc_v.at[:, part(c)], inc_h.at[:, part(c)], inc_sem.at[c]
        )

    def level_adjoint(c):
        sent(0, c, slab_block(c))

        def pair(i):
            def add(q, total):
                block = jnp.concatenate(
                    [core_s[q, 2 * i + j].reshape(TILE, LANES) for j in range(2)], axis=1
                )
                table = back[
                    pl.ds(pl.multiple_of(c * TILE, TILE), TILE),
                    pl.ds(pl.multiple_of(q * TILE, TILE), TILE),
                ]
                return total + dot(table, block)

            total = lax.fori_loop(c, CHUNKS, add, jnp.zeros((TILE, 2 * LANES), F32)).astype(BF16)
            for j in range(2):
                slabs[c, 2 * i + j] = total[:, j * LANES : (j + 1) * LANES].reshape(
                    PART, ROWS, LANES
                )

        loop(GROUP // 2, pair)
        lines[part(c), slab_rows(g), :] = slabs[c, g]
        exchange(2, c, slab_block(c), line_block(c))

    def column_adjoint(c):
        arrived(2, c, line_block(c))
        column_pass(c, colf, True)
        local_r[c, g] = filtered[part(c), slab_rows(g), :]
        exchange(3, c, filtered_block(c), local_block(c))

    def grad_copy(c):
        return pltpu.make_async_copy(alpha_v.at[part(c)], grad_h.at[part(c)], grad_sem.at[c])

    def row_adjoint(c):
        arrived(3, c, local_block(c))
        mask_lines(
            c, jnp.concatenate([local_r[c, s].reshape(LINES, LANES) for s in range(GROUP)], axis=1)
        )
        for n in range(NX // TILE):
            start = n * TILE
            total = sum(
                dot_nt(masked[k, :, start:], rowf[k, start : start + TILE, start:])
                for k in range(CLASSES)
            )
            side = slice(start, start + TILE)
            alpha = alpha_v[part(c), :, side].reshape(LINES, TILE).astype(F32)
            alpha_v[part(c), :, side] = (alpha + total).astype(BF16).reshape(PART, ROWS, TILE)
        grad_copy(c).start()

    loop(LEVELS, row_table)
    pl.semaphore_wait(barrier, GROUP + 3)

    def at(step, offset, stage):
        chunk = step - offset

        @pl.when(jnp.logical_and(chunk >= 0, chunk < CHUNKS))
        def _():
            stage(chunk)

    def forward(step):
        at(step, 3, sum_core)
        at(step, 6, gather_y)
        at(step, 4, add_x)
        at(step, 5, finish)
        at(step, 0, row_filter)
        at(step, 10, weigh)
        at(step, 3, sum_x)
        at(step, 4, sum_y)
        at(step, 7, gather_x)

        @pl.when(step == 1)
        def _():
            later_tables()

        at(step, 1, column_filter)
        at(step, 8, gather_far)

    loop(CHUNKS + 10, forward)

    def backward(step):
        at(step, 0, lambda c: level_adjoint(CHUNKS - 1 - c))
        at(step, 2, lambda c: column_adjoint(CHUNKS - 1 - c))
        at(step, 4, lambda c: row_adjoint(CHUNKS - 1 - c))

    loop(CHUNKS + 4, backward)

    def drain(c):
        sent(1, c, own_block(c))
        sent(2, c, slab_block(c))
        sent(3, c, filtered_block(c))
        y_copy(c).wait_send()
        give_y(c, mine).wait_send()
        for way in range(2):
            xin_copy(c, way).wait_send()
            xone_copy(c, way).wait_send()
            xtwo_copy(c, way).wait_send()
            give_x(c, 0, way, mine).wait_send()
            give_x(c, 1, way, other).wait_send()
            give_far(c, way, mine).wait_send()

        def one(s):
            give_core(core, c, s).wait_send()

        loop(GROUP, one)
        inc_copy(c).wait()
        grad_copy(c).wait()

    loop(CHUNKS, drain)


def on_device(alpha, pert, innov, weight, row_class, col_class, rowf, colf, level):
    any_spec = pl.BlockSpec(memory_space=pl.ANY)
    vmem_spec = pl.BlockSpec(memory_space=pltpu.VMEM)
    dma = pltpu.SemaphoreType.DMA
    block = (PART, ROWS, LANES)
    slab = (CHUNKS, GROUP) + block
    scratch = [
        pltpu.VMEM((LEVELS, ROWS, NX), BF16),
        pltpu.VMEM((2, LEVELS, ROWS, NX), BF16),
        pltpu.VMEM((2, LEVELS, ROWS, NX), BF16),
        pltpu.VMEM((CLASSES, NX, NX), BF16),
        pltpu.VMEM((CLASSES, NY, NY), BF16),
        pltpu.VMEM((CLASSES, NY, NY), BF16),
        pltpu.VMEM((LEVELS * ROWS, LEVELS * ROWS), BF16),
        pltpu.VMEM((LEVELS * ROWS, LEVELS * ROWS), BF16),
        pltpu.VMEM((CLASSES, LEVELS * ROWS, LANES), BF16),
        pltpu.VMEM((CLASSES, LEVELS, 16, LANES), BF16),
        pltpu.VMEM((2, LEVELS, ROWS, LANES), F32),
        pltpu.VMEM((CLASSES, LINES, NX), BF16),
        pltpu.VMEM(slab, BF16),
        pltpu.VMEM((LEVELS, NY, LANES), BF16),
        pltpu.VMEM((LEVELS, NY, LANES), BF16),
        pltpu.VMEM(slab, BF16),
        pltpu.VMEM(slab, BF16),
        pltpu.VMEM(slab, BF16),
        pltpu.VMEM(slab, BF16),
        pltpu.VMEM((CHUNKS, 2) + block, BF16),
        pltpu.VMEM((CHUNKS, 2) + block, BF16),
        pltpu.VMEM((CHUNKS, 2) + block, BF16),
        pltpu.VMEM((CHUNKS,) + block, BF16),
        pltpu.VMEM((CHUNKS,) + block, BF16),
        pltpu.VMEM((2,) + slab, BF16),
        pltpu.VMEM((2, LEVELS, ROWS, NX), BF16),
        dma((CHUNKS,)),
        dma((NX // TILE,)),
        dma((3,)),
        dma((CHUNKS,)),
        dma((CHUNKS,)),
    ]
    for counts in (
        (4, CHUNKS, GROUP),
        (CHUNKS,),
        (CHUNKS, 2),
        (CHUNKS, 2),
        (CHUNKS, 2),
        (CHUNKS,),
        (CHUNKS,),
        (CHUNKS, 2, 2),
        (CHUNKS, 2),
        (CHUNKS, GROUP),
    ):
        scratch += [dma(counts), dma(counts)]
    gradient, increment = pl.pallas_call(
        kernel,
        out_shape=(
            jax.ShapeDtypeStruct((LEVELS, ROWS, NX), BF16),
            jax.ShapeDtypeStruct((2, LEVELS, ROWS, NX), BF16),
        ),
        in_specs=[any_spec] * 3 + [vmem_spec] * 3 + [any_spec] * 2 + [vmem_spec],
        out_specs=(any_spec, any_spec),
        scratch_shapes=scratch,
        compiler_params=pltpu.CompilerParams(
            collective_id=0, has_side_effects=True, vmem_limit_bytes=62 * 1024 * 1024
        ),
    )(alpha[0], pert[0], innov, weight, row_class, col_class, rowf, colf, level)
    return gradient[None], increment


def solution(mesh):
    return jax.shard_map(
        on_device,
        mesh=mesh,
        in_specs=(
            P("member", None, "grid", None),
            P("member", None, None, "grid", None),
            P(None, None, "grid", None),
            P(None, None, "grid"),
            P(None, "grid"),
            P(None, "grid"),
            P(),
            P(),
            P(),
        ),
        out_specs=(P("member", None, "grid", None), P(None, None, "grid", None)),
        check_vma=False,
    )
```

```python
import functools

import jax
import jax.numpy as jnp
from jax import lax
from jax.experimental import pallas as pl
from jax.experimental.pallas import tpu as pltpu
from jax.sharding import PartitionSpec as P

MESH = pl.DeviceIdType.MESH
F32 = jnp.float32
BF16 = jnp.bfloat16

CLASSES = 3
LEVELS = 16
GROUP = 8
RING = 4
CHUNKS = 8
PART = LEVELS // CHUNKS
ROWS = 64
LANES = 128
NX = GROUP * LANES
NY = GROUP * ROWS
LINES = PART * ROWS
TILE = 256
DEEP = TILE // ROWS


def loop(count, body):
    def step(index, carry):
        body(index)
        return carry

    lax.fori_loop(0, count, step, 0)


def dot(a, b):
    return jnp.dot(a, b, preferred_element_type=F32)


def dot_nt(a, b):
    return lax.dot_general(a, b, (((1,), (1,)), ((), ())), preferred_element_type=F32)


def kernel(
    alpha_h, pert_h, innov_h, weight_ref, row_ref, col_ref, rowf_h, colf_h, level_ref,
    grad_h, inc_h,
    alpha_v, pert_v, innov_v, rowf, colf, colt, down, back, row_hot, col_hot, weight_v, masked,
    slabs, lines, filtered, local_s, local_r, core_s, core_r, x_in, x_one, x_two, y_s, y_r,
    inc, inc_v,
    alpha_sem, rowf_sem, load_sem, grad_sem, inc_sem, a2a_ss, a2a_rs, core_ss, core_rs, xin_ss, xin_rs, xone_ss, xone_rs, xtwo_ss, xtwo_rs, yr_ss, yr_rs,
    ya_ss, ya_rs, xa_ss, xa_rs, xf_ss, xf_rs, ca_ss, ca_rs,
):
    m = lax.axis_index("member")
    g = lax.axis_index("grid")
    y_hi = m // (2 * RING)
    x = lax.rem(m // 2, RING)
    core = lax.rem(m, 2)
    sibling = m + 1 - 2 * core
    across = m + 2 * RING - 4 * RING * y_hi

    def around(position, way, steps=1):
        return lax.rem(position + (steps if way == 0 else RING - steps), RING)

    def x_peer(way):
        return y_hi * (2 * RING) + around(x, way) * 2 + core

    def lane(s):
        return pl.ds(pl.multiple_of(s * LANES, LANES), LANES)

    def slab_rows(s):
        return pl.ds(pl.multiple_of(s * ROWS, ROWS), ROWS)

    def part(c):
        return pl.ds(c * PART, PART)

    barrier = pltpu.get_barrier_semaphore()

    def greet(partner):
        pl.semaphore_signal(barrier, inc=1, device_id=partner, device_id_type=MESH)

    loop(GROUP - 1, lambda step: greet((m, lax.rem(g + step + 1, GROUP))))
    for member in (x_peer(0), x_peer(1), sibling, across):
        greet((member, g))

    def alpha_load(c):
        return pltpu.make_async_copy(alpha_h.at[part(c)], alpha_v.at[part(c)], alpha_sem.at[c])

    def rowf_load(n):
        where = (slice(None), slice(0, (n + 1) * TILE), slice(n * TILE, (n + 1) * TILE))
        return pltpu.make_async_copy(rowf_h.at[where], rowf.at[where], rowf_sem.at[n])

    alpha_load(0).start()
    for n in range(NX // TILE):
        rowf_load(n).start()
    for c in range(1, CHUNKS):
        alpha_load(c).start()
    loads = [
        pltpu.make_async_copy(src, dst, load_sem.at[i])
        for i, (src, dst) in enumerate(((colf_h, colf), (pert_h, pert_v), (innov_h, innov_v)))
    ]

    diagonal = lax.broadcasted_iota(jnp.int32, (ROWS, ROWS), 0) == lax.broadcasted_iota(
        jnp.int32, (ROWS, ROWS), 1
    )

    def upright(line):
        spread = jnp.where(diagonal, jnp.broadcast_to(line, (ROWS, ROWS)), 0.0)
        return jnp.broadcast_to(jnp.sum(spread, axis=1, keepdims=True), (ROWS, LANES))

    def row_table(z):
        column = upright(row_ref[pl.ds(z, 1), :].astype(F32))
        for c in range(CLASSES):
            row_hot[c, slab_rows(z), :] = jnp.where(column == c, 1.0, 0.0).astype(BF16)

    def later_tables():
        def column_table(z):
            line = jnp.broadcast_to(col_ref[pl.ds(z, 1), :], (16, LANES))
            for c in range(CLASSES):
                col_hot[c, z] = jnp.where(line == c, 1.0, 0.0).astype(BF16)
            for t in range(2):
                weight_v[t, z] = upright(weight_ref[t, pl.ds(z, 1), :])

        loop(LEVELS, column_table)

        def clear(z):
            filtered[z] = jnp.zeros((NY, LANES), BF16)

        loop(LEVELS, clear)

        def level_table(b):
            spot = lax.broadcasted_iota(jnp.int32, (TILE, LEVELS), 0) // ROWS + b * (TILE // ROWS)
            pick = jnp.where(
                spot == lax.broadcasted_iota(jnp.int32, (TILE, LEVELS), 1), 1.0, 0.0
            ).astype(BF16)
            wide = (LEVELS, LEVELS * ROWS)
            spread = jnp.where(
                lax.broadcasted_iota(jnp.int32, wide, 0)
                == lax.broadcasted_iota(jnp.int32, wide, 1) // ROWS,
                1.0,
                0.0,
            ).astype(BF16)
            tall = (TILE, LEVELS * ROWS)
            same = lax.rem(lax.broadcasted_iota(jnp.int32, tall, 0), ROWS) == lax.rem(
                lax.broadcasted_iota(jnp.int32, tall, 1), ROWS
            )
            rows = pl.ds(pl.multiple_of(b * TILE, TILE), TILE)
            level = level_ref[...]
            down[rows, :] = jnp.where(
                same, dot(dot_nt(pick, level).astype(BF16), spread), 0.0
            ).astype(BF16)
            back[rows, :] = jnp.where(
                same, dot(dot(pick, level).astype(BF16), spread), 0.0
            ).astype(BF16)

        loop(LEVELS * ROWS // TILE, level_table)
        loads[0].wait()
        unit = jnp.where(
            lax.broadcasted_iota(jnp.int32, (NY, NY), 0)
            == lax.broadcasted_iota(jnp.int32, (NY, NY), 1),
            1.0,
            0.0,
        ).astype(BF16)

        def turn(c):
            colt[c] = dot_nt(unit, colf[c]).astype(BF16)

        loop(CLASSES, turn)

    def remote(src, dst, ss, rs, member, group):
        return pltpu.make_async_remote_copy(
            src_ref=src, dst_ref=dst, send_sem=ss, recv_sem=rs,
            device_id=(member, group), device_id_type=MESH,
        )

    def exchange(phase, c, src, dst):
        def send(step):
            peer = lax.rem(g + step + 1, GROUP)
            remote(
                src(peer), dst(g), a2a_ss.at[phase, c, peer], a2a_rs.at[phase, c, g], m, peer
            ).start()

        loop(GROUP - 1, send)

    def exchanged(phase, c, peer, block):
        return remote(
            block, block, a2a_ss.at[phase, c, peer], a2a_rs.at[phase, c, peer], m, peer
        )

    def arrived(phase, c, dst):
        def wait(step):
            peer = lax.rem(g + GROUP - 1 - step, GROUP)
            exchanged(phase, c, peer, dst(peer)).wait_recv()

        loop(GROUP - 1, wait)

    def sent(phase, c, src):
        def wait(step):
            peer = lax.rem(g + step + 1, GROUP)
            exchanged(phase, c, peer, src(peer)).wait_send()

        loop(GROUP - 1, wait)

    def line_block(c):
        return lambda s: lines.at[part(c), slab_rows(s), :]

    def filtered_block(c):
        return lambda s: filtered.at[part(c), slab_rows(s), :]

    def slab_block(c):
        return lambda s: slabs.at[c, s]

    def local_block(c):
        return lambda s: local_r.at[c, s]

    def own_block(c):
        return lambda s: local_s.at[c, s]

    def mask_lines(c, source):
        for k in range(CLASSES):
            hot = row_hot[k, pl.ds(pl.multiple_of(c * LINES, LINES), LINES), :]
            masked[k] = source * jnp.concatenate([hot] * GROUP, axis=1)

    def row_filter(c):
        alpha_load(c).wait()
        mask_lines(c, alpha_v[part(c)].reshape(LINES, NX))
        for n in range(NX // TILE):
            depth = (n + 1) * TILE

            @pl.when(c == 0)
            def _():
                rowf_load(n).wait()

            total = sum(
                dot(masked[k, :, :depth], rowf[k, :depth, n * TILE : depth]) for k in range(CLASSES)
            ).astype(BF16)
            for half in range(2):
                slabs[c, 2 * n + half] = total[:, half * LANES : (half + 1) * LANES].reshape(
                    PART, ROWS, LANES
                )
        lines[part(c), slab_rows(g), :] = slabs[c, g]
        exchange(0, c, slab_block(c), line_block(c))

        @pl.when(c == 0)
        def _():
            for load in loads:
                load.start()

    def column_pass(c, table, upper):
        def pair(i):
            z = c * PART + 2 * i
            whole = jnp.concatenate([lines[z], lines[z + 1]], axis=1)
            blocks = []
            for k in range(CLASSES):
                hot = jnp.concatenate([col_hot[k, z], col_hot[k, z + 1]], axis=1)
                blocks.append(
                    (whole.reshape(NY // 16, 16, TILE) * hot[None]).reshape(NY, TILE)
                )
            half = NY // 2
            if upper:
                first = sum(dot(table[k, :half, :], blocks[k]) for k in range(CLASSES))
                second = sum(dot(table[k, half:, half:], blocks[k][half:]) for k in range(CLASSES))
            else:
                first = sum(dot(table[k, :half, :half], blocks[k][:half]) for k in range(CLASSES))
                second = sum(dot(table[k, half:, :], blocks[k]) for k in range(CLASSES))
            for j in range(2):
                side = slice(j * LANES, (j + 1) * LANES)
                filtered[z + j, :half, :] = first[:, side].astype(BF16)
                filtered[z + j, half:, :] = second[:, side].astype(BF16)

        loop(PART // 2, pair)

    def level_block(table, c, q):
        return table[
            pl.ds(pl.multiple_of(c * LINES, LINES), LINES),
            pl.ds(pl.multiple_of(q * TILE, TILE), TILE),
        ]

    def column_filter(c):
        arrived(0, c, line_block(c))
        column_pass(c, colt, False)

        def pair(i):
            def add(q, total):
                block = jnp.concatenate(
                    [
                        filtered[pl.ds(q * DEEP, DEEP), slab_rows(2 * i + j), :].reshape(TILE, LANES)
                        for j in range(2)
                    ],
                    axis=1,
                )
                return total + dot(level_block(down, c, q), block)

            total = lax.fori_loop(
                0, (c * PART) // DEEP + 1, add, jnp.zeros((LINES, 2 * LANES), F32)
            ).astype(BF16)
            for j in range(2):
                local_s[c, 2 * i + j] = total[:, j * LANES : (j + 1) * LANES].reshape(
                    PART, ROWS, LANES
                )

        loop(GROUP // 2, pair)
        local_r[c, g] = local_s[c, g]
        exchange(1, c, own_block(c), local_block(c))

    def core_copy(c):
        return pltpu.make_async_remote_copy(
            src_ref=core_s.at[c],
            dst_ref=core_r.at[c],
            send_sem=core_ss.at[c],
            recv_sem=core_rs.at[c],
            device_id=(sibling, g),
            device_id_type=MESH,
        )

    def xin_copy(c, way):
        slab = 2 * around(x, way, 2) + way
        return remote(
            core_r.at[c, slab], x_in.at[c, way], xin_ss.at[c, way], xin_rs.at[c, way],
            x_peer(way), g,
        )

    def xone_copy(c, way):
        slab = 2 * around(x, way) + 1 - way
        return remote(
            core_r.at[c, slab], x_one.at[c, way], xone_ss.at[c, way], xone_rs.at[c, way],
            x_peer(way), g,
        )

    def xtwo_copy(c, way):
        return remote(
            x_in.at[c, way], x_two.at[c, way], xtwo_ss.at[c, way], xtwo_rs.at[c, way],
            x_peer(way), g,
        )

    def y_copy(c):
        return pltpu.make_async_remote_copy(
            src_ref=y_s.at[c],
            dst_ref=y_r.at[c],
            send_sem=yr_ss.at[c],
            recv_sem=yr_rs.at[c],
            device_id=(across, g),
            device_id_type=MESH,
        )

    def term(t, c, s):
        return pert_v[t, part(c), :, lane(s)].astype(F32) * local_r[c, s].astype(F32)

    def sum_core(c):
        arrived(1, c, local_block(c))

        @pl.when(c == 0)
        def _():
            loads[1].wait()
            loads[2].wait()

        def one(s):
            core_s[c, s] = term(1 - core, c, s).astype(BF16)

        loop(GROUP, one)
        core_copy(c).start()

    def sum_x(c):
        core_copy(c).wait_recv()

        def one(s):
            core_r[c, s] = (term(core, c, s) + core_r[c, s].astype(F32)).astype(BF16)

        loop(GROUP, one)
        for way in range(2):
            xin_copy(c, way).start()
        for way in range(2):
            xone_copy(c, way).start()

    def add_x(c):
        for way in range(2):
            xin_copy(c, way).wait_recv()
            slab = 2 * around(x, way) + way
            x_in[c, way] = (x_in[c, way].astype(F32) + core_r[c, slab].astype(F32)).astype(BF16)
            xtwo_copy(c, way).start()

    def x_total(c, j):
        total = core_r[c, 2 * x + j].astype(F32) + x_two[c, j].astype(F32)
        return total + x_one[c, 1 - j].astype(F32)

    def sum_y(c):
        for way in range(2):
            xone_copy(c, way).wait_recv()
            xtwo_copy(c, way).wait_recv()
        y_s[c] = x_total(c, 1 - y_hi).astype(BF16)
        y_copy(c).start()

    def give(ss, rs, t, c, s, member):
        return pltpu.make_async_remote_copy(
            src_ref=inc.at[t, c, s],
            dst_ref=inc.at[t, c, s],
            send_sem=ss,
            recv_sem=rs,
            device_id=(member, g),
            device_id_type=MESH,
        )

    def give_y(c, s):
        return give(ya_ss.at[c], ya_rs.at[c], core, c, s, across)

    def give_x(c, turn, way, s):
        return give(xa_ss.at[c, turn, way], xa_rs.at[c, turn, way], core, c, s, x_peer(way))

    def give_far(c, turn, s):
        return give(xf_ss.at[c, turn], xf_rs.at[c, turn], core, c, s, x_peer(turn))

    def slab_of(owner, turn):
        return 2 * owner + (y_hi if turn == 0 else 1 - y_hi)

    def give_core(t, c, s):
        return give(ca_ss.at[c, s], ca_rs.at[c, s], t, c, s, sibling)

    mine = slab_of(x, 0)
    other = slab_of(x, 1)

    def finish(c):
        y_copy(c).wait_recv()
        inc[core, c, mine] = (x_total(c, y_hi) + y_r[c].astype(F32)).astype(BF16)
        give_y(c, mine).start()
        for way in range(2):
            give_x(c, 0, way, mine).start()
        give_core(core, c, mine).start()

    def gather_y(c):
        give_y(c, other).wait_recv()
        for way in range(2):
            give_x(c, 1, way, other).start()
        give_core(core, c, other).start()

    def gather_x(c):
        for turn in range(2):
            s = slab_of(around(x, 1 - turn), turn)
            give_x(c, turn, turn, s).wait_recv()
            give_far(c, turn, s).start()
            give_core(core, c, s).start()
        for turn in range(2):
            s = slab_of(around(x, turn), turn)
            give_x(c, turn, 1 - turn, s).wait_recv()
            give_core(core, c, s).start()

    def gather_far(c):
        for turn in range(2):
            s = slab_of(around(x, 0, 2), turn)
            give_far(c, turn, s).wait_recv()
            give_core(core, c, s).start()

    def weigh(c):
        def one(s):
            give_core(1 - core, c, s).wait_recv()
            total = jnp.zeros((PART, ROWS, LANES), F32)
            for t in range(2):
                block = inc[t, c, s]
                inc_v[t, part(c), :, lane(s)] = block
                misfit = weight_v[t, part(c)] * (
                    block.astype(F32) - innov_v[t, part(c), :, lane(s)].astype(F32)
                )
                total += pert_v[t, part(c), :, lane(s)].astype(F32) * misfit
            core_s[c, s] = total.astype(BF16)

        core_copy(c).wait_send()
        loop(GROUP, one)
        inc_copy(c).start()

    def inc_copy(c):
        return pltpu.make_async_copy(
            inc_v.at[:, part(c)], inc_h.at[:, part(c)], inc_sem.at[c]
        )

    def level_adjoint(c):
        sent(0, c, slab_block(c))

        def pair(i):
            def add(q, total):
                chunks = pl.ds(q * (DEEP // PART), DEEP // PART)
                block = jnp.concatenate(
                    [core_s[chunks, 2 * i + j].reshape(TILE, LANES) for j in range(2)], axis=1
                )
                return total + dot(level_block(back, c, q), block)

            total = lax.fori_loop(
                (c * PART) // DEEP, LEVELS // DEEP, add, jnp.zeros((LINES, 2 * LANES), F32)
            ).astype(BF16)
            for j in range(2):
                slabs[c, 2 * i + j] = total[:, j * LANES : (j + 1) * LANES].reshape(
                    PART, ROWS, LANES
                )

        loop(GROUP // 2, pair)
        lines[part(c), slab_rows(g), :] = slabs[c, g]
        exchange(2, c, slab_block(c), line_block(c))

    def column_adjoint(c):
        arrived(2, c, line_block(c))
        column_pass(c, colf, True)
        local_r[c, g] = filtered[part(c), slab_rows(g), :]
        exchange(3, c, filtered_block(c), local_block(c))

    def grad_copy(c):
        return pltpu.make_async_copy(alpha_v.at[part(c)], grad_h.at[part(c)], grad_sem.at[c])

    def row_adjoint(c):
        arrived(3, c, local_block(c))
        mask_lines(
            c, jnp.concatenate([local_r[c, s].reshape(LINES, LANES) for s in range(GROUP)], axis=1)
        )
        for n in range(NX // TILE):
            start = n * TILE
            total = sum(
                dot_nt(masked[k, :, start:], rowf[k, start : start + TILE, start:])
                for k in range(CLASSES)
            )
            side = slice(start, start + TILE)
            alpha = alpha_v[part(c), :, side].reshape(LINES, TILE).astype(F32)
            alpha_v[part(c), :, side] = (alpha + total).astype(BF16).reshape(PART, ROWS, TILE)
        grad_copy(c).start()

    loop(LEVELS, row_table)
    pl.semaphore_wait(barrier, GROUP + 3)

    def at(step, offset, stage):
        chunk = step - offset

        @pl.when(jnp.logical_and(chunk >= 0, chunk < CHUNKS))
        def _():
            stage(chunk)

    def forward(step):
        at(step, 3, sum_core)
        at(step, 0, row_filter)
        at(step, 7, gather_y)
        at(step, 4, add_x)
        at(step, 8, gather_x)
        at(step, 5, sum_y)
        at(step, 9, gather_far)
        at(step, 3, sum_x)

        @pl.when(step == 1)
        def _():
            later_tables()

        at(step, 1, column_filter)
        at(step, 10, weigh)
        at(step, 5, finish)

    loop(CHUNKS + 10, forward)

    def backward(step):
        at(step, 0, lambda c: level_adjoint(CHUNKS - 1 - c))
        at(step, 3, lambda c: column_adjoint(CHUNKS - 1 - c))
        at(step, 6, lambda c: row_adjoint(CHUNKS - 1 - c))

    loop(CHUNKS + 6, backward)

    def drain(c):
        sent(1, c, own_block(c))
        sent(2, c, slab_block(c))
        sent(3, c, filtered_block(c))
        y_copy(c).wait_send()
        give_y(c, mine).wait_send()
        for way in range(2):
            xin_copy(c, way).wait_send()
            xone_copy(c, way).wait_send()
            xtwo_copy(c, way).wait_send()
            give_x(c, 0, way, mine).wait_send()
            give_x(c, 1, way, other).wait_send()
            give_far(c, way, mine).wait_send()

        def one(s):
            give_core(core, c, s).wait_send()

        loop(GROUP, one)
        inc_copy(c).wait()
        grad_copy(c).wait()

    loop(CHUNKS, drain)


def on_device(alpha, pert, innov, weight, row_class, col_class, rowf, colf, level):
    any_spec = pl.BlockSpec(memory_space=pl.ANY)
    vmem_spec = pl.BlockSpec(memory_space=pltpu.VMEM)
    dma = pltpu.SemaphoreType.DMA
    block = (PART, ROWS, LANES)
    slab = (CHUNKS, GROUP) + block
    scratch = [
        pltpu.VMEM((LEVELS, ROWS, NX), BF16),
        pltpu.VMEM((2, LEVELS, ROWS, NX), BF16),
        pltpu.VMEM((2, LEVELS, ROWS, NX), BF16),
        pltpu.VMEM((CLASSES, NX, NX), BF16),
        pltpu.VMEM((CLASSES, NY, NY), BF16),
        pltpu.VMEM((CLASSES, NY, NY), BF16),
        pltpu.VMEM((LEVELS * ROWS, LEVELS * ROWS), BF16),
        pltpu.VMEM((LEVELS * ROWS, LEVELS * ROWS), BF16),
        pltpu.VMEM((CLASSES, LEVELS * ROWS, LANES), BF16),
        pltpu.VMEM((CLASSES, LEVELS, 16, LANES), BF16),
        pltpu.VMEM((2, LEVELS, ROWS, LANES), F32),
        pltpu.VMEM((CLASSES, LINES, NX), BF16),
        pltpu.VMEM(slab, BF16),
        pltpu.VMEM((LEVELS, NY, LANES), BF16),
        pltpu.VMEM((LEVELS, NY, LANES), BF16),
        pltpu.VMEM(slab, BF16),
        pltpu.VMEM(slab, BF16),
        pltpu.VMEM(slab, BF16),
        pltpu.VMEM(slab, BF16),
        pltpu.VMEM((CHUNKS, 2) + block, BF16),
        pltpu.VMEM((CHUNKS, 2) + block, BF16),
        pltpu.VMEM((CHUNKS, 2) + block, BF16),
        pltpu.VMEM((CHUNKS,) + block, BF16),
        pltpu.VMEM((CHUNKS,) + block, BF16),
        pltpu.VMEM((2,) + slab, BF16),
        pltpu.VMEM((2, LEVELS, ROWS, NX), BF16),
        dma((CHUNKS,)),
        dma((NX // TILE,)),
        dma((3,)),
        dma((CHUNKS,)),
        dma((CHUNKS,)),
    ]
    for counts in (
        (4, CHUNKS, GROUP),
        (CHUNKS,),
        (CHUNKS, 2),
        (CHUNKS, 2),
        (CHUNKS, 2),
        (CHUNKS,),
        (CHUNKS,),
        (CHUNKS, 2, 2),
        (CHUNKS, 2),
        (CHUNKS, GROUP),
    ):
        scratch += [dma(counts), dma(counts)]
    gradient, increment = pl.pallas_call(
        kernel,
        out_shape=(
            jax.ShapeDtypeStruct((LEVELS, ROWS, NX), BF16),
            jax.ShapeDtypeStruct((2, LEVELS, ROWS, NX), BF16),
        ),
        in_specs=[any_spec] * 3 + [vmem_spec] * 3 + [any_spec] * 2 + [vmem_spec],
        out_specs=(any_spec, any_spec),
        scratch_shapes=scratch,
        compiler_params=pltpu.CompilerParams(
            collective_id=0, has_side_effects=True, vmem_limit_bytes=62 * 1024 * 1024
        ),
    )(alpha[0], pert[0], innov, weight, row_class, col_class, rowf, colf, level)
    return gradient[None], increment


def solution(mesh):
    return jax.shard_map(
        on_device,
        mesh=mesh,
        in_specs=(
            P("member", None, "grid", None),
            P("member", None, None, "grid", None),
            P(None, None, "grid", None),
            P(None, None, "grid"),
            P(None, "grid"),
            P(None, "grid"),
            P(),
            P(),
            P(),
        ),
        out_specs=(P("member", None, "grid", None), P(None, None, "grid", None)),
        check_vma=False,
    )
```

```python
import functools

import jax
import jax.numpy as jnp
from jax import lax
from jax.experimental import pallas as pl
from jax.experimental.pallas import tpu as pltpu
from jax.sharding import PartitionSpec as P

MESH = pl.DeviceIdType.MESH
F32 = jnp.float32
BF16 = jnp.bfloat16

CLASSES = 3
LEVELS = 16
GROUP = 8
RING = 4
CHUNKS = 4
PART = LEVELS // CHUNKS
ROWS = 64
ROW_BITS = 6
LANES = 128
NX = GROUP * LANES
NY = GROUP * ROWS
LINES = PART * ROWS
TILE = 256
DEEP = TILE // ROWS


def loop(count, body):
    def step(index, carry):
        body(index)
        return carry

    lax.fori_loop(0, count, step, 0)


def dot(a, b):
    return jnp.dot(a, b, preferred_element_type=F32)


def dot_nt(a, b):
    return lax.dot_general(a, b, (((1,), (1,)), ((), ())), preferred_element_type=F32)


def kernel(
    alpha_h, pert_h, innov_h, weight_ref, row_ref, col_ref, rowf_h, colf_h, level_ref,
    grad_h, inc_h,
    alpha_v, pert_v, innov_v, rowf, colf, colt, down, back, row_hot, col_hot, weight_v, masked,
    slabs, lines, filtered, local_s, local_r, core_s, core_r, x_in, x_got, y_s, y_r,
    inc, inc_v,
    alpha_sem, rowf_sem, load_sem, grad_sem, inc_sem, out_sem, a2a_ss, a2a_rs, core_ss, core_rs,
    x_ss, xin_rs, xgot_rs, yr_ss, yr_rs, give_ss, ya_rs, xa_rs, xf_rs, ca_rs,
):
    m = lax.axis_index("member")
    g = lax.axis_index("grid")
    y_hi = m // (2 * RING)
    x = lax.rem(m // 2, RING)
    core = lax.rem(m, 2)
    sibling = m + 1 - 2 * core
    across = m + 2 * RING - 4 * RING * y_hi

    def around(position, way, steps=1):
        return lax.rem(position + (steps if way == 0 else RING - steps), RING)

    def x_peer(way):
        return y_hi * (2 * RING) + around(x, way) * 2 + core

    def lane(s):
        return pl.ds(pl.multiple_of(s * LANES, LANES), LANES)

    def slab_rows(s):
        return pl.ds(pl.multiple_of(s * ROWS, ROWS), ROWS)

    def part(c):
        return pl.ds(c * PART, PART)

    barrier = pltpu.get_barrier_semaphore()

    def greet(partner):
        pl.semaphore_signal(barrier, inc=1, device_id=partner, device_id_type=MESH)

    loop(GROUP - 1, lambda step: greet((m, lax.rem(g + step + 1, GROUP))))
    for member in (x_peer(0), x_peer(1), sibling, across):
        greet((member, g))

    def alpha_load(c):
        return pltpu.make_async_copy(alpha_h.at[part(c)], alpha_v.at[part(c)], alpha_sem.at[c])

    def rowf_load(n):
        where = (slice(None), slice(0, (n + 1) * TILE), slice(n * TILE, (n + 1) * TILE))
        return pltpu.make_async_copy(rowf_h.at[where], rowf.at[where], rowf_sem.at[n])

    alpha_load(0).start()
    for n in range(NX // TILE):
        rowf_load(n).start()
    for c in range(1, CHUNKS):
        alpha_load(c).start()
    loads = [
        pltpu.make_async_copy(src, dst, load_sem.at[i])
        for i, (src, dst) in enumerate(((colf_h, colf), (pert_h, pert_v), (innov_h, innov_v)))
    ]

    diagonal = lax.broadcasted_iota(jnp.int32, (ROWS, ROWS), 0) == lax.broadcasted_iota(
        jnp.int32, (ROWS, ROWS), 1
    )

    def upright(line):
        spread = jnp.where(diagonal, jnp.broadcast_to(line, (ROWS, ROWS)), 0.0)
        return jnp.broadcast_to(jnp.sum(spread, axis=1, keepdims=True), (ROWS, LANES))

    def row_table(z):
        column = upright(row_ref[pl.ds(z, 1), :].astype(F32))
        for c in range(CLASSES):
            row_hot[c, slab_rows(z), :] = jnp.where(column == c, 1.0, 0.0).astype(BF16)

    def iota(shape, axis):
        return lax.broadcasted_iota(jnp.int32, shape, axis)

    def level_table(table, product):
        wide = (LEVELS, LEVELS * ROWS)
        spread = jnp.where(iota(wide, 0) == iota(wide, 1) >> ROW_BITS, 1.0, 0.0).astype(BF16)
        tall = (TILE, LEVELS * ROWS)
        same = (iota(tall, 0) & (ROWS - 1)) == (iota(tall, 1) & (ROWS - 1))
        level = level_ref[...]
        for b in range(LEVELS * ROWS // TILE):
            short = (TILE, LEVELS)
            spot = (iota(short, 0) >> ROW_BITS) + b * DEEP
            pick = jnp.where(spot == iota(short, 1), 1.0, 0.0).astype(BF16)
            table[b * TILE : (b + 1) * TILE, :] = jnp.where(
                same, dot(product(pick, level).astype(BF16), spread), 0.0
            ).astype(BF16)

    def column_tables():
        def column_table(z):
            line = jnp.broadcast_to(col_ref[pl.ds(z, 1), :], (16, LANES))
            for c in range(CLASSES):
                col_hot[c, z] = jnp.where(line == c, 1.0, 0.0).astype(BF16)

        loop(LEVELS, column_table)
        level_table(down, dot_nt)
        loads[0].wait()
        unit = jnp.where(iota((NY, NY), 0) == iota((NY, NY), 1), 1.0, 0.0).astype(BF16)

        def turn(c):
            colt[c] = dot_nt(unit, colf[c]).astype(BF16)

        loop(CLASSES, turn)

    def adjoint_tables():
        def weight_table(z):
            for t in range(2):
                weight_v[t, z] = upright(weight_ref[t, pl.ds(z, 1), :])

        loop(LEVELS, weight_table)
        level_table(back, dot)

    def remote(src, dst, ss, rs, member, group):
        return pltpu.make_async_remote_copy(
            src_ref=src, dst_ref=dst, send_sem=ss, recv_sem=rs,
            device_id=(member, group), device_id_type=MESH,
        )

    def exchange(phase, c, src, dst):
        def send(step):
            peer = lax.rem(g + step + 1, GROUP)
            remote(src(peer), dst(g), a2a_ss.at[phase], a2a_rs.at[phase, c], m, peer).start()

        loop(GROUP - 1, send)

    def came(sem, view):
        remote(view, view, out_sem, sem, sibling, g).wait_recv()

    def left(sem, view):
        remote(view, view, sem, out_sem, sibling, g).wait_send()

    def lines_came(phase, c):
        came(a2a_rs.at[phase, c], lines.at[part(c), pl.ds(0, (GROUP - 1) * ROWS), :])

    def local_came(phase, c):
        came(a2a_rs.at[phase, c], local_r.at[c, pl.ds(0, GROUP - 1)])

    def exchange_left(phase):
        left(a2a_ss.at[phase], lines.at[:, pl.ds(0, (GROUP - 1) * ROWS), :])

    def line_block(c):
        return lambda s: lines.at[part(c), slab_rows(s), :]

    def filtered_block(c):
        return lambda s: filtered.at[part(c), slab_rows(s), :]

    def slab_block(c):
        return lambda s: slabs.at[c, s]

    def local_block(c):
        return lambda s: local_r.at[c, s]

    def own_block(c):
        return lambda s: local_s.at[c, s]

    def mask_lines(c, source):
        for k in range(CLASSES):
            hot = row_hot[k, pl.ds(pl.multiple_of(c * LINES, LINES), LINES), :]
            masked[k] = source * jnp.concatenate([hot] * GROUP, axis=1)

    def row_filter(c):
        alpha_load(c).wait()
        mask_lines(c, alpha_v[part(c)].reshape(LINES, NX))
        for n in range(NX // TILE):
            depth = (n + 1) * TILE

            @pl.when(c == 0)
            def _():
                rowf_load(n).wait()

            total = sum(
                dot(masked[k, :, :depth], rowf[k, :depth, n * TILE : depth]) for k in range(CLASSES)
            ).astype(BF16)
            for half in range(2):
                slabs[c, 2 * n + half] = total[:, half * LANES : (half + 1) * LANES].reshape(
                    PART, ROWS, LANES
                )
        lines[part(c), slab_rows(g), :] = slabs[c, g]
        exchange(0, c, slab_block(c), line_block(c))

        @pl.when(c == 0)
        def _():
            for load in loads:
                load.start()

    def column_pass(c, table, upper):
        def pair(i):
            z = c * PART + 2 * i
            whole = jnp.concatenate([lines[z], lines[z + 1]], axis=1)
            blocks = []
            for k in range(CLASSES):
                hot = jnp.concatenate([col_hot[k, z], col_hot[k, z + 1]], axis=1)
                blocks.append(
                    (whole.reshape(NY // 16, 16, TILE) * hot[None]).reshape(NY, TILE)
                )
            half = NY // 2
            if upper:
                first = sum(dot(table[k, :half, :], blocks[k]) for k in range(CLASSES))
                second = sum(dot(table[k, half:, half:], blocks[k][half:]) for k in range(CLASSES))
            else:
                first = sum(dot(table[k, :half, :half], blocks[k][:half]) for k in range(CLASSES))
                second = sum(dot(table[k, half:, :], blocks[k]) for k in range(CLASSES))
            for j in range(2):
                side = slice(j * LANES, (j + 1) * LANES)
                filtered[z + j, :half, :] = first[:, side].astype(BF16)
                filtered[z + j, half:, :] = second[:, side].astype(BF16)

        loop(PART // 2, pair)

    def level_block(table, c, q):
        return table[
            pl.ds(pl.multiple_of(c * LINES, LINES), LINES),
            pl.ds(pl.multiple_of(q * TILE, TILE), TILE),
        ]

    def column_filter(c):
        lines_came(0, c)
        column_pass(c, colt, False)

        def pair(i):
            def add(q, total):
                block = jnp.concatenate(
                    [
                        filtered[pl.ds(q * DEEP, DEEP), slab_rows(2 * i + j), :].reshape(TILE, LANES)
                        for j in range(2)
                    ],
                    axis=1,
                )
                return total + dot(level_block(down, c, q), block)

            total = lax.fori_loop(
                0, (c * PART) // DEEP + 1, add, jnp.zeros((LINES, 2 * LANES), F32)
            ).astype(BF16)
            for j in range(2):
                local_s[c, 2 * i + j] = total[:, j * LANES : (j + 1) * LANES].reshape(
                    PART, ROWS, LANES
                )

        loop(GROUP // 2, pair)
        local_r[c, g] = local_s[c, g]
        exchange(1, c, own_block(c), local_block(c))

    def core_copy(c):
        return pltpu.make_async_remote_copy(
            src_ref=core_s.at[c],
            dst_ref=core_r.at[c],
            send_sem=core_ss.at[c],
            recv_sem=core_rs.at[c],
            device_id=(sibling, g),
            device_id_type=MESH,
        )

    def xin_slab(way):
        return 2 * around(x, way, 2) + way

    def xone_slab(way):
        return 2 * around(x, way) + 1 - way

    def xtwo_slab(way):
        return 2 * around(x, way) + way

    def x_copy(src, dst, sem, way):
        return remote(src, dst, x_ss, sem, x_peer(way), g)

    def y_copy(c):
        return pltpu.make_async_remote_copy(
            src_ref=y_s.at[c],
            dst_ref=y_r.at[c],
            send_sem=yr_ss,
            recv_sem=yr_rs.at[c],
            device_id=(across, g),
            device_id_type=MESH,
        )

    def term(t, c, s):
        return pert_v[t, part(c), :, lane(s)].astype(F32) * local_r[c, s].astype(F32)

    def sum_core(c):
        local_came(1, c)

        @pl.when(c == 0)
        def _():
            loads[1].wait()
            loads[2].wait()

        def one(s):
            core_s[c, s] = pert_v[1 - core, part(c), :, lane(s)] * local_r[c, s]

        loop(GROUP, one)
        core_copy(c).start()

    def sum_x(c):
        core_copy(c).wait_recv()

        def add(s):
            core_r[c, s] = (term(core, c, s) + core_r[c, s].astype(F32)).astype(BF16)

        for way in range(2):
            s = xin_slab(way)
            add(s)
            x_copy(core_r.at[c, s], x_in.at[c, way], xin_rs.at[c], way).start()
        for way in range(2):
            s = xone_slab(way)
            add(s)
            x_copy(core_r.at[c, s], x_got.at[c, 0, way], xgot_rs.at[c], way).start()
        for way in range(2):
            add(xtwo_slab(way))
        for j in range(2):
            add(2 * x + j)

    def add_x(c):
        came(xin_rs.at[c], x_in.at[c])
        for way in range(2):
            slab = xtwo_slab(way)
            x_in[c, way] = (x_in[c, way].astype(F32) + core_r[c, slab].astype(F32)).astype(BF16)
            x_copy(x_in.at[c, way], x_got.at[c, 1, way], xgot_rs.at[c], way).start()

    def x_total(c, j):
        total = core_r[c, 2 * x + j].astype(F32) + x_got[c, 1, j].astype(F32)
        return total + x_got[c, 0, 1 - j].astype(F32)

    def sum_y(c):
        came(xgot_rs.at[c], x_got.at[c])
        y_s[c] = x_total(c, 1 - y_hi).astype(BF16)
        y_copy(c).start()

    def give(rs, t, c, s, member):
        return remote(inc.at[t, c, s], inc.at[t, c, s], give_ss, rs, member, g)

    def give_y(c, s):
        return give(ya_rs.at[c], core, c, s, across)

    def give_x(c, way, s):
        return give(xa_rs.at[c], core, c, s, x_peer(way))

    def give_far(c, turn, s):
        return give(xf_rs.at[c], core, c, s, x_peer(turn))

    def give_core(t, c, s):
        return give(ca_rs.at[c], t, c, s, sibling)

    def slab_of(owner, turn):
        return 2 * owner + (y_hi if turn == 0 else 1 - y_hi)

    mine = slab_of(x, 0)
    other = slab_of(x, 1)

    def finish(c):
        y_copy(c).wait_recv()
        inc[core, c, mine] = (x_total(c, y_hi) + y_r[c].astype(F32)).astype(BF16)
        give_y(c, mine).start()
        for way in range(2):
            give_x(c, way, mine).start()
        give_core(core, c, mine).start()

    def gather_y(c):
        give_y(c, other).wait_recv()
        for way in range(2):
            give_x(c, way, other).start()
        give_core(core, c, other).start()

    def gather_x(c):
        came(xa_rs.at[c], inc.at[core, c, pl.ds(0, 4)])
        for turn in range(2):
            s = slab_of(around(x, 1 - turn), turn)
            give_far(c, turn, s).start()
        for turn in range(2):
            for way in range(2):
                give_core(core, c, slab_of(around(x, way), turn)).start()

    def gather_far(c):
        came(xf_rs.at[c], inc.at[core, c, pl.ds(0, 2)])
        for turn in range(2):
            give_core(core, c, slab_of(around(x, 0, 2), turn)).start()

    def weigh(c):
        def one(s):
            total = jnp.zeros((PART, ROWS, LANES), F32)
            for t in range(2):
                block = inc[t, c, s]
                inc_v[t, part(c), :, lane(s)] = block
                misfit = weight_v[t, part(c)] * (
                    block.astype(F32) - innov_v[t, part(c), :, lane(s)].astype(F32)
                )
                total += pert_v[t, part(c), :, lane(s)].astype(F32) * misfit
            core_s[c, s] = total.astype(BF16)

        core_copy(c).wait_send()
        came(ca_rs.at[c], inc.at[1 - core, c])
        loop(GROUP, one)
        inc_copy(c).start()

    def inc_copy(c):
        return pltpu.make_async_copy(
            inc_v.at[:, part(c)], inc_h.at[:, part(c)], inc_sem.at[c]
        )

    def level_adjoint(c):
        def pair(i):
            def add(q, total):
                chunks = pl.ds(q * (DEEP // PART), DEEP // PART)
                block = jnp.concatenate(
                    [core_s[chunks, 2 * i + j].reshape(TILE, LANES) for j in range(2)], axis=1
                )
                return total + dot(level_block(back, c, q), block)

            total = lax.fori_loop(
                (c * PART) // DEEP, LEVELS // DEEP, add, jnp.zeros((LINES, 2 * LANES), F32)
            ).astype(BF16)
            for j in range(2):
                slabs[c, 2 * i + j] = total[:, j * LANES : (j + 1) * LANES].reshape(
                    PART, ROWS, LANES
                )

        loop(GROUP // 2, pair)
        lines[part(c), slab_rows(g), :] = slabs[c, g]
        exchange(2, c, slab_block(c), line_block(c))

    def column_adjoint(c):
        lines_came(2, c)
        column_pass(c, colf, True)
        local_r[c, g] = filtered[part(c), slab_rows(g), :]
        exchange(3, c, filtered_block(c), local_block(c))

    def grad_copy(c):
        return pltpu.make_async_copy(alpha_v.at[part(c)], grad_h.at[part(c)], grad_sem.at[c])

    def row_adjoint(c):
        local_came(3, c)
        mask_lines(
            c, jnp.concatenate([local_r[c, s].reshape(LINES, LANES) for s in range(GROUP)], axis=1)
        )
        for n in range(NX // TILE):
            start = n * TILE
            total = sum(
                dot_nt(masked[k, :, start:], rowf[k, start : start + TILE, start:])
                for k in range(CLASSES)
            )
            side = slice(start, start + TILE)
            alpha = alpha_v[part(c), :, side].reshape(LINES, TILE).astype(F32)
            alpha_v[part(c), :, side] = (alpha + total).astype(BF16).reshape(PART, ROWS, TILE)
        grad_copy(c).start()

    loop(LEVELS, row_table)
    pl.semaphore_wait(barrier, GROUP + 3)

    def at(step, offset, stage):
        chunk = step - offset

        @pl.when(jnp.logical_and(chunk >= 0, chunk < CHUNKS))
        def _():
            stage(chunk)

    def forward(step):
        @pl.when(step == 3)
        def _():
            adjoint_tables()

        at(step, 3, sum_core)
        at(step, 6, gather_y)
        at(step, 4, add_x)
        at(step, 5, finish)
        at(step, 0, row_filter)
        at(step, 10, weigh)
        at(step, 3, sum_x)
        at(step, 4, sum_y)
        at(step, 7, gather_x)

        @pl.when(step == 1)
        def _():
            column_tables()

        at(step, 1, column_filter)
        at(step, 8, gather_far)

    loop(CHUNKS + 10, forward)

    exchange_left(0)

    def backward(step):
        at(step, 0, lambda c: level_adjoint(CHUNKS - 1 - c))
        at(step, 2, lambda c: column_adjoint(CHUNKS - 1 - c))
        at(step, 4, lambda c: row_adjoint(CHUNKS - 1 - c))

    loop(CHUNKS + 4, backward)

    for phase in range(1, 4):
        exchange_left(phase)
    left(x_ss, core_r.at[pl.ds(0, 3)])
    left(yr_ss, y_s)
    left(give_ss, pert_v.at[:, pl.ds(0, LEVELS - 1)])
    for c in range(CHUNKS):
        inc_copy(c).wait()
        grad_copy(c).wait()


def on_device(alpha, pert, innov, weight, row_class, col_class, rowf, colf, level):
    any_spec = pl.BlockSpec(memory_space=pl.ANY)
    vmem_spec = pl.BlockSpec(memory_space=pltpu.VMEM)
    dma = pltpu.SemaphoreType.DMA
    block = (PART, ROWS, LANES)
    slab = (CHUNKS, GROUP) + block
    scratch = [
        pltpu.VMEM((LEVELS, ROWS, NX), BF16),
        pltpu.VMEM((2, LEVELS, ROWS, NX), BF16),
        pltpu.VMEM((2, LEVELS, ROWS, NX), BF16),
        pltpu.VMEM((CLASSES, NX, NX), BF16),
        pltpu.VMEM((CLASSES, NY, NY), BF16),
        pltpu.VMEM((CLASSES, NY, NY), BF16),
        pltpu.VMEM((LEVELS * ROWS, LEVELS * ROWS), BF16),
        pltpu.VMEM((LEVELS * ROWS, LEVELS * ROWS), BF16),
        pltpu.VMEM((CLASSES, LEVELS * ROWS, LANES), BF16),
        pltpu.VMEM((CLASSES, LEVELS, 16, LANES), BF16),
        pltpu.VMEM((2, LEVELS, ROWS, LANES), F32),
        pltpu.VMEM((CLASSES, LINES, NX), BF16),
        pltpu.VMEM(slab, BF16),
        pltpu.VMEM((LEVELS, NY, LANES), BF16),
        pltpu.VMEM((LEVELS, NY, LANES), BF16),
        pltpu.VMEM(slab, BF16),
        pltpu.VMEM(slab, BF16),
        pltpu.VMEM(slab, BF16),
        pltpu.VMEM(slab, BF16),
        pltpu.VMEM((CHUNKS, 2) + block, BF16),
        pltpu.VMEM((CHUNKS, 2, 2) + block, BF16),
        pltpu.VMEM((CHUNKS,) + block, BF16),
        pltpu.VMEM((CHUNKS,) + block, BF16),
        pltpu.VMEM((2,) + slab, BF16),
        pltpu.VMEM((2, LEVELS, ROWS, NX), BF16),
        dma((CHUNKS,)),
        dma((NX // TILE,)),
        dma((3,)),
        dma((CHUNKS,)),
        dma((CHUNKS,)),
        dma,
        dma((4,)),
        dma((4, CHUNKS)),
        dma((CHUNKS,)),
        dma((CHUNKS,)),
        dma,
        dma((CHUNKS,)),
        dma((CHUNKS,)),
        dma,
        dma((CHUNKS,)),
        dma,
        dma((CHUNKS,)),
        dma((CHUNKS,)),
        dma((CHUNKS,)),
        dma((CHUNKS,)),
    ]
    gradient, increment = pl.pallas_call(
        kernel,
        out_shape=(
            jax.ShapeDtypeStruct((LEVELS, ROWS, NX), BF16),
            jax.ShapeDtypeStruct((2, LEVELS, ROWS, NX), BF16),
        ),
        in_specs=[any_spec] * 3 + [vmem_spec] * 3 + [any_spec] * 2 + [vmem_spec],
        out_specs=(any_spec, any_spec),
        scratch_shapes=scratch,
        compiler_params=pltpu.CompilerParams(
            collective_id=0, has_side_effects=True, vmem_limit_bytes=62 * 1024 * 1024
        ),
    )(alpha[0], pert[0], innov, weight, row_class, col_class, rowf, colf, level)
    return gradient[None], increment


def solution(mesh):
    return jax.shard_map(
        on_device,
        mesh=mesh,
        in_specs=(
            P("member", None, "grid", None),
            P("member", None, None, "grid", None),
            P(None, None, "grid", None),
            P(None, None, "grid"),
            P(None, "grid"),
            P(None, "grid"),
            P(),
            P(),
            P(),
        ),
        out_specs=(P("member", None, "grid", None), P(None, None, "grid", None)),
        check_vma=False,
    )
```

```python
import functools

import jax
import jax.numpy as jnp
from jax import lax
from jax.experimental import pallas as pl
from jax.experimental.pallas import tpu as pltpu
from jax.sharding import PartitionSpec as P

MESH = pl.DeviceIdType.MESH
F32 = jnp.float32
BF16 = jnp.bfloat16

CLASSES = 3
LEVELS = 16
GROUP = 8
RING = 4
CHUNKS = 4
PART = LEVELS // CHUNKS
ROWS = 64
ROW_BITS = 6
LANES = 128
NX = GROUP * LANES
NY = GROUP * ROWS
LINES = PART * ROWS
TILE = 256
DEEP = TILE // ROWS


def loop(count, body):
    def step(index, carry):
        body(index)
        return carry

    lax.fori_loop(0, count, step, 0)


def dot(a, b):
    return jnp.dot(a, b, preferred_element_type=F32)


def dot_nt(a, b):
    return lax.dot_general(a, b, (((1,), (1,)), ((), ())), preferred_element_type=F32)


def kernel(
    alpha_h, pert_h, innov_h, weight_ref, row_ref, col_ref, rowf_h, colf_h, level_ref,
    grad_h, inc_h,
    alpha_v, pert_v, innov_v, rowf, colf, colt, down, back, row_hot, col_hot, weight_v, masked,
    slabs, lines, filtered, turned, local_s, local_r, core_s, core_r, x_in, x_got, y_s, y_r,
    inc, inc_v,
    alpha_sem, rowf_sem, load_sem, grad_sem, inc_sem, out_sem, a2a_ss, a2a_rs, core_ss, core_rs,
    x_ss, xin_rs, xgot_rs, yr_ss, yr_rs, give_ss, ya_rs, xa_rs, xf_rs, ca_rs,
):
    m = lax.axis_index("member")
    g = lax.axis_index("grid")
    y_hi = m // (2 * RING)
    x = lax.rem(m // 2, RING)
    core = lax.rem(m, 2)
    sibling = m + 1 - 2 * core
    across = m + 2 * RING - 4 * RING * y_hi

    def around(position, way, steps=1):
        return lax.rem(position + (steps if way == 0 else RING - steps), RING)

    def x_peer(way):
        return y_hi * (2 * RING) + around(x, way) * 2 + core

    def lane(s):
        return pl.ds(pl.multiple_of(s * LANES, LANES), LANES)

    def slab_rows(s):
        return pl.ds(pl.multiple_of(s * ROWS, ROWS), ROWS)

    def part(c):
        return pl.ds(c * PART, PART)

    barrier = pltpu.get_barrier_semaphore()

    def greet(partner):
        pl.semaphore_signal(barrier, inc=1, device_id=partner, device_id_type=MESH)

    loop(GROUP - 1, lambda step: greet((m, lax.rem(g + step + 1, GROUP))))
    for member in (x_peer(0), x_peer(1), sibling, across):
        greet((member, g))

    def alpha_load(c):
        return pltpu.make_async_copy(alpha_h.at[part(c)], alpha_v.at[part(c)], alpha_sem.at[c])

    def rowf_load(n):
        where = (slice(None), slice(0, (n + 1) * TILE), slice(n * TILE, (n + 1) * TILE))
        return pltpu.make_async_copy(rowf_h.at[where], rowf.at[where], rowf_sem.at[n])

    alpha_load(0).start()
    for n in range(NX // TILE):
        rowf_load(n).start()
    for c in range(1, CHUNKS):
        alpha_load(c).start()
    loads = [
        pltpu.make_async_copy(src, dst, load_sem.at[i])
        for i, (src, dst) in enumerate(((colf_h, colf), (pert_h, pert_v), (innov_h, innov_v)))
    ]

    diagonal = lax.broadcasted_iota(jnp.int32, (ROWS, ROWS), 0) == lax.broadcasted_iota(
        jnp.int32, (ROWS, ROWS), 1
    )

    def upright(line):
        spread = jnp.where(diagonal, jnp.broadcast_to(line, (ROWS, ROWS)), 0.0)
        return jnp.broadcast_to(jnp.sum(spread, axis=1, keepdims=True), (ROWS, LANES))

    def row_table(z):
        column = upright(row_ref[pl.ds(z, 1), :].astype(F32))
        for c in range(CLASSES):
            row_hot[c, slab_rows(z), :] = jnp.where(column == c, 1.0, 0.0).astype(BF16)

    def iota(shape, axis):
        return lax.broadcasted_iota(jnp.int32, shape, axis)

    def level_table(table, product):
        wide = (LEVELS, LEVELS * ROWS)
        spread = jnp.where(iota(wide, 0) == iota(wide, 1) >> ROW_BITS, 1.0, 0.0).astype(BF16)
        tall = (TILE, LEVELS * ROWS)
        same = (iota(tall, 0) & (ROWS - 1)) == (iota(tall, 1) & (ROWS - 1))
        level = level_ref[...]
        for b in range(LEVELS * ROWS // TILE):
            short = (TILE, LEVELS)
            spot = (iota(short, 0) >> ROW_BITS) + b * DEEP
            pick = jnp.where(spot == iota(short, 1), 1.0, 0.0).astype(BF16)
            table[b * TILE : (b + 1) * TILE, :] = jnp.where(
                same, dot(product(pick, level).astype(BF16), spread), 0.0
            ).astype(BF16)

    def column_tables():
        def column_table(z):
            line = jnp.broadcast_to(col_ref[pl.ds(z, 1), :], (16, LANES))
            for c in range(CLASSES):
                col_hot[c, z] = jnp.where(line == c, 1.0, 0.0).astype(BF16)

        loop(LEVELS, column_table)
        level_table(down, dot_nt)
        loads[0].wait()
        unit = jnp.where(iota((NY, NY), 0) == iota((NY, NY), 1), 1.0, 0.0).astype(BF16)

        def turn(c):
            colt[c] = dot_nt(unit, colf[c]).astype(BF16)

        loop(CLASSES, turn)

    def adjoint_tables():
        def weight_table(z):
            for t in range(2):
                weight_v[t, z] = upright(weight_ref[t, pl.ds(z, 1), :])

        loop(LEVELS, weight_table)
        level_table(back, dot)

    def remote(src, dst, ss, rs, member, group):
        return pltpu.make_async_remote_copy(
            src_ref=src, dst_ref=dst, send_sem=ss, recv_sem=rs,
            device_id=(member, group), device_id_type=MESH,
        )

    def exchange(phase, c, src, dst):
        def send(step):
            peer = lax.rem(g + step + 1, GROUP)
            remote(src(peer), dst(g), a2a_ss.at[phase], a2a_rs.at[phase, c], m, peer).start()

        loop(GROUP - 1, send)

    def came(sem, view):
        remote(view, view, out_sem, sem, sibling, g).wait_recv()

    def left(sem, view):
        remote(view, view, sem, out_sem, sibling, g).wait_send()

    def lines_came(phase, c):
        came(a2a_rs.at[phase, c], lines.at[part(c), pl.ds(0, (GROUP - 1) * ROWS), :])

    def local_came(phase, c):
        came(a2a_rs.at[phase, c], local_r.at[c, pl.ds(0, GROUP - 1)])

    def exchange_left(phase):
        left(a2a_ss.at[phase], lines.at[:, pl.ds(0, (GROUP - 1) * ROWS), :])

    def line_block(c):
        return lambda s: lines.at[part(c), slab_rows(s), :]

    def filtered_block(c):
        return lambda s: filtered.at[part(c), slab_rows(s), :]

    def weighted_block(c):
        return lambda s: core_s.at[c, s]

    def slab_block(c):
        return lambda s: slabs.at[c, s]

    def local_block(c):
        return lambda s: local_r.at[c, s]

    def own_block(c):
        return lambda s: local_s.at[c, s]

    def mask_lines(c, source):
        for k in range(CLASSES):
            hot = row_hot[k, pl.ds(pl.multiple_of(c * LINES, LINES), LINES), :]
            masked[k] = source * jnp.concatenate([hot] * GROUP, axis=1)

    def row_filter(c):
        alpha_load(c).wait()
        mask_lines(c, alpha_v[part(c)].reshape(LINES, NX))
        for n in range(NX // TILE):
            depth = (n + 1) * TILE

            @pl.when(c == 0)
            def _():
                rowf_load(n).wait()

            total = sum(
                dot(masked[k, :, :depth], rowf[k, :depth, n * TILE : depth]) for k in range(CLASSES)
            ).astype(BF16)
            for half in range(2):
                slabs[c, 2 * n + half] = total[:, half * LANES : (half + 1) * LANES].reshape(
                    PART, ROWS, LANES
                )
        lines[part(c), slab_rows(g), :] = slabs[c, g]
        exchange(0, c, slab_block(c), line_block(c))

        @pl.when(c == 0)
        def _():
            for load in loads:
                load.start()

    def column_pass(c, source, table, upper):
        def pair(i):
            z = c * PART + 2 * i
            whole = jnp.concatenate([source[z], source[z + 1]], axis=1)
            blocks = []
            for k in range(CLASSES):
                hot = jnp.concatenate([col_hot[k, z], col_hot[k, z + 1]], axis=1)
                blocks.append(
                    (whole.reshape(NY // 16, 16, TILE) * hot[None]).reshape(NY, TILE)
                )
            half = NY // 2
            if upper:
                first = sum(dot(table[k, :half, :], blocks[k]) for k in range(CLASSES))
                second = sum(dot(table[k, half:, half:], blocks[k][half:]) for k in range(CLASSES))
            else:
                first = sum(dot(table[k, :half, :half], blocks[k][:half]) for k in range(CLASSES))
                second = sum(dot(table[k, half:, :], blocks[k]) for k in range(CLASSES))
            for j in range(2):
                side = slice(j * LANES, (j + 1) * LANES)
                filtered[z + j, :half, :] = first[:, side].astype(BF16)
                filtered[z + j, half:, :] = second[:, side].astype(BF16)

        loop(PART // 2, pair)

    def level_block(table, c, q):
        return table[
            pl.ds(pl.multiple_of(c * LINES, LINES), LINES),
            pl.ds(pl.multiple_of(q * TILE, TILE), TILE),
        ]

    def column_filter(c):
        lines_came(0, c)
        column_pass(c, lines, colt, False)

        def pair(i):
            def add(q, total):
                block = jnp.concatenate(
                    [
                        filtered[pl.ds(q * DEEP, DEEP), slab_rows(2 * i + j), :].reshape(TILE, LANES)
                        for j in range(2)
                    ],
                    axis=1,
                )
                return total + dot(level_block(down, c, q), block)

            total = lax.fori_loop(
                0, (c * PART) // DEEP + 1, add, jnp.zeros((LINES, 2 * LANES), F32)
            ).astype(BF16)
            for j in range(2):
                local_s[c, 2 * i + j] = total[:, j * LANES : (j + 1) * LANES].reshape(
                    PART, ROWS, LANES
                )

        loop(GROUP // 2, pair)
        local_r[c, g] = local_s[c, g]
        exchange(1, c, own_block(c), local_block(c))

    def core_copy(c):
        return pltpu.make_async_remote_copy(
            src_ref=core_s.at[c],
            dst_ref=core_r.at[c],
            send_sem=core_ss.at[c],
            recv_sem=core_rs.at[c],
            device_id=(sibling, g),
            device_id_type=MESH,
        )

    def xin_slab(way):
        return 2 * around(x, way, 2) + way

    def xone_slab(way):
        return 2 * around(x, way) + 1 - way

    def xtwo_slab(way):
        return 2 * around(x, way) + way

    def x_copy(src, dst, sem, way):
        return remote(src, dst, x_ss, sem, x_peer(way), g)

    def y_copy(c):
        return pltpu.make_async_remote_copy(
            src_ref=y_s.at[c],
            dst_ref=y_r.at[c],
            send_sem=yr_ss,
            recv_sem=yr_rs.at[c],
            device_id=(across, g),
            device_id_type=MESH,
        )

    def term(t, c, s):
        return pert_v[t, part(c), :, lane(s)].astype(F32) * local_r[c, s].astype(F32)

    def sum_core(c):
        local_came(1, c)

        @pl.when(c == 0)
        def _():
            loads[1].wait()
            loads[2].wait()

        def one(s):
            core_s[c, s] = pert_v[1 - core, part(c), :, lane(s)] * local_r[c, s]

        loop(GROUP, one)
        core_copy(c).start()

    def sum_x(c):
        core_copy(c).wait_recv()

        def add(s):
            core_r[c, s] = (term(core, c, s) + core_r[c, s].astype(F32)).astype(BF16)

        for way in range(2):
            s = xin_slab(way)
            add(s)
            x_copy(core_r.at[c, s], x_in.at[c, way], xin_rs.at[c], way).start()
        for way in range(2):
            s = xone_slab(way)
            add(s)
            x_copy(core_r.at[c, s], x_got.at[c, 0, way], xgot_rs.at[c], way).start()
        for way in range(2):
            add(xtwo_slab(way))
        for j in range(2):
            add(2 * x + j)

    def add_x(c):
        came(xin_rs.at[c], x_in.at[c])
        for way in range(2):
            slab = xtwo_slab(way)
            x_in[c, way] = (x_in[c, way].astype(F32) + core_r[c, slab].astype(F32)).astype(BF16)
            x_copy(x_in.at[c, way], x_got.at[c, 1, way], xgot_rs.at[c], way).start()

    def x_total(c, j):
        total = core_r[c, 2 * x + j].astype(F32) + x_got[c, 1, j].astype(F32)
        return total + x_got[c, 0, 1 - j].astype(F32)

    def sum_y(c):
        came(xgot_rs.at[c], x_got.at[c])
        y_s[c] = x_total(c, 1 - y_hi).astype(BF16)
        y_copy(c).start()

    def give(rs, t, c, s, member):
        return remote(inc.at[t, c, s], inc.at[t, c, s], give_ss, rs, member, g)

    def give_y(c, s):
        return give(ya_rs.at[c], core, c, s, across)

    def give_x(c, way, s):
        return give(xa_rs.at[c], core, c, s, x_peer(way))

    def give_far(c, turn, s):
        return give(xf_rs.at[c], core, c, s, x_peer(turn))

    def give_core(t, c, s):
        return give(ca_rs.at[c], t, c, s, sibling)

    def slab_of(owner, turn):
        return 2 * owner + (y_hi if turn == 0 else 1 - y_hi)

    mine = slab_of(x, 0)
    other = slab_of(x, 1)

    def finish(c):
        y_copy(c).wait_recv()
        inc[core, c, mine] = (x_total(c, y_hi) + y_r[c].astype(F32)).astype(BF16)
        give_y(c, mine).start()
        for way in range(2):
            give_x(c, way, mine).start()
        give_core(core, c, mine).start()

    def gather_y(c):
        give_y(c, other).wait_recv()
        for way in range(2):
            give_x(c, way, other).start()
        give_core(core, c, other).start()

    def gather_x(c):
        came(xa_rs.at[c], inc.at[core, c, pl.ds(0, 4)])
        for turn in range(2):
            s = slab_of(around(x, 1 - turn), turn)
            give_far(c, turn, s).start()
        for turn in range(2):
            for way in range(2):
                give_core(core, c, slab_of(around(x, way), turn)).start()

    def gather_far(c):
        came(xf_rs.at[c], inc.at[core, c, pl.ds(0, 2)])
        for turn in range(2):
            give_core(core, c, slab_of(around(x, 0, 2), turn)).start()

    def weigh(c):
        def one(s):
            total = jnp.zeros((PART, ROWS, LANES), F32)
            for t in range(2):
                block = inc[t, c, s]
                inc_v[t, part(c), :, lane(s)] = block
                misfit = weight_v[t, part(c)] * (
                    block.astype(F32) - innov_v[t, part(c), :, lane(s)].astype(F32)
                )
                total += pert_v[t, part(c), :, lane(s)].astype(F32) * misfit
            core_s[c, s] = total.astype(BF16)

        core_copy(c).wait_send()
        came(ca_rs.at[c], inc.at[1 - core, c])
        loop(GROUP, one)
        lines[part(c), slab_rows(g), :] = core_s[c, g]
        exchange(2, c, weighted_block(c), line_block(c))
        inc_copy(c).start()

    def inc_copy(c):
        return pltpu.make_async_copy(
            inc_v.at[:, part(c)], inc_h.at[:, part(c)], inc_sem.at[c]
        )

    def column_adjoint(c):
        lines_came(2, c)

        def pair(i):
            def add(q, total):
                block = jnp.concatenate(
                    [
                        lines[pl.ds(q * DEEP, DEEP), slab_rows(2 * i + j), :].reshape(TILE, LANES)
                        for j in range(2)
                    ],
                    axis=1,
                )
                return total + dot(level_block(back, c, q), block)

            total = lax.fori_loop(
                (c * PART) // DEEP, LEVELS // DEEP, add, jnp.zeros((LINES, 2 * LANES), F32)
            ).astype(BF16)
            for j in range(2):
                turned[part(c), slab_rows(2 * i + j), :] = total[
                    :, j * LANES : (j + 1) * LANES
                ].reshape(PART, ROWS, LANES)

        loop(GROUP // 2, pair)
        column_pass(c, turned, colf, True)
        local_r[c, g] = filtered[part(c), slab_rows(g), :]
        exchange(3, c, filtered_block(c), local_block(c))

    def grad_copy(c):
        return pltpu.make_async_copy(alpha_v.at[part(c)], grad_h.at[part(c)], grad_sem.at[c])

    def row_adjoint(c):
        local_came(3, c)
        mask_lines(
            c, jnp.concatenate([local_r[c, s].reshape(LINES, LANES) for s in range(GROUP)], axis=1)
        )
        for n in range(NX // TILE):
            start = n * TILE
            total = sum(
                dot_nt(masked[k, :, start:], rowf[k, start : start + TILE, start:])
                for k in range(CLASSES)
            )
            side = slice(start, start + TILE)
            alpha = alpha_v[part(c), :, side].reshape(LINES, TILE).astype(F32)
            alpha_v[part(c), :, side] = (alpha + total).astype(BF16).reshape(PART, ROWS, TILE)
        grad_copy(c).start()

    loop(LEVELS, row_table)
    pl.semaphore_wait(barrier, GROUP + 3)

    def at(step, offset, stage):
        chunk = step - offset

        @pl.when(jnp.logical_and(chunk >= 0, chunk < CHUNKS))
        def _():
            stage(chunk)

    def forward(step):
        at(step, 6, gather_y)
        at(step, 4, sum_x)
        at(step, 5, sum_y)
        at(step, 7, weigh)
        at(step, 6, gather_x)
        at(step, 5, finish)

        @pl.when(step == 2)
        def _():
            column_tables()

        at(step, 2, column_filter)

        @pl.when(step == 3)
        def _():
            adjoint_tables()

        at(step, 3, sum_core)
        at(step, 4, add_x)
        at(step, 6, gather_far)
        at(step, 0, row_filter)

    loop(CHUNKS + 7, forward)

    def backward(step):
        at(step, 0, lambda c: column_adjoint(CHUNKS - 1 - c))
        at(step, 2, lambda c: row_adjoint(CHUNKS - 1 - c))

    loop(CHUNKS + 2, backward)

    for phase in range(4):
        exchange_left(phase)
    left(x_ss, core_r.at[pl.ds(0, 3)])
    left(yr_ss, y_s)
    left(give_ss, pert_v.at[:, pl.ds(0, LEVELS - 1)])
    for c in range(CHUNKS):
        inc_copy(c).wait()
        grad_copy(c).wait()


def on_device(alpha, pert, innov, weight, row_class, col_class, rowf, colf, level):
    any_spec = pl.BlockSpec(memory_space=pl.ANY)
    vmem_spec = pl.BlockSpec(memory_space=pltpu.VMEM)
    dma = pltpu.SemaphoreType.DMA
    block = (PART, ROWS, LANES)
    slab = (CHUNKS, GROUP) + block
    scratch = [
        pltpu.VMEM((LEVELS, ROWS, NX), BF16),
        pltpu.VMEM((2, LEVELS, ROWS, NX), BF16),
        pltpu.VMEM((2, LEVELS, ROWS, NX), BF16),
        pltpu.VMEM((CLASSES, NX, NX), BF16),
        pltpu.VMEM((CLASSES, NY, NY), BF16),
        pltpu.VMEM((CLASSES, NY, NY), BF16),
        pltpu.VMEM((LEVELS * ROWS, LEVELS * ROWS), BF16),
        pltpu.VMEM((LEVELS * ROWS, LEVELS * ROWS), BF16),
        pltpu.VMEM((CLASSES, LEVELS * ROWS, LANES), BF16),
        pltpu.VMEM((CLASSES, LEVELS, 16, LANES), BF16),
        pltpu.VMEM((2, LEVELS, ROWS, LANES), F32),
        pltpu.VMEM((CLASSES, LINES, NX), BF16),
        pltpu.VMEM(slab, BF16),
        pltpu.VMEM((LEVELS, NY, LANES), BF16),
        pltpu.VMEM((LEVELS, NY, LANES), BF16),
        pltpu.VMEM((LEVELS, NY, LANES), BF16),
        pltpu.VMEM(slab, BF16),
        pltpu.VMEM(slab, BF16),
        pltpu.VMEM(slab, BF16),
        pltpu.VMEM(slab, BF16),
        pltpu.VMEM((CHUNKS, 2) + block, BF16),
        pltpu.VMEM((CHUNKS, 2, 2) + block, BF16),
        pltpu.VMEM((CHUNKS,) + block, BF16),
        pltpu.VMEM((CHUNKS,) + block, BF16),
        pltpu.VMEM((2,) + slab, BF16),
        pltpu.VMEM((2, LEVELS, ROWS, NX), BF16),
        dma((CHUNKS,)),
        dma((NX // TILE,)),
        dma((3,)),
        dma((CHUNKS,)),
        dma((CHUNKS,)),
        dma,
        dma((4,)),
        dma((4, CHUNKS)),
        dma((CHUNKS,)),
        dma((CHUNKS,)),
        dma,
        dma((CHUNKS,)),
        dma((CHUNKS,)),
        dma,
        dma((CHUNKS,)),
        dma,
        dma((CHUNKS,)),
        dma((CHUNKS,)),
        dma((CHUNKS,)),
        dma((CHUNKS,)),
    ]
    gradient, increment = pl.pallas_call(
        kernel,
        out_shape=(
            jax.ShapeDtypeStruct((LEVELS, ROWS, NX), BF16),
            jax.ShapeDtypeStruct((2, LEVELS, ROWS, NX), BF16),
        ),
        in_specs=[any_spec] * 3 + [vmem_spec] * 3 + [any_spec] * 2 + [vmem_spec],
        out_specs=(any_spec, any_spec),
        scratch_shapes=scratch,
        compiler_params=pltpu.CompilerParams(
            collective_id=0, has_side_effects=True, vmem_limit_bytes=62 * 1024 * 1024
        ),
    )(alpha[0], pert[0], innov, weight, row_class, col_class, rowf, colf, level)
    return gradient[None], increment


def solution(mesh):
    return jax.shard_map(
        on_device,
        mesh=mesh,
        in_specs=(
            P("member", None, "grid", None),
            P("member", None, None, "grid", None),
            P(None, None, "grid", None),
            P(None, None, "grid"),
            P(None, "grid"),
            P(None, "grid"),
            P(),
            P(),
            P(),
        ),
        out_specs=(P("member", None, "grid", None), P(None, None, "grid", None)),
        check_vma=False,
    )
```

```python
import functools

import jax
import jax.numpy as jnp
from jax import lax
from jax.experimental import pallas as pl
from jax.experimental.pallas import tpu as pltpu
from jax.sharding import PartitionSpec as P

MESH = pl.DeviceIdType.MESH
F32 = jnp.float32
BF16 = jnp.bfloat16

CLASSES = 3
LEVELS = 16
GROUP = 8
RING = 4
CHUNKS = 4
PART = LEVELS // CHUNKS
ROWS = 64
ROW_BITS = 6
LANES = 128
NX = GROUP * LANES
NY = GROUP * ROWS
LINES = PART * ROWS
TILE = 256
TILES = NX // TILE
DEEP = TILE // ROWS


def loop(count, body):
    def step(index, carry):
        body(index)
        return carry

    lax.fori_loop(0, count, step, 0)


def dot(a, b):
    return jnp.dot(a, b, preferred_element_type=F32)


def dot_nt(a, b):
    return lax.dot_general(a, b, (((1,), (1,)), ((), ())), preferred_element_type=F32)


def kernel(
    alpha_h, pert_h, innov_h, weight_ref, row_ref, col_ref, rowf_h, colf_h, level_ref,
    grad_h, inc_h,
    alpha_v, pert_v, innov_v, rowf, colf, colt, down, back, row_hot, col_hot, weight_v, masked,
    slabs, lines, filtered, turned, local_s, local_r, core_s, core_r, x_in, x_got, y_s, y_r,
    inc, inc_v,
    alpha_sem, rowf_sem, load_sem, grad_sem, inc_sem, out_sem, a2a_ss, a2a_rs, core_ss, core_rs,
    x_ss, xin_rs, xgot_rs, yr_ss, yr_rs, give_ss, ya_rs, xa_rs, xf_rs, ca_rs,
):
    m = lax.axis_index("member")
    g = lax.axis_index("grid")
    y_hi = m // (2 * RING)
    x = lax.rem(m // 2, RING)
    core = lax.rem(m, 2)
    sibling = m + 1 - 2 * core
    across = m + 2 * RING - 4 * RING * y_hi

    def around(position, way, steps=1):
        return lax.rem(position + (steps if way == 0 else RING - steps), RING)

    def x_peer(way):
        return y_hi * (2 * RING) + around(x, way) * 2 + core

    def lane(s):
        return pl.ds(pl.multiple_of(s * LANES, LANES), LANES)

    def slab_rows(s):
        return pl.ds(pl.multiple_of(s * ROWS, ROWS), ROWS)

    def part(c):
        return pl.ds(c * PART, PART)

    barrier = pltpu.get_barrier_semaphore()

    def greet(partner):
        pl.semaphore_signal(barrier, inc=1, device_id=partner, device_id_type=MESH)

    loop(GROUP - 1, lambda step: greet((m, lax.rem(g + step + 1, GROUP))))
    for member in (x_peer(0), x_peer(1), sibling, across):
        greet((member, g))

    def alpha_load(c):
        return pltpu.make_async_copy(alpha_h.at[part(c)], alpha_v.at[part(c)], alpha_sem.at[c])

    def rowf_load(n):
        where = (slice(None), slice(0, (n + 1) * TILE), slice(n * TILE, (n + 1) * TILE))
        return pltpu.make_async_copy(rowf_h.at[where], rowf.at[where], rowf_sem.at[n])

    alpha_load(0).start()
    for n in range(NX // TILE):
        rowf_load(n).start()
    for c in range(1, CHUNKS):
        alpha_load(c).start()
    loads = [
        pltpu.make_async_copy(src, dst, load_sem.at[i])
        for i, (src, dst) in enumerate(((colf_h, colf), (pert_h, pert_v), (innov_h, innov_v)))
    ]

    diagonal = lax.broadcasted_iota(jnp.int32, (ROWS, ROWS), 0) == lax.broadcasted_iota(
        jnp.int32, (ROWS, ROWS), 1
    )

    def upright(line):
        spread = jnp.where(diagonal, jnp.broadcast_to(line, (ROWS, ROWS)), 0.0)
        return jnp.broadcast_to(jnp.sum(spread, axis=1, keepdims=True), (ROWS, LANES))

    def row_table(z):
        column = upright(row_ref[pl.ds(z, 1), :].astype(F32))
        for c in range(CLASSES):
            row_hot[c, slab_rows(z), :] = jnp.where(column == c, 1.0, 0.0).astype(BF16)

    def iota(shape, axis):
        return lax.broadcasted_iota(jnp.int32, shape, axis)

    def level_table(table, product):
        wide = (LEVELS, LEVELS * ROWS)
        spread = jnp.where(iota(wide, 0) == iota(wide, 1) >> ROW_BITS, 1.0, 0.0).astype(BF16)
        tall = (TILE, LEVELS * ROWS)
        same = (iota(tall, 0) & (ROWS - 1)) == (iota(tall, 1) & (ROWS - 1))
        level = level_ref[...]
        for b in range(LEVELS * ROWS // TILE):
            short = (TILE, LEVELS)
            spot = (iota(short, 0) >> ROW_BITS) + b * DEEP
            pick = jnp.where(spot == iota(short, 1), 1.0, 0.0).astype(BF16)
            table[b * TILE : (b + 1) * TILE, :] = jnp.where(
                same, dot(product(pick, level).astype(BF16), spread), 0.0
            ).astype(BF16)

    def column_tables():
        def column_table(z):
            line = jnp.broadcast_to(col_ref[pl.ds(z, 1), :], (16, LANES))
            for c in range(CLASSES):
                col_hot[c, z] = jnp.where(line == c, 1.0, 0.0).astype(BF16)

        loop(LEVELS, column_table)
        level_table(down, dot_nt)
        loads[0].wait()
        unit = jnp.where(iota((NY, NY), 0) == iota((NY, NY), 1), 1.0, 0.0).astype(BF16)

        def turn(c):
            colt[c] = dot_nt(unit, colf[c]).astype(BF16)

        loop(CLASSES, turn)

    def adjoint_tables():
        def weight_table(z):
            for t in range(2):
                weight_v[t, z] = upright(weight_ref[t, pl.ds(z, 1), :]).astype(BF16)

        loop(LEVELS, weight_table)
        level_table(back, dot)

    def remote(src, dst, ss, rs, member, group):
        return pltpu.make_async_remote_copy(
            src_ref=src, dst_ref=dst, send_sem=ss, recv_sem=rs,
            device_id=(member, group), device_id_type=MESH,
        )

    def exchange(phase, c, src, dst):
        for step in range(1, GROUP):
            peer = lax.rem(g + step, GROUP)
            remote(src(peer), dst(g), a2a_ss.at[phase], a2a_rs.at[phase, c], m, peer).start()

    def came(sem, view):
        remote(view, view, out_sem, sem, sibling, g).wait_recv()

    def left(sem, view):
        remote(view, view, sem, out_sem, sibling, g).wait_send()

    def lines_came(phase, c):
        came(a2a_rs.at[phase, c], lines.at[part(c), pl.ds(0, (GROUP - 1) * ROWS), :])

    def local_came(phase, c):
        came(a2a_rs.at[phase, c], local_r.at[c, pl.ds(0, GROUP - 1)])

    def exchange_left(phase):
        left(a2a_ss.at[phase], lines.at[:, pl.ds(0, (GROUP - 1) * ROWS), :])

    def line_block(c):
        return lambda s: lines.at[part(c), slab_rows(s), :]

    def filtered_block(c):
        return lambda s: filtered.at[part(c), slab_rows(s), :]

    def weighted_block(c):
        return lambda s: core_s.at[c, s]

    def slab_block(c):
        return lambda s: slabs.at[c, s]

    def local_block(c):
        return lambda s: local_r.at[c, s]

    def own_block(c):
        return lambda s: local_s.at[c, s]

    def mask_lines(c, source):
        hots = [
            row_hot[k, pl.ds(pl.multiple_of(c * LINES, LINES), LINES), :] for k in range(CLASSES)
        ]
        for n in range(TILES):
            tile = source(n)
            for k in range(CLASSES):
                at_lane = (n * CLASSES + k) * TILE
                masked[:, at_lane : at_lane + TILE] = tile * jnp.concatenate([hots[k]] * 2, axis=1)

    def tile_span(n):
        return slice(n * TILE, (n + 1) * TILE)

    def row_filter(c):
        alpha_load(c).wait()
        mask_lines(c, lambda n: alpha_v[part(c), :, tile_span(n)].reshape(LINES, TILE))
        for n in range(TILES):

            @pl.when(c == 0)
            def _():
                rowf_load(n).wait()

            table = jnp.concatenate(
                [rowf[k, tile_span(d), tile_span(n)] for d in range(n + 1) for k in range(CLASSES)],
                axis=0,
            )
            total = dot(masked[:, : (n + 1) * CLASSES * TILE], table).astype(BF16)
            for half in range(2):
                slabs[c, 2 * n + half] = total[:, half * LANES : (half + 1) * LANES].reshape(
                    PART, ROWS, LANES
                )
        lines[part(c), slab_rows(g), :] = slabs[c, g]
        exchange(0, c, slab_block(c), line_block(c))

        @pl.when(c == 0)
        def _():
            for load in loads:
                load.start()

    def column_pass(c, source, table, upper):
        def pair(i):
            z = c * PART + 2 * i
            whole = jnp.concatenate([source[z], source[z + 1]], axis=1)
            blocks = []
            for k in range(CLASSES):
                hot = jnp.concatenate([col_hot[k, z], col_hot[k, z + 1]], axis=1)
                blocks.append(
                    (whole.reshape(NY // 16, 16, TILE) * hot[None]).reshape(NY, TILE)
                )
            half = NY // 2
            low = slice(0, half)
            high = slice(half, NY)

            def product(out, deep):
                return dot(
                    jnp.concatenate([table[k, out, deep] for k in range(CLASSES)], axis=1),
                    jnp.concatenate([block[deep] for block in blocks], axis=0),
                )

            first = product(low, slice(0, NY) if upper else low)
            second = product(high, high if upper else slice(0, NY))
            for j in range(2):
                side = slice(j * LANES, (j + 1) * LANES)
                filtered[z + j, :half, :] = first[:, side].astype(BF16)
                filtered[z + j, half:, :] = second[:, side].astype(BF16)

        loop(PART // 2, pair)

    def level_pass(c, table, source, target, deep):
        for chunk in range(CHUNKS):

            @pl.when(c == chunk)
            def _(chunks=deep(chunk), rows=slice(chunk * LINES, (chunk + 1) * LINES)):
                levels = slice(chunks[0] * PART, (chunks[-1] + 1) * PART)
                span = slice(chunks[0] * LINES, (chunks[-1] + 1) * LINES)

                def pair(i):
                    block = jnp.concatenate(
                        [
                            source[levels, slab_rows(2 * i + j), :].reshape(-1, LANES)
                            for j in range(2)
                        ],
                        axis=1,
                    )
                    total = dot(table[rows, span], block).astype(BF16)
                    for j in range(2):
                        target(
                            2 * i + j,
                            total[:, j * LANES : (j + 1) * LANES].reshape(PART, ROWS, LANES),
                        )

                loop(GROUP // 2, pair)

    def column_filter(c):
        lines_came(0, c)
        column_pass(c, lines, colt, False)

        def keep(s, block):
            local_s[c, s] = block

        level_pass(c, down, filtered, keep, lambda chunk: range(chunk + 1))
        local_r[c, g] = local_s[c, g]
        exchange(1, c, own_block(c), local_block(c))

    def core_copy(c):
        return pltpu.make_async_remote_copy(
            src_ref=core_s.at[c],
            dst_ref=core_r.at[c],
            send_sem=core_ss.at[c],
            recv_sem=core_rs.at[c],
            device_id=(sibling, g),
            device_id_type=MESH,
        )

    def xin_slab(way):
        return 2 * around(x, way, 2) + way

    def xone_slab(way):
        return 2 * around(x, way) + 1 - way

    def xtwo_slab(way):
        return 2 * around(x, way) + way

    def x_copy(src, dst, sem, way):
        return remote(src, dst, x_ss, sem, x_peer(way), g)

    def y_copy(c):
        return pltpu.make_async_remote_copy(
            src_ref=y_s.at[c],
            dst_ref=y_r.at[c],
            send_sem=yr_ss,
            recv_sem=yr_rs.at[c],
            device_id=(across, g),
            device_id_type=MESH,
        )

    def term(t, c, s):
        return pert_v[t, part(c), :, lane(s)] * local_r[c, s]

    def sum_core(c):
        local_came(1, c)

        @pl.when(c == 0)
        def _():
            loads[1].wait()
            loads[2].wait()

        def one(s):
            core_s[c, s] = term(1 - core, c, s)

        loop(GROUP, one)
        core_copy(c).start()

    def sum_x(c):
        core_copy(c).wait_recv()

        def add(s):
            core_r[c, s] = term(core, c, s) + core_r[c, s]

        for way in range(2):
            s = xin_slab(way)
            add(s)
            x_copy(core_r.at[c, s], x_in.at[c, way], xin_rs.at[c], way).start()
        for way in range(2):
            s = xone_slab(way)
            add(s)
            x_copy(core_r.at[c, s], x_got.at[c, 0, way], xgot_rs.at[c], way).start()
        for way in range(2):
            add(xtwo_slab(way))
        for j in range(2):
            add(2 * x + j)

    def add_x(c):
        came(xin_rs.at[c], x_in.at[c])
        for way in range(2):
            slab = xtwo_slab(way)
            x_in[c, way] = x_in[c, way] + core_r[c, slab]
            x_copy(x_in.at[c, way], x_got.at[c, 1, way], xgot_rs.at[c], way).start()

    def x_total(c, j):
        total = core_r[c, 2 * x + j].astype(F32) + x_got[c, 1, j].astype(F32)
        return total + x_got[c, 0, 1 - j].astype(F32)

    def sum_y(c):
        came(xgot_rs.at[c], x_got.at[c])
        y_s[c] = x_total(c, 1 - y_hi).astype(BF16)
        y_copy(c).start()

    def give(rs, t, c, s, member):
        return remote(inc.at[t, c, s], inc.at[t, c, s], give_ss, rs, member, g)

    def give_y(c, s):
        return give(ya_rs.at[c], core, c, s, across)

    def give_x(c, way, s):
        return give(xa_rs.at[c], core, c, s, x_peer(way))

    def give_far(c, turn, s):
        return give(xf_rs.at[c], core, c, s, x_peer(turn))

    def give_core(t, c, s):
        return give(ca_rs.at[c], t, c, s, sibling)

    def slab_of(owner, turn):
        return 2 * owner + (y_hi if turn == 0 else 1 - y_hi)

    mine = slab_of(x, 0)
    other = slab_of(x, 1)

    def finish(c):
        y_copy(c).wait_recv()
        inc[core, c, mine] = (x_total(c, y_hi) + y_r[c].astype(F32)).astype(BF16)
        give_y(c, mine).start()
        for way in range(2):
            give_x(c, way, mine).start()
        give_core(core, c, mine).start()

    def gather_y(c):
        give_y(c, other).wait_recv()
        for way in range(2):
            give_x(c, way, other).start()
        give_core(core, c, other).start()

    def gather_x(c):
        came(xa_rs.at[c], inc.at[core, c, pl.ds(0, 4)])
        for turn in range(2):
            s = slab_of(around(x, 1 - turn), turn)
            give_far(c, turn, s).start()
        for turn in range(2):
            for way in range(2):
                give_core(core, c, slab_of(around(x, way), turn)).start()

    def gather_far(c):
        came(xf_rs.at[c], inc.at[core, c, pl.ds(0, 2)])
        for turn in range(2):
            give_core(core, c, slab_of(around(x, 0, 2), turn)).start()

    def weigh(c):
        def one(s):
            total = None
            for t in range(2):
                block = inc[t, c, s]
                inc_v[t, part(c), :, lane(s)] = block
                misfit = weight_v[t, part(c)] * (block - innov_v[t, part(c), :, lane(s)])
                share = pert_v[t, part(c), :, lane(s)] * misfit
                total = share if total is None else total + share
            core_s[c, s] = total

        core_copy(c).wait_send()
        came(ca_rs.at[c], inc.at[1 - core, c])
        loop(GROUP, one)
        lines[part(c), slab_rows(g), :] = core_s[c, g]
        exchange(2, c, weighted_block(c), line_block(c))
        inc_copy(c).start()

    def inc_copy(c):
        return pltpu.make_async_copy(
            inc_v.at[:, part(c)], inc_h.at[:, part(c)], inc_sem.at[c]
        )

    def column_adjoint(c):
        lines_came(2, c)

        def keep(s, block):
            turned[part(c), slab_rows(s), :] = block

        level_pass(c, back, lines, keep, lambda chunk: range(chunk, CHUNKS))
        column_pass(c, turned, colf, True)
        local_r[c, g] = filtered[part(c), slab_rows(g), :]
        exchange(3, c, filtered_block(c), local_block(c))

    def grad_copy(c):
        return pltpu.make_async_copy(alpha_v.at[part(c)], grad_h.at[part(c)], grad_sem.at[c])

    def row_adjoint(c):
        local_came(3, c)
        mask_lines(
            c,
            lambda n: jnp.concatenate(
                [local_r[c, 2 * n + j].reshape(LINES, LANES) for j in range(2)], axis=1
            ),
        )
        for n in range(TILES):
            table = jnp.concatenate(
                [
                    rowf[k, tile_span(n), tile_span(d)]
                    for d in range(n, TILES)
                    for k in range(CLASSES)
                ],
                axis=1,
            )
            total = dot_nt(masked[:, n * CLASSES * TILE :], table)
            side = tile_span(n)
            alpha = alpha_v[part(c), :, side].reshape(LINES, TILE).astype(F32)
            alpha_v[part(c), :, side] = (alpha + total).astype(BF16).reshape(PART, ROWS, TILE)
        grad_copy(c).start()

    loop(LEVELS, row_table)
    pl.semaphore_wait(barrier, GROUP + 3)

    def at(step, offset, stage):
        chunk = step - offset

        @pl.when(jnp.logical_and(chunk >= 0, chunk < CHUNKS))
        def _():
            stage(chunk)

    def forward(step):
        at(step, 6, gather_y)
        at(step, 4, sum_x)
        at(step, 5, sum_y)
        at(step, 7, weigh)
        at(step, 6, gather_x)
        at(step, 5, finish)

        @pl.when(step == 2)
        def _():
            column_tables()

        at(step, 2, column_filter)

        @pl.when(step == 3)
        def _():
            adjoint_tables()

        at(step, 3, sum_core)
        at(step, 4, add_x)
        at(step, 6, gather_far)
        at(step, 0, row_filter)

    loop(CHUNKS + 7, forward)

    def backward(step):
        at(step, 0, lambda c: column_adjoint(CHUNKS - 1 - c))
        at(step, 2, lambda c: row_adjoint(CHUNKS - 1 - c))

    loop(CHUNKS + 2, backward)

    for phase in range(4):
        exchange_left(phase)
    left(x_ss, core_r.at[pl.ds(0, 3)])
    left(yr_ss, y_s)
    left(give_ss, pert_v.at[:, pl.ds(0, LEVELS - 1)])
    for c in range(CHUNKS):
        inc_copy(c).wait()
        grad_copy(c).wait()


def on_device(alpha, pert, innov, weight, row_class, col_class, rowf, colf, level):
    any_spec = pl.BlockSpec(memory_space=pl.ANY)
    vmem_spec = pl.BlockSpec(memory_space=pltpu.VMEM)
    dma = pltpu.SemaphoreType.DMA
    block = (PART, ROWS, LANES)
    slab = (CHUNKS, GROUP) + block
    scratch = [
        pltpu.VMEM((LEVELS, ROWS, NX), BF16),
        pltpu.VMEM((2, LEVELS, ROWS, NX), BF16),
        pltpu.VMEM((2, LEVELS, ROWS, NX), BF16),
        pltpu.VMEM((CLASSES, NX, NX), BF16),
        pltpu.VMEM((CLASSES, NY, NY), BF16),
        pltpu.VMEM((CLASSES, NY, NY), BF16),
        pltpu.VMEM((LEVELS * ROWS, LEVELS * ROWS), BF16),
        pltpu.VMEM((LEVELS * ROWS, LEVELS * ROWS), BF16),
        pltpu.VMEM((CLASSES, LEVELS * ROWS, LANES), BF16),
        pltpu.VMEM((CLASSES, LEVELS, 16, LANES), BF16),
        pltpu.VMEM((2, LEVELS, ROWS, LANES), BF16),
        pltpu.VMEM((LINES, CLASSES * NX), BF16),
        pltpu.VMEM(slab, BF16),
        pltpu.VMEM((LEVELS, NY, LANES), BF16),
        pltpu.VMEM((LEVELS, NY, LANES), BF16),
        pltpu.VMEM((LEVELS, NY, LANES), BF16),
        pltpu.VMEM(slab, BF16),
        pltpu.VMEM(slab, BF16),
        pltpu.VMEM(slab, BF16),
        pltpu.VMEM(slab, BF16),
        pltpu.VMEM((CHUNKS, 2) + block, BF16),
        pltpu.VMEM((CHUNKS, 2, 2) + block, BF16),
        pltpu.VMEM((CHUNKS,) + block, BF16),
        pltpu.VMEM((CHUNKS,) + block, BF16),
        pltpu.VMEM((2,) + slab, BF16),
        pltpu.VMEM((2, LEVELS, ROWS, NX), BF16),
        dma((CHUNKS,)),
        dma((NX // TILE,)),
        dma((3,)),
        dma((CHUNKS,)),
        dma((CHUNKS,)),
        dma,
        dma((4,)),
        dma((4, CHUNKS)),
        dma((CHUNKS,)),
        dma((CHUNKS,)),
        dma,
        dma((CHUNKS,)),
        dma((CHUNKS,)),
        dma,
        dma((CHUNKS,)),
        dma,
        dma((CHUNKS,)),
        dma((CHUNKS,)),
        dma((CHUNKS,)),
        dma((CHUNKS,)),
    ]
    gradient, increment = pl.pallas_call(
        kernel,
        out_shape=(
            jax.ShapeDtypeStruct((LEVELS, ROWS, NX), BF16),
            jax.ShapeDtypeStruct((2, LEVELS, ROWS, NX), BF16),
        ),
        in_specs=[any_spec] * 3 + [vmem_spec] * 3 + [any_spec] * 2 + [vmem_spec],
        out_specs=(any_spec, any_spec),
        scratch_shapes=scratch,
        compiler_params=pltpu.CompilerParams(
            collective_id=0, has_side_effects=True, vmem_limit_bytes=62 * 1024 * 1024
        ),
    )(alpha[0], pert[0], innov, weight, row_class, col_class, rowf, colf, level)
    return gradient[None], increment


def solution(mesh):
    return jax.shard_map(
        on_device,
        mesh=mesh,
        in_specs=(
            P("member", None, "grid", None),
            P("member", None, None, "grid", None),
            P(None, None, "grid", None),
            P(None, None, "grid"),
            P(None, "grid"),
            P(None, "grid"),
            P(),
            P(),
            P(),
        ),
        out_specs=(P("member", None, "grid", None), P(None, None, "grid", None)),
        check_vma=False,
    )
```

```python
import functools

import jax
import jax.numpy as jnp
from jax import lax
from jax.experimental import pallas as pl
from jax.experimental.pallas import tpu as pltpu
from jax.sharding import PartitionSpec as P

MESH = pl.DeviceIdType.MESH
F32 = jnp.float32
BF16 = jnp.bfloat16

CLASSES = 3
LEVELS = 16
GROUP = 8
RING = 4
CHUNKS = 4
PART = LEVELS // CHUNKS
ROWS = 64
ROW_BITS = 6
LANES = 128
NX = GROUP * LANES
NY = GROUP * ROWS
LINES = PART * ROWS
TILE = 256
TILES = NX // TILE
DEEP = TILE // ROWS


def loop(count, body):
    def step(index, carry):
        body(index)
        return carry

    lax.fori_loop(0, count, step, 0)


def dot(a, b):
    return jnp.dot(a, b, preferred_element_type=F32)


def dot_nt(a, b):
    return lax.dot_general(a, b, (((1,), (1,)), ((), ())), preferred_element_type=F32)


def kernel(
    alpha_h, pert_h, innov_h, weight_ref, row_ref, col_ref, rowf_h, colf_h, level_ref,
    grad_h, inc_h,
    alpha_v, pert_v, innov_v, rowf, colf, colt, down, back, row_hot, col_hot, weight_v, masked,
    slabs, lines, filtered, turned, local_s, local_r, core_s, core_r, x_in, x_got, y_s, y_r,
    inc, inc_v,
    alpha_sem, rowf_sem, load_sem, grad_sem, inc_sem, out_sem, a2a_ss, a2a_rs, core_ss, core_rs,
    x_ss, xin_rs, xgot_rs, yr_ss, yr_rs, give_ss, ya_rs, xa_rs, xf_rs, ca_rs,
):
    m = lax.axis_index("member")
    g = lax.axis_index("grid")
    y_hi = m // (2 * RING)
    x = lax.rem(m // 2, RING)
    core = lax.rem(m, 2)
    sibling = m + 1 - 2 * core
    across = m + 2 * RING - 4 * RING * y_hi

    def around(position, way, steps=1):
        return lax.rem(position + (steps if way == 0 else RING - steps), RING)

    def x_peer(way):
        return y_hi * (2 * RING) + around(x, way) * 2 + core

    def lane(s):
        return pl.ds(pl.multiple_of(s * LANES, LANES), LANES)

    def slab_rows(s):
        return pl.ds(pl.multiple_of(s * ROWS, ROWS), ROWS)

    def part(c):
        return pl.ds(c * PART, PART)

    barrier = pltpu.get_barrier_semaphore()

    def greet(partner):
        pl.semaphore_signal(barrier, inc=1, device_id=partner, device_id_type=MESH)

    loop(GROUP - 1, lambda step: greet((m, lax.rem(g + step + 1, GROUP))))
    for member in (x_peer(0), x_peer(1), sibling, across):
        greet((member, g))

    def alpha_load(c):
        return pltpu.make_async_copy(alpha_h.at[part(c)], alpha_v.at[part(c)], alpha_sem.at[c])

    def rowf_load(n):
        where = (slice(None), slice(0, (n + 1) * TILE), slice(n * TILE, (n + 1) * TILE))
        return pltpu.make_async_copy(rowf_h.at[where], rowf.at[where], rowf_sem.at[n])

    alpha_load(0).start()
    for n in range(NX // TILE):
        rowf_load(n).start()
    loads = [
        pltpu.make_async_copy(src, dst, load_sem.at[i])
        for i, (src, dst) in enumerate(((colf_h, colf), (pert_h, pert_v), (innov_h, innov_v)))
    ]

    diagonal = lax.broadcasted_iota(jnp.int32, (ROWS, ROWS), 0) == lax.broadcasted_iota(
        jnp.int32, (ROWS, ROWS), 1
    )

    def upright(line):
        spread = jnp.where(diagonal, jnp.broadcast_to(line, (ROWS, ROWS)), 0.0)
        return jnp.broadcast_to(jnp.sum(spread, axis=1, keepdims=True), (ROWS, LANES))

    def row_table(z):
        column = upright(row_ref[pl.ds(z, 1), :].astype(F32))
        for c in range(CLASSES):
            row_hot[c, slab_rows(z), :] = jnp.where(column == c, 1.0, 0.0).astype(BF16)

    def iota(shape, axis):
        return lax.broadcasted_iota(jnp.int32, shape, axis)

    def level_table(table, product):
        wide = (LEVELS, LEVELS * ROWS)
        spread = jnp.where(iota(wide, 0) == iota(wide, 1) >> ROW_BITS, 1.0, 0.0).astype(BF16)
        tall = (TILE, LEVELS * ROWS)
        same = (iota(tall, 0) & (ROWS - 1)) == (iota(tall, 1) & (ROWS - 1))
        level = level_ref[...]
        for b in range(LEVELS * ROWS // TILE):
            short = (TILE, LEVELS)
            spot = (iota(short, 0) >> ROW_BITS) + b * DEEP
            pick = jnp.where(spot == iota(short, 1), 1.0, 0.0).astype(BF16)
            table[b * TILE : (b + 1) * TILE, :] = jnp.where(
                same, dot(product(pick, level).astype(BF16), spread), 0.0
            ).astype(BF16)

    def column_tables():
        def column_table(z):
            line = jnp.broadcast_to(col_ref[pl.ds(z, 1), :], (16, LANES))
            for c in range(CLASSES):
                col_hot[c, z] = jnp.where(line == c, 1.0, 0.0).astype(BF16)

        loop(LEVELS, column_table)
        level_table(down, dot_nt)
        loads[0].wait()
        unit = jnp.where(iota((NY, NY), 0) == iota((NY, NY), 1), 1.0, 0.0).astype(BF16)

        def turn(c):
            colt[c] = dot_nt(unit, colf[c]).astype(BF16)

        loop(CLASSES, turn)

    def adjoint_tables():
        def weight_table(z):
            for t in range(2):
                weight_v[t, z] = upright(weight_ref[t, pl.ds(z, 1), :]).astype(BF16)

        loop(LEVELS, weight_table)
        level_table(back, dot)

    def remote(src, dst, ss, rs, member, group):
        return pltpu.make_async_remote_copy(
            src_ref=src, dst_ref=dst, send_sem=ss, recv_sem=rs,
            device_id=(member, group), device_id_type=MESH,
        )

    z_at = g // 2
    y_lo = lax.rem(g, 2)

    def send(phase, c, src, dst, peer):
        remote(src(peer), dst(g), a2a_ss.at[phase], a2a_rs.at[phase, c], m, peer).start()

    def exchange(phase, c, src, dst):
        for up, side in ((2, 0), (1, 0), (3, 0), (2, 1), (1, 1), (3, 1), (0, 1)):
            y_peer = y_lo if side == 0 else 1 - y_lo
            send(phase, c, src, dst, lax.rem(z_at + up, RING) * 2 + y_peer)

    def came(sem, view):
        remote(view, view, out_sem, sem, sibling, g).wait_recv()

    def left(sem, view):
        remote(view, view, sem, out_sem, sibling, g).wait_send()

    def lines_came(phase, c):
        came(a2a_rs.at[phase, c], lines.at[c, pl.ds(0, GROUP - 1)])

    def local_came(phase, c):
        came(a2a_rs.at[phase, c], local_r.at[c, pl.ds(0, GROUP - 1)])

    def exchange_left(phase):
        left(a2a_ss.at[phase], lines.at[:, pl.ds(0, GROUP - 1)])

    def line_block(c):
        return lambda s: lines.at[c, s]

    def filtered_block(c):
        return lambda s: filtered.at[c, s]

    def weighted_block(c):
        return lambda s: core_s.at[c, s]

    def slab_block(c):
        return lambda s: slabs.at[c, s]

    def local_block(c):
        return lambda s: local_r.at[c, s]

    def own_block(c):
        return lambda s: local_s.at[c, s]

    def mask_lines(c, source):
        hots = [
            row_hot[k, pl.ds(pl.multiple_of(c * LINES, LINES), LINES), :] for k in range(CLASSES)
        ]
        for n in range(TILES):
            tile = source(n)
            for k in range(CLASSES):
                at_lane = (n * CLASSES + k) * TILE
                masked[:, at_lane : at_lane + TILE] = tile * jnp.concatenate([hots[k]] * 2, axis=1)

    def tile_span(n):
        return slice(n * TILE, (n + 1) * TILE)

    def row_filter(c):
        alpha_load(c).wait()
        loop(PART, lambda z: row_table(c * PART + z))
        mask_lines(c, lambda n: alpha_v[part(c), :, tile_span(n)].reshape(LINES, TILE))
        for n in range(TILES):

            @pl.when(c == 0)
            def _():
                rowf_load(n).wait()

            table = jnp.concatenate(
                [rowf[k, tile_span(d), tile_span(n)] for d in range(n + 1) for k in range(CLASSES)],
                axis=0,
            )
            total = dot(masked[:, : (n + 1) * CLASSES * TILE], table).astype(BF16)
            for half in range(2):
                s = 2 * n + half
                slabs[c, s] = total[:, half * LANES : (half + 1) * LANES].reshape(
                    PART, ROWS, LANES
                )

                @pl.when(jnp.logical_and(c == 0, g != s))
                def _():
                    send(0, c, slab_block(c), line_block(c), s)

        lines[c, g] = slabs[c, g]

        @pl.when(c > 0)
        def _():
            exchange(0, c, slab_block(c), line_block(c))

        @pl.when(c == 0)
        def _():
            for load in loads:
                load.start()

    def column_pass(c, source, table, upper):
        def pair(i):
            z = c * PART + 2 * i
            whole = jnp.concatenate(
                [source[c, :, 2 * i + j].reshape(NY, LANES) for j in range(2)], axis=1
            )
            blocks = []
            for k in range(CLASSES):
                hot = jnp.concatenate([col_hot[k, z], col_hot[k, z + 1]], axis=1)
                blocks.append(
                    (whole.reshape(NY // 16, 16, TILE) * hot[None]).reshape(NY, TILE)
                )
            half = NY // 2
            low = slice(0, half)
            high = slice(half, NY)

            def product(out, deep):
                return dot(
                    jnp.concatenate([table[k, out, deep] for k in range(CLASSES)], axis=1),
                    jnp.concatenate([block[deep] for block in blocks], axis=0),
                )

            first = product(low, slice(0, NY) if upper else low)
            second = product(high, high if upper else slice(0, NY))
            for j in range(2):
                side = slice(j * LANES, (j + 1) * LANES)
                for n, total in enumerate((first, second)):
                    filtered[c, n * GROUP // 2 : (n + 1) * GROUP // 2, 2 * i + j] = (
                        total[:, side].astype(BF16).reshape(GROUP // 2, ROWS, LANES)
                    )

        loop(PART // 2, pair)

    def level_pass(c, table, source, target, deep):
        for chunk in range(CHUNKS):

            @pl.when(c == chunk)
            def _(chunks=deep(chunk), rows=slice(chunk * LINES, (chunk + 1) * LINES)):
                held = slice(chunks[0], chunks[-1] + 1)
                span = slice(chunks[0] * LINES, (chunks[-1] + 1) * LINES)

                def pair(i):
                    block = jnp.concatenate(
                        [
                            source[held, 2 * i + j].reshape(-1, LANES)
                            for j in range(2)
                        ],
                        axis=1,
                    )
                    total = dot(table[rows, span], block).astype(BF16)
                    for j in range(2):
                        target(
                            2 * i + j,
                            total[:, j * LANES : (j + 1) * LANES].reshape(PART, ROWS, LANES),
                        )

                loop(GROUP // 2, pair)

    def column_filter(c):
        lines_came(0, c)
        column_pass(c, lines, colt, False)

        def keep(s, block):
            local_s[c, s] = block

        level_pass(c, down, filtered, keep, lambda chunk: range(chunk + 1))
        local_r[c, g] = local_s[c, g]
        exchange(1, c, own_block(c), local_block(c))

    def core_copy(c):
        return pltpu.make_async_remote_copy(
            src_ref=core_s.at[c],
            dst_ref=core_r.at[c],
            send_sem=core_ss.at[c],
            recv_sem=core_rs.at[c],
            device_id=(sibling, g),
            device_id_type=MESH,
        )

    def xin_slab(way):
        return 2 * around(x, way, 2) + way

    def xone_slab(way):
        return 2 * around(x, way) + 1 - way

    def xtwo_slab(way):
        return 2 * around(x, way) + way

    def x_copy(src, dst, sem, way):
        return remote(src, dst, x_ss, sem, x_peer(way), g)

    def y_copy(c):
        return pltpu.make_async_remote_copy(
            src_ref=y_s.at[c],
            dst_ref=y_r.at[c],
            send_sem=yr_ss,
            recv_sem=yr_rs.at[c],
            device_id=(across, g),
            device_id_type=MESH,
        )

    def term(t, c, s):
        return pert_v[t, part(c), :, lane(s)] * local_r[c, s]

    def sum_core(c):
        local_came(1, c)

        @pl.when(c == 0)
        def _():
            loads[1].wait()
            loads[2].wait()

        def one(s):
            core_s[c, s] = term(1 - core, c, s)

        loop(GROUP, one)
        core_copy(c).start()

    def sum_x(c):
        core_copy(c).wait_recv()

        def add(s):
            core_r[c, s] = term(core, c, s) + core_r[c, s]

        for way in range(2):
            s = xin_slab(way)
            add(s)
            x_copy(core_r.at[c, s], x_in.at[c, way], xin_rs.at[c], way).start()
        for way in range(2):
            s = xone_slab(way)
            add(s)
            x_copy(core_r.at[c, s], x_got.at[c, 0, way], xgot_rs.at[c], way).start()
        for way in range(2):
            add(xtwo_slab(way))
        for j in range(2):
            add(2 * x + j)

    def add_x(c):
        came(xin_rs.at[c], x_in.at[c])
        for way in range(2):
            slab = xtwo_slab(way)
            x_in[c, way] = x_in[c, way] + core_r[c, slab]
            x_copy(x_in.at[c, way], x_got.at[c, 1, way], xgot_rs.at[c], way).start()

    def x_total(c, j):
        total = core_r[c, 2 * x + j].astype(F32) + x_got[c, 1, j].astype(F32)
        return total + x_got[c, 0, 1 - j].astype(F32)

    def sum_y(c):
        came(xgot_rs.at[c], x_got.at[c])
        y_s[c] = x_total(c, 1 - y_hi).astype(BF16)
        y_copy(c).start()

    def give(rs, t, c, s, member):
        return remote(inc.at[t, c, s], inc.at[t, c, s], give_ss, rs, member, g)

    def give_y(c, s):
        return give(ya_rs.at[c], core, c, s, across)

    def give_x(c, way, s):
        return give(xa_rs.at[c], core, c, s, x_peer(way))

    def give_far(c, turn, s):
        return give(xf_rs.at[c], core, c, s, x_peer(turn))

    def slab_of(owner, turn):
        return 2 * owner + (y_hi if turn == 0 else 1 - y_hi)

    mine = slab_of(x, 0)
    other = slab_of(x, 1)

    def finish(c):
        y_copy(c).wait_recv()
        inc[core, c, mine] = (x_total(c, y_hi) + y_r[c].astype(F32)).astype(BF16)
        give_y(c, mine).start()
        for way in range(2):
            give_x(c, way, mine).start()

    def gather_y(c):
        give_y(c, other).wait_recv()
        for way in range(2):
            give_x(c, way, other).start()

    def gather_x(c):
        came(xa_rs.at[c], inc.at[core, c, pl.ds(0, 4)])
        for turn in range(2):
            s = slab_of(around(x, 1 - turn), turn)
            give_far(c, turn, s).start()

    def gather_far(c):
        came(xf_rs.at[c], inc.at[core, c, pl.ds(0, 2)])
        remote(inc.at[core, c], inc.at[core, c], give_ss, ca_rs.at[c], sibling, g).start()

    def weigh(c):
        def one(s):
            total = None
            for t in range(2):
                block = inc[t, c, s]
                inc_v[t, part(c), :, lane(s)] = block
                misfit = weight_v[t, part(c)] * (block - innov_v[t, part(c), :, lane(s)])
                share = pert_v[t, part(c), :, lane(s)] * misfit
                total = share if total is None else total + share
            core_s[c, s] = total

        core_copy(c).wait_send()
        came(ca_rs.at[c], inc.at[1 - core, c])
        loop(GROUP, one)
        lines[c, g] = core_s[c, g]
        exchange(2, c, weighted_block(c), line_block(c))
        inc_copy(c).start()

    def inc_copy(c):
        return pltpu.make_async_copy(
            inc_v.at[:, part(c)], inc_h.at[:, part(c)], inc_sem.at[c]
        )

    def column_adjoint(c):
        lines_came(2, c)

        def keep(s, block):
            turned[c, s] = block

        level_pass(c, back, lines, keep, lambda chunk: range(chunk, CHUNKS))
        column_pass(c, turned, colf, True)
        local_r[c, g] = filtered[c, g]
        exchange(3, c, filtered_block(c), local_block(c))

    def grad_copy(c):
        return pltpu.make_async_copy(alpha_v.at[part(c)], grad_h.at[part(c)], grad_sem.at[c])

    def row_adjoint(c):
        local_came(3, c)
        mask_lines(
            c,
            lambda n: jnp.concatenate(
                [local_r[c, 2 * n + j].reshape(LINES, LANES) for j in range(2)], axis=1
            ),
        )
        for n in range(TILES):
            table = jnp.concatenate(
                [
                    rowf[k, tile_span(n), tile_span(d)]
                    for d in range(n, TILES)
                    for k in range(CLASSES)
                ],
                axis=1,
            )
            total = dot_nt(masked[:, n * CLASSES * TILE :], table)
            side = tile_span(n)
            alpha = alpha_v[part(c), :, side].reshape(LINES, TILE).astype(F32)
            alpha_v[part(c), :, side] = (alpha + total).astype(BF16).reshape(PART, ROWS, TILE)
        grad_copy(c).start()

    pl.semaphore_wait(barrier, GROUP + 3)
    for c in range(1, CHUNKS):
        alpha_load(c).start()

    def at(step, offset, stage):
        chunk = step - offset

        @pl.when(jnp.logical_and(chunk >= 0, chunk < CHUNKS))
        def _():
            stage(chunk)

    def forward(step):
        at(step, 6, gather_y)
        at(step, 4, sum_x)
        at(step, 5, sum_y)
        at(step, 7, weigh)
        at(step, 6, gather_x)
        at(step, 5, finish)

        @pl.when(step == 2)
        def _():
            column_tables()

        at(step, 2, column_filter)

        @pl.when(step == 3)
        def _():
            adjoint_tables()

        at(step, 3, sum_core)
        at(step, 4, add_x)
        at(step, 6, gather_far)
        at(step, 0, row_filter)

    loop(CHUNKS + 7, forward)

    def backward(step):
        at(step, 0, lambda c: column_adjoint(CHUNKS - 1 - c))
        at(step, 2, lambda c: row_adjoint(CHUNKS - 1 - c))

    loop(CHUNKS + 2, backward)

    for phase in range(4):
        exchange_left(phase)
    left(x_ss, core_r.at[pl.ds(0, 3)])
    left(yr_ss, y_s)
    left(give_ss, pert_v.at[:, pl.ds(0, LEVELS - 1)])
    for c in range(CHUNKS):
        inc_copy(c).wait()
        grad_copy(c).wait()


def on_device(alpha, pert, innov, weight, row_class, col_class, rowf, colf, level):
    any_spec = pl.BlockSpec(memory_space=pl.ANY)
    vmem_spec = pl.BlockSpec(memory_space=pltpu.VMEM)
    dma = pltpu.SemaphoreType.DMA
    block = (PART, ROWS, LANES)
    slab = (CHUNKS, GROUP) + block
    scratch = [
        pltpu.VMEM((LEVELS, ROWS, NX), BF16),
        pltpu.VMEM((2, LEVELS, ROWS, NX), BF16),
        pltpu.VMEM((2, LEVELS, ROWS, NX), BF16),
        pltpu.VMEM((CLASSES, NX, NX), BF16),
        pltpu.VMEM((CLASSES, NY, NY), BF16),
        pltpu.VMEM((CLASSES, NY, NY), BF16),
        pltpu.VMEM((LEVELS * ROWS, LEVELS * ROWS), BF16),
        pltpu.VMEM((LEVELS * ROWS, LEVELS * ROWS), BF16),
        pltpu.VMEM((CLASSES, LEVELS * ROWS, LANES), BF16),
        pltpu.VMEM((CLASSES, LEVELS, 16, LANES), BF16),
        pltpu.VMEM((2, LEVELS, ROWS, LANES), BF16),
        pltpu.VMEM((LINES, CLASSES * NX), BF16),
        pltpu.VMEM(slab, BF16),
        pltpu.VMEM(slab, BF16),
        pltpu.VMEM(slab, BF16),
        pltpu.VMEM(slab, BF16),
        pltpu.VMEM(slab, BF16),
        pltpu.VMEM(slab, BF16),
        pltpu.VMEM(slab, BF16),
        pltpu.VMEM(slab, BF16),
        pltpu.VMEM((CHUNKS, 2) + block, BF16),
        pltpu.VMEM((CHUNKS, 2, 2) + block, BF16),
        pltpu.VMEM((CHUNKS,) + block, BF16),
        pltpu.VMEM((CHUNKS,) + block, BF16),
        pltpu.VMEM((2,) + slab, BF16),
        pltpu.VMEM((2, LEVELS, ROWS, NX), BF16),
        dma((CHUNKS,)),
        dma((NX // TILE,)),
        dma((3,)),
        dma((CHUNKS,)),
        dma((CHUNKS,)),
        dma,
        dma((4,)),
        dma((4, CHUNKS)),
        dma((CHUNKS,)),
        dma((CHUNKS,)),
        dma,
        dma((CHUNKS,)),
        dma((CHUNKS,)),
        dma,
        dma((CHUNKS,)),
        dma,
        dma((CHUNKS,)),
        dma((CHUNKS,)),
        dma((CHUNKS,)),
        dma((CHUNKS,)),
    ]
    gradient, increment = pl.pallas_call(
        kernel,
        out_shape=(
            jax.ShapeDtypeStruct((LEVELS, ROWS, NX), BF16),
            jax.ShapeDtypeStruct((2, LEVELS, ROWS, NX), BF16),
        ),
        in_specs=[any_spec] * 3 + [vmem_spec] * 3 + [any_spec] * 2 + [vmem_spec],
        out_specs=(any_spec, any_spec),
        scratch_shapes=scratch,
        compiler_params=pltpu.CompilerParams(
            collective_id=0, has_side_effects=True, vmem_limit_bytes=62 * 1024 * 1024
        ),
    )(alpha[0], pert[0], innov, weight, row_class, col_class, rowf, colf, level)
    return gradient[None], increment


def solution(mesh):
    return jax.shard_map(
        on_device,
        mesh=mesh,
        in_specs=(
            P("member", None, "grid", None),
            P("member", None, None, "grid", None),
            P(None, None, "grid", None),
            P(None, None, "grid"),
            P(None, "grid"),
            P(None, "grid"),
            P(),
            P(),
            P(),
        ),
        out_specs=(P("member", None, "grid", None), P(None, None, "grid", None)),
        check_vma=False,
    )
```

```python
import functools

import jax
import jax.numpy as jnp
from jax import lax
from jax.experimental import pallas as pl
from jax.experimental.pallas import tpu as pltpu
from jax.sharding import PartitionSpec as P

MESH = pl.DeviceIdType.MESH
F32 = jnp.float32
BF16 = jnp.bfloat16

CLASSES = 3
LEVELS = 16
GROUP = 8
RING = 4
CHUNKS = 4
PART = LEVELS // CHUNKS
ROWS = 64
ROW_BITS = 6
LANES = 128
NX = GROUP * LANES
NY = GROUP * ROWS
LINES = PART * ROWS
TILE = 256
TILES = NX // TILE
WIDE = 2
DEEP = TILE // ROWS


def loop(count, body):
    def step(index, carry):
        body(index)
        return carry

    lax.fori_loop(0, count, step, 0)


def dot(a, b):
    return jnp.dot(a, b, preferred_element_type=F32)


def dot_nt(a, b):
    return lax.dot_general(a, b, (((1,), (1,)), ((), ())), preferred_element_type=F32)


def kernel(
    alpha_h, pert_h, innov_h, weight_ref, row_ref, col_ref, rowf_h, colf_h, level_ref,
    grad_h, inc_h,
    alpha_v, pert_v, innov_v, rowf, colf, colt, down, back, row_hot, col_hot, weight_v, masked,
    slabs, lines, filtered, turned, local_s, local_r, core_s, core_r, x_in, x_got, y_s, y_r,
    inc, inc_v,
    alpha_sem, rowf_sem, load_sem, grad_sem, inc_sem, out_sem, a2a_ss, a2a_rs, core_ss, core_rs,
    x_ss, xin_rs, xgot_rs, yr_ss, yr_rs, give_ss, ya_rs, xa_rs, xf_rs, ca_rs,
):
    m = lax.axis_index("member")
    g = lax.axis_index("grid")
    y_hi = m // (2 * RING)
    x = lax.rem(m // 2, RING)
    core = lax.rem(m, 2)
    sibling = m + 1 - 2 * core
    across = m + 2 * RING - 4 * RING * y_hi

    def around(position, way, steps=1):
        return lax.rem(position + (steps if way == 0 else RING - steps), RING)

    def x_peer(way):
        return y_hi * (2 * RING) + around(x, way) * 2 + core

    def lane(s):
        return pl.ds(pl.multiple_of(s * LANES, LANES), LANES)

    def slab_rows(s):
        return pl.ds(pl.multiple_of(s * ROWS, ROWS), ROWS)

    def part(c):
        return pl.ds(c * PART, PART)

    barrier = pltpu.get_barrier_semaphore()

    def greet(partner):
        pl.semaphore_signal(barrier, inc=1, device_id=partner, device_id_type=MESH)

    loop(GROUP - 1, lambda step: greet((m, lax.rem(g + step + 1, GROUP))))
    for member in (x_peer(0), x_peer(1), sibling, across):
        greet((member, g))

    def alpha_load(c):
        return pltpu.make_async_copy(alpha_h.at[part(c)], alpha_v.at[part(c)], alpha_sem.at[c])

    def rowf_load(n):
        depth = (n // WIDE + 1) * WIDE * TILE
        where = (slice(None), slice(0, depth), slice(n * TILE, (n + 1) * TILE))
        return pltpu.make_async_copy(rowf_h.at[where], rowf.at[where], rowf_sem.at[n])

    alpha_load(0).start()
    for n in range(NX // TILE):
        rowf_load(n).start()
    loads = [
        pltpu.make_async_copy(src, dst, load_sem.at[i])
        for i, (src, dst) in enumerate(((colf_h, colf), (pert_h, pert_v), (innov_h, innov_v)))
    ]

    diagonal = lax.broadcasted_iota(jnp.int32, (ROWS, ROWS), 0) == lax.broadcasted_iota(
        jnp.int32, (ROWS, ROWS), 1
    )

    def upright(line):
        spread = jnp.where(diagonal, jnp.broadcast_to(line, (ROWS, ROWS)), 0.0)
        return jnp.broadcast_to(jnp.sum(spread, axis=1, keepdims=True), (ROWS, LANES))

    def row_table(z):
        column = upright(row_ref[pl.ds(z, 1), :].astype(F32))
        for c in range(CLASSES):
            row_hot[c, slab_rows(z), :] = jnp.where(column == c, 1.0, 0.0).astype(BF16)

    def iota(shape, axis):
        return lax.broadcasted_iota(jnp.int32, shape, axis)

    def level_table(table, product):
        wide = (LEVELS, LEVELS * ROWS)
        spread = jnp.where(iota(wide, 0) == iota(wide, 1) >> ROW_BITS, 1.0, 0.0).astype(BF16)
        tall = (TILE, LEVELS * ROWS)
        same = (iota(tall, 0) & (ROWS - 1)) == (iota(tall, 1) & (ROWS - 1))
        level = level_ref[...]
        for b in range(LEVELS * ROWS // TILE):
            short = (TILE, LEVELS)
            spot = (iota(short, 0) >> ROW_BITS) + b * DEEP
            pick = jnp.where(spot == iota(short, 1), 1.0, 0.0).astype(BF16)
            table[b * TILE : (b + 1) * TILE, :] = jnp.where(
                same, dot(product(pick, level).astype(BF16), spread), 0.0
            ).astype(BF16)

    def column_tables():
        def column_table(z):
            line = jnp.broadcast_to(col_ref[pl.ds(z, 1), :], (16, LANES))
            for c in range(CLASSES):
                col_hot[c, z] = jnp.where(line == c, 1.0, 0.0).astype(BF16)

        loop(LEVELS, column_table)
        level_table(down, dot_nt)
        loads[0].wait()
        unit = jnp.where(iota((NY, NY), 0) == iota((NY, NY), 1), 1.0, 0.0).astype(BF16)

        def turn(c):
            colt[c] = dot_nt(unit, colf[c]).astype(BF16)

        loop(CLASSES, turn)

    def adjoint_tables():
        def weight_table(z):
            for t in range(2):
                weight_v[t, z] = upright(weight_ref[t, pl.ds(z, 1), :]).astype(BF16)

        loop(LEVELS, weight_table)
        level_table(back, dot)

    def remote(src, dst, ss, rs, member, group):
        return pltpu.make_async_remote_copy(
            src_ref=src, dst_ref=dst, send_sem=ss, recv_sem=rs,
            device_id=(member, group), device_id_type=MESH,
        )

    z_at = g // 2
    y_lo = lax.rem(g, 2)

    def send(phase, c, src, dst, peer):
        remote(src(peer), dst(g), a2a_ss.at[phase], a2a_rs.at[phase, c], m, peer).start()

    def exchange(phase, c, src, dst):
        for up, side in ((2, 0), (1, 0), (3, 0), (2, 1), (1, 1), (3, 1), (0, 1)):
            y_peer = y_lo if side == 0 else 1 - y_lo
            send(phase, c, src, dst, lax.rem(z_at + up, RING) * 2 + y_peer)

    def came(sem, view):
        remote(view, view, out_sem, sem, sibling, g).wait_recv()

    def left(sem, view):
        remote(view, view, sem, out_sem, sibling, g).wait_send()

    def lines_came(phase, c):
        came(a2a_rs.at[phase, c], lines.at[c, pl.ds(0, GROUP - 1)])

    def local_came(phase, c):
        came(a2a_rs.at[phase, c], local_r.at[c, pl.ds(0, GROUP - 1)])

    def exchange_left(phase):
        left(a2a_ss.at[phase], lines.at[:, pl.ds(0, GROUP - 1)])

    def line_block(c):
        return lambda s: lines.at[c, s]

    def filtered_block(c):
        return lambda s: filtered.at[c, s]

    def weighted_block(c):
        return lambda s: core_s.at[c, s]

    def slab_block(c):
        return lambda s: slabs.at[c, s]

    def local_block(c):
        return lambda s: local_r.at[c, s]

    def own_block(c):
        return lambda s: local_s.at[c, s]

    def mask_lines(c, source):
        hots = [
            row_hot[k, pl.ds(pl.multiple_of(c * LINES, LINES), LINES), :] for k in range(CLASSES)
        ]
        for n in range(TILES):
            tile = source(n)
            for k in range(CLASSES):
                at_lane = (n * CLASSES + k) * TILE
                masked[:, at_lane : at_lane + TILE] = tile * jnp.concatenate([hots[k]] * 2, axis=1)

    def tile_span(n):
        return slice(n * TILE, (n + 1) * TILE)

    def row_filter(c):
        alpha_load(c).wait()
        loop(PART, lambda z: row_table(c * PART + z))
        mask_lines(c, lambda n: alpha_v[part(c), :, tile_span(n)].reshape(LINES, TILE))
        for first in range(0, TILES, WIDE):
            last = first + WIDE

            @pl.when(c == 0)
            def _():
                for n in range(first, last):
                    rowf_load(n).wait()

            table = jnp.concatenate(
                [
                    rowf[k, tile_span(d), first * TILE : last * TILE]
                    for d in range(last)
                    for k in range(CLASSES)
                ],
                axis=0,
            )
            total = dot(masked[:, : last * CLASSES * TILE], table).astype(BF16)
            for j in range(2 * WIDE):
                s = 2 * first + j
                slabs[c, s] = total[:, j * LANES : (j + 1) * LANES].reshape(PART, ROWS, LANES)

                @pl.when(jnp.logical_and(c == 0, g != s))
                def _():
                    send(0, c, slab_block(c), line_block(c), s)

        lines[c, g] = slabs[c, g]

        @pl.when(c > 0)
        def _():
            exchange(0, c, slab_block(c), line_block(c))

        @pl.when(c == 0)
        def _():
            for load in loads:
                load.start()

    def column_pass(c, source, table, upper):
        whole = jnp.concatenate(
            [source[c, :, j].reshape(NY, LANES) for j in range(PART)], axis=1
        )
        blocks = []
        for k in range(CLASSES):
            hot = jnp.concatenate([col_hot[k, c * PART + j] for j in range(PART)], axis=1)
            blocks.append(
                (whole.reshape(NY // 16, 16, PART * LANES) * hot[None]).reshape(NY, PART * LANES)
            )
        half = NY // 2
        low = slice(0, half)
        high = slice(half, NY)

        def product(out, deep):
            return dot(
                jnp.concatenate([table[k, out, deep] for k in range(CLASSES)], axis=1),
                jnp.concatenate([block[deep] for block in blocks], axis=0),
            )

        first = product(low, slice(0, NY) if upper else low)
        second = product(high, high if upper else slice(0, NY))
        for j in range(PART):
            side = slice(j * LANES, (j + 1) * LANES)
            for n, total in enumerate((first, second)):
                filtered[c, n * GROUP // 2 : (n + 1) * GROUP // 2, j] = (
                    total[:, side].astype(BF16).reshape(GROUP // 2, ROWS, LANES)
                )

    def level_pass(c, table, source, target, deep):
        for chunk in range(CHUNKS):

            @pl.when(c == chunk)
            def _(chunks=deep(chunk), rows=slice(chunk * LINES, (chunk + 1) * LINES)):
                held = slice(chunks[0], chunks[-1] + 1)
                span = slice(chunks[0] * LINES, (chunks[-1] + 1) * LINES)

                def some(i):
                    block = jnp.concatenate(
                        [source[held, 4 * i + j].reshape(-1, LANES) for j in range(4)], axis=1
                    )
                    total = dot(table[rows, span], block).astype(BF16)
                    for j in range(4):
                        target(
                            4 * i + j,
                            total[:, j * LANES : (j + 1) * LANES].reshape(PART, ROWS, LANES),
                        )

                loop(GROUP // 4, some)

    def column_filter(c):
        lines_came(0, c)
        column_pass(c, lines, colt, False)

        def keep(s, block):
            local_s[c, s] = block

        level_pass(c, down, filtered, keep, lambda chunk: range(chunk + 1))
        local_r[c, g] = local_s[c, g]
        exchange(1, c, own_block(c), local_block(c))

    def core_copy(c):
        return pltpu.make_async_remote_copy(
            src_ref=core_s.at[c],
            dst_ref=core_r.at[c],
            send_sem=core_ss.at[c],
            recv_sem=core_rs.at[c],
            device_id=(sibling, g),
            device_id_type=MESH,
        )

    def xin_slab(way):
        return 2 * around(x, way, 2) + way

    def xone_slab(way):
        return 2 * around(x, way) + 1 - way

    def xtwo_slab(way):
        return 2 * around(x, way) + way

    def x_copy(src, dst, sem, way):
        return remote(src, dst, x_ss, sem, x_peer(way), g)

    def y_copy(c):
        return pltpu.make_async_remote_copy(
            src_ref=y_s.at[c],
            dst_ref=y_r.at[c],
            send_sem=yr_ss,
            recv_sem=yr_rs.at[c],
            device_id=(across, g),
            device_id_type=MESH,
        )

    def term(t, c, s):
        return pert_v[t, part(c), :, lane(s)] * local_r[c, s]

    def sum_core(c):
        local_came(1, c)

        @pl.when(c == 0)
        def _():
            loads[1].wait()
            loads[2].wait()

        def one(s):
            core_s[c, s] = term(1 - core, c, s)

        loop(GROUP, one)
        core_copy(c).start()

    def sum_x(c):
        core_copy(c).wait_recv()

        def add(s):
            core_r[c, s] = term(core, c, s) + core_r[c, s]

        for way in range(2):
            s = xin_slab(way)
            add(s)
            x_copy(core_r.at[c, s], x_in.at[c, way], xin_rs.at[c], way).start()
        for way in range(2):
            s = xone_slab(way)
            add(s)
            x_copy(core_r.at[c, s], x_got.at[c, 0, way], xgot_rs.at[c], way).start()
        for way in range(2):
            add(xtwo_slab(way))
        for j in range(2):
            add(2 * x + j)

    def add_x(c):
        came(xin_rs.at[c], x_in.at[c])
        for way in range(2):
            slab = xtwo_slab(way)
            x_in[c, way] = x_in[c, way] + core_r[c, slab]
            x_copy(x_in.at[c, way], x_got.at[c, 1, way], xgot_rs.at[c], way).start()

    def x_total(c, j):
        total = core_r[c, 2 * x + j].astype(F32) + x_got[c, 1, j].astype(F32)
        return total + x_got[c, 0, 1 - j].astype(F32)

    def sum_y(c):
        came(xgot_rs.at[c], x_got.at[c])
        y_s[c] = x_total(c, 1 - y_hi).astype(BF16)
        y_copy(c).start()

    def give(rs, t, c, s, member):
        return remote(inc.at[t, c, s], inc.at[t, c, s], give_ss, rs, member, g)

    def give_y(c, s):
        return give(ya_rs.at[c], core, c, s, across)

    def give_x(c, way, s):
        return give(xa_rs.at[c], core, c, s, x_peer(way))

    def give_far(c, turn, s):
        return give(xf_rs.at[c], core, c, s, x_peer(turn))

    def slab_of(owner, turn):
        return 2 * owner + (y_hi if turn == 0 else 1 - y_hi)

    mine = slab_of(x, 0)
    other = slab_of(x, 1)

    def finish(c):
        y_copy(c).wait_recv()
        inc[core, c, mine] = (x_total(c, y_hi) + y_r[c].astype(F32)).astype(BF16)
        give_y(c, mine).start()
        for way in range(2):
            give_x(c, way, mine).start()

    def gather_y(c):
        give_y(c, other).wait_recv()
        for way in range(2):
            give_x(c, way, other).start()

    def gather_x(c):
        came(xa_rs.at[c], inc.at[core, c, pl.ds(0, 4)])
        for turn in range(2):
            s = slab_of(around(x, 1 - turn), turn)
            give_far(c, turn, s).start()

    def gather_far(c):
        came(xf_rs.at[c], inc.at[core, c, pl.ds(0, 2)])
        remote(inc.at[core, c], inc.at[core, c], give_ss, ca_rs.at[c], sibling, g).start()

    def weigh(c):
        def one(s):
            total = None
            for t in range(2):
                block = inc[t, c, s]
                inc_v[t, part(c), :, lane(s)] = block
                misfit = weight_v[t, part(c)] * (block - innov_v[t, part(c), :, lane(s)])
                share = pert_v[t, part(c), :, lane(s)] * misfit
                total = share if total is None else total + share
            core_s[c, s] = total

        core_copy(c).wait_send()
        came(ca_rs.at[c], inc.at[1 - core, c])
        loop(GROUP, one)
        lines[c, g] = core_s[c, g]
        exchange(2, c, weighted_block(c), line_block(c))
        inc_copy(c).start()

    def inc_copy(c):
        return pltpu.make_async_copy(
            inc_v.at[:, part(c)], inc_h.at[:, part(c)], inc_sem.at[c]
        )

    def column_adjoint(c):
        lines_came(2, c)

        def keep(s, block):
            turned[c, s] = block

        level_pass(c, back, lines, keep, lambda chunk: range(chunk, CHUNKS))
        column_pass(c, turned, colf, True)
        local_r[c, g] = filtered[c, g]
        exchange(3, c, filtered_block(c), local_block(c))

    def grad_copy(c):
        return pltpu.make_async_copy(alpha_v.at[part(c)], grad_h.at[part(c)], grad_sem.at[c])

    def row_adjoint(c):
        local_came(3, c)
        mask_lines(
            c,
            lambda n: jnp.concatenate(
                [local_r[c, 2 * n + j].reshape(LINES, LANES) for j in range(2)], axis=1
            ),
        )
        for first in range(0, TILES, WIDE):
            side = slice(first * TILE, (first + WIDE) * TILE)
            table = jnp.concatenate(
                [
                    rowf[k, side, tile_span(d)]
                    for d in range(first, TILES)
                    for k in range(CLASSES)
                ],
                axis=1,
            )
            total = dot_nt(masked[:, first * CLASSES * TILE :], table)
            alpha = alpha_v[part(c), :, side].reshape(LINES, WIDE * TILE).astype(F32)
            alpha_v[part(c), :, side] = (
                (alpha + total).astype(BF16).reshape(PART, ROWS, WIDE * TILE)
            )
        grad_copy(c).start()

    pl.semaphore_wait(barrier, GROUP + 3)
    for c in range(1, CHUNKS):
        alpha_load(c).start()

    def at(step, offset, stage):
        chunk = step - offset

        @pl.when(jnp.logical_and(chunk >= 0, chunk < CHUNKS))
        def _():
            stage(chunk)

    def forward(step):
        at(step, 6, gather_y)
        at(step, 4, sum_x)
        at(step, 5, sum_y)
        at(step, 7, weigh)
        at(step, 6, gather_x)
        at(step, 5, finish)

        @pl.when(step == 2)
        def _():
            column_tables()

        at(step, 2, column_filter)

        @pl.when(step == 3)
        def _():
            adjoint_tables()

        at(step, 3, sum_core)
        at(step, 4, add_x)
        at(step, 6, gather_far)
        at(step, 0, row_filter)

    loop(CHUNKS + 7, forward)

    def backward(step):
        at(step, 0, lambda c: column_adjoint(CHUNKS - 1 - c))
        at(step, 2, lambda c: row_adjoint(CHUNKS - 1 - c))

    loop(CHUNKS + 2, backward)

    for phase in range(4):
        exchange_left(phase)
    left(x_ss, core_r.at[pl.ds(0, 3)])
    left(yr_ss, y_s)
    left(give_ss, pert_v.at[:, pl.ds(0, LEVELS - 1)])
    for c in range(CHUNKS):
        inc_copy(c).wait()
        grad_copy(c).wait()


def on_device(alpha, pert, innov, weight, row_class, col_class, rowf, colf, level):
    any_spec = pl.BlockSpec(memory_space=pl.ANY)
    vmem_spec = pl.BlockSpec(memory_space=pltpu.VMEM)
    dma = pltpu.SemaphoreType.DMA
    block = (PART, ROWS, LANES)
    slab = (CHUNKS, GROUP) + block
    scratch = [
        pltpu.VMEM((LEVELS, ROWS, NX), BF16),
        pltpu.VMEM((2, LEVELS, ROWS, NX), BF16),
        pltpu.VMEM((2, LEVELS, ROWS, NX), BF16),
        pltpu.VMEM((CLASSES, NX, NX), BF16),
        pltpu.VMEM((CLASSES, NY, NY), BF16),
        pltpu.VMEM((CLASSES, NY, NY), BF16),
        pltpu.VMEM((LEVELS * ROWS, LEVELS * ROWS), BF16),
        pltpu.VMEM((LEVELS * ROWS, LEVELS * ROWS), BF16),
        pltpu.VMEM((CLASSES, LEVELS * ROWS, LANES), BF16),
        pltpu.VMEM((CLASSES, LEVELS, 16, LANES), BF16),
        pltpu.VMEM((2, LEVELS, ROWS, LANES), BF16),
        pltpu.VMEM((LINES, CLASSES * NX), BF16),
        pltpu.VMEM(slab, BF16),
        pltpu.VMEM(slab, BF16),
        pltpu.VMEM(slab, BF16),
        pltpu.VMEM(slab, BF16),
        pltpu.VMEM(slab, BF16),
        pltpu.VMEM(slab, BF16),
        pltpu.VMEM(slab, BF16),
        pltpu.VMEM(slab, BF16),
        pltpu.VMEM((CHUNKS, 2) + block, BF16),
        pltpu.VMEM((CHUNKS, 2, 2) + block, BF16),
        pltpu.VMEM((CHUNKS,) + block, BF16),
        pltpu.VMEM((CHUNKS,) + block, BF16),
        pltpu.VMEM((2,) + slab, BF16),
        pltpu.VMEM((2, LEVELS, ROWS, NX), BF16),
        dma((CHUNKS,)),
        dma((NX // TILE,)),
        dma((3,)),
        dma((CHUNKS,)),
        dma((CHUNKS,)),
        dma,
        dma((4,)),
        dma((4, CHUNKS)),
        dma((CHUNKS,)),
        dma((CHUNKS,)),
        dma,
        dma((CHUNKS,)),
        dma((CHUNKS,)),
        dma,
        dma((CHUNKS,)),
        dma,
        dma((CHUNKS,)),
        dma((CHUNKS,)),
        dma((CHUNKS,)),
        dma((CHUNKS,)),
    ]
    gradient, increment = pl.pallas_call(
        kernel,
        out_shape=(
            jax.ShapeDtypeStruct((LEVELS, ROWS, NX), BF16),
            jax.ShapeDtypeStruct((2, LEVELS, ROWS, NX), BF16),
        ),
        in_specs=[any_spec] * 3 + [vmem_spec] * 3 + [any_spec] * 2 + [vmem_spec],
        out_specs=(any_spec, any_spec),
        scratch_shapes=scratch,
        compiler_params=pltpu.CompilerParams(
            collective_id=0, has_side_effects=True, vmem_limit_bytes=62 * 1024 * 1024
        ),
    )(alpha[0], pert[0], innov, weight, row_class, col_class, rowf, colf, level)
    return gradient[None], increment


def solution(mesh):
    return jax.shard_map(
        on_device,
        mesh=mesh,
        in_specs=(
            P("member", None, "grid", None),
            P("member", None, None, "grid", None),
            P(None, None, "grid", None),
            P(None, None, "grid"),
            P(None, "grid"),
            P(None, "grid"),
            P(),
            P(),
            P(),
        ),
        out_specs=(P("member", None, "grid", None), P(None, None, "grid", None)),
        check_vma=False,
    )
```

```python
import functools

import jax
import jax.numpy as jnp
from jax import lax
from jax.experimental import pallas as pl
from jax.experimental.pallas import tpu as pltpu
from jax.sharding import PartitionSpec as P

MESH = pl.DeviceIdType.MESH
F32 = jnp.float32
BF16 = jnp.bfloat16

CLASSES = 3
LEVELS = 16
GROUP = 8
RING = 4
CHUNKS = 4
PART = LEVELS // CHUNKS
ROWS = 64
ROW_BITS = 6
LANES = 128
NX = GROUP * LANES
NY = GROUP * ROWS
LINES = PART * ROWS
TILE = 256
TILES = NX // TILE
WIDE = 2
DEEP = TILE // ROWS


def loop(count, body):
    def step(index, carry):
        body(index)
        return carry

    lax.fori_loop(0, count, step, 0)


def dot(a, b):
    return jnp.dot(a, b, preferred_element_type=F32)


def dot_nt(a, b):
    return lax.dot_general(a, b, (((1,), (1,)), ((), ())), preferred_element_type=F32)


def kernel(
    alpha_h, pert_h, innov_h, weight_ref, row_ref, col_ref, rowf_h, colf_h, level_ref,
    grad_h, inc_h,
    alpha_v, pert_v, innov_v, rowf, colf, colt, down, back, row_hot, col_hot, weight_v, masked,
    slabs, lines, filtered, turned, local_s, local_r, core_s, core_r, x_in, x_got, y_s, y_r,
    inc, inc_v,
    alpha_sem, rowf_sem, load_sem, grad_sem, inc_sem, out_sem, a2a_ss, a2a_rs, core_ss, core_rs,
    x_ss, xin_rs, xgot_rs, yr_ss, yr_rs, give_ss, ya_rs, xa_rs, xf_rs, ca_rs,
):
    m = lax.axis_index("member")
    g = lax.axis_index("grid")
    y_hi = m // (2 * RING)
    x = lax.rem(m // 2, RING)
    core = lax.rem(m, 2)
    sibling = m + 1 - 2 * core
    across = m + 2 * RING - 4 * RING * y_hi

    def around(position, way, steps=1):
        return lax.rem(position + (steps if way == 0 else RING - steps), RING)

    def x_peer(way):
        return y_hi * (2 * RING) + around(x, way) * 2 + core

    def lane(s):
        return pl.ds(pl.multiple_of(s * LANES, LANES), LANES)

    def slab_rows(s):
        return pl.ds(pl.multiple_of(s * ROWS, ROWS), ROWS)

    def part(c):
        return pl.ds(c * PART, PART)

    barrier = pltpu.get_barrier_semaphore()

    def greet(partner):
        pl.semaphore_signal(barrier, inc=1, device_id=partner, device_id_type=MESH)

    loop(GROUP - 1, lambda step: greet((m, lax.rem(g + step + 1, GROUP))))
    for member in (x_peer(0), x_peer(1), sibling, across):
        greet((member, g))

    def alpha_load(c):
        return pltpu.make_async_copy(alpha_h.at[part(c)], alpha_v.at[part(c)], alpha_sem.at[c])

    def rowf_load(n):
        depth = (n // WIDE + 1) * WIDE * TILE
        where = (slice(None), slice(0, depth), slice(n * TILE, (n + 1) * TILE))
        return pltpu.make_async_copy(rowf_h.at[where], rowf.at[where], rowf_sem.at[n])

    alpha_load(0).start()
    for n in range(NX // TILE):
        rowf_load(n).start()
    loads = [
        pltpu.make_async_copy(src, dst, load_sem.at[i])
        for i, (src, dst) in enumerate(((colf_h, colf), (pert_h, pert_v), (innov_h, innov_v)))
    ]

    diagonal = lax.broadcasted_iota(jnp.int32, (ROWS, ROWS), 0) == lax.broadcasted_iota(
        jnp.int32, (ROWS, ROWS), 1
    )

    def upright(line):
        spread = jnp.where(diagonal, jnp.broadcast_to(line, (ROWS, ROWS)), 0.0)
        return jnp.broadcast_to(jnp.sum(spread, axis=1, keepdims=True), (ROWS, LANES))

    def row_table(z):
        column = upright(row_ref[pl.ds(z, 1), :].astype(F32))
        for c in range(CLASSES):
            row_hot[c, slab_rows(z), :] = jnp.where(column == c, 1.0, 0.0).astype(BF16)

    def tile_span(n):
        return slice(n * TILE, (n + 1) * TILE)

    def iota(shape, axis):
        return lax.broadcasted_iota(jnp.int32, shape, axis)

    def level_table(table, product):
        wide = (LEVELS, LEVELS * ROWS)
        spread = jnp.where(iota(wide, 0) == iota(wide, 1) >> ROW_BITS, 1.0, 0.0).astype(BF16)
        tall = (TILE, LEVELS * ROWS)
        same = (iota(tall, 0) & (ROWS - 1)) == (iota(tall, 1) & (ROWS - 1))
        level = level_ref[...]
        for b in range(LEVELS * ROWS // TILE):
            short = (TILE, LEVELS)
            spot = (iota(short, 0) >> ROW_BITS) + b * DEEP
            pick = jnp.where(spot == iota(short, 1), 1.0, 0.0).astype(BF16)
            table[b * TILE : (b + 1) * TILE, :] = jnp.where(
                same, dot(product(pick, level).astype(BF16), spread), 0.0
            ).astype(BF16)

    def column_tables():
        def column_table(z):
            line = jnp.broadcast_to(col_ref[pl.ds(z, 1), :], (16, LANES))
            for c in range(CLASSES):
                col_hot[c, z] = jnp.where(line == c, 1.0, 0.0).astype(BF16)

        loop(LEVELS, column_table)
        level_table(down, dot_nt)
        loads[0].wait()
        unit = jnp.where(iota((NY, NY), 0) == iota((NY, NY), 1), 1.0, 0.0).astype(BF16)

        def turn(c):
            colt[c] = dot_nt(unit, colf[c]).astype(BF16)

        loop(CLASSES, turn)

    def turn_rows(k):
        unit = jnp.where(iota((TILE, TILE), 0) == iota((TILE, TILE), 1), 1.0, 0.0).astype(BF16)
        for r in range(TILES):
            for d in range(r, TILES):
                rowf[k, tile_span(d), tile_span(r)] = dot_nt(
                    unit, rowf[k, tile_span(r), tile_span(d)]
                ).astype(BF16)

    def adjoint_tables():
        def weight_table(z):
            for t in range(2):
                weight_v[t, z] = upright(weight_ref[t, pl.ds(z, 1), :]).astype(BF16)

        loop(LEVELS, weight_table)
        level_table(back, dot)

    def remote(src, dst, ss, rs, member, group):
        return pltpu.make_async_remote_copy(
            src_ref=src, dst_ref=dst, send_sem=ss, recv_sem=rs,
            device_id=(member, group), device_id_type=MESH,
        )

    z_at = g // 2
    y_lo = lax.rem(g, 2)

    def send(phase, c, src, dst, peer):
        remote(src(peer), dst(g), a2a_ss.at[phase], a2a_rs.at[phase, c], m, peer).start()

    def exchange(phase, c, src, dst):
        for up, side in ((2, 0), (1, 0), (3, 0), (2, 1), (1, 1), (3, 1), (0, 1)):
            y_peer = y_lo if side == 0 else 1 - y_lo
            send(phase, c, src, dst, lax.rem(z_at + up, RING) * 2 + y_peer)

    def came(sem, view):
        remote(view, view, out_sem, sem, sibling, g).wait_recv()

    def left(sem, view):
        remote(view, view, sem, out_sem, sibling, g).wait_send()

    def lines_came(phase, c):
        came(a2a_rs.at[phase, c], lines.at[c, pl.ds(0, GROUP - 1)])

    def local_came(phase, c):
        came(a2a_rs.at[phase, c], local_r.at[c, pl.ds(0, GROUP - 1)])

    def exchange_left(phase):
        left(a2a_ss.at[phase], lines.at[:, pl.ds(0, GROUP - 1)])

    def line_block(c):
        return lambda s: lines.at[c, s]

    def filtered_block(c):
        return lambda s: filtered.at[c, s]

    def weighted_block(c):
        return lambda s: core_s.at[c, s]

    def slab_block(c):
        return lambda s: slabs.at[c, s]

    def local_block(c):
        return lambda s: local_r.at[c, s]

    def own_block(c):
        return lambda s: local_s.at[c, s]

    def mask_lines(c, source):
        hots = [
            row_hot[k, pl.ds(pl.multiple_of(c * LINES, LINES), LINES), :] for k in range(CLASSES)
        ]
        for n in range(TILES):
            tile = source(n)
            for k in range(CLASSES):
                at_lane = (n * CLASSES + k) * TILE
                masked[:, at_lane : at_lane + TILE] = tile * jnp.concatenate([hots[k]] * 2, axis=1)

    def row_filter(c):
        alpha_load(c).wait()
        loop(PART, lambda z: row_table(c * PART + z))
        mask_lines(c, lambda n: alpha_v[part(c), :, tile_span(n)].reshape(LINES, TILE))
        for first in range(0, TILES, WIDE):
            last = first + WIDE

            @pl.when(c == 0)
            def _():
                for n in range(first, last):
                    rowf_load(n).wait()

            table = jnp.concatenate(
                [
                    rowf[k, tile_span(d), first * TILE : last * TILE]
                    for d in range(last)
                    for k in range(CLASSES)
                ],
                axis=0,
            )
            total = dot(masked[:, : last * CLASSES * TILE], table).astype(BF16)
            for j in range(2 * WIDE):
                s = 2 * first + j
                slabs[c, s] = total[:, j * LANES : (j + 1) * LANES].reshape(PART, ROWS, LANES)

                @pl.when(jnp.logical_and(c == 0, g != s))
                def _():
                    send(0, c, slab_block(c), line_block(c), s)

        lines[c, g] = slabs[c, g]

        @pl.when(c > 0)
        def _():
            exchange(0, c, slab_block(c), line_block(c))

        @pl.when(c == 0)
        def _():
            for load in loads:
                load.start()

    def column_pass(c, source, table, upper):
        whole = jnp.concatenate(
            [source[c, :, j].reshape(NY, LANES) for j in range(PART)], axis=1
        )
        blocks = []
        for k in range(CLASSES):
            hot = jnp.concatenate([col_hot[k, c * PART + j] for j in range(PART)], axis=1)
            blocks.append(
                (whole.reshape(NY // 16, 16, PART * LANES) * hot[None]).reshape(NY, PART * LANES)
            )
        half = NY // 2
        low = slice(0, half)
        high = slice(half, NY)

        def product(out, deep):
            return dot(
                jnp.concatenate([table[k, out, deep] for k in range(CLASSES)], axis=1),
                jnp.concatenate([block[deep] for block in blocks], axis=0),
            )

        first = product(low, slice(0, NY) if upper else low)
        second = product(high, high if upper else slice(0, NY))
        for j in range(PART):
            side = slice(j * LANES, (j + 1) * LANES)
            for n, total in enumerate((first, second)):
                filtered[c, n * GROUP // 2 : (n + 1) * GROUP // 2, j] = (
                    total[:, side].astype(BF16).reshape(GROUP // 2, ROWS, LANES)
                )

    def level_pass(c, table, source, target, deep):
        for chunk in range(CHUNKS):

            @pl.when(c == chunk)
            def _(chunks=deep(chunk), rows=slice(chunk * LINES, (chunk + 1) * LINES)):
                held = slice(chunks[0], chunks[-1] + 1)
                span = slice(chunks[0] * LINES, (chunks[-1] + 1) * LINES)

                def some(i):
                    block = jnp.concatenate(
                        [source[held, 4 * i + j].reshape(-1, LANES) for j in range(4)], axis=1
                    )
                    total = dot(table[rows, span], block).astype(BF16)
                    for j in range(4):
                        target(
                            4 * i + j,
                            total[:, j * LANES : (j + 1) * LANES].reshape(PART, ROWS, LANES),
                        )

                loop(GROUP // 4, some)

    def column_filter(c):
        lines_came(0, c)
        column_pass(c, lines, colt, False)

        def keep(s, block):
            local_s[c, s] = block

        level_pass(c, down, filtered, keep, lambda chunk: range(chunk + 1))
        local_r[c, g] = local_s[c, g]
        exchange(1, c, own_block(c), local_block(c))

    def core_copy(c):
        return pltpu.make_async_remote_copy(
            src_ref=core_s.at[c],
            dst_ref=core_r.at[c],
            send_sem=core_ss.at[c],
            recv_sem=core_rs.at[c],
            device_id=(sibling, g),
            device_id_type=MESH,
        )

    def xin_slab(way):
        return 2 * around(x, way, 2) + way

    def xone_slab(way):
        return 2 * around(x, way) + 1 - way

    def xtwo_slab(way):
        return 2 * around(x, way) + way

    def x_copy(src, dst, sem, way):
        return remote(src, dst, x_ss, sem, x_peer(way), g)

    def y_copy(c):
        return pltpu.make_async_remote_copy(
            src_ref=y_s.at[c],
            dst_ref=y_r.at[c],
            send_sem=yr_ss,
            recv_sem=yr_rs.at[c],
            device_id=(across, g),
            device_id_type=MESH,
        )

    def term(t, c, s):
        return pert_v[t, part(c), :, lane(s)] * local_r[c, s]

    def sum_core(c):
        local_came(1, c)

        @pl.when(c == 0)
        def _():
            loads[1].wait()
            loads[2].wait()

        def one(s):
            core_s[c, s] = term(1 - core, c, s)

        loop(GROUP, one)
        core_copy(c).start()

    def sum_x(c):
        core_copy(c).wait_recv()

        def add(s):
            core_r[c, s] = term(core, c, s) + core_r[c, s]

        for way in range(2):
            s = xin_slab(way)
            add(s)
            x_copy(core_r.at[c, s], x_in.at[c, way], xin_rs.at[c], way).start()
        for way in range(2):
            s = xone_slab(way)
            add(s)
            x_copy(core_r.at[c, s], x_got.at[c, 0, way], xgot_rs.at[c], way).start()
        for way in range(2):
            add(xtwo_slab(way))
        for j in range(2):
            add(2 * x + j)

    def add_x(c):
        came(xin_rs.at[c], x_in.at[c])
        for way in range(2):
            slab = xtwo_slab(way)
            x_in[c, way] = x_in[c, way] + core_r[c, slab]
            x_copy(x_in.at[c, way], x_got.at[c, 1, way], xgot_rs.at[c], way).start()

    def x_total(c, j):
        total = core_r[c, 2 * x + j].astype(F32) + x_got[c, 1, j].astype(F32)
        return total + x_got[c, 0, 1 - j].astype(F32)

    def sum_y(c):
        came(xgot_rs.at[c], x_got.at[c])
        y_s[c] = x_total(c, 1 - y_hi).astype(BF16)
        y_copy(c).start()

    def give(rs, t, c, s, member):
        return remote(inc.at[t, c, s], inc.at[t, c, s], give_ss, rs, member, g)

    def give_y(c, s):
        return give(ya_rs.at[c], core, c, s, across)

    def give_x(c, way, s):
        return give(xa_rs.at[c], core, c, s, x_peer(way))

    def give_far(c, turn, s):
        return give(xf_rs.at[c], core, c, s, x_peer(turn))

    def slab_of(owner, turn):
        return 2 * owner + (y_hi if turn == 0 else 1 - y_hi)

    mine = slab_of(x, 0)
    other = slab_of(x, 1)

    def finish(c):
        y_copy(c).wait_recv()
        inc[core, c, mine] = (x_total(c, y_hi) + y_r[c].astype(F32)).astype(BF16)
        give_y(c, mine).start()
        for way in range(2):
            give_x(c, way, mine).start()

    def gather_y(c):
        give_y(c, other).wait_recv()
        for way in range(2):
            give_x(c, way, other).start()

    def gather_x(c):
        came(xa_rs.at[c], inc.at[core, c, pl.ds(0, 4)])
        for turn in range(2):
            s = slab_of(around(x, 1 - turn), turn)
            give_far(c, turn, s).start()

    def gather_far(c):
        came(xf_rs.at[c], inc.at[core, c, pl.ds(0, 2)])
        remote(inc.at[core, c], inc.at[core, c], give_ss, ca_rs.at[c], sibling, g).start()

    def weigh(c):
        def one(s):
            total = None
            for t in range(2):
                block = inc[t, c, s]
                inc_v[t, part(c), :, lane(s)] = block
                misfit = weight_v[t, part(c)] * (block - innov_v[t, part(c), :, lane(s)])
                share = pert_v[t, part(c), :, lane(s)] * misfit
                total = share if total is None else total + share
            core_s[c, s] = total

        core_copy(c).wait_send()
        came(ca_rs.at[c], inc.at[1 - core, c])
        loop(GROUP, one)
        lines[c, g] = core_s[c, g]
        exchange(2, c, weighted_block(c), line_block(c))
        inc_copy(c).start()

    def inc_copy(c):
        return pltpu.make_async_copy(
            inc_v.at[:, part(c)], inc_h.at[:, part(c)], inc_sem.at[c]
        )

    def column_adjoint(c):
        lines_came(2, c)

        def keep(s, block):
            turned[c, s] = block

        level_pass(c, back, lines, keep, lambda chunk: range(chunk, CHUNKS))
        column_pass(c, turned, colf, True)
        local_r[c, g] = filtered[c, g]
        exchange(3, c, filtered_block(c), local_block(c))

    def grad_copy(c):
        return pltpu.make_async_copy(alpha_v.at[part(c)], grad_h.at[part(c)], grad_sem.at[c])

    def row_adjoint(c):
        local_came(3, c)
        mask_lines(
            c,
            lambda n: jnp.concatenate(
                [local_r[c, 2 * n + j].reshape(LINES, LANES) for j in range(2)], axis=1
            ),
        )
        for n in range(TILES):
            side = tile_span(n)
            table = jnp.concatenate(
                [rowf[k, tile_span(d), side] for d in range(n, TILES) for k in range(CLASSES)],
                axis=0,
            )
            total = dot(masked[:, n * CLASSES * TILE :], table)
            alpha = alpha_v[part(c), :, side].reshape(LINES, TILE).astype(F32)
            alpha_v[part(c), :, side] = (alpha + total).astype(BF16).reshape(PART, ROWS, TILE)
        grad_copy(c).start()

    pl.semaphore_wait(barrier, GROUP + 3)
    for c in range(1, CHUNKS):
        alpha_load(c).start()

    def at(step, offset, stage):
        chunk = step - offset

        @pl.when(jnp.logical_and(chunk >= 0, chunk < CHUNKS))
        def _():
            stage(chunk)

    def forward(step):
        @pl.when(jnp.logical_and(step >= CHUNKS + 1, step < CHUNKS + 1 + CLASSES))
        def _():
            turn_rows(step - CHUNKS - 1)

        at(step, 6, gather_y)
        at(step, 4, sum_x)
        at(step, 5, sum_y)
        at(step, 7, weigh)
        at(step, 6, gather_x)
        at(step, 5, finish)

        @pl.when(step == 2)
        def _():
            column_tables()

        at(step, 2, column_filter)

        @pl.when(step == 3)
        def _():
            adjoint_tables()

        at(step, 3, sum_core)
        at(step, 4, add_x)
        at(step, 6, gather_far)
        at(step, 0, row_filter)

    loop(CHUNKS + 7, forward)

    def backward(step):
        at(step, 0, lambda c: column_adjoint(CHUNKS - 1 - c))
        at(step, 2, lambda c: row_adjoint(CHUNKS - 1 - c))

    loop(CHUNKS + 2, backward)

    for phase in range(4):
        exchange_left(phase)
    left(x_ss, core_r.at[pl.ds(0, 3)])
    left(yr_ss, y_s)
    left(give_ss, pert_v.at[:, pl.ds(0, LEVELS - 1)])
    for c in range(CHUNKS):
        inc_copy(c).wait()
        grad_copy(c).wait()


def on_device(alpha, pert, innov, weight, row_class, col_class, rowf, colf, level):
    any_spec = pl.BlockSpec(memory_space=pl.ANY)
    vmem_spec = pl.BlockSpec(memory_space=pltpu.VMEM)
    dma = pltpu.SemaphoreType.DMA
    block = (PART, ROWS, LANES)
    slab = (CHUNKS, GROUP) + block
    scratch = [
        pltpu.VMEM((LEVELS, ROWS, NX), BF16),
        pltpu.VMEM((2, LEVELS, ROWS, NX), BF16),
        pltpu.VMEM((2, LEVELS, ROWS, NX), BF16),
        pltpu.VMEM((CLASSES, NX, NX), BF16),
        pltpu.VMEM((CLASSES, NY, NY), BF16),
        pltpu.VMEM((CLASSES, NY, NY), BF16),
        pltpu.VMEM((LEVELS * ROWS, LEVELS * ROWS), BF16),
        pltpu.VMEM((LEVELS * ROWS, LEVELS * ROWS), BF16),
        pltpu.VMEM((CLASSES, LEVELS * ROWS, LANES), BF16),
        pltpu.VMEM((CLASSES, LEVELS, 16, LANES), BF16),
        pltpu.VMEM((2, LEVELS, ROWS, LANES), BF16),
        pltpu.VMEM((LINES, CLASSES * NX), BF16),
        pltpu.VMEM(slab, BF16),
        pltpu.VMEM(slab, BF16),
        pltpu.VMEM(slab, BF16),
        pltpu.VMEM(slab, BF16),
        pltpu.VMEM(slab, BF16),
        pltpu.VMEM(slab, BF16),
        pltpu.VMEM(slab, BF16),
        pltpu.VMEM(slab, BF16),
        pltpu.VMEM((CHUNKS, 2) + block, BF16),
        pltpu.VMEM((CHUNKS, 2, 2) + block, BF16),
        pltpu.VMEM((CHUNKS,) + block, BF16),
        pltpu.VMEM((CHUNKS,) + block, BF16),
        pltpu.VMEM((2,) + slab, BF16),
        pltpu.VMEM((2, LEVELS, ROWS, NX), BF16),
        dma((CHUNKS,)),
        dma((NX // TILE,)),
        dma((3,)),
        dma((CHUNKS,)),
        dma((CHUNKS,)),
        dma,
        dma((4,)),
        dma((4, CHUNKS)),
        dma((CHUNKS,)),
        dma((CHUNKS,)),
        dma,
        dma((CHUNKS,)),
        dma((CHUNKS,)),
        dma,
        dma((CHUNKS,)),
        dma,
        dma((CHUNKS,)),
        dma((CHUNKS,)),
        dma((CHUNKS,)),
        dma((CHUNKS,)),
    ]
    gradient, increment = pl.pallas_call(
        kernel,
        out_shape=(
            jax.ShapeDtypeStruct((LEVELS, ROWS, NX), BF16),
            jax.ShapeDtypeStruct((2, LEVELS, ROWS, NX), BF16),
        ),
        in_specs=[any_spec] * 3 + [vmem_spec] * 3 + [any_spec] * 2 + [vmem_spec],
        out_specs=(any_spec, any_spec),
        scratch_shapes=scratch,
        compiler_params=pltpu.CompilerParams(
            collective_id=0, has_side_effects=True, vmem_limit_bytes=62 * 1024 * 1024
        ),
    )(alpha[0], pert[0], innov, weight, row_class, col_class, rowf, colf, level)
    return gradient[None], increment


def solution(mesh):
    return jax.shard_map(
        on_device,
        mesh=mesh,
        in_specs=(
            P("member", None, "grid", None),
            P("member", None, None, "grid", None),
            P(None, None, "grid", None),
            P(None, None, "grid"),
            P(None, "grid"),
            P(None, "grid"),
            P(),
            P(),
            P(),
        ),
        out_specs=(P("member", None, "grid", None), P(None, None, "grid", None)),
        check_vma=False,
    )
```

```python
import functools

import jax
import jax.numpy as jnp
from jax import lax
from jax.experimental import pallas as pl
from jax.experimental.pallas import tpu as pltpu
from jax.sharding import PartitionSpec as P

MESH = pl.DeviceIdType.MESH
F32 = jnp.float32
BF16 = jnp.bfloat16

CLASSES = 3
LEVELS = 16
GROUP = 8
RING = 4
CHUNKS = 4
PART = LEVELS // CHUNKS
ROWS = 64
ROW_BITS = 6
LANES = 128
NX = GROUP * LANES
NY = GROUP * ROWS
LINES = PART * ROWS
TILE = 256
TILES = NX // TILE
WIDE = 2
DEEP = TILE // ROWS


def loop(count, body):
    def step(index, carry):
        body(index)
        return carry

    lax.fori_loop(0, count, step, 0)


def dot(a, b):
    return jnp.dot(a, b, preferred_element_type=F32)


def dot_nt(a, b):
    return lax.dot_general(a, b, (((1,), (1,)), ((), ())), preferred_element_type=F32)


def kernel(
    alpha_h, pert_h, innov_h, weight_ref, row_ref, col_ref, rowf_h, colf_h, level_ref,
    grad_h, inc_h,
    alpha_v, pert_v, innov_v, rowf, colf, colt, down, back, row_hot, col_hot, weight_v, masked,
    slabs, lines, filtered, turned, local_s, local_r, core_s, core_r, x_in, x_got, y_s, y_r,
    inc, inc_v,
    alpha_sem, rowf_sem, load_sem, grad_sem, inc_sem, out_sem, a2a_ss, a2a_rs, core_ss, core_rs,
    x_ss, xin_rs, xgot_rs, yr_ss, yr_rs, give_ss, xa_rs, xf_rs, ca_rs,
):
    m = lax.axis_index("member")
    g = lax.axis_index("grid")
    y_hi = m // (2 * RING)
    x = lax.rem(m // 2, RING)
    core = lax.rem(m, 2)
    sibling = m + 1 - 2 * core
    across = m + 2 * RING - 4 * RING * y_hi

    def around(position, way, steps=1):
        return lax.rem(position + (steps if way == 0 else RING - steps), RING)

    def x_peer(way):
        return y_hi * (2 * RING) + around(x, way) * 2 + core

    def lane(s):
        return pl.ds(pl.multiple_of(s * LANES, LANES), LANES)

    def slab_rows(s):
        return pl.ds(pl.multiple_of(s * ROWS, ROWS), ROWS)

    def part(c):
        return pl.ds(c * PART, PART)

    barrier = pltpu.get_barrier_semaphore()

    def greet(partner):
        pl.semaphore_signal(barrier, inc=1, device_id=partner, device_id_type=MESH)

    loop(GROUP - 1, lambda step: greet((m, lax.rem(g + step + 1, GROUP))))
    for member in (x_peer(0), x_peer(1), sibling, across):
        greet((member, g))

    def alpha_load(c):
        return pltpu.make_async_copy(alpha_h.at[part(c)], alpha_v.at[part(c)], alpha_sem.at[c])

    def rowf_load(n):
        depth = (n // WIDE + 1) * WIDE * TILE
        where = (slice(None), slice(0, depth), slice(n * TILE, (n + 1) * TILE))
        return pltpu.make_async_copy(rowf_h.at[where], rowf.at[where], rowf_sem.at[n])

    alpha_load(0).start()
    for n in range(NX // TILE):
        rowf_load(n).start()
    loads = [
        pltpu.make_async_copy(src, dst, load_sem.at[i])
        for i, (src, dst) in enumerate(((colf_h, colf), (pert_h, pert_v), (innov_h, innov_v)))
    ]

    diagonal = lax.broadcasted_iota(jnp.int32, (ROWS, ROWS), 0) == lax.broadcasted_iota(
        jnp.int32, (ROWS, ROWS), 1
    )

    def upright(line):
        spread = jnp.where(diagonal, jnp.broadcast_to(line, (ROWS, ROWS)), 0.0)
        return jnp.broadcast_to(jnp.sum(spread, axis=1, keepdims=True), (ROWS, LANES))

    def row_table(z):
        column = upright(row_ref[pl.ds(z, 1), :].astype(F32))
        for c in range(CLASSES):
            row_hot[c, slab_rows(z), :] = jnp.where(column == c, 1.0, 0.0).astype(BF16)

    def tile_span(n):
        return slice(n * TILE, (n + 1) * TILE)

    def iota(shape, axis):
        return lax.broadcasted_iota(jnp.int32, shape, axis)

    def level_table(table, product):
        wide = (LEVELS, LEVELS * ROWS)
        spread = jnp.where(iota(wide, 0) == iota(wide, 1) >> ROW_BITS, 1.0, 0.0).astype(BF16)
        tall = (TILE, LEVELS * ROWS)
        same = (iota(tall, 0) & (ROWS - 1)) == (iota(tall, 1) & (ROWS - 1))
        level = level_ref[...]
        for b in range(LEVELS * ROWS // TILE):
            short = (TILE, LEVELS)
            spot = (iota(short, 0) >> ROW_BITS) + b * DEEP
            pick = jnp.where(spot == iota(short, 1), 1.0, 0.0).astype(BF16)
            table[b * TILE : (b + 1) * TILE, :] = jnp.where(
                same, dot(product(pick, level).astype(BF16), spread), 0.0
            ).astype(BF16)

    def column_tables():
        def column_table(z):
            line = jnp.broadcast_to(col_ref[pl.ds(z, 1), :], (16, LANES))
            for c in range(CLASSES):
                col_hot[c, z] = jnp.where(line == c, 1.0, 0.0).astype(BF16)

        loop(LEVELS, column_table)
        level_table(down, dot_nt)
        loads[0].wait()
        unit = jnp.where(iota((NY, NY), 0) == iota((NY, NY), 1), 1.0, 0.0).astype(BF16)

        def turn(c):
            colt[c] = dot_nt(unit, colf[c]).astype(BF16)

        loop(CLASSES, turn)

    def turn_rows(k):
        unit = jnp.where(iota((TILE, TILE), 0) == iota((TILE, TILE), 1), 1.0, 0.0).astype(BF16)
        for r in range(TILES):
            for d in range(r, TILES):
                rowf[k, tile_span(d), tile_span(r)] = dot_nt(
                    unit, rowf[k, tile_span(r), tile_span(d)]
                ).astype(BF16)

    def adjoint_tables():
        def weight_table(z):
            for t in range(2):
                weight_v[t, z] = upright(weight_ref[t, pl.ds(z, 1), :]).astype(BF16)

        loop(LEVELS, weight_table)
        level_table(back, dot)

    def remote(src, dst, ss, rs, member, group):
        return pltpu.make_async_remote_copy(
            src_ref=src, dst_ref=dst, send_sem=ss, recv_sem=rs,
            device_id=(member, group), device_id_type=MESH,
        )

    z_at = g // 2
    y_lo = lax.rem(g, 2)

    def send(phase, c, src, dst, peer):
        remote(src(peer), dst(g), a2a_ss.at[phase], a2a_rs.at[phase, c], m, peer).start()

    def exchange(phase, c, src, dst):
        for up, side in ((2, 0), (1, 0), (3, 0), (2, 1), (1, 1), (3, 1), (0, 1)):
            y_peer = y_lo if side == 0 else 1 - y_lo
            send(phase, c, src, dst, lax.rem(z_at + up, RING) * 2 + y_peer)

    def came(sem, view):
        remote(view, view, out_sem, sem, sibling, g).wait_recv()

    def left(sem, view):
        remote(view, view, sem, out_sem, sibling, g).wait_send()

    def lines_came(phase, c):
        came(a2a_rs.at[phase, c], lines.at[c, pl.ds(0, GROUP - 1)])

    def local_came(phase, c):
        came(a2a_rs.at[phase, c], local_r.at[c, pl.ds(0, GROUP - 1)])

    def exchange_left(phase):
        left(a2a_ss.at[phase], lines.at[:, pl.ds(0, GROUP - 1)])

    def line_block(c):
        return lambda s: lines.at[c, s]

    def filtered_block(c):
        return lambda s: filtered.at[c, s]

    def weighted_block(c):
        return lambda s: core_s.at[c, s]

    def slab_block(c):
        return lambda s: slabs.at[c, s]

    def local_block(c):
        return lambda s: local_r.at[c, s]

    def own_block(c):
        return lambda s: local_s.at[c, s]

    def mask_lines(c, source):
        hots = [
            row_hot[k, pl.ds(pl.multiple_of(c * LINES, LINES), LINES), :] for k in range(CLASSES)
        ]
        for n in range(TILES):
            tile = source(n)
            for k in range(CLASSES):
                at_lane = (n * CLASSES + k) * TILE
                masked[:, at_lane : at_lane + TILE] = tile * jnp.concatenate([hots[k]] * 2, axis=1)

    def row_filter(c):
        alpha_load(c).wait()
        loop(PART, lambda z: row_table(c * PART + z))
        mask_lines(c, lambda n: alpha_v[part(c), :, tile_span(n)].reshape(LINES, TILE))
        for first in range(0, TILES, WIDE):
            last = first + WIDE

            @pl.when(c == 0)
            def _():
                for n in range(first, last):
                    rowf_load(n).wait()

            table = jnp.concatenate(
                [
                    rowf[k, tile_span(d), first * TILE : last * TILE]
                    for d in range(last)
                    for k in range(CLASSES)
                ],
                axis=0,
            )
            total = dot(masked[:, : last * CLASSES * TILE], table).astype(BF16)
            for j in range(2 * WIDE):
                s = 2 * first + j
                slabs[c, s] = total[:, j * LANES : (j + 1) * LANES].reshape(PART, ROWS, LANES)

                @pl.when(jnp.logical_and(c == 0, g != s))
                def _():
                    send(0, c, slab_block(c), line_block(c), s)

        lines[c, g] = slabs[c, g]

        @pl.when(c > 0)
        def _():
            exchange(0, c, slab_block(c), line_block(c))

        @pl.when(c == 0)
        def _():
            for load in loads:
                load.start()

    def column_pass(c, source, table, upper):
        whole = jnp.concatenate(
            [source[c, :, j].reshape(NY, LANES) for j in range(PART)], axis=1
        )
        blocks = []
        for k in range(CLASSES):
            hot = jnp.concatenate([col_hot[k, c * PART + j] for j in range(PART)], axis=1)
            blocks.append(
                (whole.reshape(NY // 16, 16, PART * LANES) * hot[None]).reshape(NY, PART * LANES)
            )
        half = NY // 2
        low = slice(0, half)
        high = slice(half, NY)

        def product(out, deep):
            return dot(
                jnp.concatenate([table[k, out, deep] for k in range(CLASSES)], axis=1),
                jnp.concatenate([block[deep] for block in blocks], axis=0),
            )

        first = product(low, slice(0, NY) if upper else low)
        second = product(high, high if upper else slice(0, NY))
        for j in range(PART):
            side = slice(j * LANES, (j + 1) * LANES)
            for n, total in enumerate((first, second)):
                filtered[c, n * GROUP // 2 : (n + 1) * GROUP // 2, j] = (
                    total[:, side].astype(BF16).reshape(GROUP // 2, ROWS, LANES)
                )

    def level_pass(c, table, source, target, deep):
        for chunk in range(CHUNKS):

            @pl.when(c == chunk)
            def _(chunks=deep(chunk), rows=slice(chunk * LINES, (chunk + 1) * LINES)):
                held = slice(chunks[0], chunks[-1] + 1)
                span = slice(chunks[0] * LINES, (chunks[-1] + 1) * LINES)

                def some(i):
                    block = jnp.concatenate(
                        [source[held, 4 * i + j].reshape(-1, LANES) for j in range(4)], axis=1
                    )
                    total = dot(table[rows, span], block).astype(BF16)
                    for j in range(4):
                        target(
                            4 * i + j,
                            total[:, j * LANES : (j + 1) * LANES].reshape(PART, ROWS, LANES),
                        )

                loop(GROUP // 4, some)

    def column_filter(c):
        lines_came(0, c)
        column_pass(c, lines, colt, False)

    def level_filter(c):
        def keep(s, block):
            local_s[c, s] = block

        level_pass(c, down, filtered, keep, lambda chunk: range(chunk + 1))
        local_r[c, g] = local_s[c, g]
        exchange(1, c, own_block(c), local_block(c))

    def core_copy(c):
        return pltpu.make_async_remote_copy(
            src_ref=core_s.at[c],
            dst_ref=core_r.at[c],
            send_sem=core_ss.at[c],
            recv_sem=core_rs.at[c],
            device_id=(sibling, g),
            device_id_type=MESH,
        )

    def xin_slab(way):
        return 2 * around(x, way, 2) + way

    def xone_slab(way):
        return 2 * around(x, way) + 1 - way

    def xtwo_slab(way):
        return 2 * around(x, way) + way

    def x_copy(src, dst, sem, way):
        return remote(src, dst, x_ss, sem, x_peer(way), g)

    def y_copy(c):
        return pltpu.make_async_remote_copy(
            src_ref=y_s.at[c],
            dst_ref=y_r.at[c],
            send_sem=yr_ss,
            recv_sem=yr_rs.at[c],
            device_id=(across, g),
            device_id_type=MESH,
        )

    def term(t, c, s):
        return pert_v[t, part(c), :, lane(s)] * local_r[c, s]

    def sum_core(c):
        local_came(1, c)

        @pl.when(c == CHUNKS - 1)
        def _():
            loads[1].wait()
            loads[2].wait()

        def one(s):
            core_s[c, s] = term(1 - core, c, s)

        loop(GROUP, one)
        core_copy(c).start()

    def sum_x(c):
        core_copy(c).wait_recv()

        def add(s):
            core_r[c, s] = term(core, c, s) + core_r[c, s]

        for way in range(2):
            s = xin_slab(way)
            add(s)
            x_copy(core_r.at[c, s], x_in.at[c, way], xin_rs.at[c], way).start()
        for way in range(2):
            s = xone_slab(way)
            add(s)
            x_copy(core_r.at[c, s], x_got.at[c, 0, way], xgot_rs.at[c], way).start()
        for way in range(2):
            add(xtwo_slab(way))
        for j in range(2):
            add(2 * x + j)

    def add_x(c):
        came(xin_rs.at[c], x_in.at[c])
        for way in range(2):
            slab = xtwo_slab(way)
            x_in[c, way] = x_in[c, way] + core_r[c, slab]
            x_copy(x_in.at[c, way], x_got.at[c, 1, way], xgot_rs.at[c], way).start()

    def sum_y(c):
        came(xgot_rs.at[c], x_got.at[c])
        for j in range(2):
            total = core_r[c, 2 * x + j].astype(F32) + x_got[c, 1, j].astype(F32)
            y_s[c, j] = (total + x_got[c, 0, 1 - j].astype(F32)).astype(BF16)
        y_copy(c).start()

    def give(rs, t, c, s, member):
        return remote(inc.at[t, c, s], inc.at[t, c, s], give_ss, rs, member, g)

    def finish(c):
        y_copy(c).wait_recv()
        for j in range(2):
            total = y_s[c, j].astype(F32) + y_r[c, j].astype(F32)
            inc[core, c, 2 * x + j] = total.astype(BF16)
        pair = inc.at[core, c, pl.ds(2 * x, 2)]
        for way in range(2):
            remote(pair, pair, give_ss, xa_rs.at[c], x_peer(way), g).start()

    def gather_x(c):
        came(xa_rs.at[c], inc.at[core, c, pl.ds(0, 4)])
        for way in range(2):
            slab = 2 * around(x, 1 - way) + way
            give(xf_rs.at[c], core, c, slab, x_peer(way)).start()

    def gather_far(c):
        came(xf_rs.at[c], inc.at[core, c, pl.ds(0, 2)])
        remote(inc.at[core, c], inc.at[core, c], give_ss, ca_rs.at[c], sibling, g).start()

    def weigh(c):
        def one(s):
            total = None
            for t in range(2):
                block = inc[t, c, s]
                inc_v[t, part(c), :, lane(s)] = block
                misfit = weight_v[t, part(c)] * (block - innov_v[t, part(c), :, lane(s)])
                share = pert_v[t, part(c), :, lane(s)] * misfit
                total = share if total is None else total + share
            core_s[c, s] = total

        core_copy(c).wait_send()
        came(ca_rs.at[c], inc.at[1 - core, c])
        loop(GROUP, one)
        lines[c, g] = core_s[c, g]
        exchange(2, c, weighted_block(c), line_block(c))
        inc_copy(c).start()

    def inc_copy(c):
        return pltpu.make_async_copy(
            inc_v.at[:, part(c)], inc_h.at[:, part(c)], inc_sem.at[c]
        )

    def column_adjoint(c):
        lines_came(2, c)

        def keep(s, block):
            turned[c, s] = block

        level_pass(c, back, lines, keep, lambda chunk: range(chunk, CHUNKS))
        column_pass(c, turned, colf, True)
        local_r[c, g] = filtered[c, g]
        exchange(3, c, filtered_block(c), local_block(c))

    def grad_copy(c):
        return pltpu.make_async_copy(alpha_v.at[part(c)], grad_h.at[part(c)], grad_sem.at[c])

    def row_adjoint(c):
        local_came(3, c)
        mask_lines(
            c,
            lambda n: jnp.concatenate(
                [local_r[c, 2 * n + j].reshape(LINES, LANES) for j in range(2)], axis=1
            ),
        )
        for n in range(TILES):
            side = tile_span(n)
            table = jnp.concatenate(
                [rowf[k, tile_span(d), side] for d in range(n, TILES) for k in range(CLASSES)],
                axis=0,
            )
            total = dot(masked[:, n * CLASSES * TILE :], table)
            alpha = alpha_v[part(c), :, side].reshape(LINES, TILE).astype(F32)
            alpha_v[part(c), :, side] = (alpha + total).astype(BF16).reshape(PART, ROWS, TILE)
        grad_copy(c).start()

    pl.semaphore_wait(barrier, GROUP + 3)
    for c in range(1, CHUNKS):
        alpha_load(c).start()

    def at(step, offset, stage):
        chunk = step - offset

        @pl.when(jnp.logical_and(chunk >= 0, chunk < CHUNKS))
        def _():
            stage(chunk)

    def front(step):
        at(step, 0, row_filter)

        @pl.when(step == 2)
        def _():
            column_tables()

        at(step, 2, column_filter)

    loop(CHUNKS + 2, front)

    def middle(step):
        def down_from(offset, stage):
            at(step, offset, lambda c: stage(CHUNKS - 1 - c))

        @pl.when(step == 2)
        def _():
            adjoint_tables()

        @pl.when(jnp.logical_and(step >= 4, step < 4 + CLASSES))
        def _():
            turn_rows(step - 4)

        down_from(1, sum_core)
        down_from(0, level_filter)
        down_from(5, column_adjoint)
        down_from(3, gather_x)
        down_from(2, sum_y)
        down_from(1, sum_x)
        down_from(3, gather_far)
        down_from(2, finish)
        down_from(3, weigh)
        down_from(1, add_x)
        down_from(7, row_adjoint)

    loop(CHUNKS + 7, middle)

    for phase in range(4):
        exchange_left(phase)
    left(x_ss, core_r.at[pl.ds(0, 3)])
    left(yr_ss, y_s)
    left(give_ss, pert_v.at[:, pl.ds(0, LEVELS - 2)])
    for c in range(CHUNKS):
        inc_copy(c).wait()
        grad_copy(c).wait()


def on_device(alpha, pert, innov, weight, row_class, col_class, rowf, colf, level):
    any_spec = pl.BlockSpec(memory_space=pl.ANY)
    vmem_spec = pl.BlockSpec(memory_space=pltpu.VMEM)
    dma = pltpu.SemaphoreType.DMA
    block = (PART, ROWS, LANES)
    slab = (CHUNKS, GROUP) + block
    scratch = [
        pltpu.VMEM((LEVELS, ROWS, NX), BF16),
        pltpu.VMEM((2, LEVELS, ROWS, NX), BF16),
        pltpu.VMEM((2, LEVELS, ROWS, NX), BF16),
        pltpu.VMEM((CLASSES, NX, NX), BF16),
        pltpu.VMEM((CLASSES, NY, NY), BF16),
        pltpu.VMEM((CLASSES, NY, NY), BF16),
        pltpu.VMEM((LEVELS * ROWS, LEVELS * ROWS), BF16),
        pltpu.VMEM((LEVELS * ROWS, LEVELS * ROWS), BF16),
        pltpu.VMEM((CLASSES, LEVELS * ROWS, LANES), BF16),
        pltpu.VMEM((CLASSES, LEVELS, 16, LANES), BF16),
        pltpu.VMEM((2, LEVELS, ROWS, LANES), BF16),
        pltpu.VMEM((LINES, CLASSES * NX), BF16),
        pltpu.VMEM(slab, BF16),
        pltpu.VMEM(slab, BF16),
        pltpu.VMEM(slab, BF16),
        pltpu.VMEM(slab, BF16),
        pltpu.VMEM(slab, BF16),
        pltpu.VMEM(slab, BF16),
        pltpu.VMEM(slab, BF16),
        pltpu.VMEM(slab, BF16),
        pltpu.VMEM((CHUNKS, 2) + block, BF16),
        pltpu.VMEM((CHUNKS, 2, 2) + block, BF16),
        pltpu.VMEM((CHUNKS, 2) + block, BF16),
        pltpu.VMEM((CHUNKS, 2) + block, BF16),
        pltpu.VMEM((2,) + slab, BF16),
        pltpu.VMEM((2, LEVELS, ROWS, NX), BF16),
        dma((CHUNKS,)),
        dma((NX // TILE,)),
        dma((3,)),
        dma((CHUNKS,)),
        dma((CHUNKS,)),
        dma,
        dma((4,)),
        dma((4, CHUNKS)),
        dma((CHUNKS,)),
        dma((CHUNKS,)),
        dma,
        dma((CHUNKS,)),
        dma((CHUNKS,)),
        dma,
        dma((CHUNKS,)),
        dma,
        dma((CHUNKS,)),
        dma((CHUNKS,)),
        dma((CHUNKS,)),
    ]
    gradient, increment = pl.pallas_call(
        kernel,
        out_shape=(
            jax.ShapeDtypeStruct((LEVELS, ROWS, NX), BF16),
            jax.ShapeDtypeStruct((2, LEVELS, ROWS, NX), BF16),
        ),
        in_specs=[any_spec] * 3 + [vmem_spec] * 3 + [any_spec] * 2 + [vmem_spec],
        out_specs=(any_spec, any_spec),
        scratch_shapes=scratch,
        compiler_params=pltpu.CompilerParams(
            collective_id=0, has_side_effects=True, vmem_limit_bytes=62 * 1024 * 1024
        ),
    )(alpha[0], pert[0], innov, weight, row_class, col_class, rowf, colf, level)
    return gradient[None], increment


def solution(mesh):
    return jax.shard_map(
        on_device,
        mesh=mesh,
        in_specs=(
            P("member", None, "grid", None),
            P("member", None, None, "grid", None),
            P(None, None, "grid", None),
            P(None, None, "grid"),
            P(None, "grid"),
            P(None, "grid"),
            P(),
            P(),
            P(),
        ),
        out_specs=(P("member", None, "grid", None), P(None, None, "grid", None)),
        check_vma=False,
    )
```

```python
import functools

import jax
import jax.numpy as jnp
from jax import lax
from jax.experimental import pallas as pl
from jax.experimental.pallas import tpu as pltpu
from jax.sharding import PartitionSpec as P

MESH = pl.DeviceIdType.MESH
F32 = jnp.float32
BF16 = jnp.bfloat16

CLASSES = 3
LEVELS = 16
GROUP = 8
RING = 4
CHUNKS = 4
PART = LEVELS // CHUNKS
ROWS = 64
ROW_BITS = 6
LANES = 128
NX = GROUP * LANES
NY = GROUP * ROWS
LINES = PART * ROWS
PAIR = 2
TILE = 256
TILES = NX // TILE
WIDE = 2
DEEP = TILE // ROWS


def loop(count, body):
    def step(index, carry):
        body(index)
        return carry

    lax.fori_loop(0, count, step, 0)


def dot(a, b):
    return jnp.dot(a, b, preferred_element_type=F32)


def dot_nt(a, b):
    return lax.dot_general(a, b, (((1,), (1,)), ((), ())), preferred_element_type=F32)


def kernel(
    alpha_h, pert_h, innov_h, weight_ref, row_ref, col_ref, rowf_h, colf_h, level_ref,
    grad_h, inc_h,
    alpha_v, pert_v, innov_v, rowf, colf, colt, down, back, row_hot, col_hot, weight_v, masked,
    slabs, lines, filtered, turned, local_s, local_r, core_s, core_r, x_in, x_got, y_s, y_r,
    inc, inc_v,
    alpha_sem, rowf_sem, load_sem, grad_sem, inc_sem, out_sem, a2a_ss, a2a_rs, core_ss, core_rs,
    x_ss, xin_rs, xgot_rs, yr_ss, yr_rs, give_ss, xa_rs, xf_rs, ca_rs,
):
    m = lax.axis_index("member")
    g = lax.axis_index("grid")
    y_hi = m // (2 * RING)
    x = lax.rem(m // 2, RING)
    core = lax.rem(m, 2)
    sibling = m + 1 - 2 * core
    across = m + 2 * RING - 4 * RING * y_hi

    def around(position, way, steps=1):
        return lax.rem(position + (steps if way == 0 else RING - steps), RING)

    def x_peer(way):
        return y_hi * (2 * RING) + around(x, way) * 2 + core

    def lane(s):
        return pl.ds(pl.multiple_of(s * LANES, LANES), LANES)

    def slab_rows(s):
        return pl.ds(pl.multiple_of(s * ROWS, ROWS), ROWS)

    def part(c):
        return pl.ds(c * PART, PART)

    barrier = pltpu.get_barrier_semaphore()

    def greet(partner):
        pl.semaphore_signal(barrier, inc=1, device_id=partner, device_id_type=MESH)

    loop(GROUP - 1, lambda step: greet((m, lax.rem(g + step + 1, GROUP))))
    for member in (x_peer(0), x_peer(1), sibling, across):
        greet((member, g))

    def alpha_load(c):
        return pltpu.make_async_copy(alpha_h.at[part(c)], alpha_v.at[part(c)], alpha_sem.at[c])

    def rowf_load(n):
        depth = (n // WIDE + 1) * WIDE * TILE
        where = (slice(None), slice(0, depth), slice(n * TILE, (n + 1) * TILE))
        return pltpu.make_async_copy(rowf_h.at[where], rowf.at[where], rowf_sem.at[n])

    alpha_load(0).start()
    for n in range(NX // TILE):
        rowf_load(n).start()
    loads = [
        pltpu.make_async_copy(src, dst, load_sem.at[i])
        for i, (src, dst) in enumerate(((colf_h, colf), (pert_h, pert_v), (innov_h, innov_v)))
    ]

    diagonal = lax.broadcasted_iota(jnp.int32, (ROWS, ROWS), 0) == lax.broadcasted_iota(
        jnp.int32, (ROWS, ROWS), 1
    )

    def upright(line):
        spread = jnp.where(diagonal, jnp.broadcast_to(line, (ROWS, ROWS)), 0.0)
        return jnp.broadcast_to(jnp.sum(spread, axis=1, keepdims=True), (ROWS, LANES))

    def row_table(z):
        column = upright(row_ref[pl.ds(z, 1), :].astype(F32))
        for c in range(CLASSES):
            row_hot[c, slab_rows(z), :] = jnp.where(column == c, 1.0, 0.0).astype(BF16)

    def tile_span(n):
        return slice(n * TILE, (n + 1) * TILE)

    def iota(shape, axis):
        return lax.broadcasted_iota(jnp.int32, shape, axis)

    def level_table(table, product):
        wide = (LEVELS, LEVELS * ROWS)
        spread = jnp.where(iota(wide, 0) == iota(wide, 1) >> ROW_BITS, 1.0, 0.0).astype(BF16)
        tall = (TILE, LEVELS * ROWS)
        same = (iota(tall, 0) & (ROWS - 1)) == (iota(tall, 1) & (ROWS - 1))
        level = level_ref[...]
        for b in range(LEVELS * ROWS // TILE):
            short = (TILE, LEVELS)
            spot = (iota(short, 0) >> ROW_BITS) + b * DEEP
            pick = jnp.where(spot == iota(short, 1), 1.0, 0.0).astype(BF16)
            table[b * TILE : (b + 1) * TILE, :] = jnp.where(
                same, dot(product(pick, level).astype(BF16), spread), 0.0
            ).astype(BF16)

    def column_tables():
        def column_table(z):
            line = jnp.broadcast_to(col_ref[pl.ds(z, 1), :], (16, LANES))
            for c in range(CLASSES):
                col_hot[c, z] = jnp.where(line == c, 1.0, 0.0).astype(BF16)

        loop(LEVELS, column_table)
        level_table(down, dot_nt)
        loads[0].wait()
        unit = jnp.where(iota((NY, NY), 0) == iota((NY, NY), 1), 1.0, 0.0).astype(BF16)

        def turn(c):
            colt[c] = dot_nt(unit, colf[c]).astype(BF16)

        loop(CLASSES, turn)

    def turn_rows(k):
        unit = jnp.where(iota((TILE, TILE), 0) == iota((TILE, TILE), 1), 1.0, 0.0).astype(BF16)
        for r in range(TILES):
            for d in range(r, TILES):
                rowf[k, tile_span(d), tile_span(r)] = dot_nt(
                    unit, rowf[k, tile_span(r), tile_span(d)]
                ).astype(BF16)

    def adjoint_tables():
        def weight_table(z):
            for t in range(2):
                weight_v[t, z] = upright(weight_ref[t, pl.ds(z, 1), :]).astype(BF16)

        loop(LEVELS, weight_table)
        level_table(back, dot)

    def remote(src, dst, ss, rs, member, group):
        return pltpu.make_async_remote_copy(
            src_ref=src, dst_ref=dst, send_sem=ss, recv_sem=rs,
            device_id=(member, group), device_id_type=MESH,
        )

    z_at = g // 2
    y_lo = lax.rem(g, 2)

    def send(phase, c, src, dst, peer):
        remote(src(peer), dst(g), a2a_ss.at[phase], a2a_rs.at[phase, c], m, peer).start()

    def exchange(phase, c, src, dst):
        for up, side in ((2, 0), (1, 0), (3, 0), (2, 1), (1, 1), (3, 1), (0, 1)):
            y_peer = y_lo if side == 0 else 1 - y_lo
            send(phase, c, src, dst, lax.rem(z_at + up, RING) * 2 + y_peer)

    def came(sem, view):
        remote(view, view, out_sem, sem, sibling, g).wait_recv()

    def left(sem, view):
        remote(view, view, sem, out_sem, sibling, g).wait_send()

    def lines_came(phase, c):
        came(a2a_rs.at[phase, c], lines.at[c, pl.ds(0, GROUP - 1)])

    def local_came(phase, c):
        came(a2a_rs.at[phase, c], local_r.at[c, pl.ds(0, GROUP - 1)])

    def exchange_left(phase):
        left(a2a_ss.at[phase], lines.at[:, pl.ds(0, GROUP - 1)])

    def line_block(c):
        return lambda s: lines.at[c, s]

    def filtered_block(c):
        return lambda s: filtered.at[c, s]

    def weighted_block(c):
        return lambda s: core_s.at[c, s]

    def slab_block(c):
        return lambda s: slabs.at[c, s]

    def local_block(c):
        return lambda s: local_r.at[c, s]

    def own_block(c):
        return lambda s: local_s.at[c, s]

    def mask_lines(c, source):
        span = pl.ds(pl.multiple_of(c * LINES, LINES), PAIR * LINES)
        hots = [row_hot[k, span, :] for k in range(CLASSES)]
        for n in range(TILES):
            tile = source(n)
            for k in range(CLASSES):
                at_lane = (n * CLASSES + k) * TILE
                masked[:, at_lane : at_lane + TILE] = tile * jnp.concatenate([hots[k]] * 2, axis=1)

    def levels(c):
        return pl.ds(c * PART, PAIR * PART)

    def row_filter(c):
        @pl.when(lax.rem(c, PAIR) == 0)
        def _():
            filter_rows(c)

        lines[c, g] = slabs[c, g]

        @pl.when(c > 0)
        def _():
            exchange(0, c, slab_block(c), line_block(c))

        @pl.when(c == 0)
        def _():
            for load in loads:
                load.start()

    def filter_rows(c):
        for j in range(PAIR):
            alpha_load(c + j).wait()
        loop(PAIR * PART, lambda z: row_table(c * PART + z))
        mask_lines(c, lambda n: alpha_v[levels(c), :, tile_span(n)].reshape(PAIR * LINES, TILE))
        for first in range(0, TILES, WIDE):
            last = first + WIDE

            @pl.when(c == 0)
            def _():
                for n in range(first, last):
                    rowf_load(n).wait()

            table = jnp.concatenate(
                [
                    rowf[k, tile_span(d), first * TILE : last * TILE]
                    for d in range(last)
                    for k in range(CLASSES)
                ],
                axis=0,
            )
            total = dot(masked[:, : last * CLASSES * TILE], table).astype(BF16)
            for j in range(2 * WIDE):
                s = 2 * first + j
                slabs[pl.ds(c, PAIR), s] = total[:, j * LANES : (j + 1) * LANES].reshape(
                    PAIR, PART, ROWS, LANES
                )

                @pl.when(jnp.logical_and(c == 0, g != s))
                def _():
                    send(0, c, slab_block(c), line_block(c), s)

    def column_pass(c, source, table, upper):
        whole = jnp.concatenate(
            [source[c, :, j].reshape(NY, LANES) for j in range(PART)], axis=1
        )
        blocks = []
        for k in range(CLASSES):
            hot = jnp.concatenate([col_hot[k, c * PART + j] for j in range(PART)], axis=1)
            blocks.append(
                (whole.reshape(NY // 16, 16, PART * LANES) * hot[None]).reshape(NY, PART * LANES)
            )
        half = NY // 2
        low = slice(0, half)
        high = slice(half, NY)

        def product(out, deep):
            return dot(
                jnp.concatenate([table[k, out, deep] for k in range(CLASSES)], axis=1),
                jnp.concatenate([block[deep] for block in blocks], axis=0),
            )

        first = product(low, slice(0, NY) if upper else low)
        second = product(high, high if upper else slice(0, NY))
        for j in range(PART):
            side = slice(j * LANES, (j + 1) * LANES)
            for n, total in enumerate((first, second)):
                filtered[c, n * GROUP // 2 : (n + 1) * GROUP // 2, j] = (
                    total[:, side].astype(BF16).reshape(GROUP // 2, ROWS, LANES)
                )

    def level_pass(c, table, source, target, deep):
        for chunk in range(CHUNKS):

            @pl.when(c == chunk)
            def _(chunks=deep(chunk), rows=slice(chunk * LINES, (chunk + 1) * LINES)):
                held = slice(chunks[0], chunks[-1] + 1)
                span = slice(chunks[0] * LINES, (chunks[-1] + 1) * LINES)

                def some(i):
                    block = jnp.concatenate(
                        [source[held, 4 * i + j].reshape(-1, LANES) for j in range(4)], axis=1
                    )
                    total = dot(table[rows, span], block).astype(BF16)
                    for j in range(4):
                        target(
                            4 * i + j,
                            total[:, j * LANES : (j + 1) * LANES].reshape(PART, ROWS, LANES),
                        )

                loop(GROUP // 4, some)

    def column_filter(c):
        lines_came(0, c)
        column_pass(c, lines, colt, False)

        def keep(s, block):
            local_s[c, s] = block

        level_pass(c, down, filtered, keep, lambda chunk: range(chunk + 1))
        local_r[c, g] = local_s[c, g]
        exchange(1, c, own_block(c), local_block(c))

    def core_copy(c):
        return pltpu.make_async_remote_copy(
            src_ref=core_s.at[c],
            dst_ref=core_r.at[c],
            send_sem=core_ss.at[c],
            recv_sem=core_rs.at[c],
            device_id=(sibling, g),
            device_id_type=MESH,
        )

    def xin_slab(way):
        return 2 * around(x, way, 2) + way

    def xone_slab(way):
        return 2 * around(x, way) + 1 - way

    def xtwo_slab(way):
        return 2 * around(x, way) + way

    def x_copy(src, dst, sem, way):
        return remote(src, dst, x_ss, sem, x_peer(way), g)

    def y_copy(c):
        return pltpu.make_async_remote_copy(
            src_ref=y_s.at[c],
            dst_ref=y_r.at[c],
            send_sem=yr_ss,
            recv_sem=yr_rs.at[c],
            device_id=(across, g),
            device_id_type=MESH,
        )

    def term(t, c, s):
        return pert_v[t, part(c), :, lane(s)] * local_r[c, s]

    def sum_core(c):
        local_came(1, c)

        @pl.when(c == 0)
        def _():
            loads[1].wait()
            loads[2].wait()

        def one(s):
            core_s[c, s] = term(1 - core, c, s)

        loop(GROUP, one)
        core_copy(c).start()

    def sum_x(c):
        core_copy(c).wait_recv()

        def add(s):
            core_r[c, s] = term(core, c, s) + core_r[c, s]

        for way in range(2):
            s = xin_slab(way)
            add(s)
            x_copy(core_r.at[c, s], x_in.at[c, way], xin_rs.at[c], way).start()
        for way in range(2):
            s = xone_slab(way)
            add(s)
            x_copy(core_r.at[c, s], x_got.at[c, 0, way], xgot_rs.at[c], way).start()
        for way in range(2):
            add(xtwo_slab(way))
        for j in range(2):
            add(2 * x + j)

    def add_x(c):
        came(xin_rs.at[c], x_in.at[c])
        for way in range(2):
            slab = xtwo_slab(way)
            x_in[c, way] = x_in[c, way] + core_r[c, slab]
            x_copy(x_in.at[c, way], x_got.at[c, 1, way], xgot_rs.at[c], way).start()

    def sum_y(c):
        came(xgot_rs.at[c], x_got.at[c])
        for j in range(2):
            total = core_r[c, 2 * x + j].astype(F32) + x_got[c, 1, j].astype(F32)
            y_s[c, j] = (total + x_got[c, 0, 1 - j].astype(F32)).astype(BF16)
        y_copy(c).start()

    def give(rs, t, c, s, member):
        return remote(inc.at[t, c, s], inc.at[t, c, s], give_ss, rs, member, g)

    def finish(c):
        y_copy(c).wait_recv()
        for j in range(2):
            total = y_s[c, j].astype(F32) + y_r[c, j].astype(F32)
            inc[core, c, 2 * x + j] = total.astype(BF16)
        pair = inc.at[core, c, pl.ds(2 * x, 2)]
        for way in range(2):
            remote(pair, pair, give_ss, xa_rs.at[c], x_peer(way), g).start()

    def gather_x(c):
        came(xa_rs.at[c], inc.at[core, c, pl.ds(0, 4)])
        for way in range(2):
            slab = 2 * around(x, 1 - way) + way
            give(xf_rs.at[c], core, c, slab, x_peer(way)).start()

    def gather_far(c):
        came(xf_rs.at[c], inc.at[core, c, pl.ds(0, 2)])
        remote(inc.at[core, c], inc.at[core, c], give_ss, ca_rs.at[c], sibling, g).start()

    def weigh(c):
        def one(s):
            total = None
            for t in range(2):
                block = inc[t, c, s]
                inc_v[t, part(c), :, lane(s)] = block
                misfit = weight_v[t, part(c)] * (block - innov_v[t, part(c), :, lane(s)])
                share = pert_v[t, part(c), :, lane(s)] * misfit
                total = share if total is None else total + share
            core_s[c, s] = total

        core_copy(c).wait_send()
        came(ca_rs.at[c], inc.at[1 - core, c])
        loop(GROUP, one)
        lines[c, g] = core_s[c, g]
        exchange(2, c, weighted_block(c), line_block(c))
        inc_copy(c).start()

    def inc_copy(c):
        return pltpu.make_async_copy(
            inc_v.at[:, part(c)], inc_h.at[:, part(c)], inc_sem.at[c]
        )

    def column_adjoint(c):
        lines_came(2, c)

        def keep(s, block):
            turned[c, s] = block

        level_pass(c, back, lines, keep, lambda chunk: range(chunk, CHUNKS))
        column_pass(c, turned, colf, True)
        local_r[c, g] = filtered[c, g]
        exchange(3, c, filtered_block(c), local_block(c))

    def grad_copy(c):
        return pltpu.make_async_copy(alpha_v.at[part(c)], grad_h.at[part(c)], grad_sem.at[c])

    def row_adjoint(c):
        local_came(3, c)

        @pl.when(lax.rem(c, PAIR) == 0)
        def _():
            adjoin_rows(c)

    def adjoin_rows(c):
        mask_lines(
            c,
            lambda n: jnp.concatenate(
                [
                    local_r[pl.ds(c, PAIR), 2 * n + j].reshape(PAIR * LINES, LANES)
                    for j in range(2)
                ],
                axis=1,
            ),
        )
        for n in range(TILES):
            side = tile_span(n)
            table = jnp.concatenate(
                [rowf[k, tile_span(d), side] for d in range(n, TILES) for k in range(CLASSES)],
                axis=0,
            )
            total = dot(masked[:, n * CLASSES * TILE :], table)
            alpha = alpha_v[levels(c), :, side].reshape(PAIR * LINES, TILE).astype(F32)
            alpha_v[levels(c), :, side] = (
                (alpha + total).astype(BF16).reshape(PAIR * PART, ROWS, TILE)
            )
        for j in range(PAIR):
            grad_copy(c + j).start()

    pl.semaphore_wait(barrier, GROUP + 3)
    for c in range(1, CHUNKS):
        alpha_load(c).start()

    def at(step, offset, stage):
        chunk = step - offset

        @pl.when(jnp.logical_and(chunk >= 0, chunk < CHUNKS))
        def _():
            stage(chunk)

    def forward(step):
        @pl.when(jnp.logical_and(step >= CHUNKS + 1, step < CHUNKS + 1 + CLASSES))
        def _():
            turn_rows(step - CHUNKS - 1)

        @pl.when(step == 4)
        def _():
            adjoint_tables()

        at(step, 4, sum_core)
        at(step, 6, finish)
        at(step, 7, gather_far)
        at(step, 5, sum_y)
        at(step, 1, row_filter)
        at(step, 4, sum_x)
        at(step, 7, weigh)

        @pl.when(step == 2)
        def _():
            column_tables()

        at(step, 2, column_filter)
        at(step, 6, gather_x)
        at(step, 4, add_x)

    loop(CHUNKS + 7, forward)

    def backward(step):
        at(step, 0, lambda c: column_adjoint(CHUNKS - 1 - c))
        at(step, 2, lambda c: row_adjoint(CHUNKS - 1 - c))

    loop(CHUNKS + 2, backward)

    for phase in range(4):
        exchange_left(phase)
    left(x_ss, core_r.at[pl.ds(0, 3)])
    left(yr_ss, y_s)
    left(give_ss, pert_v.at[:, pl.ds(0, LEVELS - 2)])
    for c in range(CHUNKS):
        inc_copy(c).wait()
        grad_copy(c).wait()


def on_device(alpha, pert, innov, weight, row_class, col_class, rowf, colf, level):
    any_spec = pl.BlockSpec(memory_space=pl.ANY)
    vmem_spec = pl.BlockSpec(memory_space=pltpu.VMEM)
    dma = pltpu.SemaphoreType.DMA
    block = (PART, ROWS, LANES)
    slab = (CHUNKS, GROUP) + block
    scratch = [
        pltpu.VMEM((LEVELS, ROWS, NX), BF16),
        pltpu.VMEM((2, LEVELS, ROWS, NX), BF16),
        pltpu.VMEM((2, LEVELS, ROWS, NX), BF16),
        pltpu.VMEM((CLASSES, NX, NX), BF16),
        pltpu.VMEM((CLASSES, NY, NY), BF16),
        pltpu.VMEM((CLASSES, NY, NY), BF16),
        pltpu.VMEM((LEVELS * ROWS, LEVELS * ROWS), BF16),
        pltpu.VMEM((LEVELS * ROWS, LEVELS * ROWS), BF16),
        pltpu.VMEM((CLASSES, LEVELS * ROWS, LANES), BF16),
        pltpu.VMEM((CLASSES, LEVELS, 16, LANES), BF16),
        pltpu.VMEM((2, LEVELS, ROWS, LANES), BF16),
        pltpu.VMEM((PAIR * LINES, CLASSES * NX), BF16),
        pltpu.VMEM(slab, BF16),
        pltpu.VMEM(slab, BF16),
        pltpu.VMEM(slab, BF16),
        pltpu.VMEM(slab, BF16),
        pltpu.VMEM(slab, BF16),
        pltpu.VMEM(slab, BF16),
        pltpu.VMEM(slab, BF16),
        pltpu.VMEM(slab, BF16),
        pltpu.VMEM((CHUNKS, 2) + block, BF16),
        pltpu.VMEM((CHUNKS, 2, 2) + block, BF16),
        pltpu.VMEM((CHUNKS, 2) + block, BF16),
        pltpu.VMEM((CHUNKS, 2) + block, BF16),
        pltpu.VMEM((2,) + slab, BF16),
        pltpu.VMEM((2, LEVELS, ROWS, NX), BF16),
        dma((CHUNKS,)),
        dma((NX // TILE,)),
        dma((3,)),
        dma((CHUNKS,)),
        dma((CHUNKS,)),
        dma,
        dma((4,)),
        dma((4, CHUNKS)),
        dma((CHUNKS,)),
        dma((CHUNKS,)),
        dma,
        dma((CHUNKS,)),
        dma((CHUNKS,)),
        dma,
        dma((CHUNKS,)),
        dma,
        dma((CHUNKS,)),
        dma((CHUNKS,)),
        dma((CHUNKS,)),
    ]
    gradient, increment = pl.pallas_call(
        kernel,
        out_shape=(
            jax.ShapeDtypeStruct((LEVELS, ROWS, NX), BF16),
            jax.ShapeDtypeStruct((2, LEVELS, ROWS, NX), BF16),
        ),
        in_specs=[any_spec] * 3 + [vmem_spec] * 3 + [any_spec] * 2 + [vmem_spec],
        out_specs=(any_spec, any_spec),
        scratch_shapes=scratch,
        compiler_params=pltpu.CompilerParams(
            collective_id=0, has_side_effects=True, vmem_limit_bytes=62 * 1024 * 1024
        ),
    )(alpha[0], pert[0], innov, weight, row_class, col_class, rowf, colf, level)
    return gradient[None], increment


def solution(mesh):
    return jax.shard_map(
        on_device,
        mesh=mesh,
        in_specs=(
            P("member", None, "grid", None),
            P("member", None, None, "grid", None),
            P(None, None, "grid", None),
            P(None, None, "grid"),
            P(None, "grid"),
            P(None, "grid"),
            P(),
            P(),
            P(),
        ),
        out_specs=(P("member", None, "grid", None), P(None, None, "grid", None)),
        check_vma=False,
    )
```

```python
import functools

import jax
import jax.numpy as jnp
from jax import lax
from jax.experimental import pallas as pl
from jax.experimental.pallas import tpu as pltpu
from jax.sharding import PartitionSpec as P

MESH = pl.DeviceIdType.MESH
F32 = jnp.float32
BF16 = jnp.bfloat16

CLASSES = 3
LEVELS = 16
GROUP = 8
RING = 4
CHUNKS = 4
PART = LEVELS // CHUNKS
ROWS = 64
ROW_BITS = 6
LANES = 128
NX = GROUP * LANES
NY = GROUP * ROWS
LINES = PART * ROWS
PAIR = 2
TILE = 256
TILES = NX // TILE
WIDE = 2
DEEP = TILE // ROWS


def loop(count, body):
    def step(index, carry):
        body(index)
        return carry

    lax.fori_loop(0, count, step, 0)


def dot(a, b):
    return jnp.dot(a, b, preferred_element_type=F32)


def dot_nt(a, b):
    return lax.dot_general(a, b, (((1,), (1,)), ((), ())), preferred_element_type=F32)


def kernel(
    alpha_h, pert_h, innov_h, weight_ref, row_ref, col_ref, rowf_h, colf_h, level_ref,
    grad_h, inc_h,
    alpha_v, pert_v, innov_v, rowf, colf, colt, down, back, row_hot, weight_v, masked,
    slabs, lines, filtered, turned, local_s, local_r, core_s, core_r, x_in, x_got, y_s, y_r,
    inc, inc_v,
    alpha_sem, rowf_sem, load_sem, grad_sem, inc_sem, out_sem, a2a_ss, a2a_rs, core_ss, core_rs,
    x_ss, xin_rs, xgot_rs, yr_ss, yr_rs, give_ss, xa_rs, xf_rs, ca_rs,
):
    m = lax.axis_index("member")
    g = lax.axis_index("grid")
    y_hi = m // (2 * RING)
    x = lax.rem(m // 2, RING)
    core = lax.rem(m, 2)
    sibling = m + 1 - 2 * core
    across = m + 2 * RING - 4 * RING * y_hi

    def around(position, way, steps=1):
        return lax.rem(position + (steps if way == 0 else RING - steps), RING)

    def x_peer(way):
        return y_hi * (2 * RING) + around(x, way) * 2 + core

    def lane(s):
        return pl.ds(pl.multiple_of(s * LANES, LANES), LANES)

    def slab_rows(s):
        return pl.ds(pl.multiple_of(s * ROWS, ROWS), ROWS)

    def part(c):
        return pl.ds(c * PART, PART)

    barrier = pltpu.get_barrier_semaphore()

    def greet(partner):
        pl.semaphore_signal(barrier, inc=1, device_id=partner, device_id_type=MESH)

    loop(GROUP - 1, lambda step: greet((m, lax.rem(g + step + 1, GROUP))))
    for member in (x_peer(0), x_peer(1), sibling, across):
        greet((member, g))

    def alpha_load(c):
        return pltpu.make_async_copy(alpha_h.at[part(c)], alpha_v.at[part(c)], alpha_sem.at[c])

    def rowf_load(n):
        depth = (n // WIDE + 1) * WIDE * TILE
        where = (slice(None), slice(0, depth), slice(n * TILE, (n + 1) * TILE))
        return pltpu.make_async_copy(rowf_h.at[where], rowf.at[where], rowf_sem.at[n])

    alpha_load(0).start()
    for n in range(NX // TILE):
        rowf_load(n).start()
    loads = [
        pltpu.make_async_copy(src, dst, load_sem.at[i])
        for i, (src, dst) in enumerate(((colf_h, colf), (pert_h, pert_v), (innov_h, innov_v)))
    ]

    diagonal = lax.broadcasted_iota(jnp.int32, (ROWS, ROWS), 0) == lax.broadcasted_iota(
        jnp.int32, (ROWS, ROWS), 1
    )

    def upright(line):
        spread = jnp.where(diagonal, jnp.broadcast_to(line, (ROWS, ROWS)), 0.0)
        return jnp.broadcast_to(jnp.sum(spread, axis=1, keepdims=True), (ROWS, LANES))

    def row_table(z):
        column = upright(row_ref[pl.ds(z, 1), :].astype(F32))
        for c in range(CLASSES):
            row_hot[c, slab_rows(z), :] = jnp.where(column == c, 1.0, 0.0).astype(BF16)

    def tile_span(n):
        return slice(n * TILE, (n + 1) * TILE)

    def iota(shape, axis):
        return lax.broadcasted_iota(jnp.int32, shape, axis)

    def level_table(table, product):
        wide = (LEVELS, LEVELS * ROWS)
        spread = jnp.where(iota(wide, 0) == iota(wide, 1) >> ROW_BITS, 1.0, 0.0).astype(BF16)
        tall = (TILE, LEVELS * ROWS)
        same = (iota(tall, 0) & (ROWS - 1)) == (iota(tall, 1) & (ROWS - 1))
        level = level_ref[...]
        for b in range(LEVELS * ROWS // TILE):
            short = (TILE, LEVELS)
            spot = (iota(short, 0) >> ROW_BITS) + b * DEEP
            pick = jnp.where(spot == iota(short, 1), 1.0, 0.0).astype(BF16)
            table[b * TILE : (b + 1) * TILE, :] = jnp.where(
                same, dot(product(pick, level).astype(BF16), spread), 0.0
            ).astype(BF16)

    def column_tables():
        level_table(down, dot_nt)
        loads[0].wait()
        unit = jnp.where(iota((NY, NY), 0) == iota((NY, NY), 1), 1.0, 0.0).astype(BF16)

        def turn(c):
            colt[c] = dot_nt(unit, colf[c]).astype(BF16)

        loop(CLASSES, turn)

    def turn_rows(k):
        unit = jnp.where(iota((TILE, TILE), 0) == iota((TILE, TILE), 1), 1.0, 0.0).astype(BF16)
        for r in range(TILES):
            for d in range(r, TILES):
                rowf[k, tile_span(d), tile_span(r)] = dot_nt(
                    unit, rowf[k, tile_span(r), tile_span(d)]
                ).astype(BF16)

    def adjoint_tables():
        def weight_table(z):
            for t in range(2):
                weight_v[t, z] = upright(weight_ref[t, pl.ds(z, 1), :]).astype(BF16)

        loop(LEVELS, weight_table)
        level_table(back, dot)

    def remote(src, dst, ss, rs, member, group):
        return pltpu.make_async_remote_copy(
            src_ref=src, dst_ref=dst, send_sem=ss, recv_sem=rs,
            device_id=(member, group), device_id_type=MESH,
        )

    z_at = g // 2
    y_lo = lax.rem(g, 2)

    def send(phase, c, src, dst, peer):
        remote(src(peer), dst(g), a2a_ss.at[phase], a2a_rs.at[phase, c], m, peer).start()

    def exchange(phase, c, src, dst):
        for up, side in ((2, 0), (1, 0), (3, 0), (2, 1), (1, 1), (3, 1), (0, 1)):
            y_peer = y_lo if side == 0 else 1 - y_lo
            send(phase, c, src, dst, lax.rem(z_at + up, RING) * 2 + y_peer)

    def came(sem, view):
        remote(view, view, out_sem, sem, sibling, g).wait_recv()

    def left(sem, view):
        remote(view, view, sem, out_sem, sibling, g).wait_send()

    def lines_came(phase, c):
        came(a2a_rs.at[phase, c], lines.at[c, pl.ds(0, GROUP - 1)])

    def local_came(phase, c):
        came(a2a_rs.at[phase, c], local_r.at[c, pl.ds(0, GROUP - 1)])

    def exchange_left(phase):
        left(a2a_ss.at[phase], lines.at[:, pl.ds(0, GROUP - 1)])

    def line_block(c):
        return lambda s: lines.at[c, s]

    def filtered_block(c):
        return lambda s: filtered.at[c, s]

    def weighted_block(c):
        return lambda s: core_s.at[c, s]

    def slab_block(c):
        return lambda s: slabs.at[c, s]

    def local_block(c):
        return lambda s: local_r.at[c, s]

    def own_block(c):
        return lambda s: local_s.at[c, s]

    def mask_lines(c, source):
        span = pl.ds(pl.multiple_of(c * LINES, LINES), PAIR * LINES)
        hots = [row_hot[k, span, :] for k in range(CLASSES)]
        for n in range(TILES):
            tile = source(n)
            for k in range(CLASSES):
                at_lane = (n * CLASSES + k) * TILE
                masked[:, at_lane : at_lane + TILE] = tile * jnp.concatenate([hots[k]] * 2, axis=1)

    def levels(c):
        return pl.ds(c * PART, PAIR * PART)

    def row_filter(c):
        @pl.when(lax.rem(c, PAIR) == 0)
        def _():
            filter_rows(c)

        lines[c, g] = slabs[c, g]

        @pl.when(c > 0)
        def _():
            exchange(0, c, slab_block(c), line_block(c))

        @pl.when(c == 0)
        def _():
            for load in loads:
                load.start()

    def filter_rows(c):
        for j in range(PAIR):
            alpha_load(c + j).wait()
        loop(PAIR * PART, lambda z: row_table(c * PART + z))
        mask_lines(c, lambda n: alpha_v[levels(c), :, tile_span(n)].reshape(PAIR * LINES, TILE))
        for first in range(0, TILES, WIDE):
            last = first + WIDE

            @pl.when(c == 0)
            def _():
                for n in range(first, last):
                    rowf_load(n).wait()

            table = jnp.concatenate(
                [
                    rowf[k, tile_span(d), first * TILE : last * TILE]
                    for d in range(last)
                    for k in range(CLASSES)
                ],
                axis=0,
            )
            total = dot(masked[:, : last * CLASSES * TILE], table).astype(BF16)
            for j in range(2 * WIDE):
                s = 2 * first + j
                slabs[pl.ds(c, PAIR), s] = total[:, j * LANES : (j + 1) * LANES].reshape(
                    PAIR, PART, ROWS, LANES
                )

                @pl.when(jnp.logical_and(c == 0, g != s))
                def _():
                    send(0, c, slab_block(c), line_block(c), s)

    def column_pass(c, source, table, upper):
        whole = jnp.concatenate(
            [source[c, :, j].reshape(NY, LANES) for j in range(PART)], axis=1
        )
        kind = jnp.concatenate([col_ref[pl.ds(c * PART + j, 1), :] for j in range(PART)], axis=1)
        kind = jnp.broadcast_to(kind, (NY // 2, PART * LANES))

        def pick(products):
            return jnp.where(kind == 0, products[0], jnp.where(kind == 1, products[1], products[2]))

        def product(rows, deep):
            stacked = jnp.concatenate([table[k, rows, deep] for k in range(CLASSES)], axis=0)
            total = dot(stacked, whole[deep])
            count = total.shape[0] // CLASSES
            return [total[k * count : (k + 1) * count] for k in range(CLASSES)]

        half = NY // 2
        low = slice(0, half)
        high = slice(half, NY)
        both = slice(0, NY)
        wide = product(both, high if upper else low)
        narrow = product(low if upper else high, low if upper else high)
        first = pick([block[low] for block in wide])
        second = pick([block[high] for block in wide])
        if upper:
            first += pick(narrow)
        else:
            second += pick(narrow)
        for j in range(PART):
            side = slice(j * LANES, (j + 1) * LANES)
            for n, total in enumerate((first, second)):
                filtered[c, n * GROUP // 2 : (n + 1) * GROUP // 2, j] = (
                    total[:, side].astype(BF16).reshape(GROUP // 2, ROWS, LANES)
                )

    def level_pass(c, table, source, target, deep):
        for chunk in range(CHUNKS):

            @pl.when(c == chunk)
            def _(chunks=deep(chunk), rows=slice(chunk * LINES, (chunk + 1) * LINES)):
                held = slice(chunks[0], chunks[-1] + 1)
                span = slice(chunks[0] * LINES, (chunks[-1] + 1) * LINES)

                def some(i):
                    block = jnp.concatenate(
                        [source[held, 4 * i + j].reshape(-1, LANES) for j in range(4)], axis=1
                    )
                    total = dot(table[rows, span], block).astype(BF16)
                    for j in range(4):
                        target(
                            4 * i + j,
                            total[:, j * LANES : (j + 1) * LANES].reshape(PART, ROWS, LANES),
                        )

                loop(GROUP // 4, some)

    def column_filter(c):
        lines_came(0, c)
        column_pass(c, lines, colt, False)

        def keep(s, block):
            local_s[c, s] = block

        level_pass(c, down, filtered, keep, lambda chunk: range(chunk + 1))
        local_r[c, g] = local_s[c, g]
        exchange(1, c, own_block(c), local_block(c))

    def core_copy(c):
        return pltpu.make_async_remote_copy(
            src_ref=core_s.at[c],
            dst_ref=core_r.at[c],
            send_sem=core_ss.at[c],
            recv_sem=core_rs.at[c],
            device_id=(sibling, g),
            device_id_type=MESH,
        )

    def xin_slab(way):
        return 2 * around(x, way, 2) + way

    def xone_slab(way):
        return 2 * around(x, way) + 1 - way

    def xtwo_slab(way):
        return 2 * around(x, way) + way

    def x_copy(src, dst, sem, way):
        return remote(src, dst, x_ss, sem, x_peer(way), g)

    def y_copy(c):
        return pltpu.make_async_remote_copy(
            src_ref=y_s.at[c],
            dst_ref=y_r.at[c],
            send_sem=yr_ss,
            recv_sem=yr_rs.at[c],
            device_id=(across, g),
            device_id_type=MESH,
        )

    def term(t, c, s):
        return pert_v[t, part(c), :, lane(s)] * local_r[c, s]

    def sum_core(c):
        local_came(1, c)

        @pl.when(c == 0)
        def _():
            loads[1].wait()
            loads[2].wait()

        def one(s):
            core_s[c, s] = term(1 - core, c, s)

        loop(GROUP, one)
        core_copy(c).start()

    def sum_x(c):
        core_copy(c).wait_recv()

        def add(s):
            core_r[c, s] = term(core, c, s) + core_r[c, s]

        for way in range(2):
            s = xin_slab(way)
            add(s)
            x_copy(core_r.at[c, s], x_in.at[c, way], xin_rs.at[c], way).start()
        for way in range(2):
            s = xone_slab(way)
            add(s)
            x_copy(core_r.at[c, s], x_got.at[c, 0, way], xgot_rs.at[c], way).start()
        for way in range(2):
            add(xtwo_slab(way))
        for j in range(2):
            add(2 * x + j)

    def add_x(c):
        came(xin_rs.at[c], x_in.at[c])
        for way in range(2):
            slab = xtwo_slab(way)
            x_in[c, way] = x_in[c, way] + core_r[c, slab]
            x_copy(x_in.at[c, way], x_got.at[c, 1, way], xgot_rs.at[c], way).start()

    def sum_y(c):
        came(xgot_rs.at[c], x_got.at[c])
        for j in range(2):
            total = core_r[c, 2 * x + j].astype(F32) + x_got[c, 1, j].astype(F32)
            y_s[c, j] = (total + x_got[c, 0, 1 - j].astype(F32)).astype(BF16)
        y_copy(c).start()

    def give(rs, t, c, s, member):
        return remote(inc.at[t, c, s], inc.at[t, c, s], give_ss, rs, member, g)

    def finish(c):
        y_copy(c).wait_recv()
        for j in range(2):
            total = y_s[c, j].astype(F32) + y_r[c, j].astype(F32)
            inc[core, c, 2 * x + j] = total.astype(BF16)
        pair = inc.at[core, c, pl.ds(2 * x, 2)]
        for way in range(2):
            remote(pair, pair, give_ss, xa_rs.at[c], x_peer(way), g).start()

    def gather_x(c):
        came(xa_rs.at[c], inc.at[core, c, pl.ds(0, 4)])
        for way in range(2):
            slab = 2 * around(x, 1 - way) + way
            give(xf_rs.at[c], core, c, slab, x_peer(way)).start()

    def gather_far(c):
        came(xf_rs.at[c], inc.at[core, c, pl.ds(0, 2)])
        remote(inc.at[core, c], inc.at[core, c], give_ss, ca_rs.at[c], sibling, g).start()

    def weigh(c):
        def one(s):
            total = None
            for t in range(2):
                block = inc[t, c, s]
                inc_v[t, part(c), :, lane(s)] = block
                misfit = weight_v[t, part(c)] * (block - innov_v[t, part(c), :, lane(s)])
                share = pert_v[t, part(c), :, lane(s)] * misfit
                total = share if total is None else total + share
            core_s[c, s] = total

        core_copy(c).wait_send()
        came(ca_rs.at[c], inc.at[1 - core, c])
        loop(GROUP, one)
        lines[c, g] = core_s[c, g]
        exchange(2, c, weighted_block(c), line_block(c))
        inc_copy(c).start()

    def inc_copy(c):
        return pltpu.make_async_copy(
            inc_v.at[:, part(c)], inc_h.at[:, part(c)], inc_sem.at[c]
        )

    def column_adjoint(c):
        lines_came(2, c)

        def keep(s, block):
            turned[c, s] = block

        level_pass(c, back, lines, keep, lambda chunk: range(chunk, CHUNKS))
        column_pass(c, turned, colf, True)
        local_r[c, g] = filtered[c, g]
        exchange(3, c, filtered_block(c), local_block(c))

    def grad_copy(c):
        return pltpu.make_async_copy(alpha_v.at[part(c)], grad_h.at[part(c)], grad_sem.at[c])

    def row_adjoint(c):
        local_came(3, c)

        @pl.when(lax.rem(c, PAIR) == 0)
        def _():
            adjoin_rows(c)

    def adjoin_rows(c):
        mask_lines(
            c,
            lambda n: jnp.concatenate(
                [
                    local_r[pl.ds(c, PAIR), 2 * n + j].reshape(PAIR * LINES, LANES)
                    for j in range(2)
                ],
                axis=1,
            ),
        )
        for n in range(TILES):
            side = tile_span(n)
            table = jnp.concatenate(
                [rowf[k, tile_span(d), side] for d in range(n, TILES) for k in range(CLASSES)],
                axis=0,
            )
            total = dot(masked[:, n * CLASSES * TILE :], table)
            alpha = alpha_v[levels(c), :, side].reshape(PAIR * LINES, TILE).astype(F32)
            alpha_v[levels(c), :, side] = (
                (alpha + total).astype(BF16).reshape(PAIR * PART, ROWS, TILE)
            )
        for j in range(PAIR):
            grad_copy(c + j).start()

    pl.semaphore_wait(barrier, GROUP + 3)
    for c in range(1, CHUNKS):
        alpha_load(c).start()

    def at(step, offset, stage):
        chunk = step - offset

        @pl.when(jnp.logical_and(chunk >= 0, chunk < CHUNKS))
        def _():
            stage(chunk)

    def forward(step):
        @pl.when(jnp.logical_and(step >= CHUNKS + 1, step < CHUNKS + 1 + CLASSES))
        def _():
            turn_rows(step - CHUNKS - 1)

        @pl.when(step == 4)
        def _():
            adjoint_tables()

        at(step, 4, sum_core)
        at(step, 6, finish)
        at(step, 7, gather_far)
        at(step, 5, sum_y)
        at(step, 1, row_filter)
        at(step, 4, sum_x)
        at(step, 7, weigh)

        @pl.when(step == 2)
        def _():
            column_tables()

        at(step, 2, column_filter)
        at(step, 6, gather_x)
        at(step, 4, add_x)

    loop(CHUNKS + 7, forward)

    def backward(step):
        at(step, 0, lambda c: column_adjoint(CHUNKS - 1 - c))
        at(step, 2, lambda c: row_adjoint(CHUNKS - 1 - c))

    loop(CHUNKS + 2, backward)

    for phase in range(4):
        exchange_left(phase)
    left(x_ss, core_r.at[pl.ds(0, 3)])
    left(yr_ss, y_s)
    left(give_ss, pert_v.at[:, pl.ds(0, LEVELS - 2)])
    for c in range(CHUNKS):
        inc_copy(c).wait()
        grad_copy(c).wait()


def on_device(alpha, pert, innov, weight, row_class, col_class, rowf, colf, level):
    any_spec = pl.BlockSpec(memory_space=pl.ANY)
    vmem_spec = pl.BlockSpec(memory_space=pltpu.VMEM)
    dma = pltpu.SemaphoreType.DMA
    block = (PART, ROWS, LANES)
    slab = (CHUNKS, GROUP) + block
    scratch = [
        pltpu.VMEM((LEVELS, ROWS, NX), BF16),
        pltpu.VMEM((2, LEVELS, ROWS, NX), BF16),
        pltpu.VMEM((2, LEVELS, ROWS, NX), BF16),
        pltpu.VMEM((CLASSES, NX, NX), BF16),
        pltpu.VMEM((CLASSES, NY, NY), BF16),
        pltpu.VMEM((CLASSES, NY, NY), BF16),
        pltpu.VMEM((LEVELS * ROWS, LEVELS * ROWS), BF16),
        pltpu.VMEM((LEVELS * ROWS, LEVELS * ROWS), BF16),
        pltpu.VMEM((CLASSES, LEVELS * ROWS, LANES), BF16),
        pltpu.VMEM((2, LEVELS, ROWS, LANES), BF16),
        pltpu.VMEM((PAIR * LINES, CLASSES * NX), BF16),
        pltpu.VMEM(slab, BF16),
        pltpu.VMEM(slab, BF16),
        pltpu.VMEM(slab, BF16),
        pltpu.VMEM(slab, BF16),
        pltpu.VMEM(slab, BF16),
        pltpu.VMEM(slab, BF16),
        pltpu.VMEM(slab, BF16),
        pltpu.VMEM(slab, BF16),
        pltpu.VMEM((CHUNKS, 2) + block, BF16),
        pltpu.VMEM((CHUNKS, 2, 2) + block, BF16),
        pltpu.VMEM((CHUNKS, 2) + block, BF16),
        pltpu.VMEM((CHUNKS, 2) + block, BF16),
        pltpu.VMEM((2,) + slab, BF16),
        pltpu.VMEM((2, LEVELS, ROWS, NX), BF16),
        dma((CHUNKS,)),
        dma((NX // TILE,)),
        dma((3,)),
        dma((CHUNKS,)),
        dma((CHUNKS,)),
        dma,
        dma((4,)),
        dma((4, CHUNKS)),
        dma((CHUNKS,)),
        dma((CHUNKS,)),
        dma,
        dma((CHUNKS,)),
        dma((CHUNKS,)),
        dma,
        dma((CHUNKS,)),
        dma,
        dma((CHUNKS,)),
        dma((CHUNKS,)),
        dma((CHUNKS,)),
    ]
    gradient, increment = pl.pallas_call(
        kernel,
        out_shape=(
            jax.ShapeDtypeStruct((LEVELS, ROWS, NX), BF16),
            jax.ShapeDtypeStruct((2, LEVELS, ROWS, NX), BF16),
        ),
        in_specs=[any_spec] * 3 + [vmem_spec] * 3 + [any_spec] * 2 + [vmem_spec],
        out_specs=(any_spec, any_spec),
        scratch_shapes=scratch,
        compiler_params=pltpu.CompilerParams(
            collective_id=0, has_side_effects=True, vmem_limit_bytes=62 * 1024 * 1024
        ),
    )(alpha[0], pert[0], innov, weight, row_class, col_class, rowf, colf, level)
    return gradient[None], increment


def solution(mesh):
    return jax.shard_map(
        on_device,
        mesh=mesh,
        in_specs=(
            P("member", None, "grid", None),
            P("member", None, None, "grid", None),
            P(None, None, "grid", None),
            P(None, None, "grid"),
            P(None, "grid"),
            P(None, "grid"),
            P(),
            P(),
            P(),
        ),
        out_specs=(P("member", None, "grid", None), P(None, None, "grid", None)),
        check_vma=False,
    )
```

```python
import functools

import jax
import jax.numpy as jnp
from jax import lax
from jax.experimental import pallas as pl
from jax.experimental.pallas import tpu as pltpu
from jax.sharding import PartitionSpec as P

MESH = pl.DeviceIdType.MESH
F32 = jnp.float32
BF16 = jnp.bfloat16

CLASSES = 3
LEVELS = 16
GROUP = 8
RING = 4
CHUNKS = 4
PIECES = 4
PART = LEVELS // CHUNKS
ROWS = 64
ROW_BITS = 6
LANES = 128
NX = GROUP * LANES
NY = GROUP * ROWS
LINES = PART * ROWS
PAIR = 2
TILE = 256
TILES = NX // TILE
WIDE = 2
DEEP = TILE // ROWS


def loop(count, body):
    def step(index, carry):
        body(index)
        return carry

    lax.fori_loop(0, count, step, 0)


def dot(a, b):
    return jnp.dot(a, b, preferred_element_type=F32)


def dot_nt(a, b):
    return lax.dot_general(a, b, (((1,), (1,)), ((), ())), preferred_element_type=F32)


def kernel(
    alpha_h, pert_h, innov_h, weight_ref, row_ref, col_ref, rowf_h, colf_h, level_ref,
    grad_h, inc_h,
    alpha_v, pert_v, innov_v, rowf, colf, colt, down, back, row_hot, weight_v, masked,
    slabs, lines, filtered, turned, local_s, local_r, core_s, core_r, x_in, x_got, y_s, y_r,
    inc, inc_v,
    alpha_sem, rowf_sem, load_sem, grad_sem, inc_sem, out_sem, a2a_ss, a2a_rs, core_ss, core_rs,
    x_ss, xin_rs, xgot_rs, yr_ss, yr_rs, give_ss, xa_rs, xf_rs, ca_rs,
):
    m = lax.axis_index("member")
    g = lax.axis_index("grid")
    y_hi = m // (2 * RING)
    x = lax.rem(m // 2, RING)
    core = lax.rem(m, 2)
    sibling = m + 1 - 2 * core
    across = m + 2 * RING - 4 * RING * y_hi

    def around(position, way, steps=1):
        return lax.rem(position + (steps if way == 0 else RING - steps), RING)

    def x_peer(way):
        return y_hi * (2 * RING) + around(x, way) * 2 + core

    def lane(s):
        return pl.ds(pl.multiple_of(s * LANES, LANES), LANES)

    def slab_rows(s):
        return pl.ds(pl.multiple_of(s * ROWS, ROWS), ROWS)

    def part(c):
        return pl.ds(c * PART, PART)

    barrier = pltpu.get_barrier_semaphore()

    def greet(partner):
        pl.semaphore_signal(barrier, inc=1, device_id=partner, device_id_type=MESH)

    loop(GROUP - 1, lambda step: greet((m, lax.rem(g + step + 1, GROUP))))
    for member in (x_peer(0), x_peer(1), sibling, across):
        greet((member, g))

    def alpha_load(c):
        return pltpu.make_async_copy(alpha_h.at[part(c)], alpha_v.at[part(c)], alpha_sem.at[c])

    def rowf_load(n):
        depth = (n // WIDE + 1) * WIDE * TILE
        where = (slice(None), slice(0, depth), slice(n * TILE, (n + 1) * TILE))
        return pltpu.make_async_copy(rowf_h.at[where], rowf.at[where], rowf_sem.at[n])

    alpha_load(0).start()
    for n in range(NX // TILE):
        rowf_load(n).start()
    loads = [
        pltpu.make_async_copy(src, dst, load_sem.at[i])
        for i, (src, dst) in enumerate(((colf_h, colf), (pert_h, pert_v), (innov_h, innov_v)))
    ]

    diagonal = lax.broadcasted_iota(jnp.int32, (ROWS, ROWS), 0) == lax.broadcasted_iota(
        jnp.int32, (ROWS, ROWS), 1
    )

    def upright(line):
        spread = jnp.where(diagonal, jnp.broadcast_to(line, (ROWS, ROWS)), 0.0)
        return jnp.broadcast_to(jnp.sum(spread, axis=1, keepdims=True), (ROWS, LANES))

    def row_table(z):
        column = upright(row_ref[pl.ds(z, 1), :].astype(F32))
        for c in range(CLASSES):
            row_hot[c, slab_rows(z), :] = jnp.where(column == c, 1.0, 0.0).astype(BF16)

    def tile_span(n):
        return slice(n * TILE, (n + 1) * TILE)

    def iota(shape, axis):
        return lax.broadcasted_iota(jnp.int32, shape, axis)

    def level_table(table, product):
        wide = (LEVELS, LEVELS * ROWS)
        spread = jnp.where(iota(wide, 0) == iota(wide, 1) >> ROW_BITS, 1.0, 0.0).astype(BF16)
        tall = (TILE, LEVELS * ROWS)
        same = (iota(tall, 0) & (ROWS - 1)) == (iota(tall, 1) & (ROWS - 1))
        level = level_ref[...]
        for b in range(LEVELS * ROWS // TILE):
            short = (TILE, LEVELS)
            spot = (iota(short, 0) >> ROW_BITS) + b * DEEP
            pick = jnp.where(spot == iota(short, 1), 1.0, 0.0).astype(BF16)
            table[b * TILE : (b + 1) * TILE, :] = jnp.where(
                same, dot(product(pick, level).astype(BF16), spread), 0.0
            ).astype(BF16)

    def column_tables():
        level_table(down, dot_nt)
        loads[0].wait()
        unit = jnp.where(iota((NY, NY), 0) == iota((NY, NY), 1), 1.0, 0.0).astype(BF16)

        def turn(c):
            colt[c] = dot_nt(unit, colf[c]).astype(BF16)

        loop(CLASSES, turn)

    def turn_rows(k):
        unit = jnp.where(iota((TILE, TILE), 0) == iota((TILE, TILE), 1), 1.0, 0.0).astype(BF16)
        for r in range(TILES):
            for d in range(r, TILES):
                rowf[k, tile_span(d), tile_span(r)] = dot_nt(
                    unit, rowf[k, tile_span(r), tile_span(d)]
                ).astype(BF16)

    def adjoint_tables():
        def weight_table(z):
            for t in range(2):
                weight_v[t, z] = upright(weight_ref[t, pl.ds(z, 1), :]).astype(BF16)

        loop(LEVELS, weight_table)
        level_table(back, dot)

    def remote(src, dst, ss, rs, member, group):
        return pltpu.make_async_remote_copy(
            src_ref=src, dst_ref=dst, send_sem=ss, recv_sem=rs,
            device_id=(member, group), device_id_type=MESH,
        )

    z_at = g // 2
    y_lo = lax.rem(g, 2)

    def send(phase, c, src, dst, peer):
        remote(src(peer), dst(g), a2a_ss.at[phase], a2a_rs.at[phase, c], m, peer).start()

    def peers():
        for up, side in ((2, 0), (1, 0), (3, 0), (2, 1), (1, 1), (3, 1), (0, 1)):
            yield lax.rem(z_at + up, RING) * 2 + (y_lo if side == 0 else 1 - y_lo)

    def exchange(phase, c, src, dst):
        for peer in peers():
            send(phase, c, src, dst, peer)

    def came(sem, view):
        remote(view, view, out_sem, sem, sibling, g).wait_recv()

    def left(sem, view):
        remote(view, view, sem, out_sem, sibling, g).wait_send()

    def lines_came(phase, c):
        came(a2a_rs.at[phase, c], lines.at[c, pl.ds(0, GROUP - 1)])

    def local_came(phase, c):
        came(a2a_rs.at[phase, c], local_r.at[c, pl.ds(0, GROUP - 1)])

    def exchange_left(phase):
        left(a2a_ss.at[phase], lines.at[:, pl.ds(0, GROUP - 1)])

    def line_block(c):
        return lambda s: lines.at[c, s]

    def filtered_block(c):
        return lambda s: filtered.at[c, s]

    def weighted_block(c):
        return lambda s: core_s.at[c, s]

    def slab_block(c):
        return lambda s: slabs.at[c, s]

    def local_block(c):
        return lambda s: local_r.at[c, s]

    def own_block(c):
        return lambda s: local_s.at[c, s]

    def mask_lines(c, source):
        span = pl.ds(pl.multiple_of(c * LINES, LINES), PAIR * LINES)
        hots = [row_hot[k, span, :] for k in range(CLASSES)]
        for n in range(TILES):
            tile = source(n)
            for k in range(CLASSES):
                at_lane = (n * CLASSES + k) * TILE
                masked[:, at_lane : at_lane + TILE] = tile * jnp.concatenate([hots[k]] * 2, axis=1)

    def levels(c):
        return pl.ds(c * PART, PAIR * PART)

    def row_filter(c):
        @pl.when(lax.rem(c, PAIR) == 0)
        def _():
            filter_rows(c)

        lines[c, g] = slabs[c, g]

        @pl.when(c > 0)
        def _():
            exchange(0, c, slab_block(c), line_block(c))

        @pl.when(c == 0)
        def _():
            for load in loads:
                load.start()

    def filter_rows(c):
        for j in range(PAIR):
            alpha_load(c + j).wait()
        loop(PAIR * PART, lambda z: row_table(c * PART + z))
        mask_lines(c, lambda n: alpha_v[levels(c), :, tile_span(n)].reshape(PAIR * LINES, TILE))
        for first in range(0, TILES, WIDE):
            last = first + WIDE

            @pl.when(c == 0)
            def _():
                for n in range(first, last):
                    rowf_load(n).wait()

            table = jnp.concatenate(
                [
                    rowf[k, tile_span(d), first * TILE : last * TILE]
                    for d in range(last)
                    for k in range(CLASSES)
                ],
                axis=0,
            )
            total = dot(masked[:, : last * CLASSES * TILE], table).astype(BF16)
            for j in range(2 * WIDE):
                s = 2 * first + j
                slabs[pl.ds(c, PAIR), s] = total[:, j * LANES : (j + 1) * LANES].reshape(
                    PAIR, PART, ROWS, LANES
                )

                @pl.when(jnp.logical_and(c == 0, g != s))
                def _():
                    send(0, c, slab_block(c), line_block(c), s)

    def column_pass(c, source, table, upper):
        whole = jnp.concatenate(
            [source[c, :, j].reshape(NY, LANES) for j in range(PART)], axis=1
        )
        kind = jnp.concatenate([col_ref[pl.ds(c * PART + j, 1), :] for j in range(PART)], axis=1)
        kind = jnp.broadcast_to(kind, (NY // 2, PART * LANES))

        def pick(products):
            return jnp.where(kind == 0, products[0], jnp.where(kind == 1, products[1], products[2]))

        def product(rows, deep):
            stacked = jnp.concatenate([table[k, rows, deep] for k in range(CLASSES)], axis=0)
            total = dot(stacked, whole[deep])
            count = total.shape[0] // CLASSES
            return [total[k * count : (k + 1) * count] for k in range(CLASSES)]

        half = NY // 2
        low = slice(0, half)
        high = slice(half, NY)
        both = slice(0, NY)
        wide = product(both, high if upper else low)
        narrow = product(low if upper else high, low if upper else high)
        first = pick([block[low] for block in wide])
        second = pick([block[high] for block in wide])
        if upper:
            first += pick(narrow)
        else:
            second += pick(narrow)
        for j in range(PART):
            side = slice(j * LANES, (j + 1) * LANES)
            for n, total in enumerate((first, second)):
                filtered[c, n * GROUP // 2 : (n + 1) * GROUP // 2, j] = (
                    total[:, side].astype(BF16).reshape(GROUP // 2, ROWS, LANES)
                )

    def level_pass(c, table, source, target, deep):
        for chunk in range(CHUNKS):

            @pl.when(c == chunk)
            def _(chunks=deep(chunk), rows=slice(chunk * LINES, (chunk + 1) * LINES)):
                held = slice(chunks[0], chunks[-1] + 1)
                span = slice(chunks[0] * LINES, (chunks[-1] + 1) * LINES)

                def some(i):
                    block = jnp.concatenate(
                        [source[held, 4 * i + j].reshape(-1, LANES) for j in range(4)], axis=1
                    )
                    total = dot(table[rows, span], block).astype(BF16)
                    for j in range(4):
                        target(
                            4 * i + j,
                            total[:, j * LANES : (j + 1) * LANES].reshape(PART, ROWS, LANES),
                        )

                loop(GROUP // 4, some)

    def column_filter(c):
        lines_came(0, c)
        column_pass(c, lines, colt, False)

        def keep(s, block):
            local_s[c, s] = block

            @pl.when(s != g)
            def _():
                send(1, c, own_block(c), local_block(c), s)

        level_pass(c, down, filtered, keep, lambda chunk: range(chunk + 1))
        local_r[c, g] = local_s[c, g]

    def core_copy(c, part_of):
        return remote(
            core_s.at[c, part_of], core_r.at[c, part_of], core_ss.at[c], core_rs.at[c], sibling, g
        )

    def xin_slab(way):
        return 2 * around(x, way, 2) + way

    def xone_slab(way):
        return 2 * around(x, way) + 1 - way

    def xtwo_slab(way):
        return 2 * around(x, way) + way

    def x_copy(src, dst, sem, way):
        return remote(src, dst, x_ss, sem, x_peer(way), g)

    def y_copy(c):
        return pltpu.make_async_remote_copy(
            src_ref=y_s.at[c],
            dst_ref=y_r.at[c],
            send_sem=yr_ss,
            recv_sem=yr_rs.at[c],
            device_id=(across, g),
            device_id_type=MESH,
        )

    def term(t, c, s):
        return pert_v[t, part(c), :, lane(s)] * local_r[c, s]

    def sum_core(c):
        local_came(1, c)

        @pl.when(c == 0)
        def _():
            loads[1].wait()
            loads[2].wait()

        def one(s):
            core_s[c, s] = term(1 - core, c, s)

        for first in range(0, GROUP, GROUP // 2):
            loop(GROUP // 2, lambda s: one(first + s))
            core_copy(c, pl.ds(first, GROUP // 2)).start()

    def sum_x(c):
        came(core_rs.at[c], core_r.at[c])

        def add(s):
            core_r[c, s] = term(core, c, s) + core_r[c, s]

        for way in range(2):
            s = xin_slab(way)
            add(s)
            x_copy(core_r.at[c, s], x_in.at[c, way], xin_rs.at[c], way).start()
        for way in range(2):
            s = xone_slab(way)
            add(s)
            x_copy(core_r.at[c, s], x_got.at[c, 0, way], xgot_rs.at[c], way).start()
        for way in range(2):
            add(xtwo_slab(way))
        for j in range(2):
            add(2 * x + j)

    def add_x(c):
        came(xin_rs.at[c], x_in.at[c])
        for way in range(2):
            slab = xtwo_slab(way)
            x_in[c, way] = x_in[c, way] + core_r[c, slab]
            x_copy(x_in.at[c, way], x_got.at[c, 1, way], xgot_rs.at[c], way).start()

    def sum_y(c):
        came(xgot_rs.at[c], x_got.at[c])
        for j in range(2):
            total = core_r[c, 2 * x + j].astype(F32) + x_got[c, 1, j].astype(F32)
            y_s[c, j] = (total + x_got[c, 0, 1 - j].astype(F32)).astype(BF16)
        y_copy(c).start()

    def give(rs, t, c, s, member):
        return remote(inc.at[t, c, s], inc.at[t, c, s], give_ss, rs, member, g)

    def give_core(c, owner):
        pair = inc.at[core, c, pl.ds(2 * owner, 2)]
        remote(pair, pair, give_ss, ca_rs.at[c], sibling, g).start()

    def finish(c):
        y_copy(c).wait_recv()
        for j in range(2):
            total = y_s[c, j].astype(F32) + y_r[c, j].astype(F32)
            inc[core, c, 2 * x + j] = total.astype(BF16)
        pair = inc.at[core, c, pl.ds(2 * x, 2)]
        for way in range(2):
            remote(pair, pair, give_ss, xa_rs.at[c], x_peer(way), g).start()
        give_core(c, x)

    def gather_x(c):
        came(xa_rs.at[c], inc.at[core, c, pl.ds(0, 4)])
        for way in range(2):
            slab = 2 * around(x, 1 - way) + way
            give(xf_rs.at[c], core, c, slab, x_peer(way)).start()
        for way in range(2):
            give_core(c, around(x, way))

    def gather_far(c):
        came(xf_rs.at[c], inc.at[core, c, pl.ds(0, 2)])
        give_core(c, around(x, 0, 2))

    def weigh(c):
        def one(s):
            total = None
            for t in range(2):
                block = inc[t, c, s]
                inc_v[t, part(c), :, lane(s)] = block
                misfit = weight_v[t, part(c)] * (block - innov_v[t, part(c), :, lane(s)])
                share = pert_v[t, part(c), :, lane(s)] * misfit
                total = share if total is None else total + share
            core_s[c, s] = total

        left(core_ss.at[c], core_s.at[c])
        came(ca_rs.at[c], inc.at[1 - core, c])
        for peer in peers():
            one(peer)
            send(2, c, weighted_block(c), line_block(c), peer)
        one(g)
        lines[c, g] = core_s[c, g]
        inc_copy(c).start()

    def inc_copy(c):
        return pltpu.make_async_copy(
            inc_v.at[:, part(c)], inc_h.at[:, part(c)], inc_sem.at[c]
        )

    def column_adjoint(c):
        lines_came(2, c)

        def keep(s, block):
            turned[c, s] = block

        level_pass(c, back, lines, keep, lambda chunk: range(chunk, CHUNKS))
        column_pass(c, turned, colf, True)
        local_r[c, g] = filtered[c, g]
        exchange(3, c, filtered_block(c), local_block(c))

    def grad_copy(c):
        return pltpu.make_async_copy(alpha_v.at[part(c)], grad_h.at[part(c)], grad_sem.at[c])

    def row_adjoint(c):
        local_came(3, c)

        @pl.when(lax.rem(c, PAIR) == 0)
        def _():
            adjoin_rows(c)

    def adjoin_rows(c):
        mask_lines(
            c,
            lambda n: jnp.concatenate(
                [
                    local_r[pl.ds(c, PAIR), 2 * n + j].reshape(PAIR * LINES, LANES)
                    for j in range(2)
                ],
                axis=1,
            ),
        )
        for n in range(TILES):
            side = tile_span(n)
            table = jnp.concatenate(
                [rowf[k, tile_span(d), side] for d in range(n, TILES) for k in range(CLASSES)],
                axis=0,
            )
            total = dot(masked[:, n * CLASSES * TILE :], table)
            alpha = alpha_v[levels(c), :, side].reshape(PAIR * LINES, TILE).astype(F32)
            alpha_v[levels(c), :, side] = (
                (alpha + total).astype(BF16).reshape(PAIR * PART, ROWS, TILE)
            )
        for j in range(PAIR):
            grad_copy(c + j).start()

    pl.semaphore_wait(barrier, GROUP + 3)
    for c in range(1, CHUNKS):
        alpha_load(c).start()

    def at(step, offset, stage):
        chunk = step - offset

        @pl.when(jnp.logical_and(chunk >= 0, chunk < CHUNKS))
        def _():
            stage(chunk)

    def forward(step):
        @pl.when(jnp.logical_and(step >= CHUNKS + 1, step < CHUNKS + 1 + CLASSES))
        def _():
            turn_rows(step - CHUNKS - 1)

        @pl.when(step == 4)
        def _():
            adjoint_tables()

        at(step, 4, sum_core)
        at(step, 6, finish)
        at(step, 7, gather_far)
        at(step, 5, sum_y)
        at(step, 1, row_filter)
        at(step, 4, sum_x)
        at(step, 7, weigh)

        @pl.when(step == 2)
        def _():
            column_tables()

        at(step, 2, column_filter)
        at(step, 6, gather_x)
        at(step, 4, add_x)

    loop(CHUNKS + 7, forward)

    def backward(step):
        at(step, 0, lambda c: column_adjoint(CHUNKS - 1 - c))
        at(step, 2, lambda c: row_adjoint(CHUNKS - 1 - c))

    loop(CHUNKS + 2, backward)

    for phase in range(4):
        exchange_left(phase)
    left(x_ss, core_r.at[pl.ds(0, 3)])
    left(yr_ss, y_s)
    left(give_ss, pert_v.at[:, pl.ds(0, LEVELS - 2)])
    for c in range(CHUNKS):
        inc_copy(c).wait()
        grad_copy(c).wait()


def hand_over(grad_in, inc_in, grad_out, inc_out, grad_v, inc_v, in_sem, out_sem):
    pieces = []
    for source, held, target in ((inc_in, inc_v, inc_out), (grad_in, grad_v, grad_out)):
        size = source.shape[0] // PIECES
        for i in range(PIECES):
            span = pl.ds(i * size, size)
            sems = in_sem.at[len(pieces)], out_sem.at[len(pieces)]
            pieces.append(
                (
                    pltpu.make_async_copy(source.at[span], held.at[span], sems[0]),
                    pltpu.make_async_copy(held.at[span], target.at[span], sems[1]),
                )
            )
    for take, _ in pieces:
        take.start()
    for take, put in pieces:
        take.wait()
        put.start()
    for _, put in pieces:
        put.wait()


def on_device(alpha, pert, innov, weight, row_class, col_class, rowf, colf, level):
    any_spec = pl.BlockSpec(memory_space=pl.ANY)
    vmem_spec = pl.BlockSpec(memory_space=pltpu.VMEM)
    dma = pltpu.SemaphoreType.DMA
    block = (PART, ROWS, LANES)
    slab = (CHUNKS, GROUP) + block
    scratch = [
        pltpu.VMEM((LEVELS, ROWS, NX), BF16),
        pltpu.VMEM((2, LEVELS, ROWS, NX), BF16),
        pltpu.VMEM((2, LEVELS, ROWS, NX), BF16),
        pltpu.VMEM((CLASSES, NX, NX), BF16),
        pltpu.VMEM((CLASSES, NY, NY), BF16),
        pltpu.VMEM((CLASSES, NY, NY), BF16),
        pltpu.VMEM((LEVELS * ROWS, LEVELS * ROWS), BF16),
        pltpu.VMEM((LEVELS * ROWS, LEVELS * ROWS), BF16),
        pltpu.VMEM((CLASSES, LEVELS * ROWS, LANES), BF16),
        pltpu.VMEM((2, LEVELS, ROWS, LANES), BF16),
        pltpu.VMEM((PAIR * LINES, CLASSES * NX), BF16),
        pltpu.VMEM(slab, BF16),
        pltpu.VMEM(slab, BF16),
        pltpu.VMEM(slab, BF16),
        pltpu.VMEM(slab, BF16),
        pltpu.VMEM(slab, BF16),
        pltpu.VMEM(slab, BF16),
        pltpu.VMEM(slab, BF16),
        pltpu.VMEM(slab, BF16),
        pltpu.VMEM((CHUNKS, 2) + block, BF16),
        pltpu.VMEM((CHUNKS, 2, 2) + block, BF16),
        pltpu.VMEM((CHUNKS, 2) + block, BF16),
        pltpu.VMEM((CHUNKS, 2) + block, BF16),
        pltpu.VMEM((2,) + slab, BF16),
        pltpu.VMEM((2, LEVELS, ROWS, NX), BF16),
        dma((CHUNKS,)),
        dma((NX // TILE,)),
        dma((3,)),
        dma((CHUNKS,)),
        dma((CHUNKS,)),
        dma,
        dma((4,)),
        dma((4, CHUNKS)),
        dma((CHUNKS,)),
        dma((CHUNKS,)),
        dma,
        dma((CHUNKS,)),
        dma((CHUNKS,)),
        dma,
        dma((CHUNKS,)),
        dma,
        dma((CHUNKS,)),
        dma((CHUNKS,)),
        dma((CHUNKS,)),
    ]
    gradient, increment = pl.pallas_call(
        kernel,
        out_shape=(
            jax.ShapeDtypeStruct((LEVELS, ROWS, NX), BF16),
            jax.ShapeDtypeStruct((2, LEVELS, ROWS, NX), BF16),
        ),
        in_specs=[any_spec] * 3 + [vmem_spec] * 3 + [any_spec] * 2 + [vmem_spec],
        out_specs=(any_spec, any_spec),
        scratch_shapes=scratch,
        compiler_params=pltpu.CompilerParams(
            collective_id=0, has_side_effects=True, vmem_limit_bytes=62 * 1024 * 1024
        ),
    )(alpha[0], pert[0], innov, weight, row_class, col_class, rowf, colf, level)
    shapes = (gradient.shape, (2 * LEVELS, ROWS, NX))
    gradient, increment = pl.pallas_call(
        hand_over,
        out_shape=tuple(jax.ShapeDtypeStruct(shape, BF16) for shape in shapes),
        in_specs=[any_spec] * 2,
        out_specs=(any_spec, any_spec),
        scratch_shapes=[pltpu.VMEM(shape, BF16) for shape in shapes]
        + [dma((2 * PIECES,)), dma((2 * PIECES,))],
        compiler_params=pltpu.CompilerParams(vmem_limit_bytes=62 * 1024 * 1024),
    )(gradient, increment.reshape(shapes[1]))
    return gradient[None], increment.reshape(2, LEVELS, ROWS, NX)


def solution(mesh):
    return jax.shard_map(
        on_device,
        mesh=mesh,
        in_specs=(
            P("member", None, "grid", None),
            P("member", None, None, "grid", None),
            P(None, None, "grid", None),
            P(None, None, "grid"),
            P(None, "grid"),
            P(None, "grid"),
            P(),
            P(),
            P(),
        ),
        out_specs=(P("member", None, "grid", None), P(None, None, "grid", None)),
        check_vma=False,
    )
```

```python
import functools

import jax
import jax.numpy as jnp
from jax import lax
from jax.experimental import pallas as pl
from jax.experimental.pallas import tpu as pltpu
from jax.sharding import PartitionSpec as P

MESH = pl.DeviceIdType.MESH
F32 = jnp.float32
BF16 = jnp.bfloat16

CLASSES = 3
LEVELS = 16
GROUP = 8
RING = 4
CHUNKS = 4
PART = LEVELS // CHUNKS
ROWS = 64
ROW_BITS = 6
LANES = 128
NX = GROUP * LANES
NY = GROUP * ROWS
LINES = PART * ROWS
PAIR = 2
TILE = 256
TILES = NX // TILE
WIDE = 2
DEEP = TILE // ROWS


def loop(count, body):
    def step(index, carry):
        body(index)
        return carry

    lax.fori_loop(0, count, step, 0)


def dot(a, b):
    return jnp.dot(a, b, preferred_element_type=F32)


def dot_nt(a, b):
    return lax.dot_general(a, b, (((1,), (1,)), ((), ())), preferred_element_type=F32)


def kernel(
    alpha_h, pert_h, innov_h, weight_ref, row_ref, col_ref, rowf_h, colf_h, level_ref,
    gradient, increment,
    alpha_v, pert_v, innov_v, rowf, colf, colt, down, back, row_hot, weight_v, masked,
    slabs, lines, filtered, local_s, local_r, core_s, core_r, x_in, x_got, y_s, y_r, inc,
    alpha_sem, rowf_sem, load_sem, out_sem, a2a_ss, a2a_rs, core_ss, core_rs,
    x_ss, xin_rs, xgot_rs, yr_ss, yr_rs, give_ss, xa_rs, xf_rs, ca_rs,
):
    m = lax.axis_index("member")
    g = lax.axis_index("grid")
    y_hi = m // (2 * RING)
    x = lax.rem(m // 2, RING)
    core = lax.rem(m, 2)
    sibling = m + 1 - 2 * core
    across = m + 2 * RING - 4 * RING * y_hi

    def around(position, way, steps=1):
        return lax.rem(position + (steps if way == 0 else RING - steps), RING)

    def x_peer(way):
        return y_hi * (2 * RING) + around(x, way) * 2 + core

    def lane(s):
        return pl.ds(pl.multiple_of(s * LANES, LANES), LANES)

    def slab_rows(s):
        return pl.ds(pl.multiple_of(s * ROWS, ROWS), ROWS)

    def part(c):
        return pl.ds(c * PART, PART)

    barrier = pltpu.get_barrier_semaphore()

    def greet(partner):
        pl.semaphore_signal(barrier, inc=1, device_id=partner, device_id_type=MESH)

    loop(GROUP - 1, lambda step: greet((m, lax.rem(g + step + 1, GROUP))))
    for member in (x_peer(0), x_peer(1), sibling, across):
        greet((member, g))

    def alpha_load(c):
        return pltpu.make_async_copy(alpha_h.at[part(c)], alpha_v.at[part(c)], alpha_sem.at[c])

    def rowf_load(n):
        depth = (n // WIDE + 1) * WIDE * TILE
        where = (slice(None), slice(0, depth), slice(n * TILE, (n + 1) * TILE))
        return pltpu.make_async_copy(rowf_h.at[where], rowf.at[where], rowf_sem.at[n])

    alpha_load(0).start()
    for n in range(NX // TILE):
        rowf_load(n).start()
    loads = [
        pltpu.make_async_copy(src, dst, load_sem.at[i])
        for i, (src, dst) in enumerate(((colf_h, colf), (pert_h, pert_v), (innov_h, innov_v)))
    ]

    diagonal = lax.broadcasted_iota(jnp.int32, (ROWS, ROWS), 0) == lax.broadcasted_iota(
        jnp.int32, (ROWS, ROWS), 1
    )

    def upright(line):
        spread = jnp.where(diagonal, jnp.broadcast_to(line, (ROWS, ROWS)), 0.0)
        return jnp.broadcast_to(jnp.sum(spread, axis=1, keepdims=True), (ROWS, LANES))

    def row_table(z):
        column = upright(row_ref[pl.ds(z, 1), :].astype(F32))
        for c in range(CLASSES):
            row_hot[c, slab_rows(z), :] = jnp.where(column == c, 1.0, 0.0).astype(BF16)

    def tile_span(n):
        return slice(n * TILE, (n + 1) * TILE)

    def iota(shape, axis):
        return lax.broadcasted_iota(jnp.int32, shape, axis)

    def level_table(table, product):
        wide = (LEVELS, LEVELS * ROWS)
        spread = jnp.where(iota(wide, 0) == iota(wide, 1) >> ROW_BITS, 1.0, 0.0).astype(BF16)
        tall = (TILE, LEVELS * ROWS)
        same = (iota(tall, 0) & (ROWS - 1)) == (iota(tall, 1) & (ROWS - 1))
        level = level_ref[...]
        for b in range(LEVELS * ROWS // TILE):
            short = (TILE, LEVELS)
            spot = (iota(short, 0) >> ROW_BITS) + b * DEEP
            pick = jnp.where(spot == iota(short, 1), 1.0, 0.0).astype(BF16)
            table[b * TILE : (b + 1) * TILE, :] = jnp.where(
                same, dot(product(pick, level).astype(BF16), spread), 0.0
            ).astype(BF16)

    def column_tables():
        level_table(down, dot_nt)
        loads[0].wait()
        unit = jnp.where(iota((NY, NY), 0) == iota((NY, NY), 1), 1.0, 0.0).astype(BF16)

        def turn(c):
            colt[c] = dot_nt(unit, colf[c]).astype(BF16)

        loop(CLASSES, turn)

    def turn_rows(k):
        unit = jnp.where(iota((TILE, TILE), 0) == iota((TILE, TILE), 1), 1.0, 0.0).astype(BF16)
        for r in range(TILES):
            for d in range(r, TILES):
                rowf[k, tile_span(d), tile_span(r)] = dot_nt(
                    unit, rowf[k, tile_span(r), tile_span(d)]
                ).astype(BF16)

    def adjoint_tables():
        def weight_table(z):
            for t in range(2):
                weight_v[t, z] = upright(weight_ref[t, pl.ds(z, 1), :]).astype(BF16)

        loop(LEVELS, weight_table)
        level_table(back, dot)

    def remote(src, dst, ss, rs, member, group):
        return pltpu.make_async_remote_copy(
            src_ref=src, dst_ref=dst, send_sem=ss, recv_sem=rs,
            device_id=(member, group), device_id_type=MESH,
        )

    z_at = g // 2
    y_lo = lax.rem(g, 2)

    def send(phase, c, src, dst, peer):
        remote(src(peer), dst(g), a2a_ss.at[phase], a2a_rs.at[phase, c], m, peer).start()

    def peers():
        for up, side in ((2, 0), (1, 0), (3, 0), (2, 1), (1, 1), (3, 1), (0, 1)):
            yield lax.rem(z_at + up, RING) * 2 + (y_lo if side == 0 else 1 - y_lo)

    def exchange(phase, c, src, dst):
        for peer in peers():
            send(phase, c, src, dst, peer)

    def came(sem, view):
        remote(view, view, out_sem, sem, sibling, g).wait_recv()

    def left(sem, view):
        remote(view, view, sem, out_sem, sibling, g).wait_send()

    def lines_came(phase, c):
        came(a2a_rs.at[phase, c], lines.at[c, pl.ds(0, GROUP - 1)])

    def local_came(phase, c):
        came(a2a_rs.at[phase, c], local_r.at[c, pl.ds(0, GROUP - 1)])

    def exchange_left(phase):
        left(a2a_ss.at[phase], lines.at[:, pl.ds(0, GROUP - 1)])

    def line_block(c):
        return lambda s: lines.at[c, s]

    def filtered_block(c):
        return lambda s: filtered.at[c, s]

    def weighted_block(c):
        return lambda s: core_s.at[c, s]

    def slab_block(c):
        return lambda s: slabs.at[c, s]

    def local_block(c):
        return lambda s: local_r.at[c, s]

    def own_block(c):
        return lambda s: local_s.at[c, s]

    def mask_lines(c, source):
        span = pl.ds(pl.multiple_of(c * LINES, LINES), PAIR * LINES)
        hots = [row_hot[k, span, :] for k in range(CLASSES)]
        for n in range(TILES):
            tile = source(n)
            for k in range(CLASSES):
                at_lane = (n * CLASSES + k) * TILE
                masked[:, at_lane : at_lane + TILE] = tile * jnp.concatenate([hots[k]] * 2, axis=1)

    def levels(c):
        return pl.ds(c * PART, PAIR * PART)

    def row_filter(c):
        @pl.when(lax.rem(c, PAIR) == 0)
        def _():
            filter_rows(c)

        lines[c, g] = slabs[c, g]

        @pl.when(c > 0)
        def _():
            exchange(0, c, slab_block(c), line_block(c))

        @pl.when(c == 0)
        def _():
            for load in loads:
                load.start()

    def filter_rows(c):
        for j in range(PAIR):
            alpha_load(c + j).wait()
        loop(PAIR * PART, lambda z: row_table(c * PART + z))
        mask_lines(c, lambda n: alpha_v[levels(c), :, tile_span(n)].reshape(PAIR * LINES, TILE))
        for first in range(0, TILES, WIDE):
            last = first + WIDE

            @pl.when(c == 0)
            def _():
                for n in range(first, last):
                    rowf_load(n).wait()

            table = jnp.concatenate(
                [
                    rowf[k, tile_span(d), first * TILE : last * TILE]
                    for d in range(last)
                    for k in range(CLASSES)
                ],
                axis=0,
            )
            total = dot(masked[:, : last * CLASSES * TILE], table).astype(BF16)
            for j in range(2 * WIDE):
                s = 2 * first + j
                slabs[pl.ds(c, PAIR), s] = total[:, j * LANES : (j + 1) * LANES].reshape(
                    PAIR, PART, ROWS, LANES
                )

                @pl.when(jnp.logical_and(c == 0, g != s))
                def _():
                    send(0, c, slab_block(c), line_block(c), s)

    def column_pass(c, source, table, upper):
        whole = jnp.concatenate(
            [source[c, :, j].reshape(NY, LANES) for j in range(PART)], axis=1
        )
        kind = jnp.concatenate([col_ref[pl.ds(c * PART + j, 1), :] for j in range(PART)], axis=1)
        kind = jnp.broadcast_to(kind, (NY // 2, PART * LANES))

        def pick(products):
            return jnp.where(kind == 0, products[0], jnp.where(kind == 1, products[1], products[2]))

        def product(rows, deep):
            stacked = jnp.concatenate([table[k, rows, deep] for k in range(CLASSES)], axis=0)
            total = dot(stacked, whole[deep])
            count = total.shape[0] // CLASSES
            return [total[k * count : (k + 1) * count] for k in range(CLASSES)]

        half = NY // 2
        low = slice(0, half)
        high = slice(half, NY)
        both = slice(0, NY)
        wide = product(both, high if upper else low)
        narrow = product(low if upper else high, low if upper else high)
        first = pick([block[low] for block in wide])
        second = pick([block[high] for block in wide])
        if upper:
            first += pick(narrow)
        else:
            second += pick(narrow)
        for j in range(PART):
            side = slice(j * LANES, (j + 1) * LANES)
            for n, total in enumerate((first, second)):
                filtered[c, n * GROUP // 2 : (n + 1) * GROUP // 2, j] = (
                    total[:, side].astype(BF16).reshape(GROUP // 2, ROWS, LANES)
                )

    def level_pass(c, table, source, target, deep):
        for chunk in range(CHUNKS):

            @pl.when(c == chunk)
            def _(chunks=deep(chunk), rows=slice(chunk * LINES, (chunk + 1) * LINES)):
                held = slice(chunks[0], chunks[-1] + 1)
                span = slice(chunks[0] * LINES, (chunks[-1] + 1) * LINES)

                def some(i):
                    block = jnp.concatenate(
                        [source[held, 4 * i + j].reshape(-1, LANES) for j in range(4)], axis=1
                    )
                    total = dot(table[rows, span], block).astype(BF16)
                    for j in range(4):
                        target(
                            4 * i + j,
                            total[:, j * LANES : (j + 1) * LANES].reshape(PART, ROWS, LANES),
                        )

                loop(GROUP // 4, some)

    def column_filter(c):
        lines_came(0, c)
        column_pass(c, lines, colt, False)

        def keep(s, block):
            local_s[c, s] = block

            @pl.when(s != g)
            def _():
                send(1, c, own_block(c), local_block(c), s)

        level_pass(c, down, filtered, keep, lambda chunk: range(chunk + 1))
        local_r[c, g] = local_s[c, g]

    def core_copy(c, part_of):
        return remote(
            core_s.at[c, part_of], core_r.at[c, part_of], core_ss.at[c], core_rs.at[c], sibling, g
        )

    def xin_slab(way):
        return 2 * around(x, way, 2) + way

    def xone_slab(way):
        return 2 * around(x, way) + 1 - way

    def xtwo_slab(way):
        return 2 * around(x, way) + way

    def x_copy(src, dst, sem, way):
        return remote(src, dst, x_ss, sem, x_peer(way), g)

    def y_copy(c):
        return pltpu.make_async_remote_copy(
            src_ref=y_s.at[c],
            dst_ref=y_r.at[c],
            send_sem=yr_ss,
            recv_sem=yr_rs.at[c],
            device_id=(across, g),
            device_id_type=MESH,
        )

    def term(t, c, s):
        return pert_v[t, part(c), :, lane(s)] * local_r[c, s]

    def sum_core(c):
        local_came(1, c)

        @pl.when(c == 0)
        def _():
            loads[1].wait()
            loads[2].wait()

        def one(s):
            core_s[c, s] = term(1 - core, c, s)

        for first in range(0, GROUP, GROUP // 2):
            loop(GROUP // 2, lambda s: one(first + s))
            core_copy(c, pl.ds(first, GROUP // 2)).start()

    def sum_x(c):
        came(core_rs.at[c], core_r.at[c])

        def add(s):
            core_r[c, s] = term(core, c, s) + core_r[c, s]

        for way in range(2):
            s = xin_slab(way)
            add(s)
            x_copy(core_r.at[c, s], x_in.at[c, way], xin_rs.at[c], way).start()
        for way in range(2):
            s = xone_slab(way)
            add(s)
            x_copy(core_r.at[c, s], x_got.at[c, 0, way], xgot_rs.at[c], way).start()
        for way in range(2):
            add(xtwo_slab(way))
        for j in range(2):
            add(2 * x + j)

    def add_x(c):
        came(xin_rs.at[c], x_in.at[c])
        for way in range(2):
            slab = xtwo_slab(way)
            x_in[c, way] = x_in[c, way] + core_r[c, slab]
            x_copy(x_in.at[c, way], x_got.at[c, 1, way], xgot_rs.at[c], way).start()

    def sum_y(c):
        came(xgot_rs.at[c], x_got.at[c])
        for j in range(2):
            total = core_r[c, 2 * x + j].astype(F32) + x_got[c, 1, j].astype(F32)
            y_s[c, j] = (total + x_got[c, 0, 1 - j].astype(F32)).astype(BF16)
        y_copy(c).start()

    def give(rs, t, c, s, member):
        return remote(inc.at[t, c, s], inc.at[t, c, s], give_ss, rs, member, g)

    def give_core(c, owner):
        pair = inc.at[core, c, pl.ds(2 * owner, 2)]
        remote(pair, pair, give_ss, ca_rs.at[c], sibling, g).start()

    def finish(c):
        y_copy(c).wait_recv()
        for j in range(2):
            total = y_s[c, j].astype(F32) + y_r[c, j].astype(F32)
            inc[core, c, 2 * x + j] = total.astype(BF16)
        pair = inc.at[core, c, pl.ds(2 * x, 2)]
        for way in range(2):
            remote(pair, pair, give_ss, xa_rs.at[c], x_peer(way), g).start()
        give_core(c, x)

    def gather_x(c):
        came(xa_rs.at[c], inc.at[core, c, pl.ds(0, 4)])
        for way in range(2):
            slab = 2 * around(x, 1 - way) + way
            give(xf_rs.at[c], core, c, slab, x_peer(way)).start()
        for way in range(2):
            give_core(c, around(x, way))

    def gather_far(c):
        came(xf_rs.at[c], inc.at[core, c, pl.ds(0, 2)])
        give_core(c, around(x, 0, 2))

    def weigh(c):
        def one(s):
            total = None
            for t in range(2):
                block = inc[t, c, s]
                misfit = weight_v[t, part(c)] * (block - innov_v[t, part(c), :, lane(s)])
                increment[t, part(c), :, lane(s)] = block
                share = pert_v[t, part(c), :, lane(s)] * misfit
                total = share if total is None else total + share
            core_s[c, s] = total

        left(core_ss.at[c], core_s.at[c])
        came(ca_rs.at[c], inc.at[1 - core, c])
        for peer in peers():
            one(peer)
            send(2, c, weighted_block(c), line_block(c), peer)
        one(g)
        lines[c, g] = core_s[c, g]

    def column_adjoint(c):
        lines_came(2, c)

        def keep(s, block):
            local_s[c, s] = block

        level_pass(c, back, lines, keep, lambda chunk: range(chunk, CHUNKS))
        column_pass(c, local_s, colf, True)
        local_r[c, g] = filtered[c, g]
        exchange(3, c, filtered_block(c), local_block(c))

    def row_adjoint(c):
        local_came(3, c)

        @pl.when(lax.rem(c, PAIR) == 0)
        def _():
            adjoin_rows(c)

    def adjoin_rows(c):
        mask_lines(
            c,
            lambda n: jnp.concatenate(
                [
                    local_r[pl.ds(c, PAIR), 2 * n + j].reshape(PAIR * LINES, LANES)
                    for j in range(2)
                ],
                axis=1,
            ),
        )
        for n in range(TILES):
            side = tile_span(n)
            table = jnp.concatenate(
                [rowf[k, tile_span(d), side] for d in range(n, TILES) for k in range(CLASSES)],
                axis=0,
            )
            total = dot(masked[:, n * CLASSES * TILE :], table)
            alpha = alpha_v[levels(c), :, side].reshape(PAIR * LINES, TILE).astype(F32)
            gradient[levels(c), :, side] = (
                (alpha + total).astype(BF16).reshape(PAIR * PART, ROWS, TILE)
            )


    pl.semaphore_wait(barrier, GROUP + 3)
    for c in range(1, CHUNKS):
        alpha_load(c).start()

    def at(step, offset, stage):
        chunk = step - offset

        @pl.when(jnp.logical_and(chunk >= 0, chunk < CHUNKS))
        def _():
            stage(chunk)

    def forward(step):
        @pl.when(jnp.logical_and(step >= CHUNKS + 1, step < CHUNKS + 1 + CLASSES))
        def _():
            turn_rows(step - CHUNKS - 1)

        @pl.when(step == 4)
        def _():
            adjoint_tables()

        at(step, 4, sum_core)
        at(step, 6, finish)
        at(step, 7, gather_far)
        at(step, 5, sum_y)
        at(step, 1, row_filter)
        at(step, 4, sum_x)
        at(step, 7, weigh)

        @pl.when(step == 2)
        def _():
            column_tables()

        at(step, 2, column_filter)
        at(step, 6, gather_x)
        at(step, 4, add_x)

    loop(CHUNKS + 7, forward)

    exchange_left(1)

    def backward(step):
        at(step, 0, lambda c: column_adjoint(CHUNKS - 1 - c))
        at(step, 2, lambda c: row_adjoint(CHUNKS - 1 - c))

    loop(CHUNKS + 2, backward)

    for phase in (0, 2, 3):
        exchange_left(phase)
    left(x_ss, core_r.at[pl.ds(0, 3)])
    left(yr_ss, y_s)
    left(give_ss, pert_v.at[:, pl.ds(0, LEVELS - 2)])


def on_device(alpha, pert, innov, weight, row_class, col_class, rowf, colf, level):
    any_spec = pl.BlockSpec(memory_space=pl.ANY)
    vmem_spec = pl.BlockSpec(memory_space=pltpu.VMEM)
    dma = pltpu.SemaphoreType.DMA
    block = (PART, ROWS, LANES)
    slab = (CHUNKS, GROUP) + block
    scratch = [
        pltpu.VMEM((LEVELS, ROWS, NX), BF16),
        pltpu.VMEM((2, LEVELS, ROWS, NX), BF16),
        pltpu.VMEM((2, LEVELS, ROWS, NX), BF16),
        pltpu.VMEM((CLASSES, NX, NX), BF16),
        pltpu.VMEM((CLASSES, NY, NY), BF16),
        pltpu.VMEM((CLASSES, NY, NY), BF16),
        pltpu.VMEM((LEVELS * ROWS, LEVELS * ROWS), BF16),
        pltpu.VMEM((LEVELS * ROWS, LEVELS * ROWS), BF16),
        pltpu.VMEM((CLASSES, LEVELS * ROWS, LANES), BF16),
        pltpu.VMEM((2, LEVELS, ROWS, LANES), BF16),
        pltpu.VMEM((PAIR * LINES, CLASSES * NX), BF16),
        pltpu.VMEM(slab, BF16),
        pltpu.VMEM(slab, BF16),
        pltpu.VMEM(slab, BF16),
        pltpu.VMEM(slab, BF16),
        pltpu.VMEM(slab, BF16),
        pltpu.VMEM(slab, BF16),
        pltpu.VMEM(slab, BF16),
        pltpu.VMEM((CHUNKS, 2) + block, BF16),
        pltpu.VMEM((CHUNKS, 2, 2) + block, BF16),
        pltpu.VMEM((CHUNKS, 2) + block, BF16),
        pltpu.VMEM((CHUNKS, 2) + block, BF16),
        pltpu.VMEM((2,) + slab, BF16),
        dma((CHUNKS,)),
        dma((NX // TILE,)),
        dma((3,)),
        dma,
        dma((4,)),
        dma((4, CHUNKS)),
        dma((CHUNKS,)),
        dma((CHUNKS,)),
        dma,
        dma((CHUNKS,)),
        dma((CHUNKS,)),
        dma,
        dma((CHUNKS,)),
        dma,
        dma((CHUNKS,)),
        dma((CHUNKS,)),
        dma((CHUNKS,)),
    ]
    gradient, increment = pl.pallas_call(
        kernel,
        out_shape=(
            pltpu.VMEM((LEVELS, ROWS, NX), BF16),
            pltpu.VMEM((2, LEVELS, ROWS, NX), BF16),
        ),
        in_specs=[any_spec] * 3 + [vmem_spec] * 3 + [any_spec] * 2 + [vmem_spec],
        out_specs=(vmem_spec, vmem_spec),
        scratch_shapes=scratch,
        compiler_params=pltpu.CompilerParams(
            collective_id=0, has_side_effects=True, vmem_limit_bytes=56 * 1024 * 1024
        ),
    )(alpha[0], pert[0], innov, weight, row_class, col_class, rowf, colf, level)
    return gradient[None], increment


def solution(mesh):
    return jax.shard_map(
        on_device,
        mesh=mesh,
        in_specs=(
            P("member", None, "grid", None),
            P("member", None, None, "grid", None),
            P(None, None, "grid", None),
            P(None, None, "grid"),
            P(None, "grid"),
            P(None, "grid"),
            P(),
            P(),
            P(),
        ),
        out_specs=(P("member", None, "grid", None), P(None, None, "grid", None)),
        check_vma=False,
    )
```

```python
import functools

import jax
import jax.numpy as jnp
from jax import lax
from jax.experimental import pallas as pl
from jax.experimental.pallas import tpu as pltpu
from jax.sharding import PartitionSpec as P

MESH = pl.DeviceIdType.MESH
F32 = jnp.float32
BF16 = jnp.bfloat16

CLASSES = 3
LEVELS = 16
GROUP = 8
RING = 4
CHUNKS = 4
PART = LEVELS // CHUNKS
ROWS = 64
ROW_BITS = 6
LANES = 128
NX = GROUP * LANES
NY = GROUP * ROWS
LINES = PART * ROWS
PAIR = 2
TILE = 256
TILES = NX // TILE
WIDE = 2
DEEP = TILE // ROWS


def loop(count, body):
    def step(index, carry):
        body(index)
        return carry

    lax.fori_loop(0, count, step, 0)


def dot(a, b):
    return jnp.dot(a, b, preferred_element_type=F32)


def dot_nt(a, b):
    return lax.dot_general(a, b, (((1,), (1,)), ((), ())), preferred_element_type=F32)


def kernel(
    alpha_h, pert_h, innov_h, weight_ref, row_ref, col_ref, rowf_h, colf_h, level_ref,
    gradient, increment,
    alpha_v, pert_v, innov_v, rowf, colf, colt, down, back, row_hot, weight_v, masked,
    slabs, lines, filtered, local_s, local_r, core_s, core_r, x_in, x_got, y_s, y_r, inc,
    alpha_sem, rowf_sem, load_sem, out_sem, a2a_ss, a2a_rs, core_ss, core_rs,
    x_ss, xin_rs, xgot_rs, yr_ss, yr_rs, give_ss, xa_rs, xf_rs, ca_rs,
):
    m = lax.axis_index("member")
    g = lax.axis_index("grid")
    y_hi = m // (2 * RING)
    x = lax.rem(m // 2, RING)
    core = lax.rem(m, 2)
    sibling = m + 1 - 2 * core
    across = m + 2 * RING - 4 * RING * y_hi

    def around(position, way, steps=1):
        return lax.rem(position + (steps if way == 0 else RING - steps), RING)

    def x_peer(way):
        return y_hi * (2 * RING) + around(x, way) * 2 + core

    def lane(s):
        return pl.ds(pl.multiple_of(s * LANES, LANES), LANES)

    def slab_rows(s):
        return pl.ds(pl.multiple_of(s * ROWS, ROWS), ROWS)

    def part(c):
        return pl.ds(c * PART, PART)

    barrier = pltpu.get_barrier_semaphore()

    def greet(partner):
        pl.semaphore_signal(barrier, inc=1, device_id=partner, device_id_type=MESH)

    loop(GROUP - 1, lambda step: greet((m, lax.rem(g + step + 1, GROUP))))
    for member in (x_peer(0), x_peer(1), sibling, across):
        greet((member, g))

    def alpha_load(c):
        return pltpu.make_async_copy(alpha_h.at[part(c)], alpha_v.at[part(c)], alpha_sem.at[c])

    def rowf_load(n):
        depth = (n // WIDE + 1) * WIDE * TILE
        where = (slice(None), slice(0, depth), slice(n * TILE, (n + 1) * TILE))
        return pltpu.make_async_copy(rowf_h.at[where], rowf.at[where], rowf_sem.at[n])

    alpha_load(0).start()
    for n in range(NX // TILE):
        rowf_load(n).start()
    loads = [
        pltpu.make_async_copy(src, dst, load_sem.at[i])
        for i, (src, dst) in enumerate(((colf_h, colf), (pert_h, pert_v), (innov_h, innov_v)))
    ]

    diagonal = lax.broadcasted_iota(jnp.int32, (ROWS, ROWS), 0) == lax.broadcasted_iota(
        jnp.int32, (ROWS, ROWS), 1
    )

    def upright(line):
        spread = jnp.where(diagonal, jnp.broadcast_to(line, (ROWS, ROWS)), 0.0)
        return jnp.broadcast_to(jnp.sum(spread, axis=1, keepdims=True), (ROWS, LANES))

    def row_table(z):
        column = upright(row_ref[pl.ds(z, 1), :].astype(F32))
        for c in range(CLASSES):
            row_hot[c, slab_rows(z), :] = jnp.where(column == c, 1.0, 0.0).astype(BF16)

    def tile_span(n):
        return slice(n * TILE, (n + 1) * TILE)

    def iota(shape, axis):
        return lax.broadcasted_iota(jnp.int32, shape, axis)

    def level_table(table, product):
        wide = (LEVELS, LEVELS * ROWS)
        spread = jnp.where(iota(wide, 0) == iota(wide, 1) >> ROW_BITS, 1.0, 0.0).astype(BF16)
        tall = (TILE, LEVELS * ROWS)
        same = (iota(tall, 0) & (ROWS - 1)) == (iota(tall, 1) & (ROWS - 1))
        level = level_ref[...]
        for b in range(LEVELS * ROWS // TILE):
            short = (TILE, LEVELS)
            spot = (iota(short, 0) >> ROW_BITS) + b * DEEP
            pick = jnp.where(spot == iota(short, 1), 1.0, 0.0).astype(BF16)
            table[b * TILE : (b + 1) * TILE, :] = jnp.where(
                same, dot(product(pick, level).astype(BF16), spread), 0.0
            ).astype(BF16)

    def column_tables():
        level_table(down, dot_nt)
        loads[0].wait()
        unit = jnp.where(iota((NY, NY), 0) == iota((NY, NY), 1), 1.0, 0.0).astype(BF16)

        def turn(c):
            colt[c] = dot_nt(unit, colf[c]).astype(BF16)

        loop(CLASSES, turn)

    def turn_rows(k):
        unit = jnp.where(iota((TILE, TILE), 0) == iota((TILE, TILE), 1), 1.0, 0.0).astype(BF16)
        for r in range(TILES):
            for d in range(r, TILES):
                rowf[k, tile_span(d), tile_span(r)] = dot_nt(
                    unit, rowf[k, tile_span(r), tile_span(d)]
                ).astype(BF16)

    def adjoint_tables():
        def weight_table(z):
            for t in range(2):
                weight_v[t, z] = upright(weight_ref[t, pl.ds(z, 1), :]).astype(BF16)

        loop(LEVELS, weight_table)
        level_table(back, dot)

    def remote(src, dst, ss, rs, member, group):
        return pltpu.make_async_remote_copy(
            src_ref=src, dst_ref=dst, send_sem=ss, recv_sem=rs,
            device_id=(member, group), device_id_type=MESH,
        )

    z_at = g // 2
    y_lo = lax.rem(g, 2)

    def send(phase, c, src, dst, peer):
        remote(src(peer), dst(g), a2a_ss.at[phase], a2a_rs.at[phase, c], m, peer).start()

    def peers():
        for up, side in ((2, 0), (1, 0), (3, 0), (2, 1), (1, 1), (3, 1), (0, 1)):
            yield lax.rem(z_at + up, RING) * 2 + (y_lo if side == 0 else 1 - y_lo)

    def exchange(phase, c, src, dst):
        for peer in peers():
            send(phase, c, src, dst, peer)

    def came(sem, view):
        remote(view, view, out_sem, sem, sibling, g).wait_recv()

    def left(sem, view):
        remote(view, view, sem, out_sem, sibling, g).wait_send()

    def lines_came(phase, c):
        came(a2a_rs.at[phase, c], lines.at[c, pl.ds(0, GROUP - 1)])

    def local_came(phase, c):
        came(a2a_rs.at[phase, c], local_r.at[c, pl.ds(0, GROUP - 1)])

    def exchange_left(phase):
        left(a2a_ss.at[phase], lines.at[:, pl.ds(0, GROUP - 1)])

    def line_block(c):
        return lambda s: lines.at[c, s]

    def filtered_block(c):
        return lambda s: filtered.at[c, s]

    def weighted_block(c):
        return lambda s: core_s.at[c, s]

    def slab_block(c):
        return lambda s: slabs.at[c, s]

    def local_block(c):
        return lambda s: local_r.at[c, s]

    def own_block(c):
        return lambda s: local_s.at[c, s]

    def mask_lines(c, source):
        span = pl.ds(pl.multiple_of(c * LINES, LINES), PAIR * LINES)
        hots = [row_hot[k, span, :] for k in range(CLASSES)]
        for n in range(TILES):
            tile = source(n)
            for k in range(CLASSES):
                at_lane = (n * CLASSES + k) * TILE
                masked[:, at_lane : at_lane + TILE] = tile * jnp.concatenate([hots[k]] * 2, axis=1)

    def levels(c):
        return pl.ds(c * PART, PAIR * PART)

    def row_filter(c):
        @pl.when(lax.rem(c, PAIR) == 0)
        def _():
            filter_rows(c)

        lines[c, g] = slabs[c, g]

        @pl.when(c > 0)
        def _():
            exchange(0, c, slab_block(c), line_block(c))

        @pl.when(c == 0)
        def _():
            for load in loads:
                load.start()

    def filter_rows(c):
        for j in range(PAIR):
            alpha_load(c + j).wait()
        loop(PAIR * PART, lambda z: row_table(c * PART + z))
        mask_lines(c, lambda n: alpha_v[levels(c), :, tile_span(n)].reshape(PAIR * LINES, TILE))
        for first in range(0, TILES, WIDE):
            last = first + WIDE

            @pl.when(c == 0)
            def _():
                for n in range(first, last):
                    rowf_load(n).wait()

            table = jnp.concatenate(
                [
                    rowf[k, tile_span(d), first * TILE : last * TILE]
                    for d in range(last)
                    for k in range(CLASSES)
                ],
                axis=0,
            )
            total = dot(masked[:, : last * CLASSES * TILE], table).astype(BF16)
            for j in range(2 * WIDE):
                s = 2 * first + j
                slabs[pl.ds(c, PAIR), s] = total[:, j * LANES : (j + 1) * LANES].reshape(
                    PAIR, PART, ROWS, LANES
                )

                @pl.when(jnp.logical_and(c == 0, g != s))
                def _():
                    send(0, c, slab_block(c), line_block(c), s)

    def column_pass(c, source, table, upper):
        whole = jnp.concatenate(
            [source[c, :, j].reshape(NY, LANES) for j in range(PART)], axis=1
        )
        kind = jnp.concatenate([col_ref[pl.ds(c * PART + j, 1), :] for j in range(PART)], axis=1)
        kind = jnp.broadcast_to(kind, (NY // 2, PART * LANES))

        def pick(products):
            return jnp.where(kind == 0, products[0], jnp.where(kind == 1, products[1], products[2]))

        def product(rows, deep):
            stacked = jnp.concatenate([table[k, rows, deep] for k in range(CLASSES)], axis=0)
            total = dot(stacked, whole[deep])
            count = total.shape[0] // CLASSES
            return [total[k * count : (k + 1) * count] for k in range(CLASSES)]

        half = NY // 2
        low = slice(0, half)
        high = slice(half, NY)
        both = slice(0, NY)
        wide = product(both, high if upper else low)
        narrow = product(low if upper else high, low if upper else high)
        first = pick([block[low] for block in wide])
        second = pick([block[high] for block in wide])
        if upper:
            first += pick(narrow)
        else:
            second += pick(narrow)
        for j in range(PART):
            side = slice(j * LANES, (j + 1) * LANES)
            for n, total in enumerate((first, second)):
                filtered[c, n * GROUP // 2 : (n + 1) * GROUP // 2, j] = (
                    total[:, side].astype(BF16).reshape(GROUP // 2, ROWS, LANES)
                )

    def level_pass(c, table, source, target, deep):
        for chunk in range(CHUNKS):

            @pl.when(c == chunk)
            def _(chunks=deep(chunk), rows=slice(chunk * LINES, (chunk + 1) * LINES)):
                held = slice(chunks[0], chunks[-1] + 1)
                span = slice(chunks[0] * LINES, (chunks[-1] + 1) * LINES)

                def some(i):
                    block = jnp.concatenate(
                        [source[held, 4 * i + j].reshape(-1, LANES) for j in range(4)], axis=1
                    )
                    total = dot(table[rows, span], block).astype(BF16)
                    for j in range(4):
                        target(
                            4 * i + j,
                            total[:, j * LANES : (j + 1) * LANES].reshape(PART, ROWS, LANES),
                        )

                loop(GROUP // 4, some)

    def column_filter(c):
        lines_came(0, c)
        column_pass(c, lines, colt, False)

        def keep(s, block):
            local_s[c, s] = block

            @pl.when(s != g)
            def _():
                send(1, c, own_block(c), local_block(c), s)

        level_pass(c, down, filtered, keep, lambda chunk: range(chunk + 1))
        local_r[c, g] = local_s[c, g]

    def core_copy(c, part_of):
        return remote(
            core_s.at[c, part_of], core_r.at[c, part_of], core_ss.at[c], core_rs.at[c], sibling, g
        )

    def xin_slab(way):
        return 2 * around(x, way, 2) + way

    def xone_slab(way):
        return 2 * around(x, way) + 1 - way

    def xtwo_slab(way):
        return 2 * around(x, way) + way

    def x_copy(src, dst, sem, way):
        return remote(src, dst, x_ss, sem, x_peer(way), g)

    def y_copy(c):
        return pltpu.make_async_remote_copy(
            src_ref=y_s.at[c],
            dst_ref=y_r.at[c],
            send_sem=yr_ss,
            recv_sem=yr_rs.at[c],
            device_id=(across, g),
            device_id_type=MESH,
        )

    def term(t, c, s):
        return pert_v[t, part(c), :, lane(s)] * local_r[c, s]

    def sum_core(c):
        local_came(1, c)

        @pl.when(c == 0)
        def _():
            loads[1].wait()
            loads[2].wait()

        def one(s):
            core_s[c, s] = term(1 - core, c, s)

        for first in range(0, GROUP, GROUP // 2):
            loop(GROUP // 2, lambda s: one(first + s))
            core_copy(c, pl.ds(first, GROUP // 2)).start()

    def sum_x(c):
        came(core_rs.at[c], core_r.at[c])

        def add(s):
            core_r[c, s] = term(core, c, s) + core_r[c, s]

        for way in range(2):
            s = xin_slab(way)
            add(s)
            x_copy(core_r.at[c, s], x_in.at[c, way], xin_rs.at[c], way).start()
        for way in range(2):
            s = xone_slab(way)
            add(s)
            x_copy(core_r.at[c, s], x_got.at[c, 0, way], xgot_rs.at[c], way).start()
        for way in range(2):
            add(xtwo_slab(way))
        for j in range(2):
            add(2 * x + j)

    def add_x(c):
        came(xin_rs.at[c], x_in.at[c])
        for way in range(2):
            slab = xtwo_slab(way)
            x_in[c, way] = x_in[c, way] + core_r[c, slab]
            x_copy(x_in.at[c, way], x_got.at[c, 1, way], xgot_rs.at[c], way).start()

    def sum_y(c):
        came(xgot_rs.at[c], x_got.at[c])
        for j in range(2):
            total = core_r[c, 2 * x + j].astype(F32) + x_got[c, 1, j].astype(F32)
            y_s[c, j] = (total + x_got[c, 0, 1 - j].astype(F32)).astype(BF16)
        y_copy(c).start()

    def give(rs, t, c, s, member):
        return remote(inc.at[t, c, s], inc.at[t, c, s], give_ss, rs, member, g)

    def give_core(c, owner):
        pair = inc.at[core, c, pl.ds(2 * owner, 2)]
        remote(pair, pair, give_ss, ca_rs.at[c], sibling, g).start()

    def finish(c):
        y_copy(c).wait_recv()
        for j in range(2):
            total = y_s[c, j].astype(F32) + y_r[c, j].astype(F32)
            inc[core, c, 2 * x + j] = total.astype(BF16)
        pair = inc.at[core, c, pl.ds(2 * x, 2)]
        for way in range(2):
            remote(pair, pair, give_ss, xa_rs.at[c], x_peer(way), g).start()
        give_core(c, x)

    def gather_x(c):
        came(xa_rs.at[c], inc.at[core, c, pl.ds(0, 4)])
        for way in range(2):
            slab = 2 * around(x, 1 - way) + way
            give(xf_rs.at[c], core, c, slab, x_peer(way)).start()
        for way in range(2):
            give_core(c, around(x, way))

    def gather_far(c):
        came(xf_rs.at[c], inc.at[core, c, pl.ds(0, 2)])
        give_core(c, around(x, 0, 2))

    def weigh(c):
        def one(s):
            total = None
            for t in range(2):
                block = inc[t, c, s]
                misfit = weight_v[t, part(c)] * (block - innov_v[t, part(c), :, lane(s)])
                increment[t, part(c), :, lane(s)] = block
                share = pert_v[t, part(c), :, lane(s)] * misfit
                total = share if total is None else total + share
            core_s[c, s] = total

        left(core_ss.at[c], core_s.at[c])
        came(ca_rs.at[c], inc.at[1 - core, c])
        for peer in peers():
            one(peer)
            send(2, c, weighted_block(c), line_block(c), peer)
        one(g)
        lines[c, g] = core_s[c, g]

    def column_adjoint(c):
        lines_came(2, c)

        def keep(s, block):
            local_s[c, s] = block

        level_pass(c, back, lines, keep, lambda chunk: range(chunk, CHUNKS))
        column_pass(c, local_s, colf, True)
        local_r[c, g] = filtered[c, g]
        exchange(3, c, filtered_block(c), local_block(c))

    def row_adjoint(c):
        local_came(3, c)

        @pl.when(lax.rem(c, PAIR) == 0)
        def _():
            adjoin_rows(c)

    def adjoin_rows(c):
        mask_lines(
            c,
            lambda n: jnp.concatenate(
                [
                    local_r[pl.ds(c, PAIR), 2 * n + j].reshape(PAIR * LINES, LANES)
                    for j in range(2)
                ],
                axis=1,
            ),
        )
        for n in range(TILES):
            side = tile_span(n)
            table = jnp.concatenate(
                [rowf[k, tile_span(d), side] for d in range(n, TILES) for k in range(CLASSES)],
                axis=0,
            )
            total = dot(masked[:, n * CLASSES * TILE :], table)
            alpha = alpha_v[levels(c), :, side].reshape(PAIR * LINES, TILE).astype(F32)
            gradient[levels(c), :, side] = (
                (alpha + total).astype(BF16).reshape(PAIR * PART, ROWS, TILE)
            )


    pl.semaphore_wait(barrier, GROUP + 3)
    for c in range(1, CHUNKS):
        alpha_load(c).start()

    def at(step, offset, stage):
        chunk = step - offset

        @pl.when(jnp.logical_and(chunk >= 0, chunk < CHUNKS))
        def _():
            stage(chunk)

    def forward(step):
        @pl.when(jnp.logical_and(step >= CHUNKS + 1, step < CHUNKS + 1 + CLASSES))
        def _():
            turn_rows(step - CHUNKS - 1)

        @pl.when(step == 4)
        def _():
            adjoint_tables()

        at(step, 4, sum_x)

        @pl.when(step == 2)
        def _():
            column_tables()

        at(step, 2, column_filter)
        at(step, 7, gather_x)
        at(step, 6, finish)
        at(step, 8, weigh)
        at(step, 3, sum_core)
        at(step, 5, sum_y)
        at(step, 7, gather_far)
        at(step, 4, add_x)
        at(step, 0, row_filter)

    loop(CHUNKS + 8, forward)

    exchange_left(1)

    def backward(step):
        at(step, 0, lambda c: column_adjoint(CHUNKS - 1 - c))
        at(step, 2, lambda c: row_adjoint(CHUNKS - 1 - c))

    loop(CHUNKS + 2, backward)

    for phase in (0, 2, 3):
        exchange_left(phase)
    left(x_ss, core_r.at[pl.ds(0, 3)])
    left(yr_ss, y_s)
    left(give_ss, pert_v.at[:, pl.ds(0, LEVELS - 2)])


def on_device(alpha, pert, innov, weight, row_class, col_class, rowf, colf, level):
    any_spec = pl.BlockSpec(memory_space=pl.ANY)
    vmem_spec = pl.BlockSpec(memory_space=pltpu.VMEM)
    dma = pltpu.SemaphoreType.DMA
    block = (PART, ROWS, LANES)
    slab = (CHUNKS, GROUP) + block
    scratch = [
        pltpu.VMEM((LEVELS, ROWS, NX), BF16),
        pltpu.VMEM((2, LEVELS, ROWS, NX), BF16),
        pltpu.VMEM((2, LEVELS, ROWS, NX), BF16),
        pltpu.VMEM((CLASSES, NX, NX), BF16),
        pltpu.VMEM((CLASSES, NY, NY), BF16),
        pltpu.VMEM((CLASSES, NY, NY), BF16),
        pltpu.VMEM((LEVELS * ROWS, LEVELS * ROWS), BF16),
        pltpu.VMEM((LEVELS * ROWS, LEVELS * ROWS), BF16),
        pltpu.VMEM((CLASSES, LEVELS * ROWS, LANES), BF16),
        pltpu.VMEM((2, LEVELS, ROWS, LANES), BF16),
        pltpu.VMEM((PAIR * LINES, CLASSES * NX), BF16),
        pltpu.VMEM(slab, BF16),
        pltpu.VMEM(slab, BF16),
        pltpu.VMEM(slab, BF16),
        pltpu.VMEM(slab, BF16),
        pltpu.VMEM(slab, BF16),
        pltpu.VMEM(slab, BF16),
        pltpu.VMEM(slab, BF16),
        pltpu.VMEM((CHUNKS, 2) + block, BF16),
        pltpu.VMEM((CHUNKS, 2, 2) + block, BF16),
        pltpu.VMEM((CHUNKS, 2) + block, BF16),
        pltpu.VMEM((CHUNKS, 2) + block, BF16),
        pltpu.VMEM((2,) + slab, BF16),
        dma((CHUNKS,)),
        dma((NX // TILE,)),
        dma((3,)),
        dma,
        dma((4,)),
        dma((4, CHUNKS)),
        dma((CHUNKS,)),
        dma((CHUNKS,)),
        dma,
        dma((CHUNKS,)),
        dma((CHUNKS,)),
        dma,
        dma((CHUNKS,)),
        dma,
        dma((CHUNKS,)),
        dma((CHUNKS,)),
        dma((CHUNKS,)),
    ]
    gradient, increment = pl.pallas_call(
        kernel,
        out_shape=(
            pltpu.VMEM((LEVELS, ROWS, NX), BF16),
            pltpu.VMEM((2, LEVELS, ROWS, NX), BF16),
        ),
        in_specs=[any_spec] * 3 + [vmem_spec] * 3 + [any_spec] * 2 + [vmem_spec],
        out_specs=(vmem_spec, vmem_spec),
        scratch_shapes=scratch,
        compiler_params=pltpu.CompilerParams(
            collective_id=0, has_side_effects=True, vmem_limit_bytes=56 * 1024 * 1024
        ),
    )(alpha[0], pert[0], innov, weight, row_class, col_class, rowf, colf, level)
    return gradient[None], increment


def solution(mesh):
    return jax.shard_map(
        on_device,
        mesh=mesh,
        in_specs=(
            P("member", None, "grid", None),
            P("member", None, None, "grid", None),
            P(None, None, "grid", None),
            P(None, None, "grid"),
            P(None, "grid"),
            P(None, "grid"),
            P(),
            P(),
            P(),
        ),
        out_specs=(P("member", None, "grid", None), P(None, None, "grid", None)),
        check_vma=False,
    )
```

```python
import functools

import jax
import jax.numpy as jnp
from jax import lax
from jax.experimental import pallas as pl
from jax.experimental.pallas import tpu as pltpu
from jax.sharding import PartitionSpec as P

MESH = pl.DeviceIdType.MESH
F32 = jnp.float32
BF16 = jnp.bfloat16

CLASSES = 3
LEVELS = 16
GROUP = 8
RING = 4
CHUNKS = 4
PART = LEVELS // CHUNKS
ROWS = 64
ROW_BITS = 6
LANES = 128
NX = GROUP * LANES
NY = GROUP * ROWS
LINES = PART * ROWS
PAIR = 1
TILE = 256
TILES = NX // TILE
WIDE = 2
DEEP = TILE // ROWS


def loop(count, body):
    def step(index, carry):
        body(index)
        return carry

    lax.fori_loop(0, count, step, 0)


def dot(a, b):
    return jnp.dot(a, b, preferred_element_type=F32)


def dot_nt(a, b):
    return lax.dot_general(a, b, (((1,), (1,)), ((), ())), preferred_element_type=F32)


def kernel(
    alpha_h, pert_h, innov_h, weight_ref, row_ref, col_ref, rowf_h, colf_h, level_ref,
    gradient, increment,
    alpha_v, pert_v, innov_v, rowf, colf, colt, down, back, row_hot, weight_v, masked,
    slabs, lines, filtered, local_s, local_r, core_s, core_r, x_in, x_got, y_s, y_r, inc,
    alpha_sem, rowf_sem, load_sem, out_sem, a2a_ss, a2a_rs, core_ss, core_rs,
    x_ss, xin_rs, xgot_rs, yr_ss, yr_rs, give_ss, xa_rs, xf_rs, ca_rs,
):
    m = lax.axis_index("member")
    g = lax.axis_index("grid")
    y_hi = m // (2 * RING)
    x = lax.rem(m // 2, RING)
    core = lax.rem(m, 2)
    sibling = m + 1 - 2 * core
    across = m + 2 * RING - 4 * RING * y_hi

    def around(position, way, steps=1):
        return lax.rem(position + (steps if way == 0 else RING - steps), RING)

    def x_peer(way):
        return y_hi * (2 * RING) + around(x, way) * 2 + core

    def lane(s):
        return pl.ds(pl.multiple_of(s * LANES, LANES), LANES)

    def slab_rows(s):
        return pl.ds(pl.multiple_of(s * ROWS, ROWS), ROWS)

    def part(c):
        return pl.ds(c * PART, PART)

    barrier = pltpu.get_barrier_semaphore()

    def greet(partner):
        pl.semaphore_signal(barrier, inc=1, device_id=partner, device_id_type=MESH)

    loop(GROUP - 1, lambda step: greet((m, lax.rem(g + step + 1, GROUP))))
    for member in (x_peer(0), x_peer(1), sibling, across):
        greet((member, g))

    def alpha_load(c):
        return pltpu.make_async_copy(alpha_h.at[part(c)], alpha_v.at[part(c)], alpha_sem.at[c])

    def rowf_load(n):
        depth = (n // WIDE + 1) * WIDE * TILE
        where = (slice(None), slice(0, depth), slice(n * TILE, (n + 1) * TILE))
        return pltpu.make_async_copy(rowf_h.at[where], rowf.at[where], rowf_sem.at[n])

    alpha_load(0).start()
    for n in range(NX // TILE):
        rowf_load(n).start()
    loads = [
        pltpu.make_async_copy(src, dst, load_sem.at[i])
        for i, (src, dst) in enumerate(((colf_h, colf), (pert_h, pert_v), (innov_h, innov_v)))
    ]

    diagonal = lax.broadcasted_iota(jnp.int32, (ROWS, ROWS), 0) == lax.broadcasted_iota(
        jnp.int32, (ROWS, ROWS), 1
    )

    def upright(line):
        spread = jnp.where(diagonal, jnp.broadcast_to(line, (ROWS, ROWS)), 0.0)
        return jnp.broadcast_to(jnp.sum(spread, axis=1, keepdims=True), (ROWS, LANES))

    def row_table(z):
        column = upright(row_ref[pl.ds(z, 1), :].astype(F32))
        for c in range(CLASSES):
            row_hot[c, slab_rows(z), :] = jnp.where(column == c, 1.0, 0.0).astype(BF16)

    def tile_span(n):
        return slice(n * TILE, (n + 1) * TILE)

    def iota(shape, axis):
        return lax.broadcasted_iota(jnp.int32, shape, axis)

    def level_table(table, product):
        wide = (LEVELS, LEVELS * ROWS)
        spread = jnp.where(iota(wide, 0) == iota(wide, 1) >> ROW_BITS, 1.0, 0.0).astype(BF16)
        tall = (TILE, LEVELS * ROWS)
        same = (iota(tall, 0) & (ROWS - 1)) == (iota(tall, 1) & (ROWS - 1))
        level = level_ref[...]
        for b in range(LEVELS * ROWS // TILE):
            short = (TILE, LEVELS)
            spot = (iota(short, 0) >> ROW_BITS) + b * DEEP
            pick = jnp.where(spot == iota(short, 1), 1.0, 0.0).astype(BF16)
            table[b * TILE : (b + 1) * TILE, :] = jnp.where(
                same, dot(product(pick, level).astype(BF16), spread), 0.0
            ).astype(BF16)

    def column_tables():
        level_table(down, dot_nt)
        loads[0].wait()
        unit = jnp.where(iota((NY, NY), 0) == iota((NY, NY), 1), 1.0, 0.0).astype(BF16)

        def turn(c):
            colt[c] = dot_nt(unit, colf[c]).astype(BF16)

        loop(CLASSES, turn)

    def turn_rows(k):
        unit = jnp.where(iota((TILE, TILE), 0) == iota((TILE, TILE), 1), 1.0, 0.0).astype(BF16)
        for r in range(TILES):
            for d in range(r, TILES):
                rowf[k, tile_span(d), tile_span(r)] = dot_nt(
                    unit, rowf[k, tile_span(r), tile_span(d)]
                ).astype(BF16)

    def adjoint_tables():
        def weight_table(z):
            for t in range(2):
                weight_v[t, z] = upright(weight_ref[t, pl.ds(z, 1), :]).astype(BF16)

        loop(LEVELS, weight_table)
        level_table(back, dot)

    def remote(src, dst, ss, rs, member, group):
        return pltpu.make_async_remote_copy(
            src_ref=src, dst_ref=dst, send_sem=ss, recv_sem=rs,
            device_id=(member, group), device_id_type=MESH,
        )

    z_at = g // 2
    y_lo = lax.rem(g, 2)

    def send(phase, c, src, dst, peer):
        remote(src(peer), dst(g), a2a_ss.at[phase], a2a_rs.at[phase, c], m, peer).start()

    def peers():
        for up, side in ((2, 0), (1, 0), (3, 0), (2, 1), (1, 1), (3, 1), (0, 1)):
            yield lax.rem(z_at + up, RING) * 2 + (y_lo if side == 0 else 1 - y_lo)

    def exchange(phase, c, src, dst):
        for peer in peers():
            send(phase, c, src, dst, peer)

    def came(sem, view):
        remote(view, view, out_sem, sem, sibling, g).wait_recv()

    def left(sem, view):
        remote(view, view, sem, out_sem, sibling, g).wait_send()

    def lines_came(phase, c):
        came(a2a_rs.at[phase, c], lines.at[c, pl.ds(0, GROUP - 1)])

    def local_came(phase, c):
        came(a2a_rs.at[phase, c], local_r.at[c, pl.ds(0, GROUP - 1)])

    def exchange_left(phase):
        left(a2a_ss.at[phase], lines.at[:, pl.ds(0, GROUP - 1)])

    def line_block(c):
        return lambda s: lines.at[c, s]

    def filtered_block(c):
        return lambda s: filtered.at[c, s]

    def weighted_block(c):
        return lambda s: core_s.at[c, s]

    def slab_block(c):
        return lambda s: slabs.at[c, s]

    def local_block(c):
        return lambda s: local_r.at[c, s]

    def own_block(c):
        return lambda s: local_s.at[c, s]

    def mask_lines(c, source):
        span = pl.ds(pl.multiple_of(c * LINES, LINES), PAIR * LINES)
        hots = [row_hot[k, span, :] for k in range(CLASSES)]
        for n in range(TILES):
            tile = source(n)
            for k in range(CLASSES):
                at_lane = (n * CLASSES + k) * TILE
                masked[:, at_lane : at_lane + TILE] = tile * jnp.concatenate([hots[k]] * 2, axis=1)

    def levels(c):
        return pl.ds(c * PART, PAIR * PART)

    def row_filter(c):
        @pl.when(lax.rem(c, PAIR) == 0)
        def _():
            filter_rows(c)

        lines[c, g] = slabs[c, g]

        @pl.when(c > 0)
        def _():
            exchange(0, c, slab_block(c), line_block(c))

        @pl.when(c == 0)
        def _():
            for load in loads:
                load.start()

    def filter_rows(c):
        for j in range(PAIR):
            alpha_load(c + j).wait()
        loop(PAIR * PART, lambda z: row_table(c * PART + z))
        mask_lines(c, lambda n: alpha_v[levels(c), :, tile_span(n)].reshape(PAIR * LINES, TILE))
        for first in range(0, TILES, WIDE):
            last = first + WIDE

            @pl.when(c == 0)
            def _():
                for n in range(first, last):
                    rowf_load(n).wait()

            table = jnp.concatenate(
                [
                    rowf[k, tile_span(d), first * TILE : last * TILE]
                    for d in range(last)
                    for k in range(CLASSES)
                ],
                axis=0,
            )
            total = dot(masked[:, : last * CLASSES * TILE], table).astype(BF16)
            for j in range(2 * WIDE):
                s = 2 * first + j
                slabs[pl.ds(c, PAIR), s] = total[:, j * LANES : (j + 1) * LANES].reshape(
                    PAIR, PART, ROWS, LANES
                )

                @pl.when(jnp.logical_and(c == 0, g != s))
                def _():
                    send(0, c, slab_block(c), line_block(c), s)

    def column_pass(c, source, table, upper):
        whole = jnp.concatenate(
            [source[c, :, j].reshape(NY, LANES) for j in range(PART)], axis=1
        )
        kind = jnp.concatenate([col_ref[pl.ds(c * PART + j, 1), :] for j in range(PART)], axis=1)
        kind = jnp.broadcast_to(kind, (NY // 2, PART * LANES))

        def pick(products):
            return jnp.where(kind == 0, products[0], jnp.where(kind == 1, products[1], products[2]))

        def product(rows, deep):
            stacked = jnp.concatenate([table[k, rows, deep] for k in range(CLASSES)], axis=0)
            total = dot(stacked, whole[deep])
            count = total.shape[0] // CLASSES
            return [total[k * count : (k + 1) * count] for k in range(CLASSES)]

        half = NY // 2
        low = slice(0, half)
        high = slice(half, NY)
        both = slice(0, NY)
        wide = product(both, high if upper else low)
        narrow = product(low if upper else high, low if upper else high)
        first = pick([block[low] for block in wide])
        second = pick([block[high] for block in wide])
        if upper:
            first += pick(narrow)
        else:
            second += pick(narrow)
        for j in range(PART):
            side = slice(j * LANES, (j + 1) * LANES)
            for n, total in enumerate((first, second)):
                filtered[c, n * GROUP // 2 : (n + 1) * GROUP // 2, j] = (
                    total[:, side].astype(BF16).reshape(GROUP // 2, ROWS, LANES)
                )

    def level_pass(c, table, source, target, deep):
        for chunk in range(CHUNKS):

            @pl.when(c == chunk)
            def _(chunks=deep(chunk), rows=slice(chunk * LINES, (chunk + 1) * LINES)):
                held = slice(chunks[0], chunks[-1] + 1)
                span = slice(chunks[0] * LINES, (chunks[-1] + 1) * LINES)

                def some(i):
                    block = jnp.concatenate(
                        [source[held, 4 * i + j].reshape(-1, LANES) for j in range(4)], axis=1
                    )
                    total = dot(table[rows, span], block).astype(BF16)
                    for j in range(4):
                        target(
                            4 * i + j,
                            total[:, j * LANES : (j + 1) * LANES].reshape(PART, ROWS, LANES),
                        )

                loop(GROUP // 4, some)

    def column_filter(c):
        lines_came(0, c)
        column_pass(c, lines, colt, False)

        def keep(s, block):
            local_s[c, s] = block

            @pl.when(s != g)
            def _():
                send(1, c, own_block(c), local_block(c), s)

        level_pass(c, down, filtered, keep, lambda chunk: range(chunk + 1))
        local_r[c, g] = local_s[c, g]

    def core_copy(c, part_of):
        return remote(
            core_s.at[c, part_of], core_r.at[c, part_of], core_ss.at[c], core_rs.at[c], sibling, g
        )

    def xin_slab(way):
        return 2 * around(x, way, 2) + way

    def xone_slab(way):
        return 2 * around(x, way) + 1 - way

    def xtwo_slab(way):
        return 2 * around(x, way) + way

    def x_copy(src, dst, sem, way):
        return remote(src, dst, x_ss, sem, x_peer(way), g)

    def y_copy(c):
        return pltpu.make_async_remote_copy(
            src_ref=y_s.at[c],
            dst_ref=y_r.at[c],
            send_sem=yr_ss,
            recv_sem=yr_rs.at[c],
            device_id=(across, g),
            device_id_type=MESH,
        )

    def term(t, c, s):
        return pert_v[t, part(c), :, lane(s)] * local_r[c, s]

    def sum_core(c):
        local_came(1, c)

        @pl.when(c == 0)
        def _():
            loads[1].wait()
            loads[2].wait()

        def one(s):
            core_s[c, s] = term(1 - core, c, s)

        for first in range(0, GROUP, GROUP // 2):
            loop(GROUP // 2, lambda s: one(first + s))
            core_copy(c, pl.ds(first, GROUP // 2)).start()

    def sum_x(c):
        came(core_rs.at[c], core_r.at[c])

        def add(s):
            core_r[c, s] = term(core, c, s) + core_r[c, s]

        for way in range(2):
            s = xin_slab(way)
            add(s)
            x_copy(core_r.at[c, s], x_in.at[c, way], xin_rs.at[c], way).start()
        for way in range(2):
            s = xone_slab(way)
            add(s)
            x_copy(core_r.at[c, s], x_got.at[c, 0, way], xgot_rs.at[c], way).start()
        for way in range(2):
            add(xtwo_slab(way))
        for j in range(2):
            add(2 * x + j)

    def add_x(c):
        came(xin_rs.at[c], x_in.at[c])
        for way in range(2):
            slab = xtwo_slab(way)
            x_in[c, way] = x_in[c, way] + core_r[c, slab]
            x_copy(x_in.at[c, way], x_got.at[c, 1, way], xgot_rs.at[c], way).start()

    def sum_y(c):
        came(xgot_rs.at[c], x_got.at[c])
        for j in range(2):
            total = core_r[c, 2 * x + j].astype(F32) + x_got[c, 1, j].astype(F32)
            y_s[c, j] = (total + x_got[c, 0, 1 - j].astype(F32)).astype(BF16)
        y_copy(c).start()

    def give(rs, t, c, s, member):
        return remote(inc.at[t, c, s], inc.at[t, c, s], give_ss, rs, member, g)

    def give_core(c, owner):
        pair = inc.at[core, c, pl.ds(2 * owner, 2)]
        remote(pair, pair, give_ss, ca_rs.at[c], sibling, g).start()

    def finish(c):
        y_copy(c).wait_recv()
        for j in range(2):
            total = y_s[c, j].astype(F32) + y_r[c, j].astype(F32)
            inc[core, c, 2 * x + j] = total.astype(BF16)
        pair = inc.at[core, c, pl.ds(2 * x, 2)]
        for way in range(2):
            remote(pair, pair, give_ss, xa_rs.at[c], x_peer(way), g).start()
        give_core(c, x)

    def gather_x(c):
        came(xa_rs.at[c], inc.at[core, c, pl.ds(0, 4)])
        for way in range(2):
            slab = 2 * around(x, 1 - way) + way
            give(xf_rs.at[c], core, c, slab, x_peer(way)).start()
        for way in range(2):
            give_core(c, around(x, way))

    def gather_far(c):
        came(xf_rs.at[c], inc.at[core, c, pl.ds(0, 2)])
        give_core(c, around(x, 0, 2))

    def weigh(c):
        def one(s):
            total = None
            for t in range(2):
                block = inc[t, c, s]
                misfit = weight_v[t, part(c)] * (block - innov_v[t, part(c), :, lane(s)])
                increment[t, part(c), :, lane(s)] = block
                share = pert_v[t, part(c), :, lane(s)] * misfit
                total = share if total is None else total + share
            core_s[c, s] = total

        left(core_ss.at[c], core_s.at[c])
        came(ca_rs.at[c], inc.at[1 - core, c])
        for peer in peers():
            one(peer)
            send(2, c, weighted_block(c), line_block(c), peer)
        one(g)
        lines[c, g] = core_s[c, g]

    def column_adjoint(c):
        lines_came(2, c)

        def keep(s, block):
            local_s[c, s] = block

        level_pass(c, back, lines, keep, lambda chunk: range(chunk, CHUNKS))
        column_pass(c, local_s, colf, True)
        local_r[c, g] = filtered[c, g]
        exchange(3, c, filtered_block(c), local_block(c))

    def row_adjoint(c):
        local_came(3, c)

        @pl.when(lax.rem(c, PAIR) == 0)
        def _():
            adjoin_rows(c)

    def adjoin_rows(c):
        mask_lines(
            c,
            lambda n: jnp.concatenate(
                [
                    local_r[pl.ds(c, PAIR), 2 * n + j].reshape(PAIR * LINES, LANES)
                    for j in range(2)
                ],
                axis=1,
            ),
        )
        for n in range(TILES):
            side = tile_span(n)
            table = jnp.concatenate(
                [rowf[k, tile_span(d), side] for d in range(n, TILES) for k in range(CLASSES)],
                axis=0,
            )
            total = dot(masked[:, n * CLASSES * TILE :], table)
            alpha = alpha_v[levels(c), :, side].reshape(PAIR * LINES, TILE).astype(F32)
            gradient[levels(c), :, side] = (
                (alpha + total).astype(BF16).reshape(PAIR * PART, ROWS, TILE)
            )


    pl.semaphore_wait(barrier, GROUP + 3)
    for c in range(1, CHUNKS):
        alpha_load(c).start()

    def at(step, offset, stage):
        chunk = step - offset

        @pl.when(jnp.logical_and(chunk >= 0, chunk < CHUNKS))
        def _():
            stage(chunk)

    def forward(step):
        @pl.when(jnp.logical_and(step >= CHUNKS + 1, step < CHUNKS + 1 + CLASSES))
        def _():
            turn_rows(step - CHUNKS - 1)

        @pl.when(step == 4)
        def _():
            adjoint_tables()

        at(step, 4, sum_core)
        at(step, 6, finish)
        at(step, 7, gather_far)
        at(step, 5, sum_y)
        at(step, 1, row_filter)
        at(step, 4, sum_x)
        at(step, 7, weigh)

        @pl.when(step == 2)
        def _():
            column_tables()

        at(step, 2, column_filter)
        at(step, 6, gather_x)
        at(step, 4, add_x)

    loop(CHUNKS + 7, forward)

    exchange_left(1)

    def backward(step):
        at(step, 0, lambda c: column_adjoint(CHUNKS - 1 - c))
        at(step, 2, lambda c: row_adjoint(CHUNKS - 1 - c))

    loop(CHUNKS + 2, backward)

    for phase in (0, 2, 3):
        exchange_left(phase)
    left(x_ss, core_r.at[pl.ds(0, 3)])
    left(yr_ss, y_s)
    left(give_ss, pert_v.at[:, pl.ds(0, LEVELS - 2)])


def on_device(alpha, pert, innov, weight, row_class, col_class, rowf, colf, level):
    any_spec = pl.BlockSpec(memory_space=pl.ANY)
    vmem_spec = pl.BlockSpec(memory_space=pltpu.VMEM)
    dma = pltpu.SemaphoreType.DMA
    block = (PART, ROWS, LANES)
    slab = (CHUNKS, GROUP) + block
    scratch = [
        pltpu.VMEM((LEVELS, ROWS, NX), BF16),
        pltpu.VMEM((2, LEVELS, ROWS, NX), BF16),
        pltpu.VMEM((2, LEVELS, ROWS, NX), BF16),
        pltpu.VMEM((CLASSES, NX, NX), BF16),
        pltpu.VMEM((CLASSES, NY, NY), BF16),
        pltpu.VMEM((CLASSES, NY, NY), BF16),
        pltpu.VMEM((LEVELS * ROWS, LEVELS * ROWS), BF16),
        pltpu.VMEM((LEVELS * ROWS, LEVELS * ROWS), BF16),
        pltpu.VMEM((CLASSES, LEVELS * ROWS, LANES), BF16),
        pltpu.VMEM((2, LEVELS, ROWS, LANES), BF16),
        pltpu.VMEM((PAIR * LINES, CLASSES * NX), BF16),
        pltpu.VMEM(slab, BF16),
        pltpu.VMEM(slab, BF16),
        pltpu.VMEM(slab, BF16),
        pltpu.VMEM(slab, BF16),
        pltpu.VMEM(slab, BF16),
        pltpu.VMEM(slab, BF16),
        pltpu.VMEM(slab, BF16),
        pltpu.VMEM((CHUNKS, 2) + block, BF16),
        pltpu.VMEM((CHUNKS, 2, 2) + block, BF16),
        pltpu.VMEM((CHUNKS, 2) + block, BF16),
        pltpu.VMEM((CHUNKS, 2) + block, BF16),
        pltpu.VMEM((2,) + slab, BF16),
        dma((CHUNKS,)),
        dma((NX // TILE,)),
        dma((3,)),
        dma,
        dma((4,)),
        dma((4, CHUNKS)),
        dma((CHUNKS,)),
        dma((CHUNKS,)),
        dma,
        dma((CHUNKS,)),
        dma((CHUNKS,)),
        dma,
        dma((CHUNKS,)),
        dma,
        dma((CHUNKS,)),
        dma((CHUNKS,)),
        dma((CHUNKS,)),
    ]
    gradient, increment = pl.pallas_call(
        kernel,
        out_shape=(
            pltpu.VMEM((LEVELS, ROWS, NX), BF16),
            pltpu.VMEM((2, LEVELS, ROWS, NX), BF16),
        ),
        in_specs=[any_spec] * 3 + [vmem_spec] * 3 + [any_spec] * 2 + [vmem_spec],
        out_specs=(vmem_spec, vmem_spec),
        scratch_shapes=scratch,
        compiler_params=pltpu.CompilerParams(
            collective_id=0, has_side_effects=True, vmem_limit_bytes=56 * 1024 * 1024
        ),
    )(alpha[0], pert[0], innov, weight, row_class, col_class, rowf, colf, level)
    return gradient[None], increment


def solution(mesh):
    return jax.shard_map(
        on_device,
        mesh=mesh,
        in_specs=(
            P("member", None, "grid", None),
            P("member", None, None, "grid", None),
            P(None, None, "grid", None),
            P(None, None, "grid"),
            P(None, "grid"),
            P(None, "grid"),
            P(),
            P(),
            P(),
        ),
        out_specs=(P("member", None, "grid", None), P(None, None, "grid", None)),
        check_vma=False,
    )
```
